32 devices in a mesh: dp: 4 (over x, core), fsdp: 8 (over z, y).
Axes of the slice: x: 2, y: 2, z: 4, core: 2. Of those that a mesh axis runs over, the one named last changes fastest.
Arguments:
- hidden: float32 [32, 128, 2048], P(('dp', 'fsdp')), may hold values from -6 to 6
- cotangent: float32 [32, 128, 2048], P(('dp', 'fsdp')), may hold values from -6 to 6
- groups: int32 [32], P(('dp', 'fsdp')), may hold values from 0 to 7, never falling along the last dimension, each value on 1 to 8 neighbouring positions
- group_weights: float32 [8], replicated, may hold values from 0.5 to 20
- input_weight: bfloat16 [2, 2048, 8192], P(None, ('dp', 'fsdp')), may hold values from -0.125 to 0.125
- select_weight: bfloat16 [2, 4096, 160], P(None, ('dp', 'fsdp')), may hold values from -0.09375 to 0.09375
- rate_weight: bfloat16 [2, 128, 4096], P(None, None, ('dp', 'fsdp')), may hold values from -0.5 to 0.5
- output_weight: bfloat16 [2, 4096, 2048], P(None, ('dp', 'fsdp')), may hold values from -0.375 to 0.375
- norm_gain: bfloat16 [2, 2048], P(None, ('dp', 'fsdp')), may hold values from 0.099609375 to 1.8984375
- conv_taps: bfloat16 [2, 4, 4096], P(None, None, ('dp', 'fsdp')), may hold values from -3 to 3
- conv_shift: bfloat16 [2, 4096], P(None, ('dp', 'fsdp')), may hold values from -3 to 3
- rate_shift: bfloat16 [2, 4096], P(None, ('dp', 'fsdp')), may hold values from -4 to 4
- skip_gain: bfloat16 [2, 4096], P(None, ('dp', 'fsdp')), may hold values from 0.099609375 to 1.8984375
Outputs:
- hidden_out: float32 [32, 128, 2048], P(('dp', 'fsdp'))
- hidden_gradient: float32 [32, 128, 2048], P(('dp', 'fsdp'))
- gradient_input_weight: float32 [2, 2048, 8192], P(None, ('dp', 'fsdp'))
- gradient_select_weight: float32 [2, 4096, 160], P(None, ('dp', 'fsdp'))
- gradient_rate_weight: float32 [2, 128, 4096], P(None, None, ('dp', 'fsdp'))
- gradient_output_weight: float32 [2, 4096, 2048], P(None, ('dp', 'fsdp'))
- gradient_norm_gain: float32 [2, 2048], P(None, ('dp', 'fsdp'))
- gradient_conv_taps: float32 [2, 4, 4096], P(None, None, ('dp', 'fsdp'))
- gradient_conv_shift: float32 [2, 4096], P(None, ('dp', 'fsdp'))
- gradient_rate_shift: float32 [2, 4096], P(None, ('dp', 'fsdp'))
- gradient_skip_gain: float32 [2, 4096], P(None, ('dp', 'fsdp'))
- beta_mean: float32 [2], replicated
- beta_max: float32 [2], replicated
The draws below stay inside these ranges and needn't reach their ends.
Inputs may be any that keep to these rules, and one draw needn't show every extreme that they name: `groups`: the group numbers never fall from one sequence to the next.
All inputs are finite; a program needn't handle non-finite values.
Results may differ from the reference program's by a relative error of at most 0.017.
The reference program's roundings to bfloat16 on the way count: a program that leaves them out, or rounds other values in their place, can miss the bound.
Values may be sent and summed in bfloat16 or wider, within the bound.
A program may use at most 448 MiB of HBM per device.

```python
import math
import jax
import jax.numpy as jnp
import numpy as np
from jax import lax

D = 2048
INNER = 4096
STATE = 16
RANK = 128
CONV = 4
LAYERS = 2
BLOCK = 32
GROUPS = 8
SEQ_LEN = 128
BATCH = 32
SELECT = 160


def draw_group_weights(key, part):
    ladder = jnp.arange(GROUPS).astype(jnp.float32) / (GROUPS - 1)
    jitter = jax.random.uniform(key, (GROUPS,), jnp.float32, 0.8, 1.25)
    return 10.0 ** ladder * jitter


def steps_of(rng, shape, shards, least, largest):
    gain = 1.0
    for dim, parts in shards:
        draws = jax.random.uniform(jax.random.fold_in(jax.random.fold_in(rng, 6), dim), (parts,), jnp.float32, least / len(shards), largest / len(shards))
        gain = gain * jnp.repeat(jnp.exp(draws), shape[dim] // parts).reshape((-1,) + (1,) * (len(shape) - 1 - dim))
    return gain


def split_up(number_of, total, limit, skew):
    weights = [(1 << 20) // math.isqrt(grade ** skew) + 1 for grade in range(2, number_of + 1)]
    spare, given = total - limit - (number_of - 1), [1] * (number_of - 1)
    while spare > 0:
        free = [i for i in range(number_of - 1) if given[i] < limit]
        mass, left = sum([weights[i] for i in free]), spare
        for i in free:
            extra = min(limit - given[i], max(1, left * weights[i] // mass), spare)
            given[i] = given[i] + extra
            spare = spare - extra
    return np.array([limit] + given)


def ragged_sizes(stream_key, count, total, bound, skew):
    if count == 2:
        one = jax.random.randint(stream_key, (), max(1, total - bound), min(bound, total - 1) + 1)
        return jnp.stack([one, total - one])
    sizes = jnp.asarray(split_up(count, total, bound, skew), jnp.int32)
    twos = (count - 1) // 2
    giver, sink = sizes[1:1 + 2 * twos:2], sizes[2:2 + 2 * twos:2]
    slack = jnp.minimum(giver - 1, bound - sink)
    shifted = jax.random.randint(jax.random.fold_in(stream_key, 1), (twos,), 0, 1 << 20) % (slack + 1)
    sizes = sizes.at[1:1 + 2 * twos:2].set(giver - shifted).at[2:2 + 2 * twos:2].set(sink + shifted)
    return sizes[jax.random.permutation(jax.random.fold_in(stream_key, 2), count)]


def normal_values(key, shape, scale, bound, pieces=(), held_as=jnp.bfloat16):
    array = scale * jax.random.normal(key, shape, jnp.float32)
    if pieces:
        array = array * steps_of(key, shape, pieces, -0.22, 0.18)
    return jnp.clip(array, -bound, bound).astype(held_as)


def setup_inputs(seed: int = 0) -> dict:
    keys = jax.random.split(jax.random.key(seed), 14)
    return {
        "hidden": normal_values(keys[0], (BATCH, SEQ_LEN, D), 1.0, 6.0, ((0, 32),), jnp.float32),
        "cotangent": normal_values(keys[1], (BATCH, SEQ_LEN, D), 1.0, 6.0, ((0, 32),), jnp.float32),
        "groups": jnp.searchsorted(jnp.cumsum(ragged_sizes(keys[2], GROUPS, BATCH, 2 * BATCH // GROUPS, 1)), jnp.arange(BATCH), side="right").astype(jnp.int32),
        "group_weights": draw_group_weights(jax.random.fold_in(keys[13], 71), 0),
        "input_weight": normal_values(keys[4], (LAYERS, D, 2 * INNER), D ** -0.5, 0.125, ((1, 32),)),
        "select_weight": normal_values(keys[5], (LAYERS, INNER, SELECT), INNER ** -0.5, 0.09375, ((1, 32),)),
        "rate_weight": normal_values(keys[6], (LAYERS, RANK, INNER), RANK ** -0.5, 0.5, ((2, 32),)),
        "output_weight": normal_values(keys[7], (LAYERS, INNER, D), (INNER // 16) ** -0.5, 0.375, ((1, 32),)),
        "norm_gain": jnp.clip(1.0 + 0.18 * jax.random.normal(keys[8], (LAYERS, D), jnp.float32), 0.099609375, 1.8984375).astype(jnp.bfloat16),
        "conv_taps": normal_values(keys[9], (LAYERS, CONV, INNER), CONV ** -0.5, 3.0, ((2, 32),)),
        "conv_shift": normal_values(keys[10], (LAYERS, INNER), 0.5, 3.0, ((1, 32),)),
        "rate_shift": normal_values(keys[11], (LAYERS, INNER), 1.0, 4.0, ((1, 32),)),
        "skip_gain": jnp.clip(1.0 + 0.18 * jax.random.normal(keys[12], (LAYERS, INNER), jnp.float32), 0.099609375, 1.8984375).astype(jnp.bfloat16),
    }


@jax.custom_vjp
def low(v):
    return lax.optimization_barrier(v.astype(jnp.bfloat16)).astype(jnp.float32)

@jax.custom_vjp
def low_back(v):
    return v

def low_keep(v):
    return (low(v), None)

def low_pass(kept, grad):
    return (grad,)

def back_keep(v):
    return (v, None)

def back_low(kept, grad):
    return (low(grad),)
low.defvjp(low_keep, low_pass)
low_back.defvjp(back_keep, back_low)
eps = 1e-05

def matmul(left, right):
    return jnp.einsum('...k,kn->...n', left, right, precision=lax.Precision.HIGHEST)

def rms_scale(stream_rows, gain_float):
    return stream_rows * lax.rsqrt(lax.optimization_barrier(jnp.mean(jnp.square(stream_rows), axis=-1, keepdims=True)) + eps) * gain_float

def causal_conv(inner_part, taps_float, shift_float):
    length = inner_part.shape[1]
    padded = jnp.pad(inner_part, ((0, 0), (CONV - 1, 0), (0, 0)))
    summed = shift_float + jnp.zeros_like(inner_part)
    for offset in range(CONV):
        summed = summed + taps_float[offset] * padded[:, offset:offset + length]
    return jax.nn.silu(summed)

def block_steps(carried, inputs):
    act_blk, step_blk, key_blk, query_blk = inputs
    outputs = []
    for offset in range(act_blk.shape[1]):
        key_now = key_blk[:, offset, None, :]
        decayed = 1.0 - step_blk[:, offset, :, None] * jnp.square(key_now)
        carried = decayed * carried + (step_blk[:, offset] * act_blk[:, offset])[:, :, None] * key_now
        outputs.append(lax.optimization_barrier(jnp.sum(carried * query_blk[:, offset, None, :], axis=-1)))
    return (carried, jnp.stack(outputs, axis=1))

def recurrence(activated, step_size, keys_part, query_part):
    seq_count, length, channels = activated.shape
    block_count = length // BLOCK

    def regroup(values):
        return jnp.moveaxis(values.reshape(seq_count, block_count, BLOCK, values.shape[-1]), 1, 0)
    initial = jnp.zeros((seq_count, channels, keys_part.shape[-1]), jnp.float32)
    finished, outputs = lax.scan(jax.checkpoint(block_steps), initial, (regroup(activated), regroup(step_size), regroup(keys_part), regroup(query_part)))
    return jnp.moveaxis(outputs, 0, 1).reshape(seq_count, length, channels)

def mixer_core(activated, keys_part, query_part, rate_pre, rate_float, skip_float, gate_part):
    beta_rate = jax.nn.sigmoid(rate_pre + rate_float)
    step_size = beta_rate / (1.0 + beta_rate * lax.optimization_barrier(jnp.sum(jnp.square(keys_part), axis=-1, keepdims=True)))
    scanned = recurrence(activated, step_size, keys_part, query_part)
    return (scanned + skip_float * activated) * jax.nn.silu(gate_part)

def layer_forward(stream_rows, params):
    input_weight, select_weight, rate_weight, output_weight, norm_gain, conv_taps, conv_shift, rate_shift, skip_gain = params
    normed = low(rms_scale(stream_rows, norm_gain))
    entry_rows = low_back(matmul(normed, input_weight))
    activated = low(causal_conv(entry_rows[..., :INNER], conv_taps, conv_shift))
    projected = low_back(matmul(activated, select_weight))
    low_rank = low(projected[..., :RANK])
    rate_pre = low_back(matmul(low_rank, rate_weight))
    beta_rate = jax.nn.sigmoid(rate_pre + rate_shift)
    mixed = low(mixer_core(activated, projected[..., RANK:RANK + STATE], projected[..., RANK + STATE:], rate_pre, rate_shift, skip_gain, entry_rows[..., INNER:]))
    return (stream_rows + low_back(matmul(mixed, output_weight)), (lax.optimization_barrier(jnp.sum(beta_rate, axis=(1, 2))), lax.optimization_barrier(jnp.max(beta_rate, axis=(1, 2)))))

def reference(hidden, cotangent, groups, group_weights, input_weight, select_weight, rate_weight, output_weight, norm_gain, conv_taps, conv_shift, rate_shift, skip_gain):
    weights = tuple((tensor.astype(jnp.float32) for tensor in (input_weight, select_weight, rate_weight, output_weight, norm_gain, conv_taps, conv_shift, rate_shift, skip_gain)))
    labels = jnp.arange(GROUPS).astype(jnp.int32)
    seq_weight = lax.optimization_barrier(jnp.sum(jnp.where(groups[:, None] == labels[None, :], group_weights[None, :], 0.0), axis=1))
    seq_scale = seq_weight / jnp.mean(seq_weight)

    def forward(stream_rows, params):
        sums = []
        peaks = []
        for which_layer in range(LAYERS):
            stream_rows, stats = layer_forward(stream_rows, tuple((tensor[which_layer] for tensor in params)))
            sums.append(stats[0])
            peaks.append(stats[1])
        return (stream_rows, (jnp.stack(sums), jnp.stack(peaks)))

    def per_group(running, inputs):
        grads_run, sum_run, peak_run = running
        hidden_blk, cot_blk, scale_blk = inputs
        outputs, pullback, stats = jax.vjp(forward, hidden_blk, weights, has_aux=True)
        back_hidden, back_params = pullback(cot_blk * scale_blk[:, None, None])
        grads_run = tuple((left + right for left, right in zip(grads_run, back_params)))
        weighted_sum = lax.optimization_barrier(jnp.sum(stats[0] * scale_blk[None, :], axis=1))
        weighted_peak = lax.optimization_barrier(jnp.max(stats[1] * scale_blk[None, :], axis=1))
        return ((grads_run, sum_run + weighted_sum, jnp.maximum(peak_run, weighted_peak)), (outputs, back_hidden))

    def regroup(values):
        return values.reshape((BATCH // 8, 8) + values.shape[1:])
    initial = (tuple((jnp.zeros_like(tensor) for tensor in weights)), jnp.zeros((LAYERS,), jnp.float32), jnp.full((LAYERS,), -1.0, jnp.float32))
    (summed, beta_total, beta_peak), (outputs, back_hidden) = lax.scan(per_group, initial, (regroup(hidden), regroup(cotangent), regroup(seq_scale)))
    beta_mean = beta_total / (BATCH * SEQ_LEN * INNER)
    return (outputs.reshape(hidden.shape), back_hidden.reshape(hidden.shape), summed[0], summed[1], summed[2], summed[3], summed[4], summed[5], summed[6], summed[7], summed[8], beta_mean, beta_peak)
```

```python
import functools

import jax
import jax.numpy as jnp
from jax import lax
from jax.sharding import PartitionSpec as P
import jax.experimental.pallas as pl
import jax.experimental.pallas.tpu as pltpu

INNER = 4096
STATE = 16
RANK = 128
CONV = 4
LAYERS = 2
WAYS = 4
TP = 8
STEPS = 16

eps = 1e-05
MESH = pl.DeviceIdType.MESH
f32 = jnp.float32
bf16 = jnp.bfloat16
VM = pl.BlockSpec(memory_space=pltpu.VMEM)
HB = pl.BlockSpec(memory_space=pl.ANY)


def place():
    dp, fs = lax.axis_index("dp"), lax.axis_index("fsdp")
    return dp // 2, lax.rem(dp, 2), fs // WAYS, lax.rem(fs, WAYS)


def device(x, core, zh, q):
    return (x * 2 + core, zh * WAYS + q)


def remote(src, dst, send, recv, target):
    return pltpu.make_async_remote_copy(
        src_ref=src, dst_ref=dst, send_sem=send, recv_sem=recv, device_id=target, device_id_type=MESH
    )


def greet(targets):
    barrier = pltpu.get_barrier_semaphore()
    for target in targets:
        pl.semaphore_signal(barrier, inc=1, device_id=target, device_id_type=MESH)
    pl.semaphore_wait(barrier, len(targets))


def tp_peers():
    x, core, zh, q = place()
    peers = []
    for dc in (0, 1):
        for dq in (1, 3, 2, 0):
            if dc == 0 and dq == 0:
                continue
            other_core = lax.rem(core + dc, 2)
            to_q, from_q = lax.rem(q + dq, WAYS), lax.rem(q + WAYS - dq, WAYS)
            peers.append(
                (device(x, other_core, zh, to_q), other_core * WAYS + to_q, other_core * WAYS + from_q)
            )
    return peers


def dp_peers(zh_size):
    x, core, zh, q = place()
    side = device(1 - x, core, zh, q)
    far = []
    for dz in range(1, zh_size):
        to_z, from_z = lax.rem(zh + dz, zh_size), lax.rem(zh + zh_size - dz, zh_size)
        far.append((device(x, core, to_z, q), to_z, from_z))
    return side, far


def weights_kernel(
    zh_size, win, wout, mats, small, misc, o_win, o_wout, o_mats, o_small, o_misc,
    tp_send, tp_recv, z_send, z_recv, x_send, x_recv, own_sem,
):
    x, core, zh, q = place()
    me = core * WAYS + q
    peers = tp_peers()
    side, far = dp_peers(zh_size)
    greet([p[0] for p in peers] + [side] + [f[0] for f in far])

    def row(xx, zz, rank):
        return ((xx * 2 + rank // WAYS) * zh_size + zz) * WAYS + lax.rem(rank, WAYS)

    waits = []
    own = []
    for i, (src, dst) in enumerate(
        (
            (win.at[me], o_win.at[row(x, zh, me)]),
            (misc, o_misc.at[row(x, zh, me)]),
            (wout, o_wout.at[x * zh_size + zh]),
            (mats, o_mats.at[x * zh_size + zh]),
            (small, o_small.at[x * zh_size + zh]),
        )
    ):
        copy = pltpu.make_async_copy(src, dst, own_sem.at[i])
        copy.start()
        own.append(copy)
    arrive = []
    for i, (target, rank, source) in enumerate(peers):
        for j, (src, dst) in enumerate(
            ((win.at[rank], o_win.at[row(x, zh, me)]), (misc, o_misc.at[row(x, zh, me)]))
        ):
            copy = remote(src, dst, tp_send.at[i, j], tp_recv.at[i, j], target)
            copy.start()
            arrive.append((copy, source, j))
            waits.append(copy)

    onward = []

    def spread(item, src, view):
        for k, (target, to_z, from_z) in enumerate(far):
            copy = remote(src, view(x, zh), z_send.at[item, k], z_recv.at[item, k], target)
            copy.start()
            waits.append(copy)
            onward.append((copy, item, k, view, from_z))
        copy = remote(src, view(x, zh), x_send.at[item, 0], x_recv.at[item, 0], side)
        copy.start()
        waits.append(copy)

    spread(0, win.at[me], lambda xx, zz: o_win.at[row(xx, zz, me)])
    spread(1, misc, lambda xx, zz: o_misc.at[row(xx, zz, me)])
    spread(2, small, lambda xx, zz: o_small.at[xx * zh_size + zz])
    spread(3, mats, lambda xx, zz: o_mats.at[xx * zh_size + zz])
    recv_done = set()
    item = 4
    for copy, source, j in arrive:
        copy.wait_recv()
        recv_done.add(id(copy))
        out = (o_win, o_misc)[j]
        view = functools.partial(lambda out, source, xx, zz: out.at[row(xx, zz, source)], out, source)
        spread(item, view(x, zh), view)
        item += 1
    spread(item, wout, lambda xx, zz: o_wout.at[xx * zh_size + zz])
    for copy, it, k, view, from_z in onward:
        copy.wait_recv()
        recv_done.add(id(copy))
        again = remote(view(x, from_z), view(x, from_z), x_send.at[it, k + 1], x_recv.at[it, k + 1], side)
        again.start()
        waits.append(again)
    for copy in waits:
        copy.wait_send()
        if id(copy) not in recv_done:
            copy.wait_recv()
    for copy in own:
        copy.wait()


def gather_weights(zh_size, call, win, wout, mats, small, misc):
    groups = 2 * zh_size
    count = groups * TP
    items = 5 + 2 * (TP - 1)
    dma = pltpu.SemaphoreType.DMA
    many = lambda a, n: jax.ShapeDtypeStruct((n,) + a.shape, a.dtype)
    return pl.pallas_call(
        functools.partial(weights_kernel, zh_size),
        out_shape=[
            jax.ShapeDtypeStruct((count,) + win.shape[1:], win.dtype),
            many(wout, groups), many(mats, groups), many(small, groups), many(misc, count),
        ],
        in_specs=[HB] * 5,
        out_specs=[HB] * 5,
        scratch_shapes=[
            dma((TP - 1, 2)), dma((TP - 1, 2)),
            dma((items, max(1, zh_size - 1))), dma((items, max(1, zh_size - 1))),
            dma((items, zh_size)), dma((items, zh_size)), dma((5,)),
        ],
        compiler_params=pltpu.CompilerParams(collective_id=1, has_side_effects=True),
        name="gather_weights",
    )(win, wout, mats, small, misc)


def tp_gather_kernel(x_ref, o_ref, f_send, f_recv, s_send, s_recv, own_sem):
    x, core, zh, q = place()
    sibling = device(x, 1 - core, zh, q)
    far = []
    for dq in (1, 3, 2):
        far.append((device(x, core, zh, lax.rem(q + dq, WAYS)), lax.rem(q + WAYS - dq, WAYS)))
    greet([t for t, _ in far] + [sibling])
    me = core * WAYS + q
    first = []
    for i, (target, _) in enumerate(far):
        copy = remote(x_ref, o_ref.at[me], f_send.at[i], f_recv.at[i], target)
        copy.start()
        first.append(copy)
    near = [remote(x_ref, o_ref.at[me], s_send.at[3], s_recv.at[3], sibling)]
    near[0].start()
    own = pltpu.make_async_copy(x_ref, o_ref.at[me], own_sem)
    own.start()
    for i, (_, source) in enumerate(far):
        first[i].wait_recv()
        slot = core * WAYS + source
        copy = remote(o_ref.at[slot], o_ref.at[slot], s_send.at[i], s_recv.at[i], sibling)
        copy.start()
        near.append(copy)
    for copy in first:
        copy.wait_send()
    for copy in near:
        copy.wait()
    own.wait()


def tp_gather(rows):
    dma = pltpu.SemaphoreType.DMA
    return pl.pallas_call(
        tp_gather_kernel,
        out_shape=jax.ShapeDtypeStruct((TP,) + rows.shape, rows.dtype),
        in_specs=[HB],
        out_specs=HB,
        scratch_shapes=[dma((3,)), dma((3,)), dma((4,)), dma((4,)), dma],
        compiler_params=pltpu.CompilerParams(collective_id=2, has_side_effects=True),
        name="tp_gather",
    )(rows)


def tp_scatter_kernel(p_ref, o_ref, near_buf, far_out, far_in, s_send, s_recv, f_send, f_recv):
    x, core, zh, q = place()
    sibling = device(x, 1 - core, zh, q)
    far = []
    for dq in (1, 3, 2):
        far.append((device(x, core, zh, lax.rem(q + dq, WAYS)), lax.rem(q + dq, WAYS)))
    greet([t for t, _ in far] + [sibling])
    near = []
    for i, to_q in enumerate([t for _, t in far] + [q]):
        copy = remote(
            p_ref.at[(1 - core) * WAYS + to_q], near_buf.at[i], s_send.at[i], s_recv.at[i], sibling
        )
        copy.start()
        near.append(copy)
    first = []
    for i, (target, to_q) in enumerate(far):
        near[i].wait_recv()
        far_out[i] = (
            p_ref[core * WAYS + to_q].astype(f32) + near_buf[i].astype(f32)
        ).astype(bf16)
        copy = remote(far_out.at[i], far_in.at[i], f_send.at[i], f_recv.at[i], target)
        copy.start()
        first.append(copy)
    near[3].wait_recv()
    o_ref[...] = p_ref[core * WAYS + q].astype(f32) + near_buf[3].astype(f32)
    for i in range(3):
        first[i].wait_recv()
        o_ref[...] += far_in[i].astype(f32)
    for copy in near + first:
        copy.wait_send()


def tp_scatter(partial):
    dma = pltpu.SemaphoreType.DMA
    block = partial.shape[1:]
    return pl.pallas_call(
        tp_scatter_kernel,
        out_shape=jax.ShapeDtypeStruct(block, f32),
        in_specs=[VM],
        out_specs=VM,
        scratch_shapes=[
            pltpu.VMEM((4,) + block, bf16), pltpu.VMEM((3,) + block, bf16), pltpu.VMEM((3,) + block, bf16),
            dma((4,)), dma((4,)), dma((3,)), dma((3,)),
        ],
        compiler_params=pltpu.CompilerParams(
            collective_id=3, has_side_effects=True, vmem_limit_bytes=40 * 2**20
        ),
        name="tp_scatter",
    )(partial)


def tp_sum_kernel(p_ref, own_ref, o_ref, all_ref, parts, a_send, a_recv, b_send, b_recv, c_send, c_recv):
    x, core, zh, q = place()
    me = core * WAYS + q
    peers = tp_peers()
    greet([p[0] for p in peers])
    one, two = [], []
    for i, (target, rank, _) in enumerate(peers):
        copy = remote(p_ref.at[rank], parts.at[i], a_send.at[i], a_recv.at[i], target)
        copy.start()
        one.append(copy)
        copy = remote(own_ref, all_ref.at[me], c_send.at[i], c_recv.at[i], target)
        copy.start()
        two.append(copy)
    all_ref[me] = own_ref[...]
    total = p_ref[me]
    for i in range(TP - 1):
        one[i].wait_recv()
        total = total + parts[i]
    o_ref[me] = total
    for i, (target, rank, _) in enumerate(peers):
        copy = remote(o_ref.at[me], o_ref.at[me], b_send.at[i], b_recv.at[i], target)
        copy.start()
        two.append(copy)
    for copy in one:
        copy.wait_send()
    for copy in two:
        copy.wait()


def tp_sum(partial, own):
    dma = pltpu.SemaphoreType.DMA
    return pl.pallas_call(
        tp_sum_kernel,
        out_shape=[
            jax.ShapeDtypeStruct(partial.shape, f32),
            jax.ShapeDtypeStruct((TP,) + own.shape, f32),
        ],
        in_specs=[VM, VM],
        out_specs=[VM, VM],
        scratch_shapes=[pltpu.VMEM((TP - 1,) + partial.shape[1:], f32)] + [dma((TP - 1,))] * 6,
        compiler_params=pltpu.CompilerParams(
            collective_id=4, has_side_effects=True, vmem_limit_bytes=40 * 2**20
        ),
        name="tp_sum",
    )(partial, own)


def gradients_kernel(
    zh_size, win, wout, mats, small, stats, gain, o_win, o_wout, o_mats, o_small, o_stats,
    win_x, wout_x, mats_x, small_x, stats_x, win_s, wout_s, mats_s, small_s, stats_s,
    win_z, wout_z, mats_z, small_z, stats_z, win_t, gain_t, vectors,
    x_send, x_recv, z_send, z_recv, t_send, t_recv, g_send, g_recv,
):
    x, core, zh, q = place()
    me = core * WAYS + q
    peers = tp_peers()
    side, far = dp_peers(zh_size)
    greet([p[0] for p in peers] + [side] + [f[0] for f in far])
    waits = []
    gains = []
    for i, (target, rank, _) in enumerate(peers):
        copy = remote(gain.at[rank], gain_t.at[i], g_send.at[i], g_recv.at[i], target)
        copy.start()
        gains.append(copy)

    add = lambda a, b: a + b
    chunks = [
        (win.at[:, 0], win_x.at[0], win_s.at[0], win_z.at[0], add),
        (win.at[:, 1], win_x.at[1], win_s.at[1], win_z.at[1], add),
        (wout, wout_x, wout_s, wout_z, add),
        (mats, mats_x, mats_s, mats_z, add),
        (vectors, small_x, small_s, small_z, add),
        (stats, stats_x, stats_s, stats_z, None),
    ]

    def join(a, b, op):
        a, b = a.astype(f32), b.astype(f32)
        if op is None:
            line = lax.broadcasted_iota(jnp.int32, a.shape, len(a.shape) - 2)
            return jnp.where(line < 4, a + b, jnp.maximum(a, b))
        return op(a, b)

    sends = []

    def to_side(c):
        src, near = chunks[c][:2]
        copy = remote(src.at[1 - x], near, x_send.at[c], x_recv.at[c], side)
        copy.start()
        sends.append(copy)

    to_side(0)
    to_side(1)
    total = gain[me]
    for i in range(TP - 1):
        gains[i].wait_recv()
        total = total + gain_t[i]
    vectors[...] = small[...]
    for g in range(2 * zh_size):
        vectors[g // zh_size, g % zh_size, 8:9, :] = total[g : g + 1, :]
    passed = []
    for c in range(len(chunks)):
        src, near, mine, buf, op = chunks[c]
        sends[c].wait_recv()
        mine[...] = join(src[x], near[...], op).astype(mine.dtype)
        moved = []
        for k, (target, to_z, _) in enumerate(far):
            copy = remote(mine.at[to_z], buf.at[k], z_send.at[c, k], z_recv.at[c, k], target)
            copy.start()
            moved.append(copy)
        passed.append(moved)
        if c + 2 < len(chunks):
            to_side(c + 2)
    outs = [None, None, o_wout, o_mats, o_small, o_stats]
    turn = []
    for c in range(len(chunks)):
        src, near, mine, buf, op = chunks[c]
        value = join(src[x, zh], near[zh], op)
        for k in range(zh_size - 1):
            passed[c][k].wait_recv()
            value = join(value, buf[k], op)
        if c < 2:
            win_t[c] = value.astype(bf16).reshape(win_t.shape[1:])
        else:
            outs[c][...] = value
        if c == 1:
            for i, (target, rank, _) in enumerate(peers):
                copy = remote(
                    win_t.at[rank // WAYS, lax.rem(rank, WAYS)], o_win.at[me], t_send.at[i], t_recv.at[i], target
                )
                copy.start()
                turn.append(copy)
    o_win[me] = win_t[core, q]
    for copy in gains + sends:
        copy.wait_send()
    for moved in passed:
        for copy in moved:
            copy.wait_send()
    for copy in turn:
        copy.wait()


def scatter_gradients(zh_size, win, wout, mats, small, stats, gain):
    dma = pltpu.SemaphoreType.DMA
    far = max(1, zh_size - 1)
    v = lambda shape, dtype: pltpu.VMEM(shape, dtype)
    rows = win.shape[3] // WAYS
    tail = lambda a: a.shape[1:]
    deep = lambda a: (far,) + a.shape[2:]
    ins = (win, wout, mats, small, stats)
    win_deep = (2, far) + win.shape[3:]
    near = [v((2,) + win.shape[2:], bf16)] + [v(tail(a), a.dtype) for a in ins[1:]]
    held = [v((2,) + win.shape[2:], bf16)] + [v(tail(a), a.dtype) for a in ins[1:]]
    buf = [v(win_deep, bf16)] + [v(deep(a), a.dtype) for a in ins[1:]]
    return pl.pallas_call(
        functools.partial(gradients_kernel, zh_size),
        out_shape=[jax.ShapeDtypeStruct((TP, rows, win.shape[4]), bf16)]
        + [jax.ShapeDtypeStruct(a.shape[2:], f32) for a in ins[1:]],
        in_specs=[VM] * 6,
        out_specs=[VM] * 5,
        scratch_shapes=near + held + buf
        + [v((2, WAYS, rows, win.shape[4]), bf16), v((TP - 1,) + gain.shape[1:], f32), v(small.shape, f32)]
        + [dma((6,)), dma((6,)), dma((6, far)), dma((6, far))]
        + [dma((TP - 1,))] * 4,
        input_output_aliases={},
        compiler_params=pltpu.CompilerParams(
            collective_id=5, has_side_effects=True, vmem_limit_bytes=56 * 2**20
        ),
        name="scatter_gradients",
    )(*ins, gain)


def spread_keys(kq, lane):
    a = kq.astype(bf16).astype(f32)
    rest = kq - a
    b = rest.astype(bf16).astype(f32)
    c = rest - b
    return jnp.where(lane < 32, a, jnp.where(lane < 64, b, c)).astype(bf16)


def forward_kernel(act_ref, step_ref, kq_ref, e_ref, y_ref, keep_ref, state, wide):
    tokens, seqs, channels = act_ref.shape
    parts = channels // 128
    rows_of = STEPS * seqs
    lane = lax.broadcasted_iota(jnp.int32, (rows_of, 128), 1)
    state[...] = jnp.zeros_like(state)

    def block(b, carry):
        keep_ref[b] = state[...]
        rows = pl.ds(pl.multiple_of(b * rows_of, rows_of), rows_of)
        wide[...] = jnp.dot(spread_keys(kq_ref[rows, :], lane), e_ref[...], preferred_element_type=f32)

        def one(j, carry):
            t = b * STEPS + j
            r = pl.ds(pl.multiple_of(j * seqs, seqs), seqs)
            acts = [act_ref[t, :, c * 128 : (c + 1) * 128] for c in range(parts)]
            steps = [step_ref[t, :, c * 128 : (c + 1) * 128] for c in range(parts)]
            sums = [None] * parts
            for n in range(STATE):
                key = wide[r, n * 128 : (n + 1) * 128]
                query = wide[r, (STATE + n) * 128 : (STATE + n + 1) * 128]
                for c in range(parts):
                    s = state[n, c]
                    s = s + (steps[c] * key) * (acts[c] - key * s)
                    state[n, c] = s
                    sums[c] = s * query if sums[c] is None else sums[c] + s * query
            for c in range(parts):
                y_ref[t, :, c * 128 : (c + 1) * 128] = sums[c]
            return carry

        return lax.fori_loop(0, STEPS, one, carry)

    lax.fori_loop(0, tokens // STEPS, block, 0)


def spreader():
    one = jnp.repeat(jnp.eye(32, dtype=bf16), 128, axis=1)
    return jnp.concatenate([one, one, one, jnp.zeros_like(one)], axis=0)


def recur_forward(act, step, kq):
    tokens, seqs, channels = act.shape
    parts = channels // 128
    return pl.pallas_call(
        forward_kernel,
        out_shape=[
            jax.ShapeDtypeStruct(act.shape, f32),
            jax.ShapeDtypeStruct((tokens // STEPS, STATE, parts, seqs, 128), f32),
        ],
        in_specs=[VM] * 4,
        out_specs=[VM] * 2,
        scratch_shapes=[
            pltpu.VMEM((STATE, parts, seqs, 128), f32),
            pltpu.VMEM((STEPS * seqs, 32 * 128), f32),
        ],
        compiler_params=pltpu.CompilerParams(vmem_limit_bytes=56 * 2**20),
        name="recur_forward",
    )(act, step, kq, spreader())


def backward_kernel(
    act_ref, step_ref, kq_ref, e_ref, et_ref, gsum_ref, keep_ref, gstep_ref, gact_ref, gkq_ref,
    states, lam, wide, terms,
):
    tokens, seqs, channels = act_ref.shape
    parts = channels // 128
    rows_of = STEPS * seqs
    lane = lax.broadcasted_iota(jnp.int32, (rows_of, 128), 1)
    lam[...] = jnp.zeros_like(lam)

    def cut(ref, t):
        return [ref[t, :, c * 128 : (c + 1) * 128] for c in range(parts)]

    def plus(a, b):
        return b if a is None else a + b

    def block(bi, carry):
        b = tokens // STEPS - 1 - bi
        states[0] = keep_ref[b]
        rows = pl.ds(pl.multiple_of(b * rows_of, rows_of), rows_of)
        wide[...] = jnp.dot(spread_keys(kq_ref[rows, :], lane), e_ref[...], preferred_element_type=f32)

        def again(j, carry):
            t = b * STEPS + j
            r = pl.ds(pl.multiple_of(j * seqs, seqs), seqs)
            acts, steps = cut(act_ref, t), cut(step_ref, t)
            for n in range(STATE):
                key = wide[r, n * 128 : (n + 1) * 128]
                for c in range(parts):
                    s = states[j, n, c]
                    states[j + 1, n, c] = s + (steps[c] * key) * (acts[c] - key * s)
            return carry

        lax.fori_loop(0, STEPS, again, 0)

        def back(jj, carry):
            j = STEPS - 1 - jj
            t = b * STEPS + j
            r = pl.ds(pl.multiple_of(j * seqs, seqs), seqs)
            acts, steps, gsums = cut(act_ref, t), cut(step_ref, t), cut(gsum_ref, t)
            first, second = [None] * parts, [None] * parts
            for n in range(STATE):
                key = wide[r, n * 128 : (n + 1) * 128]
                query = wide[r, (STATE + n) * 128 : (STATE + n + 1) * 128]
                key_term, query_term = None, None
                for c in range(parts):
                    before, after = states[j, n, c], states[j + 1, n, c]
                    grad = lam[n, c] + gsums[c] * query
                    w = key * before
                    d = acts[c] - w
                    gk = grad * key
                    first[c] = plus(first[c], gk * d)
                    second[c] = plus(second[c], gk)
                    key_term = plus(key_term, (steps[c] * grad) * (d - w))
                    query_term = plus(query_term, gsums[c] * after)
                    lam[n, c] = grad - (steps[c] * key) * gk
                terms[r, n * 128 : (n + 1) * 128] = key_term
                terms[r, (STATE + n) * 128 : (STATE + n + 1) * 128] = query_term
            for c in range(parts):
                gstep_ref[t, :, c * 128 : (c + 1) * 128] = first[c]
                gact_ref[t, :, c * 128 : (c + 1) * 128] = steps[c] * second[c]
            return carry

        lax.fori_loop(0, STEPS, back, 0)
        p = terms[...]
        high = p.astype(bf16)
        low = (p - high.astype(f32)).astype(bf16)
        gkq_ref[rows, :] = jnp.dot(high, et_ref[...], preferred_element_type=f32) + jnp.dot(
            low, et_ref[...], preferred_element_type=f32
        )
        return carry

    lax.fori_loop(0, tokens // STEPS, block, 0)


def recur_backward(act, step, kq, gsum, keep):
    tokens, seqs, channels = act.shape
    parts = channels // 128
    fold = jnp.pad(jnp.repeat(jnp.eye(32, dtype=bf16), 128, axis=0), ((0, 0), (0, 96)))
    return pl.pallas_call(
        backward_kernel,
        out_shape=[
            jax.ShapeDtypeStruct(act.shape, f32),
            jax.ShapeDtypeStruct(act.shape, f32),
            jax.ShapeDtypeStruct((tokens * seqs, 128), f32),
        ],
        in_specs=[VM] * 7,
        out_specs=[VM] * 3,
        scratch_shapes=[
            pltpu.VMEM((STEPS + 1, STATE, parts, seqs, 128), f32),
            pltpu.VMEM((STATE, parts, seqs, 128), f32),
            pltpu.VMEM((STEPS * seqs, 32 * 128), f32),
            pltpu.VMEM((STEPS * seqs, 32 * 128), f32),
        ],
        compiler_params=pltpu.CompilerParams(vmem_limit_bytes=60 * 2**20),
        name="recur_backward",
    )(act, step, kq, spreader(), fold, gsum, keep)


def dot(a, b, contract, out=f32):
    return lax.dot_general(a, b, (contract, ((), ())), preferred_element_type=out)


def rms(stream):
    return lax.rsqrt(jnp.mean(jnp.square(stream), axis=-1, keepdims=True) + eps)


def shifted(values, by):
    length = values.shape[0]
    if by == 0:
        return values
    if by > 0:
        return jnp.pad(values, ((by, 0), (0, 0), (0, 0)))[:length]
    return jnp.pad(values, ((0, -by), (0, 0), (0, 0)))[-by:]


def forward_layer(stream, w):
    tokens = stream.shape[0]
    normed = (stream * rms(stream) * w["gain"]).astype(bf16)
    rows = tp_gather(normed).reshape(TP * tokens, -1)
    entry = dot(rows, w["win"], ((1,), (0,))).reshape(TP, tokens, -1).transpose(1, 0, 2)
    half = entry.shape[-1] // 2
    inner, gate = entry[..., :half], entry[..., half:]
    conv = w["shift"] + sum(w["taps"][j] * shifted(inner, CONV - 1 - j) for j in range(CONV))
    act = jax.nn.silu(conv).astype(bf16)
    flat = act.reshape(tokens * TP, half)
    projected = dot(flat, w["select"], ((1,), (0,)))
    low = projected[:, :RANK]
    kq = projected[:, RANK:]
    whole = jnp.concatenate([low, kq, kq, kq, jnp.zeros_like(kq)], axis=1)
    summed, _ = tp_sum(whole.reshape(TP, tokens, -1), jnp.zeros((8, 128), f32))
    summed = summed.reshape(tokens * TP, -1)
    low16 = summed[:, :RANK].astype(bf16)
    kq = summed[:, RANK:]
    rate_pre = dot(low16, w["rate"], ((1,), (1,))).reshape(tokens, TP, half)
    beta = jax.nn.sigmoid(rate_pre + w["rate_shift"])
    norm = jnp.sum(jnp.square(kq[:, :STATE]), axis=-1).reshape(tokens, TP, 1)
    step = beta / (1.0 + beta * norm)
    act32 = act.astype(f32)
    recurrent, keep = recur_forward(act32, step, kq)
    mixed = ((recurrent + w["skip"] * act32) * jax.nn.silu(gate)).astype(bf16)
    mixed = mixed.transpose(1, 0, 2).reshape(TP * tokens, half)
    partial = dot(mixed, w["wout"], ((1,), (0,)), bf16).reshape(TP, tokens, -1)
    result = stream + tp_scatter(partial)
    beta_sums = jnp.sum(beta, axis=(0, 2))
    beta_peaks = jnp.max(beta, axis=(0, 2))
    kept = (stream, rows, inner, gate, conv, act, low16, kq, beta, norm, step, recurrent, keep, mixed)
    return result, kept, (beta_sums, beta_peaks)


def backward_layer(grad, kept, w, stats):
    stream, rows, inner, gate, conv, act, low16, kq, beta, norm, step, recurrent, keep, mixed = kept
    tokens = stream.shape[0]
    half = gate.shape[-1]
    gout = tp_gather(grad.astype(bf16)).reshape(TP * tokens, -1)
    slope_out = dot(mixed, gout, ((0,), (0,)), bf16)
    gmixed = dot(gout, w["wout"], ((1,), (1,))).reshape(TP, tokens, half).transpose(1, 0, 2)
    act32 = act.astype(f32)
    sig = jax.nn.sigmoid(gate)
    gsum = gmixed * (gate * sig)
    ggate = gmixed * (recurrent + w["skip"] * act32) * (sig * (1.0 + gate * (1.0 - sig)))
    slope_skip = jnp.sum(gsum * act32, axis=(0, 1))
    gstep, gact, gkq = recur_backward(act32, step, kq, gsum, keep)
    gact = gact + w["skip"] * gsum
    inverse = 1.0 / jnp.square(1.0 + beta * norm)
    gnorm = -jnp.sum(gstep * jnp.square(beta) * inverse, axis=-1).reshape(tokens * TP, 1)
    grate = gstep * inverse * beta * (1.0 - beta)
    slope_rate_shift = jnp.sum(grate, axis=(0, 1))
    grate16 = grate.astype(bf16).reshape(tokens * TP, half)
    slope_rate = dot(grate16, low16, ((0,), (0,)), bf16)
    grank = dot(grate16, w["rate"], ((1,), (0,)))
    gkeys = gkq[:, :STATE] + 2.0 * kq[:, :STATE] * gnorm
    whole = jnp.concatenate([grank, gkeys, gkq[:, STATE:]], axis=1)
    summed, stats = tp_sum(whole.reshape(TP, tokens, -1), stats)
    gproj = summed.reshape(tokens * TP, -1)[:, : RANK + 2 * STATE].astype(bf16)
    slope_select = dot(act.reshape(tokens * TP, half), gproj, ((0,), (0,)), bf16)
    gact = gact + dot(gproj, w["select"], ((1,), (1,))).reshape(tokens, TP, half)
    sig = jax.nn.sigmoid(conv)
    gconv = gact * (sig * (1.0 + conv * (1.0 - sig)))
    slope_shift = jnp.sum(gconv, axis=(0, 1))
    slope_taps = [jnp.sum(gconv * shifted(inner, CONV - 1 - j), axis=(0, 1)) for j in range(CONV)]
    ginner = sum(w["taps"][j] * shifted(gconv, j - CONV + 1) for j in range(CONV))
    gentry = jnp.concatenate([ginner, ggate], axis=-1).astype(bf16)
    gentry = gentry.transpose(1, 0, 2).reshape(TP * tokens, 2 * half)
    slope_in = dot(rows, gentry, ((0,), (0,)), bf16)
    partial = dot(gentry, w["win"], ((1,), (1,)), bf16).reshape(TP, tokens, -1)
    gnormed = tp_scatter(partial)
    r = rms(stream)
    slope_gain = jnp.sum(gnormed * stream * r, axis=0)
    scaled = gnormed * w["gain"]
    grad = grad + r * scaled - stream * (r * r * r) * jnp.mean(stream * scaled, axis=-1, keepdims=True)
    vectors = jnp.stack(slope_taps + [slope_shift, slope_rate_shift, slope_skip])
    return grad, (slope_in, slope_out, slope_rate, slope_select, vectors, slope_gain), stats


def on_device(
    hidden, cotangent, groups, group_weights, input_weight, select_weight, rate_weight,
    output_weight, norm_gain, conv_taps, conv_shift, rate_shift, skip_gain,
):
    fsdp = lax.axis_size("fsdp")
    zh_size = fsdp // WAYS
    count = 2 * 2 * fsdp
    group_count = 2 * zh_size
    share = conv_shift.shape[1]
    gains = norm_gain.shape[1]
    depth = input_weight.shape[1]
    x, core, zh, q = place()

    labels = jnp.arange(group_weights.shape[0])
    own_weight = jnp.sum(jnp.where(groups[:, None] == labels[None, :], group_weights[None, :], 0.0))

    weights = []
    for l in range(LAYERS):
        win = input_weight[l].reshape(depth, 2, 2, 2, zh_size, WAYS, share)
        win = win.transpose(3, 5, 0, 1, 2, 4, 6).reshape(TP, depth, 2 * group_count * share)
        mats = jnp.concatenate([rate_weight[l].T, select_weight[l]], axis=1)
        small = jnp.concatenate(
            [conv_taps[l], conv_shift[l][None], rate_shift[l][None], skip_gain[l][None], skip_gain[l][None]]
        ).astype(f32)
        small = jnp.pad(small, ((0, 0), (0, 128 - share)))
        misc = jnp.pad(norm_gain[l].astype(f32)[None], ((0, 7), (0, 128 - gains)))
        misc = misc.at[1, :].set(own_weight)
        win, wout, mats, small, misc = gather_weights(zh_size, l, win, output_weight[l], mats, small, misc)
        mats = mats.reshape(group_count * share, -1)
        small = small[:, :, :share].transpose(1, 0, 2).reshape(8, group_count * share)
        weights.append(
            dict(
                win=win.reshape(count * depth, -1), wout=wout.reshape(group_count * share, -1),
                rate=mats[:, :RANK], select=mats[:, RANK:], taps=small[:CONV], shift=small[CONV],
                rate_shift=small[CONV + 1], skip=small[CONV + 2],
                gain=misc[:, 0, :gains].reshape(count * gains),
            )
        )
        if l == 0:
            all_weights = misc[:, 1, 0]
    scales = all_weights / jnp.mean(all_weights)
    table = scales.reshape(2, 2, zh_size, WAYS)
    own_scale = table[x, core, zh, q]
    group_scale = table[x, :, zh, :].reshape(TP)

    stream = hidden[0]
    kept_all, stat_rows = [], []
    for l in range(LAYERS):
        stream, kept, (sums, peaks) = forward_layer(stream, weights[l])
        kept_all.append(kept)
        stat_rows.append((jnp.sum(sums * group_scale), jnp.max(peaks * group_scale)))
    rows = [s for s, _ in stat_rows] + [jnp.zeros((), f32)] * (4 - LAYERS)
    rows += [p for _, p in stat_rows] + [jnp.zeros((), f32)] * (4 - LAYERS)
    own_stats = jnp.broadcast_to(jnp.stack(rows)[:, None], (8, 128))

    grad = cotangent[0] * own_scale
    shares = [None] * LAYERS
    for l in reversed(range(LAYERS)):
        grad, slopes, stats = backward_layer(grad, kept_all[l], weights[l], own_stats)
        slope_in, slope_out, slope_rate, slope_select, vectors, slope_gain = slopes
        stats = jnp.concatenate([jnp.sum(stats[:, :4], axis=0), jnp.max(stats[:, 4:], axis=0)])
        stats = jnp.broadcast_to(stats, (2, zh_size, 8, 128))
        win = slope_in.reshape(2, 2, zh_size, WAYS * depth, -1)
        wout = slope_out.reshape(2, zh_size, share, -1)
        mats = jnp.concatenate([slope_rate, slope_select], axis=1).reshape(2, zh_size, share, -1)
        small = vectors.reshape(7, group_count, share).transpose(1, 0, 2)
        small = jnp.pad(small, ((0, 0), (0, 9), (0, 128 - share))).reshape(2, zh_size, 16, 128)
        gain = slope_gain.reshape(2, 2, zh_size, WAYS, gains).transpose(1, 3, 0, 2, 4)
        gain = gain.reshape(TP, group_count, gains)
        gain = jnp.pad(gain, ((0, 0), (0, -group_count % 8), (0, 128 - gains)))
        shares[l] = scatter_gradients(zh_size, win, wout, mats, small, stats, gain)
    outs = [[] for _ in range(9)]
    for l in range(LAYERS):
        win, wout, mats, small, stats = shares[l]
        win = win.reshape(2, WAYS, depth, 2, 2, zh_size, share).transpose(2, 3, 4, 0, 5, 1, 6)
        outs[0].append(win.reshape(depth, -1).astype(f32))
        outs[1].append(mats[:, RANK:])
        outs[2].append(mats[:, :RANK].T)
        outs[3].append(wout)
        outs[4].append(small[8, :gains])
        outs[5].append(small[:CONV, :share])
        outs[6].append(small[CONV, :share])
        outs[7].append(small[CONV + 1, :share])
        outs[8].append(small[CONV + 2, :share])
    stacked = tuple(jnp.stack(o) for o in outs)
    beta_mean = stats[:LAYERS, 0] / (count * hidden.shape[1] * INNER)
    beta_max = stats[4 : 4 + LAYERS, 0]
    return (stream[None], grad[None]) + stacked + (beta_mean, beta_max)


def solution(mesh):
    both = ("dp", "fsdp")
    placed = (
        P(both, None, None), P(both, None, None), P(both), P(),
        P(None, both, None), P(None, both, None), P(None, None, both), P(None, both, None),
        P(None, both), P(None, None, both), P(None, both), P(None, both), P(None, both),
    )
    return jax.shard_map(
        on_device,
        mesh=mesh,
        in_specs=placed,
        out_specs=(P(both, None, None), P(both, None, None)) + placed[4:] + (P(), P()),
        check_vma=False,
    )
```

```python
import functools

import jax
import jax.numpy as jnp
from jax import lax
from jax.sharding import PartitionSpec as P
import jax.experimental.pallas as pl
import jax.experimental.pallas.tpu as pltpu

INNER = 4096
STATE = 16
RANK = 128
CONV = 4
LAYERS = 2
WAYS = 4
TP = 8
STEPS = 16

eps = 1e-05
MESH = pl.DeviceIdType.MESH
f32 = jnp.float32
bf16 = jnp.bfloat16
VM = pl.BlockSpec(memory_space=pltpu.VMEM)
HB = pl.BlockSpec(memory_space=pl.ANY)


def place():
    dp, fs = lax.axis_index("dp"), lax.axis_index("fsdp")
    return dp // 2, lax.rem(dp, 2), fs // WAYS, lax.rem(fs, WAYS)


def device(x, core, zh, q):
    return (x * 2 + core, zh * WAYS + q)


def remote(src, dst, send, recv, target):
    return pltpu.make_async_remote_copy(
        src_ref=src, dst_ref=dst, send_sem=send, recv_sem=recv, device_id=target, device_id_type=MESH
    )


def cost(us):
    return pl.CostEstimate(flops=int(us * 1.1e9), bytes_accessed=0, transcendentals=0)


def greet(targets):
    barrier = pltpu.get_barrier_semaphore()
    for target in targets:
        pl.semaphore_signal(barrier, inc=1, device_id=target, device_id_type=MESH)
    pl.semaphore_wait(barrier, len(targets))


def tp_peers():
    x, core, zh, q = place()
    peers = []
    for dc in (0, 1):
        for dq in (1, 3, 2, 0):
            if dc == 0 and dq == 0:
                continue
            other_core = lax.rem(core + dc, 2)
            to_q, from_q = lax.rem(q + dq, WAYS), lax.rem(q + WAYS - dq, WAYS)
            peers.append(
                (device(x, other_core, zh, to_q), other_core * WAYS + to_q, other_core * WAYS + from_q)
            )
    return peers


def dp_peers(zh_size):
    x, core, zh, q = place()
    side = device(1 - x, core, zh, q)
    far = []
    for dz in range(1, zh_size):
        to_z, from_z = lax.rem(zh + dz, zh_size), lax.rem(zh + zh_size - dz, zh_size)
        far.append((device(x, core, to_z, q), to_z, from_z))
    return side, far


def weights_kernel(
    zh_size, win, late, small, misc, o_win, o_late, o_small, o_misc,
    tp_send, tp_recv, z_send, z_recv, x_send, x_recv, own_sem,
):
    x, core, zh, q = place()
    me = core * WAYS + q
    peers = tp_peers()
    side, far = dp_peers(zh_size)
    greet([p[0] for p in peers] + [side] + [f[0] for f in far])

    def row(xx, zz, rank):
        return ((xx * 2 + rank // WAYS) * zh_size + zz) * WAYS + lax.rem(rank, WAYS)

    waits = []
    own = []
    for i, (src, dst) in enumerate(
        (
            (win.at[me], o_win.at[row(x, zh, me)]),
            (misc, o_misc.at[row(x, zh, me)]),
            (small, o_small.at[x * zh_size + zh]),
            (late.at[me], o_late.at[me]),
        )
    ):
        copy = pltpu.make_async_copy(src, dst, own_sem.at[i])
        copy.start()
        own.append(copy)
    arrive = []
    last = []
    for i, (target, rank, source) in enumerate(peers):
        for j, (src, dst) in enumerate(
            ((win.at[rank], o_win.at[row(x, zh, me)]), (misc, o_misc.at[row(x, zh, me)]))
        ):
            copy = remote(src, dst, tp_send.at[i, j], tp_recv.at[i, j], target)
            copy.start()
            arrive.append((copy, source, j))
            waits.append(copy)

    onward = []

    def spread(item, src, view):
        for k, (target, to_z, from_z) in enumerate(far):
            copy = remote(src, view(x, zh), z_send.at[item, k], z_recv.at[item, k], target)
            copy.start()
            waits.append(copy)
            onward.append((copy, item, k, view, from_z))
        copy = remote(src, view(x, zh), x_send.at[item, 0], x_recv.at[item, 0], side)
        copy.start()
        waits.append(copy)

    spread(0, win.at[me], lambda xx, zz: o_win.at[row(xx, zz, me)])
    spread(1, misc, lambda xx, zz: o_misc.at[row(xx, zz, me)])
    spread(2, small, lambda xx, zz: o_small.at[xx * zh_size + zz])
    recv_done = set()
    item = 3
    for copy, source, j in arrive:
        copy.wait_recv()
        recv_done.add(id(copy))
        out = (o_win, o_misc)[j]
        view = functools.partial(lambda out, source, xx, zz: out.at[row(xx, zz, source)], out, source)
        spread(item, view(x, zh), view)
        item += 1
    for i, (target, rank, source) in enumerate(peers):
        copy = remote(late.at[rank], o_late.at[me], tp_send.at[i, 2], tp_recv.at[i, 2], target)
        copy.start()
        waits.append(copy)
    for copy, it, k, view, from_z in onward:
        copy.wait_recv()
        recv_done.add(id(copy))
        again = remote(view(x, from_z), view(x, from_z), x_send.at[it, k + 1], x_recv.at[it, k + 1], side)
        again.start()
        waits.append(again)
    for copy in waits:
        copy.wait_send()
        if id(copy) not in recv_done:
            copy.wait_recv()
    for copy in own:
        copy.wait()


def gather_weights(zh_size, win, late, small, misc):
    groups = 2 * zh_size
    count = groups * TP
    items = 3 + 2 * (TP - 1)
    dma = pltpu.SemaphoreType.DMA
    many = lambda a, n: jax.ShapeDtypeStruct((n,) + a.shape, a.dtype)
    return pl.pallas_call(
        functools.partial(weights_kernel, zh_size),
        out_shape=[
            jax.ShapeDtypeStruct((count,) + win.shape[1:], win.dtype),
            jax.ShapeDtypeStruct(late.shape, late.dtype),
            many(small, groups), many(misc, count),
        ],
        in_specs=[HB] * 4,
        out_specs=[HB] * 4,
        scratch_shapes=[
            dma((TP - 1, 3)), dma((TP - 1, 3)),
            dma((items, max(1, zh_size - 1))), dma((items, max(1, zh_size - 1))),
            dma((items, zh_size)), dma((items, zh_size)), dma((4,)),
        ],
        compiler_params=pltpu.CompilerParams(collective_id=1, has_side_effects=True),
        name="gather_weights",
        cost_estimate=cost(90),
    )(win, late, small, misc)


def swap(value, zh_size, turn_x, turn_z):
    fsdp = zh_size * WAYS
    pairs = []
    for x in (0, 1):
        for core in (0, 1):
            for zh in range(zh_size):
                for q in range(WAYS):
                    a = (x * 2 + core) * fsdp + zh * WAYS + q
                    b = ((x + turn_x) % 2 * 2 + core) * fsdp + (zh + turn_z) % zh_size * WAYS + q
                    pairs.append((a, b))
    return lax.ppermute(value, ("dp", "fsdp"), pairs)


def dp_gather(piece, zh_size):
    x, core, zh, q = place()
    blocks = [piece] + [swap(piece, zh_size, 0, k) for k in range(1, zh_size)]
    other = [swap(block, zh_size, 1, 0) for block in blocks]
    out = jnp.zeros((2, piece.shape[0], zh_size) + piece.shape[1:], piece.dtype)
    zero = (0,) * (piece.ndim - 1)
    for k in range(zh_size):
        at = lax.rem(zh + zh_size - k, zh_size)
        for xx, block in ((x, blocks[k]), (1 - x, other[k])):
            out = lax.dynamic_update_slice(out, block[None, :, None], (xx, 0, at) + zero)
    return out


def dp_scatter(partial, zh_size, near=None):
    x, core, zh, q = place()
    pick = lambda a, i: lax.dynamic_index_in_dim(a, i, 0, keepdims=False)
    if near is None:
        near = swap(pick(partial, 1 - x), zh_size, 1, 0)
    half = pick(partial, x).astype(f32) + near.astype(f32)
    total = pick(half, zh)
    half = half.astype(bf16)
    for k in range(1, zh_size):
        total = total + swap(pick(half, lax.rem(zh + k, zh_size)), zh_size, 0, k).astype(f32)
    return total


def tp_gather_kernel(x_ref, o_ref, f_send, f_recv, s_send, s_recv, own_sem):
    x, core, zh, q = place()
    sibling = device(x, 1 - core, zh, q)
    far = []
    for dq in (1, 3, 2):
        far.append((device(x, core, zh, lax.rem(q + dq, WAYS)), lax.rem(q + WAYS - dq, WAYS)))
    greet([t for t, _ in far] + [sibling])
    me = core * WAYS + q
    first = []
    for i, (target, _) in enumerate(far):
        copy = remote(x_ref, o_ref.at[me], f_send.at[i], f_recv.at[i], target)
        copy.start()
        first.append(copy)
    near = [remote(x_ref, o_ref.at[me], s_send.at[3], s_recv.at[3], sibling)]
    near[0].start()
    own = pltpu.make_async_copy(x_ref, o_ref.at[me], own_sem)
    own.start()
    for i, (_, source) in enumerate(far):
        first[i].wait_recv()
        slot = core * WAYS + source
        copy = remote(o_ref.at[slot], o_ref.at[slot], s_send.at[i], s_recv.at[i], sibling)
        copy.start()
        near.append(copy)
    for copy in first:
        copy.wait_send()
    for copy in near:
        copy.wait()
    own.wait()


def tp_gather(rows):
    dma = pltpu.SemaphoreType.DMA
    return pl.pallas_call(
        tp_gather_kernel,
        out_shape=jax.ShapeDtypeStruct((TP,) + rows.shape, rows.dtype),
        in_specs=[HB],
        out_specs=HB,
        scratch_shapes=[dma((3,)), dma((3,)), dma((4,)), dma((4,)), dma],
        compiler_params=pltpu.CompilerParams(collective_id=2, has_side_effects=True),
        name="tp_gather",
        cost_estimate=cost(28),
    )(rows)


def tp_scatter_kernel(p_ref, o_ref, near_buf, far_out, far_in, s_send, s_recv, f_send, f_recv):
    x, core, zh, q = place()
    sibling = device(x, 1 - core, zh, q)
    far = []
    for dq in (1, 3, 2):
        far.append((device(x, core, zh, lax.rem(q + dq, WAYS)), lax.rem(q + dq, WAYS)))
    greet([t for t, _ in far] + [sibling])
    near = []
    for i, to_q in enumerate([t for _, t in far] + [q]):
        copy = remote(
            p_ref.at[(1 - core) * WAYS + to_q], near_buf.at[i], s_send.at[i], s_recv.at[i], sibling
        )
        copy.start()
        near.append(copy)
    first = []
    for i, (target, to_q) in enumerate(far):
        near[i].wait_recv()
        far_out[i] = (
            p_ref[core * WAYS + to_q].astype(f32) + near_buf[i].astype(f32)
        ).astype(bf16)
        copy = remote(far_out.at[i], far_in.at[i], f_send.at[i], f_recv.at[i], target)
        copy.start()
        first.append(copy)
    near[3].wait_recv()
    o_ref[...] = p_ref[core * WAYS + q].astype(f32) + near_buf[3].astype(f32)
    for i in range(3):
        first[i].wait_recv()
        o_ref[...] += far_in[i].astype(f32)
    for copy in near + first:
        copy.wait_send()


def tp_scatter(partial):
    dma = pltpu.SemaphoreType.DMA
    block = partial.shape[1:]
    return pl.pallas_call(
        tp_scatter_kernel,
        out_shape=jax.ShapeDtypeStruct(block, f32),
        in_specs=[VM],
        out_specs=VM,
        scratch_shapes=[
            pltpu.VMEM((4,) + block, bf16), pltpu.VMEM((3,) + block, bf16), pltpu.VMEM((3,) + block, bf16),
            dma((4,)), dma((4,)), dma((3,)), dma((3,)),
        ],
        compiler_params=pltpu.CompilerParams(
            collective_id=3, has_side_effects=True, vmem_limit_bytes=40 * 2**20
        ),
        name="tp_scatter",
        cost_estimate=cost(28),
    )(partial)


def lanes_of(shape):
    return lax.broadcasted_iota(jnp.int32, shape, 1)


def encode(v):
    tail = v[:, RANK:]
    lane = lanes_of(tail.shape)
    high = tail.astype(bf16).astype(f32)
    low = pltpu.roll(tail - high, 32, 1)
    both = jnp.where(lane < 32, high, jnp.where(lane < 64, low, 0.0))
    return jnp.concatenate([v[:, :RANK].astype(bf16), both.astype(bf16)], axis=1)


def decode(v):
    tail = v[:, RANK:].astype(f32)
    lane = lanes_of(tail.shape)
    tail = jnp.where(lane < 32, tail + pltpu.roll(tail, 96, 1), 0.0)
    return jnp.concatenate([v[:, :RANK].astype(f32), tail], axis=1)


def tp_sum_kernel(
    p_ref, own_ref, o_ref, all_ref, out, parts, a_send, a_recv, b_send, b_recv, c_send, c_recv
):
    x, core, zh, q = place()
    me = core * WAYS + q
    peers = tp_peers()
    greet([p[0] for p in peers])
    one, two = [], []
    for i, (target, rank, _) in enumerate(peers):
        out[i] = encode(p_ref[rank])
        copy = remote(out.at[i], parts.at[i], a_send.at[i], a_recv.at[i], target)
        copy.start()
        one.append(copy)
    for i, (target, rank, _) in enumerate(peers):
        copy = remote(own_ref, all_ref.at[me], c_send.at[i], c_recv.at[i], target)
        copy.start()
        two.append(copy)
    all_ref[me] = own_ref[...]
    total = p_ref[me]
    for i in range(TP - 1):
        one[i].wait_recv()
        total = total + decode(parts[i])
    o_ref[me] = encode(total)
    for i, (target, rank, _) in enumerate(peers):
        copy = remote(o_ref.at[me], o_ref.at[me], b_send.at[i], b_recv.at[i], target)
        copy.start()
        two.append(copy)
    for copy in one:
        copy.wait_send()
    for copy in two:
        copy.wait()


def tp_sum(partial, own):
    dma = pltpu.SemaphoreType.DMA
    part = pltpu.VMEM((TP - 1,) + partial.shape[1:], bf16)
    return pl.pallas_call(
        tp_sum_kernel,
        out_shape=[
            jax.ShapeDtypeStruct(partial.shape, bf16),
            jax.ShapeDtypeStruct((TP,) + own.shape, f32),
        ],
        in_specs=[VM, VM],
        out_specs=[VM, VM],
        scratch_shapes=[part, part] + [dma((TP - 1,))] * 6,
        compiler_params=pltpu.CompilerParams(
            collective_id=4, has_side_effects=True, vmem_limit_bytes=40 * 2**20
        ),
        name="tp_sum",
        cost_estimate=cost(18),
    )(partial, own)


def gradients_kernel(
    zh_size, win, small, stats, gain, late, o_win, o_small, o_stats, o_late,
    win_x, small_x, stats_x, win_s, small_s, stats_s, win_z, small_z, stats_z, win_t, gain_t, vectors,
    x_send, x_recv, z_send, z_recv, t_send, t_recv, l_send, l_recv, g_send, g_recv,
):
    x, core, zh, q = place()
    me = core * WAYS + q
    peers = tp_peers()
    side, far = dp_peers(zh_size)
    greet([p[0] for p in peers] + [side] + [f[0] for f in far])
    gains = []
    turn = []
    for i, (target, rank, _) in enumerate(peers):
        copy = remote(gain.at[rank], gain_t.at[i], g_send.at[i], g_recv.at[i], target)
        copy.start()
        gains.append(copy)

    chunks = [
        (win.at[:, 0], win_x.at[0], win_s.at[0], win_z.at[0], False),
        (win.at[:, 1], win_x.at[1], win_s.at[1], win_z.at[1], False),
        (vectors, small_x, small_s, small_z, False),
        (stats, stats_x, stats_s, stats_z, True),
    ]

    def join(a, b, peaks):
        a, b = a.astype(f32), b.astype(f32)
        if peaks:
            line = lax.broadcasted_iota(jnp.int32, a.shape, len(a.shape) - 2)
            return jnp.where(line < 4, a + b, jnp.maximum(a, b))
        return a + b

    sends = []

    def to_side(c):
        src, near = chunks[c][:2]
        copy = remote(src.at[1 - x], near, x_send.at[c], x_recv.at[c], side)
        copy.start()
        sends.append(copy)

    to_side(0)
    to_side(1)
    for i, (target, rank, _) in enumerate(peers):
        copy = remote(late.at[rank], o_late.at[me], l_send.at[i], l_recv.at[i], target)
        copy.start()
        turn.append(copy)
    o_late[me] = late[me]
    total = gain[me]
    for i in range(TP - 1):
        gains[i].wait_recv()
        total = total + gain_t[i]
    vectors[...] = small[...]
    for l in range(LAYERS):
        for g in range(2 * zh_size):
            at = l * 2 * zh_size + g
            vectors[g // zh_size, g % zh_size, l * 16 + 8 : l * 16 + 9, :] = total[at : at + 1, :]
    passed = []
    for c in range(len(chunks)):
        src, near, mine, buf, peaks = chunks[c]
        sends[c].wait_recv()
        mine[...] = join(src[x], near[...], peaks).astype(mine.dtype)
        moved = []
        for k, (target, to_z, _) in enumerate(far):
            copy = remote(mine.at[to_z], buf.at[k], z_send.at[c, k], z_recv.at[c, k], target)
            copy.start()
            moved.append(copy)
        passed.append(moved)
        if c + 2 < len(chunks):
            to_side(c + 2)
    outs = [None, None, o_small, o_stats]
    for c in range(len(chunks)):
        src, near, mine, buf, peaks = chunks[c]
        value = join(src[x, zh], near[zh], peaks)
        for k in range(zh_size - 1):
            passed[c][k].wait_recv()
            value = join(value, buf[k], peaks)
        if c < 2:
            win_t[c] = value.astype(bf16).reshape(win_t.shape[1:])
        else:
            outs[c][...] = value
        if c == 1:
            for i, (target, rank, _) in enumerate(peers):
                copy = remote(
                    win_t.at[rank // WAYS, lax.rem(rank, WAYS)], o_win.at[me], t_send.at[i], t_recv.at[i], target
                )
                copy.start()
                turn.append(copy)
    o_win[me] = win_t[core, q]
    for copy in gains + sends:
        copy.wait_send()
    for moved in passed:
        for copy in moved:
            copy.wait_send()
    for copy in turn:
        copy.wait()


def scatter_gradients(zh_size, win, small, stats, gain, late):
    dma = pltpu.SemaphoreType.DMA
    far = max(1, zh_size - 1)
    v = lambda shape, dtype: pltpu.VMEM(shape, dtype)
    rows = win.shape[3] // WAYS
    ins = (small, stats)
    near = [v((2,) + win.shape[2:], bf16)] + [v(a.shape[1:], a.dtype) for a in ins]
    buf = [v((2, far) + win.shape[3:], bf16)] + [v((far,) + a.shape[2:], a.dtype) for a in ins]
    block = jax.ShapeDtypeStruct((TP, rows, win.shape[4]), bf16)
    return pl.pallas_call(
        functools.partial(gradients_kernel, zh_size),
        out_shape=[block] + [jax.ShapeDtypeStruct(a.shape[2:], f32) for a in ins] + [block],
        in_specs=[VM] * 5,
        out_specs=[VM] * 4,
        scratch_shapes=near + near + buf
        + [v((2, WAYS, rows, win.shape[4]), bf16), v((TP - 1,) + gain.shape[1:], f32), v(small.shape, f32)]
        + [dma((4,)), dma((4,)), dma((4, far)), dma((4, far))]
        + [dma((TP - 1,))] * 6,
        compiler_params=pltpu.CompilerParams(
            collective_id=5, has_side_effects=True, vmem_limit_bytes=56 * 2**20
        ),
        name="scatter_gradients",
        cost_estimate=cost(90),
    )(win, *ins, gain, late)


def spread_keys(kq, lane):
    a = kq.astype(bf16).astype(f32)
    rest = kq - a
    b = rest.astype(bf16).astype(f32)
    c = rest - b
    return jnp.where(lane < 32, a, jnp.where(lane < 64, b, c)).astype(bf16)


def forward_kernel(act_ref, step_ref, kq_ref, e_ref, y_ref, keep_ref, state, wide):
    tokens, seqs, channels = act_ref.shape
    parts = channels // 128
    rows_of = STEPS * seqs
    lane = lax.broadcasted_iota(jnp.int32, (rows_of, 128), 1)
    state[...] = jnp.zeros_like(state)

    def block(b, carry):
        keep_ref[b] = state[...]
        rows = pl.ds(pl.multiple_of(b * rows_of, rows_of), rows_of)
        wide[...] = jnp.dot(spread_keys(kq_ref[rows, :], lane), e_ref[...], preferred_element_type=f32)

        def one(j, carry):
            t = b * STEPS + j
            r = pl.ds(pl.multiple_of(j * seqs, seqs), seqs)
            acts = [act_ref[t, :, c * 128 : (c + 1) * 128] for c in range(parts)]
            steps = [step_ref[t, :, c * 128 : (c + 1) * 128] for c in range(parts)]
            sums = [None] * parts
            for n in range(STATE):
                key = wide[r, n * 128 : (n + 1) * 128]
                query = wide[r, (STATE + n) * 128 : (STATE + n + 1) * 128]
                for c in range(parts):
                    s = state[n, c]
                    s = s + (steps[c] * key) * (acts[c] - key * s)
                    state[n, c] = s
                    sums[c] = s * query if sums[c] is None else sums[c] + s * query
            for c in range(parts):
                y_ref[t, :, c * 128 : (c + 1) * 128] = sums[c]
            return carry

        return lax.fori_loop(0, STEPS, one, carry)

    lax.fori_loop(0, tokens // STEPS, block, 0)


def spreader():
    one = jnp.repeat(jnp.eye(32, dtype=bf16), 128, axis=1)
    return jnp.concatenate([one, one, one, jnp.zeros_like(one)], axis=0)


def recur_forward(act, step, kq):
    tokens, seqs, channels = act.shape
    parts = channels // 128
    return pl.pallas_call(
        forward_kernel,
        out_shape=[
            jax.ShapeDtypeStruct(act.shape, f32),
            jax.ShapeDtypeStruct((tokens // STEPS, STATE, parts, seqs, 128), f32),
        ],
        in_specs=[VM] * 4,
        out_specs=[VM] * 2,
        scratch_shapes=[
            pltpu.VMEM((STATE, parts, seqs, 128), f32),
            pltpu.VMEM((STEPS * seqs, 32 * 128), f32),
        ],
        compiler_params=pltpu.CompilerParams(vmem_limit_bytes=56 * 2**20),
        name="recur_forward",
        cost_estimate=cost(16),
    )(act, step, kq, spreader())


def backward_kernel(
    act_ref, step_ref, kq_ref, e_ref, et_ref, gsum_ref, keep_ref, slope_ref, gstep_ref, gact_ref, gkq_ref,
    near_ref, states, lam, wide, terms, send, recv,
):
    x, core, zh, q = place()
    side = device(1 - x, core, zh, q)
    greet([side])
    swap_half = remote(slope_ref.at[1 - x], near_ref, send, recv, side)
    swap_half.start()
    tokens, seqs, channels = act_ref.shape
    parts = channels // 128
    rows_of = STEPS * seqs
    lane = lax.broadcasted_iota(jnp.int32, (rows_of, 128), 1)
    lam[...] = jnp.zeros_like(lam)

    def cut(ref, t):
        return [ref[t, :, c * 128 : (c + 1) * 128] for c in range(parts)]

    def plus(a, b):
        return b if a is None else a + b

    def block(bi, carry):
        b = tokens // STEPS - 1 - bi
        states[0] = keep_ref[b]
        rows = pl.ds(pl.multiple_of(b * rows_of, rows_of), rows_of)
        wide[...] = jnp.dot(spread_keys(kq_ref[rows, :], lane), e_ref[...], preferred_element_type=f32)

        def again(j, carry):
            t = b * STEPS + j
            r = pl.ds(pl.multiple_of(j * seqs, seqs), seqs)
            acts, steps = cut(act_ref, t), cut(step_ref, t)
            for n in range(STATE):
                key = wide[r, n * 128 : (n + 1) * 128]
                for c in range(parts):
                    s = states[j, n, c]
                    states[j + 1, n, c] = s + (steps[c] * key) * (acts[c] - key * s)
            return carry

        lax.fori_loop(0, STEPS, again, 0)

        def back(jj, carry):
            j = STEPS - 1 - jj
            t = b * STEPS + j
            r = pl.ds(pl.multiple_of(j * seqs, seqs), seqs)
            acts, steps, gsums = cut(act_ref, t), cut(step_ref, t), cut(gsum_ref, t)
            first, second = [None] * parts, [None] * parts
            for n in range(STATE):
                key = wide[r, n * 128 : (n + 1) * 128]
                query = wide[r, (STATE + n) * 128 : (STATE + n + 1) * 128]
                key_term, query_term = None, None
                for c in range(parts):
                    before, after = states[j, n, c], states[j + 1, n, c]
                    grad = lam[n, c] + gsums[c] * query
                    w = key * before
                    d = acts[c] - w
                    gk = grad * key
                    first[c] = plus(first[c], gk * d)
                    second[c] = plus(second[c], gk)
                    key_term = plus(key_term, (steps[c] * grad) * (d - w))
                    query_term = plus(query_term, gsums[c] * after)
                    lam[n, c] = grad - (steps[c] * key) * gk
                terms[r, n * 128 : (n + 1) * 128] = key_term
                terms[r, (STATE + n) * 128 : (STATE + n + 1) * 128] = query_term
            for c in range(parts):
                gstep_ref[t, :, c * 128 : (c + 1) * 128] = first[c]
                gact_ref[t, :, c * 128 : (c + 1) * 128] = steps[c] * second[c]
            return carry

        lax.fori_loop(0, STEPS, back, 0)
        p = terms[...]
        high = p.astype(bf16)
        low = (p - high.astype(f32)).astype(bf16)
        gkq_ref[rows, :] = jnp.dot(high, et_ref[...], preferred_element_type=f32) + jnp.dot(
            low, et_ref[...], preferred_element_type=f32
        )
        return carry

    lax.fori_loop(0, tokens // STEPS, block, 0)
    swap_half.wait()


def recur_backward(act, step, kq, gsum, keep, slope):
    tokens, seqs, channels = act.shape
    parts = channels // 128
    fold = jnp.pad(jnp.repeat(jnp.eye(32, dtype=bf16), 128, axis=0), ((0, 0), (0, 96)))
    return pl.pallas_call(
        backward_kernel,
        out_shape=[
            jax.ShapeDtypeStruct(act.shape, f32),
            jax.ShapeDtypeStruct(act.shape, f32),
            jax.ShapeDtypeStruct((tokens * seqs, 128), f32),
            jax.ShapeDtypeStruct(slope.shape[1:], slope.dtype),
        ],
        in_specs=[VM] * 7 + [HB],
        out_specs=[VM] * 3 + [HB],
        scratch_shapes=[
            pltpu.VMEM((STEPS + 1, STATE, parts, seqs, 128), f32),
            pltpu.VMEM((STATE, parts, seqs, 128), f32),
            pltpu.VMEM((STEPS * seqs, 32 * 128), f32),
            pltpu.VMEM((STEPS * seqs, 32 * 128), f32),
            pltpu.SemaphoreType.DMA, pltpu.SemaphoreType.DMA,
        ],
        compiler_params=pltpu.CompilerParams(
            collective_id=6, has_side_effects=True, vmem_limit_bytes=60 * 2**20
        ),
        name="recur_backward",
        cost_estimate=cost(40),
    )(act, step, kq, spreader(), fold, gsum, keep, slope)


def dot(a, b, contract, out=f32):
    return lax.dot_general(a, b, (contract, ((), ())), preferred_element_type=out)


def rms(stream):
    return lax.rsqrt(jnp.mean(jnp.square(stream), axis=-1, keepdims=True) + eps)


def shifted(values, by):
    length = values.shape[0]
    if by == 0:
        return values
    if by > 0:
        return jnp.pad(values, ((by, 0), (0, 0), (0, 0)))[:length]
    return jnp.pad(values, ((0, -by), (0, 0), (0, 0)))[-by:]


def forward_layer(stream, w):
    tokens = stream.shape[0]
    normed = (stream * rms(stream) * w["gain"]).astype(bf16)
    rows = tp_gather(normed).reshape(TP * tokens, -1)
    entry = dot(rows, w["win"], ((1,), (0,))).reshape(TP, tokens, -1).transpose(1, 0, 2)
    half = entry.shape[-1] // 2
    inner, gate = entry[..., :half], entry[..., half:]
    conv = w["shift"] + sum(w["taps"][j] * shifted(inner, CONV - 1 - j) for j in range(CONV))
    act = jax.nn.silu(conv).astype(bf16)
    flat = act.reshape(tokens * TP, half)
    whole = dot(flat, jnp.pad(w["select"], ((0, 0), (0, 96))), ((1,), (0,)))
    summed, _ = tp_sum(whole.reshape(TP, tokens, -1), jnp.zeros((8, 128), f32))
    summed = summed.reshape(tokens * TP, -1)
    low16 = summed[:, :RANK]
    kq = summed[:, RANK : RANK + 32].astype(f32) + summed[:, RANK + 32 : RANK + 64].astype(f32)
    kq = jnp.concatenate([kq, kq, kq, jnp.zeros_like(kq)], axis=1)
    rate_pre = dot(low16, w["rate"], ((1,), (1,))).reshape(tokens, TP, half)
    beta = jax.nn.sigmoid(rate_pre + w["rate_shift"])
    norm = jnp.sum(jnp.square(kq[:, :STATE]), axis=-1).reshape(tokens, TP, 1)
    step = beta / (1.0 + beta * norm)
    act32 = act.astype(f32)
    recurrent, keep = recur_forward(act32, step, kq)
    mixed = ((recurrent + w["skip"] * act32) * jax.nn.silu(gate)).astype(bf16)
    mixed = mixed.transpose(1, 0, 2).reshape(TP * tokens, half)
    partial = dot(mixed, w["wout"], ((1,), (0,)), bf16).reshape(TP, tokens, -1)
    result = stream + tp_scatter(partial)
    beta_sums = jnp.sum(beta, axis=(0, 2))
    beta_peaks = jnp.max(beta, axis=(0, 2))
    kept = (stream, rows, inner, gate, conv, act, low16, kq, beta, norm, step, recurrent, keep, mixed)
    return result, kept, (beta_sums, beta_peaks)


def backward_layer(grad, kept, w, stats):
    stream, rows, inner, gate, conv, act, low16, kq, beta, norm, step, recurrent, keep, mixed = kept
    tokens = stream.shape[0]
    half = gate.shape[-1]
    gout = tp_gather(grad.astype(bf16)).reshape(TP * tokens, -1)
    slope_out = dot(mixed, gout, ((0,), (0,)), bf16)
    gmixed = dot(gout, w["wout"], ((1,), (1,))).reshape(TP, tokens, half).transpose(1, 0, 2)
    act32 = act.astype(f32)
    sig = jax.nn.sigmoid(gate)
    gsum = gmixed * (gate * sig)
    ggate = gmixed * (recurrent + w["skip"] * act32) * (sig * (1.0 + gate * (1.0 - sig)))
    slope_skip = jnp.sum(gsum * act32, axis=(0, 1))
    slope_out = slope_out.reshape(2, lax.axis_size("fsdp") // WAYS, -1, slope_out.shape[1])
    gstep, gact, gkq, slope_near = recur_backward(act32, step, kq, gsum, keep, slope_out)
    slope_out = (slope_out, slope_near)
    gact = gact + w["skip"] * gsum
    inverse = 1.0 / jnp.square(1.0 + beta * norm)
    gnorm = -jnp.sum(gstep * jnp.square(beta) * inverse, axis=-1).reshape(tokens * TP, 1)
    grate = gstep * inverse * beta * (1.0 - beta)
    slope_rate_shift = jnp.sum(grate, axis=(0, 1))
    grate16 = grate.astype(bf16).reshape(tokens * TP, half)
    slope_rate = dot(grate16, low16, ((0,), (0,)), bf16)
    grank = dot(grate16, w["rate"], ((1,), (0,)))
    gkeys = gkq[:, :STATE] + 2.0 * kq[:, :STATE] * gnorm
    whole = jnp.concatenate([grank, gkeys, gkq[:, STATE:]], axis=1)
    summed, stats = tp_sum(whole.reshape(TP, tokens, -1), stats)
    gproj = summed.reshape(tokens * TP, -1)[:, : RANK + 2 * STATE]
    slope_select = dot(act.reshape(tokens * TP, half), gproj, ((0,), (0,)), bf16)
    gact = gact + dot(gproj, w["select"], ((1,), (1,))).reshape(tokens, TP, half)
    sig = jax.nn.sigmoid(conv)
    gconv = gact * (sig * (1.0 + conv * (1.0 - sig)))
    slope_shift = jnp.sum(gconv, axis=(0, 1))
    slope_taps = [jnp.sum(gconv * shifted(inner, CONV - 1 - j), axis=(0, 1)) for j in range(CONV)]
    ginner = sum(w["taps"][j] * shifted(gconv, j - CONV + 1) for j in range(CONV))
    gentry = jnp.concatenate([ginner, ggate], axis=-1).astype(bf16)
    gentry = gentry.transpose(1, 0, 2).reshape(TP * tokens, 2 * half)
    slope_in = dot(rows, gentry, ((0,), (0,)), bf16)
    partial = dot(gentry, w["win"], ((1,), (1,)), bf16).reshape(TP, tokens, -1)
    gnormed = tp_scatter(partial)
    r = rms(stream)
    slope_gain = jnp.sum(gnormed * stream * r, axis=0)
    scaled = gnormed * w["gain"]
    grad = grad + r * scaled - stream * (r * r * r) * jnp.mean(stream * scaled, axis=-1, keepdims=True)
    vectors = jnp.stack(slope_taps + [slope_shift, slope_rate_shift, slope_skip])
    return grad, (slope_in, slope_out, slope_rate, slope_select, vectors, slope_gain), stats


def on_device(
    hidden, cotangent, groups, group_weights, input_weight, select_weight, rate_weight,
    output_weight, norm_gain, conv_taps, conv_shift, rate_shift, skip_gain,
):
    fsdp = lax.axis_size("fsdp")
    zh_size = fsdp // WAYS
    count = 2 * 2 * fsdp
    group_count = 2 * zh_size
    share = conv_shift.shape[1]
    gains = norm_gain.shape[1]
    depth = input_weight.shape[1]
    x, core, zh, q = place()

    labels = jnp.arange(group_weights.shape[0])
    own_weight = jnp.sum(jnp.where(groups[:, None] == labels[None, :], group_weights[None, :], 0.0))

    wins, mats, smalls, misc = [], [], [], []
    for l in range(LAYERS):
        win = input_weight[l].reshape(depth, 2, 2, 2, zh_size, WAYS, share)
        wins.append(win.transpose(3, 5, 0, 1, 2, 4, 6).reshape(TP, depth, 2 * group_count * share))
        mats.append(jnp.concatenate([rate_weight[l].T, output_weight[l], select_weight[l]], axis=1))
        small = jnp.concatenate(
            [conv_taps[l], conv_shift[l][None], rate_shift[l][None], skip_gain[l][None], skip_gain[l][None]]
        ).astype(f32)
        smalls.append(jnp.pad(small, ((0, 0), (0, 128 - share))))
        misc.append(jnp.pad(norm_gain[l].astype(f32)[None], ((0, 0), (0, 128 - gains))))
    misc = jnp.concatenate(misc + [jnp.full((8 - LAYERS, 128), own_weight)])
    win, late, small, misc = gather_weights(zh_size, wins[0], wins[1], jnp.concatenate(smalls), misc)
    all_weights = misc[:, LAYERS, 0]
    small = small[:, :, :share].transpose(1, 0, 2).reshape(LAYERS, 8, group_count * share)
    late = late.reshape(2, WAYS * depth, -1)
    wins = [win.reshape(count * depth, -1), dp_gather(late, zh_size).reshape(count * depth, -1)]
    weights = []
    width = output_weight.shape[2]
    for l in range(LAYERS):
        m = dp_gather(mats[l][None], zh_size).reshape(group_count * share, -1)
        weights.append(
            dict(
                win=wins[l], rate=m[:, :RANK], wout=m[:, RANK : RANK + width], select=m[:, RANK + width :],
                taps=small[l, :CONV], shift=small[l, CONV], rate_shift=small[l, CONV + 1],
                skip=small[l, CONV + 2], gain=misc[:, l, :gains].reshape(count * gains),
            )
        )
    scales = all_weights / jnp.mean(all_weights)
    table = scales.reshape(2, 2, zh_size, WAYS)
    own_scale = table[x, core, zh, q]
    group_scale = table[x, :, zh, :].reshape(TP)

    stream = hidden[0]
    kept_all, stat_rows = [], []
    for l in range(LAYERS):
        stream, kept, (sums, peaks) = forward_layer(stream, weights[l])
        kept_all.append(kept)
        stat_rows.append((jnp.sum(sums * group_scale), jnp.max(peaks * group_scale)))
    rows = [s for s, _ in stat_rows] + [jnp.zeros((), f32)] * (4 - LAYERS)
    rows += [p for _, p in stat_rows] + [jnp.zeros((), f32)] * (4 - LAYERS)
    own_stats = jnp.broadcast_to(jnp.stack(rows)[:, None], (8, 128))

    grad = cotangent[0] * own_scale
    shares, smalls, gain_sums = [None] * LAYERS, [None] * LAYERS, [None] * LAYERS
    for l in reversed(range(LAYERS)):
        grad, slopes, stats = backward_layer(grad, kept_all[l], weights[l], own_stats)
        slope_in, slope_out, slope_rate, slope_select, vectors, slope_gain = slopes
        m = jnp.concatenate([slope_rate, slope_select], axis=1)
        m = dp_scatter(m.reshape(2, zh_size, share, -1), zh_size)
        shares[l] = (
            slope_in.reshape(2, 2, zh_size, WAYS * depth, -1), m,
            dp_scatter(slope_out[0], zh_size, slope_out[1]),
        )
        small = vectors.reshape(7, group_count, share).transpose(1, 0, 2)
        smalls[l] = jnp.pad(small, ((0, 0), (0, 9), (0, 128 - share)))
        gain = slope_gain.reshape(2, 2, zh_size, WAYS, gains).transpose(1, 3, 0, 2, 4)
        gain_sums[l] = gain.reshape(TP, group_count, gains)
    stats = jnp.concatenate([jnp.sum(stats[:, :4], axis=0), jnp.max(stats[:, 4:], axis=0)])
    stats = jnp.broadcast_to(stats, (2, zh_size, 8, 128))
    small = jnp.concatenate(smalls, axis=1).reshape(2, zh_size, 16 * LAYERS, 128)
    gain = jnp.concatenate(gain_sums, axis=1)
    gain = jnp.pad(gain, ((0, 0), (0, -gain.shape[1] % 8), (0, 128 - gains)))
    late = shares[1][0].swapaxes(1, 2).reshape(2, zh_size, TP * depth, -1)
    late = dp_scatter(late, zh_size).astype(bf16).reshape(TP, depth, -1)
    first, small, stats, late = scatter_gradients(zh_size, shares[0][0], small, stats, gain, late)
    outs = [[] for _ in range(9)]
    for l, win in enumerate((first, late)):
        m = shares[l][1]
        win = win.reshape(2, WAYS, depth, 2, 2, zh_size, share).transpose(2, 3, 4, 0, 5, 1, 6)
        outs[0].append(win.reshape(depth, -1).astype(f32))
        outs[1].append(m[:, RANK:])
        outs[2].append(m[:, :RANK].T)
        outs[3].append(shares[l][2])
        vec = small[16 * l : 16 * (l + 1)]
        outs[4].append(vec[8, :gains])
        outs[5].append(vec[:CONV, :share])
        outs[6].append(vec[CONV, :share])
        outs[7].append(vec[CONV + 1, :share])
        outs[8].append(vec[CONV + 2, :share])
    stacked = tuple(jnp.stack(o) for o in outs)
    beta_mean = stats[:LAYERS, 0] / (count * hidden.shape[1] * INNER)
    beta_max = stats[4 : 4 + LAYERS, 0]
    return (stream[None], grad[None]) + stacked + (beta_mean, beta_max)


def solution(mesh):
    both = ("dp", "fsdp")
    placed = (
        P(both, None, None), P(both, None, None), P(both), P(),
        P(None, both, None), P(None, both, None), P(None, None, both), P(None, both, None),
        P(None, both), P(None, None, both), P(None, both), P(None, both), P(None, both),
    )
    return jax.shard_map(
        on_device,
        mesh=mesh,
        in_specs=placed,
        out_specs=(P(both, None, None), P(both, None, None)) + placed[4:] + (P(), P()),
        check_vma=False,
    )
```

```python
import functools

import jax
import jax.numpy as jnp
from jax import lax
from jax.sharding import PartitionSpec as P
import jax.experimental.pallas as pl
import jax.experimental.pallas.tpu as pltpu

INNER = 4096
STATE = 16
RANK = 128
CONV = 4
LAYERS = 2
WAYS = 4
TP = 8
STEPS = 16

eps = 1e-05
MESH = pl.DeviceIdType.MESH
f32 = jnp.float32
bf16 = jnp.bfloat16
VM = pl.BlockSpec(memory_space=pltpu.VMEM)
HB = pl.BlockSpec(memory_space=pl.ANY)


def place():
    dp, fs = lax.axis_index("dp"), lax.axis_index("fsdp")
    return dp // 2, lax.rem(dp, 2), fs // WAYS, lax.rem(fs, WAYS)


def device(x, core, zh, q):
    return (x * 2 + core, zh * WAYS + q)


def remote(src, dst, send, recv, target):
    return pltpu.make_async_remote_copy(
        src_ref=src, dst_ref=dst, send_sem=send, recv_sem=recv, device_id=target, device_id_type=MESH
    )


def cost(us):
    return pl.CostEstimate(flops=int(us * 1.1e9), bytes_accessed=0, transcendentals=0)


def greet(targets):
    barrier = pltpu.get_barrier_semaphore()
    for target in targets:
        pl.semaphore_signal(barrier, inc=1, device_id=target, device_id_type=MESH)
    pl.semaphore_wait(barrier, len(targets))


def tp_peers():
    x, core, zh, q = place()
    peers = []
    for dc in (0, 1):
        for dq in (1, 3, 2, 0):
            if dc == 0 and dq == 0:
                continue
            other_core = lax.rem(core + dc, 2)
            to_q, from_q = lax.rem(q + dq, WAYS), lax.rem(q + WAYS - dq, WAYS)
            peers.append(
                (device(x, other_core, zh, to_q), other_core * WAYS + to_q, other_core * WAYS + from_q)
            )
    return peers


def dp_peers(zh_size):
    x, core, zh, q = place()
    side = device(1 - x, core, zh, q)
    far = []
    for dz in range(1, zh_size):
        to_z, from_z = lax.rem(zh + dz, zh_size), lax.rem(zh + zh_size - dz, zh_size)
        far.append((device(x, core, to_z, q), to_z, from_z))
    return side, far


def weights_kernel(
    zh_size, win, late, small, misc, mats, o_win, o_late, o_small, o_misc, o_mats,
    tp_send, tp_recv, z_send, z_recv, x_send, x_recv, own_sem,
):
    x, core, zh, q = place()
    me = core * WAYS + q
    peers = tp_peers()
    side, far = dp_peers(zh_size)
    greet([p[0] for p in peers] + [side] + [f[0] for f in far])

    def row(xx, zz, rank):
        return ((xx * 2 + rank // WAYS) * zh_size + zz) * WAYS + lax.rem(rank, WAYS)

    waits = []
    own = []
    for i, (src, dst) in enumerate(
        (
            (win.at[me], o_win.at[row(x, zh, me)]),
            (misc, o_misc.at[row(x, zh, me)]),
            (small, o_small.at[x * zh_size + zh]),
            (late.at[me], o_late.at[me]),
            (mats, o_mats.at[x * zh_size + zh]),
        )
    ):
        copy = pltpu.make_async_copy(src, dst, own_sem.at[i])
        copy.start()
        own.append(copy)
    arrive = []
    last = []
    for i, (target, rank, source) in enumerate(peers):
        for j, (src, dst) in enumerate(
            ((win.at[rank], o_win.at[row(x, zh, me)]), (misc, o_misc.at[row(x, zh, me)]))
        ):
            copy = remote(src, dst, tp_send.at[i, j], tp_recv.at[i, j], target)
            copy.start()
            arrive.append((copy, source, j))
            waits.append(copy)

    onward = []

    def spread(item, src, view):
        for k, (target, to_z, from_z) in enumerate(far):
            copy = remote(src, view(x, zh), z_send.at[item, k], z_recv.at[item, k], target)
            copy.start()
            waits.append(copy)
            onward.append((copy, item, k, view, from_z))
        copy = remote(src, view(x, zh), x_send.at[item, 0], x_recv.at[item, 0], side)
        copy.start()
        waits.append(copy)

    spread(0, win.at[me], lambda xx, zz: o_win.at[row(xx, zz, me)])
    spread(1, misc, lambda xx, zz: o_misc.at[row(xx, zz, me)])
    spread(2, small, lambda xx, zz: o_small.at[xx * zh_size + zz])
    spread(3, mats, lambda xx, zz: o_mats.at[xx * zh_size + zz])
    recv_done = set()
    item = 4
    for copy, source, j in arrive:
        copy.wait_recv()
        recv_done.add(id(copy))
        out = (o_win, o_misc)[j]
        view = functools.partial(lambda out, source, xx, zz: out.at[row(xx, zz, source)], out, source)
        spread(item, view(x, zh), view)
        item += 1
    for i, (target, rank, source) in enumerate(peers):
        copy = remote(late.at[rank], o_late.at[me], tp_send.at[i, 2], tp_recv.at[i, 2], target)
        copy.start()
        waits.append(copy)
    for copy, it, k, view, from_z in onward:
        copy.wait_recv()
        recv_done.add(id(copy))
        again = remote(view(x, from_z), view(x, from_z), x_send.at[it, k + 1], x_recv.at[it, k + 1], side)
        again.start()
        waits.append(again)
    for copy in waits:
        copy.wait_send()
        if id(copy) not in recv_done:
            copy.wait_recv()
    for copy in own:
        copy.wait()


def gather_weights(zh_size, win, late, small, misc, mats):
    groups = 2 * zh_size
    count = groups * TP
    items = 4 + 2 * (TP - 1)
    dma = pltpu.SemaphoreType.DMA
    many = lambda a, n: jax.ShapeDtypeStruct((n,) + a.shape, a.dtype)
    return pl.pallas_call(
        functools.partial(weights_kernel, zh_size),
        out_shape=[
            jax.ShapeDtypeStruct((count,) + win.shape[1:], win.dtype),
            jax.ShapeDtypeStruct(late.shape, late.dtype),
            many(small, groups), many(misc, count), many(mats, groups),
        ],
        in_specs=[HB] * 5,
        out_specs=[HB] * 5,
        scratch_shapes=[
            dma((TP - 1, 3)), dma((TP - 1, 3)),
            dma((items, max(1, zh_size - 1))), dma((items, max(1, zh_size - 1))),
            dma((items, zh_size)), dma((items, zh_size)), dma((5,)),
        ],
        compiler_params=pltpu.CompilerParams(collective_id=1, has_side_effects=True),
        name="gather_weights",
        cost_estimate=cost(90),
    )(win, late, small, misc, mats)


def tp_gather_kernel(x_ref, o_ref, f_send, f_recv, s_send, s_recv, own_sem):
    x, core, zh, q = place()
    sibling = device(x, 1 - core, zh, q)
    far = []
    for dq in (1, 3, 2):
        far.append((device(x, core, zh, lax.rem(q + dq, WAYS)), lax.rem(q + WAYS - dq, WAYS)))
    greet([t for t, _ in far] + [sibling])
    me = core * WAYS + q
    first = []
    for i, (target, _) in enumerate(far):
        copy = remote(x_ref, o_ref.at[me], f_send.at[i], f_recv.at[i], target)
        copy.start()
        first.append(copy)
    near = [remote(x_ref, o_ref.at[me], s_send.at[3], s_recv.at[3], sibling)]
    near[0].start()
    own = pltpu.make_async_copy(x_ref, o_ref.at[me], own_sem)
    own.start()
    for i, (_, source) in enumerate(far):
        first[i].wait_recv()
        slot = core * WAYS + source
        copy = remote(o_ref.at[slot], o_ref.at[slot], s_send.at[i], s_recv.at[i], sibling)
        copy.start()
        near.append(copy)
    for copy in first:
        copy.wait_send()
    for copy in near:
        copy.wait()
    own.wait()


def tp_gather(rows):
    dma = pltpu.SemaphoreType.DMA
    return pl.pallas_call(
        tp_gather_kernel,
        out_shape=jax.ShapeDtypeStruct((TP,) + rows.shape, rows.dtype),
        in_specs=[HB],
        out_specs=HB,
        scratch_shapes=[dma((3,)), dma((3,)), dma((4,)), dma((4,)), dma],
        compiler_params=pltpu.CompilerParams(collective_id=2, has_side_effects=True),
        name="tp_gather",
        cost_estimate=cost(28),
    )(rows)


def lanes_of(shape):
    return lax.broadcasted_iota(jnp.int32, shape, 1)


def encode(v):
    tail = v[:, RANK:]
    lane = lanes_of(tail.shape)
    high = tail.astype(bf16).astype(f32)
    low = pltpu.roll(tail - high, 32, 1)
    both = jnp.where(lane < 32, high, jnp.where(lane < 64, low, 0.0))
    return jnp.concatenate([v[:, :RANK].astype(bf16), both.astype(bf16)], axis=1)


def decode(v):
    tail = v[:, RANK:].astype(f32)
    lane = lanes_of(tail.shape)
    tail = jnp.where(lane < 32, tail + pltpu.roll(tail, 96, 1), 0.0)
    return jnp.concatenate([v[:, :RANK].astype(f32), tail], axis=1)


class Gather:
    sems = staticmethod(lambda dma: [dma((3,)), dma((3,)), dma((4,)), dma((4,)), dma])

    def __init__(self, src, out, sems):
        self.src, self.out = src, out
        self.f_send, self.f_recv, self.s_send, self.s_recv, self.own_sem = sems
        x, core, zh, q = place()
        self.core, self.me = core, core * WAYS + q
        self.sibling = device(x, 1 - core, zh, q)
        self.far = [
            (device(x, core, zh, lax.rem(q + dq, WAYS)), lax.rem(q + WAYS - dq, WAYS)) for dq in (1, 3, 2)
        ]

    def start(self):
        dst = self.out.at[self.me]
        self.first = [
            remote(self.src, dst, self.f_send.at[i], self.f_recv.at[i], target)
            for i, (target, _) in enumerate(self.far)
        ]
        self.near = [remote(self.src, dst, self.s_send.at[3], self.s_recv.at[3], self.sibling)]
        for copy in self.first + self.near:
            copy.start()
        self.own = pltpu.make_async_copy(self.src, dst, self.own_sem)
        self.own.start()

    def onward(self):
        for i, (_, source) in enumerate(self.far):
            self.first[i].wait_recv()
            slot = self.out.at[self.core * WAYS + source]
            copy = remote(slot, slot, self.s_send.at[i], self.s_recv.at[i], self.sibling)
            copy.start()
            self.near.append(copy)

    def finish(self):
        for copy in self.first:
            copy.wait_send()
        for copy in self.near:
            copy.wait()
        self.own.wait()


class Scatter:
    sems = staticmethod(lambda dma: [dma((4,)), dma((4,)), dma((3,)), dma((3,))])

    @staticmethod
    def buffers(block):
        return [pltpu.VMEM((4,) + block, bf16), pltpu.VMEM((3,) + block, bf16), pltpu.VMEM((3,) + block, bf16)]

    def __init__(self, partial, buffers, sems):
        self.partial = partial
        self.near_buf, self.far_out, self.far_in = buffers
        self.s_send, self.s_recv, self.f_send, self.f_recv = sems
        x, core, zh, q = place()
        self.core = core
        self.sibling = device(x, 1 - core, zh, q)
        self.turns = [lax.rem(q + dq, WAYS) for dq in (1, 3, 2, 0)]
        self.targets = [device(x, core, zh, t) for t in self.turns[:3]]
        self.near, self.first = [None] * 4, [None] * 3

    def to_sibling(self, i):
        slot = (1 - self.core) * WAYS + self.turns[i]
        self.near[i] = remote(
            self.partial.at[slot], self.near_buf.at[i], self.s_send.at[i], self.s_recv.at[i], self.sibling
        )
        self.near[i].start()

    def joined(self, i):
        self.near[i].wait_recv()
        return self.partial[self.core * WAYS + self.turns[i]].astype(f32) + self.near_buf[i].astype(f32)

    def across(self, i):
        self.far_out[i] = self.joined(i).astype(bf16)
        self.first[i] = remote(
            self.far_out.at[i], self.far_in.at[i], self.f_send.at[i], self.f_recv.at[i], self.targets[i]
        )
        self.first[i].start()

    def total(self):
        value = self.joined(3)
        for i in range(3):
            self.first[i].wait_recv()
            value = value + self.far_in[i].astype(f32)
        for copy in self.near + self.first:
            copy.wait_send()
        return value


class Spread:
    @staticmethod
    def sems(dma, zh_size):
        far = max(1, zh_size - 1)
        return [dma((far,)), dma((far,)), dma((zh_size,)), dma((zh_size,)), dma]

    def __init__(self, zh_size, src, view, sems):
        self.src, self.view = src, view
        self.z_send, self.z_recv, self.x_send, self.x_recv, self.own_sem = sems
        self.x, _, self.zh, _ = place()
        self.side, self.far = dp_peers(zh_size)

    def start(self):
        dst = self.view(self.x, self.zh)
        self.along = [
            remote(self.src, dst, self.z_send.at[k], self.z_recv.at[k], target)
            for k, (target, _, _) in enumerate(self.far)
        ]
        self.over = [remote(self.src, dst, self.x_send.at[0], self.x_recv.at[0], self.side)]
        for copy in self.along + self.over:
            copy.start()
        self.own = pltpu.make_async_copy(self.src, dst, self.own_sem)
        self.own.start()

    def onward(self):
        for k, (_, _, source) in enumerate(self.far):
            self.along[k].wait_recv()
            slot = self.view(self.x, source)
            copy = remote(slot, slot, self.x_send.at[k + 1], self.x_recv.at[k + 1], self.side)
            copy.start()
            self.over.append(copy)

    def finish(self):
        for copy in self.along:
            copy.wait_send()
        for copy in self.over:
            copy.wait()
        self.own.wait()


class Sum:
    sems = staticmethod(lambda dma: [dma((TP - 1,))] * 4)

    def __init__(self, payload, parts, out, sems):
        self.payload, self.parts, self.out = payload, parts, out
        self.a_send, self.a_recv, self.b_send, self.b_recv = sems
        x, core, zh, q = place()
        self.me = core * WAYS + q
        self.peers = tp_peers()

    def start(self):
        self.one = [
            remote(self.payload.at[rank], self.parts.at[i], self.a_send.at[i], self.a_recv.at[i], target)
            for i, (target, rank, _) in enumerate(self.peers)
        ]
        for copy in self.one:
            copy.start()

    def middle(self, own):
        total = own
        for i in range(TP - 1):
            self.one[i].wait_recv()
            total = total + decode(self.parts[i])
        self.out[self.me] = encode(total)
        self.two = [
            remote(self.out.at[self.me], self.out.at[self.me], self.b_send.at[i], self.b_recv.at[i], target)
            for i, (target, _, _) in enumerate(self.peers)
        ]
        for copy in self.two:
            copy.start()

    def finish(self):
        for copy in self.one:
            copy.wait_send()
        for copy in self.two:
            copy.wait()


def call(body, name, collective, ins, outs, scratch, **options):
    names = list(ins) + list(outs) + list(scratch)

    def kernel(*refs):
        named, refs = {}, list(refs)
        flat = []
        for key in names:
            kind = scratch.get(key)
            if isinstance(kind, list):
                named[key] = refs[: len(kind)]
                refs = refs[len(kind) :]
            else:
                named[key] = refs.pop(0)
        body(named)

    flat = []
    for kind in scratch.values():
        flat += kind if isinstance(kind, list) else [kind]
    values = pl.pallas_call(
        kernel,
        out_shape=[shape for shape, _ in outs.values()],
        in_specs=[spec for _, spec in ins.values()],
        out_specs=[spec for _, spec in outs.values()],
        scratch_shapes=flat,
        compiler_params=pltpu.CompilerParams(
            collective_id=collective, has_side_effects=True, vmem_limit_bytes=63 * 2**20
        ),
        name=name,
    )(*[array for array, _ in ins.values()])
    return dict(zip(outs, values))


def gradients_kernel(
    zh_size, win, near, mats, small, stats, gain, late, o_win, o_mats, o_small, o_stats, o_late,
    mats_x, small_x, stats_x, win_s, mats_s, small_s, stats_s, win_z, mats_z, small_z, stats_z, win_t, gain_t, stats_t, vectors, stats_v,
    x_send, x_recv, z_send, z_recv, t_send, t_recv, l_send, l_recv, g_send, g_recv, s_send, s_recv,
):
    x, core, zh, q = place()
    me = core * WAYS + q
    peers = tp_peers()
    side, far = dp_peers(zh_size)
    greet([p[0] for p in peers] + [side] + [f[0] for f in far])
    gains = []
    turn = []
    for i, (target, rank, _) in enumerate(peers):
        copy = remote(gain.at[rank], gain_t.at[i], g_send.at[i], g_recv.at[i], target)
        copy.start()
        gains.append(copy)
    shown = []
    for i, (target, rank, _) in enumerate(peers):
        copy = remote(stats, stats_t.at[i], s_send.at[i], s_recv.at[i], target)
        copy.start()
        shown.append(copy)

    chunks = [
        (win.at[:, 0], near.at[0], win_s.at[0], win_z.at[0], False),
        (win.at[:, 1], near.at[1], win_s.at[1], win_z.at[1], False),
        (mats, mats_x, mats_s, mats_z, False),
        (vectors, small_x, small_s, small_z, False),
        (stats_v, stats_x, stats_s, stats_z, True),
    ]

    def join(a, b, peaks):
        a, b = a.astype(f32), b.astype(f32)
        if peaks:
            line = lax.broadcasted_iota(jnp.int32, a.shape, len(a.shape) - 2)
            return jnp.where(line < 4, a + b, jnp.maximum(a, b))
        return a + b

    sends = [None, None]

    def to_side(c):
        src, arrived = chunks[c][:2]
        copy = remote(src.at[1 - x], arrived, x_send.at[c], x_recv.at[c], side)
        copy.start()
        sends.append(copy)

    passed = []

    def pass_on(c):
        src, arrived, mine, buf, peaks = chunks[c]
        if sends[c] is not None:
            sends[c].wait_recv()
        mine[...] = join(src[x], arrived[...], peaks).astype(mine.dtype)
        moved = []
        for k, (target, to_z, _) in enumerate(far):
            copy = remote(mine.at[to_z], buf.at[k], z_send.at[c, k], z_recv.at[c, k], target)
            copy.start()
            moved.append(copy)
        passed.append(moved)

    to_side(2)
    pass_on(0)
    pass_on(1)
    for i, (target, rank, _) in enumerate(peers):
        copy = remote(late.at[rank], o_late.at[me], l_send.at[i], l_recv.at[i], target)
        copy.start()
        turn.append(copy)
    o_late[me] = late[me]
    total = gain[me]
    for i in range(TP - 1):
        gains[i].wait_recv()
        total = total + gain_t[i]
    vectors[...] = small[...]
    for l in range(LAYERS):
        for g in range(2 * zh_size):
            at = l * 2 * zh_size + g
            vectors[g // zh_size, g % zh_size, l * 16 + 8 : l * 16 + 9, :] = total[at : at + 1, :]
    seen = stats[...]
    for i in range(TP - 1):
        shown[i].wait_recv()
        seen = join(seen, stats_t[i], True)
    stats_v[...] = jnp.broadcast_to(seen, stats_v.shape)
    to_side(3)
    to_side(4)
    for c in range(2, len(chunks)):
        pass_on(c)
    outs = [None, None, o_mats, o_small, o_stats]
    for c in range(len(chunks)):
        src, arrived, mine, buf, peaks = chunks[c]
        value = join(src[x, zh], arrived[zh], peaks)
        for k in range(zh_size - 1):
            passed[c][k].wait_recv()
            value = join(value, buf[k], peaks)
        if c < 2:
            win_t[c] = value.astype(bf16).reshape(win_t.shape[1:])
        else:
            outs[c][...] = value
        if c == 1:
            for i, (target, rank, _) in enumerate(peers):
                copy = remote(
                    win_t.at[rank // WAYS, lax.rem(rank, WAYS)], o_win.at[me], t_send.at[i], t_recv.at[i], target
                )
                copy.start()
                turn.append(copy)
    o_win[me] = win_t[core, q]
    for copy in gains + shown + sends[2:]:
        copy.wait_send()
    for moved in passed:
        for copy in moved:
            copy.wait_send()
    for copy in turn:
        copy.wait()


def scatter_gradients(zh_size, win, near, mats, small, stats, gain, late):
    dma = pltpu.SemaphoreType.DMA
    far = max(1, zh_size - 1)
    v = lambda shape, dtype: pltpu.VMEM(shape, dtype)
    rows = win.shape[3] // WAYS
    every = jax.ShapeDtypeStruct((2, zh_size) + stats.shape, f32)
    ins = (mats, small, every)
    held = [v(a.shape[1:], a.dtype) for a in ins]
    sums = [v((2,) + win.shape[2:], bf16)] + held
    buf = [v((2, far) + win.shape[3:], bf16)] + [v((far,) + a.shape[2:], a.dtype) for a in ins]
    block = jax.ShapeDtypeStruct((TP, rows, win.shape[4]), bf16)
    return pl.pallas_call(
        functools.partial(gradients_kernel, zh_size),
        out_shape=[block] + [jax.ShapeDtypeStruct(a.shape[2:], f32) for a in ins] + [block],
        in_specs=[VM] * 7,
        out_specs=[VM] * 5,
        scratch_shapes=held + sums + buf
        + [v((2, WAYS, rows, win.shape[4]), bf16), v((TP - 1,) + gain.shape[1:], f32)]
        + [v((TP - 1,) + stats.shape, f32), v(small.shape, f32), v(every.shape, f32)]
        + [dma((5,)), dma((5,)), dma((5, far)), dma((5, far))]
        + [dma((TP - 1,))] * 8,
        compiler_params=pltpu.CompilerParams(
            collective_id=5, has_side_effects=True, vmem_limit_bytes=56 * 2**20
        ),
        name="scatter_gradients",
        cost_estimate=cost(90),
    )(win, near, mats, small, stats, gain, late)


def spread_keys(kq, lane):
    a = kq.astype(bf16).astype(f32)
    rest = kq - a
    b = rest.astype(bf16).astype(f32)
    c = rest - b
    return jnp.where(lane < 32, a, jnp.where(lane < 64, b, c)).astype(bf16)


def spreader():
    one = jnp.repeat(jnp.eye(32, dtype=bf16), 128, axis=1)
    return jnp.concatenate([one, one, one, jnp.zeros_like(one)], axis=0)


def dot(a, b, contract, out=f32):
    return lax.dot_general(a, b, (contract, ((), ())), preferred_element_type=out)


def rms(stream):
    return lax.rsqrt(jnp.mean(jnp.square(stream), axis=-1, keepdims=True) + eps)


LANES = 128


def struct(*shape, dtype=f32):
    return jax.ShapeDtypeStruct(shape, dtype)


def at_block(b, size):
    return pl.ds(pl.multiple_of(b * size, size), size)


def conv_of(entry, vec, row, size, c):
    cols = slice(c * LANES, (c + 1) * LANES)
    conv = vec[CONV : CONV + 1, cols]
    for j in range(CONV):
        conv = conv + vec[j : j + 1, cols] * entry[c, pl.ds(pl.multiple_of(row + TP * j, TP), size), :]
    return conv


def wide_of(ref, rows, parts):
    return jnp.concatenate([ref[c, rows, :] for c in range(parts)], axis=1)


def row_sum(value):
    return jnp.sum(value.reshape(-1, TP, value.shape[1]), axis=0)


def square_sum(kq):
    lane = lanes_of(kq.shape)
    return jnp.sum(jnp.where(lane < STATE, kq * kq, 0.0), axis=1, keepdims=True)


def forward_layer(zh_size, xg, win, mats, wout, vec, scale, nxt=None):
    tokens, width = xg.shape[1], xg.shape[2]
    half = win.shape[1] // 2
    parts = half // LANES
    rows = tokens * TP
    size = STEPS * TP
    blocks = rows // size
    halo = (CONV - 1) * TP
    dma = pltpu.SemaphoreType.DMA
    last = nxt is None
    groups = 2 * zh_size
    ins = dict(
        xg=(xg, VM), win=(win, VM), mats=(mats, VM), wout=(wout, HB if not last else VM), vec=(vec, VM),
        scale=(scale, VM), e=(spreader(), VM),
    )
    outs = dict(
        entry=(struct(2 * parts, halo + rows, LANES), VM), beta=(struct(parts, rows, LANES), VM),
        kq=(struct(rows, LANES), VM), proj=(struct(TP, size, 2 * LANES, dtype=bf16), VM),
        y=(struct(parts, rows, LANES), VM), keep=(struct(blocks, STATE, parts, TP, LANES), VM),
        mixed=(struct(TP, tokens, half, dtype=bf16), VM), stats=(struct(2, TP, LANES), VM),
    )
    scratch = dict(
        act=pltpu.VMEM((parts, rows, LANES), f32), step=pltpu.VMEM((parts, rows, LANES), f32),
        payload=pltpu.VMEM((TP, size, 2 * LANES), bf16), parts=pltpu.VMEM((TP - 1, size, 2 * LANES), bf16),
        own=pltpu.VMEM((size, 2 * LANES), f32),
        state=pltpu.VMEM((STATE, parts, TP, LANES), f32), wide=pltpu.VMEM((size, 32 * LANES), f32),
        part=pltpu.VMEM((TP, tokens, width), bf16),
        scatter_buf=Scatter.buffers((tokens, width)),
        sum_sems=Sum.sems(dma), scatter_sems=Scatter.sems(dma),
    )
    outs["result"] = (struct(tokens, width), VM)
    if not last:
        ins.update(
            h=(nxt["h"], VM), gain=(nxt["gain"], VM), win1=(nxt["win"], HB), mats1=(nxt["mats"], HB), wout1=(nxt["wout"], HB)
        )
        outs.update(
            wout_all=(struct(groups, *wout.shape, dtype=bf16), VM),
            win1_all=(struct(2, 2, zh_size, *nxt["win"].shape[1:], dtype=bf16), HB),
            mats1_all=(struct(groups, *nxt["mats"].shape, dtype=bf16), HB),
            wout1_all=(struct(groups, *nxt["wout"].shape, dtype=bf16), HB),
            xg1=(struct(TP, tokens, width, dtype=bf16), HB),
        )
        scratch.update(
            normed=pltpu.VMEM((tokens, width), bf16), gather_sems=Gather.sems(dma),
            d0=Spread.sems(dma, zh_size), d1=Spread.sems(dma, zh_size), d2=Spread.sems(dma, zh_size),
            d3=Spread.sems(dma, zh_size),
        )

    def body(r):
        targets = [p[0] for p in tp_peers()]
        if not last:
            side, far = dp_peers(zh_size)
            targets += [side] + [f[0] for f in far]
        greet(targets)
        entry, act, step, beta, kq, y = r["entry"], r["act"], r["step"], r["beta"], r["kq"], r["y"]
        if not last:
            index = lambda ref: lambda xx, zz: ref.at[xx * zh_size + zz]
            early = Spread(zh_size, r["wout"], index(r["wout_all"]), r["d0"])
            moves = [
                Spread(zh_size, r["win1"], lambda xx, zz: r["win1_all"].at[xx, :, zz], r["d1"]),
                Spread(zh_size, r["wout1"], index(r["wout1_all"]), r["d2"]),
                Spread(zh_size, r["mats1"], index(r["mats1_all"]), r["d3"]),
            ]
            early.start()

        entry[:, :halo, :] = jnp.zeros((2 * parts, halo, LANES), f32)
        tile = 2 * LANES
        for p in range(TP // 2):

            def columns(n, carry, p=p):
                cols = at_block(n, tile)
                out = jnp.dot(
                    r["xg"][2 * p : 2 * p + 2].reshape(2 * tokens, width), r["win"][:, cols],
                    preferred_element_type=f32,
                )
                for j in range(2):
                    for c in range(2):
                        entry[2 * n + c, pl.ds(halo + 2 * p + j, tokens, stride=TP), :] = out[
                            j * tokens : (j + 1) * tokens, c * LANES : (c + 1) * LANES
                        ]
                return carry

            lax.fori_loop(0, 2 * half // tile, columns, 0)
        if not last:
            moves[0].start()

        total = Sum(r["payload"], r["parts"], r["proj"], r["sum_sems"])

        def project(b, carry):
            rs = at_block(b, size)
            for c in range(parts):
                conv = conv_of(entry, r["vec"], b * size, size, c)
                act[c, rs, :] = (conv * jax.nn.sigmoid(conv)).astype(bf16).astype(f32)
            out = jnp.dot(
                wide_of(act, rs, parts).astype(bf16), r["mats"][:, RANK:], preferred_element_type=f32
            )
            r["payload"][b] = encode(out)

            @pl.when(b == total.me)
            def _():
                r["own"][...] = out

            return carry

        lax.fori_loop(0, blocks, project, 0)
        total.start()
        total.middle(r["own"][...])
        total.finish()
        if not last:
            early.onward()
            moves[1].start()
            moves[2].start()

        r["stats"][...] = jnp.zeros((2, TP, LANES), f32)

        def rates(b, carry):
            rs = at_block(b, size)
            tail = decode(r["proj"][b])[:, RANK:]
            keys = tail + pltpu.roll(tail, 32, 1) + pltpu.roll(tail, 64, 1)
            kq[rs, :] = keys
            norm = square_sum(keys)
            pre = dot(r["proj"][b, :, :RANK], r["mats"][:, :RANK], ((1,), (1,)))
            for c in range(parts):
                cols = slice(c * LANES, (c + 1) * LANES)
                rate = jax.nn.sigmoid(pre[:, cols] + r["vec"][CONV + 1 : CONV + 2, cols])
                beta[c, rs, :] = rate
                step[c, rs, :] = rate / (1.0 + rate * norm)
                r["stats"][0] += row_sum(rate)
                r["stats"][1] = jnp.maximum(
                    r["stats"][1], jnp.max(rate.reshape(-1, TP, LANES), axis=0)
                )
            return carry

        lax.fori_loop(0, blocks, rates, 0)
        r["stats"][0] = r["stats"][0] * r["scale"][...]
        r["stats"][1] = r["stats"][1] * r["scale"][...]

        lane = lanes_of((size, LANES))
        state, wide = r["state"], r["wide"]
        state[...] = jnp.zeros_like(state)

        def block(b, carry):
            r["keep"][b] = state[...]
            wide[...] = jnp.dot(spread_keys(kq[at_block(b, size), :], lane), r["e"][...], preferred_element_type=f32)

            def one(j, carry):
                t = at_block(b * STEPS + j, TP)
                w = at_block(j, TP)
                acts = [act[c, t, :] for c in range(parts)]
                steps = [step[c, t, :] for c in range(parts)]
                sums = [None] * parts
                for n in range(STATE):
                    key = wide[w, n * LANES : (n + 1) * LANES]
                    query = wide[w, (STATE + n) * LANES : (STATE + n + 1) * LANES]
                    for c in range(parts):
                        s = state[n, c]
                        s = s + (steps[c] * key) * (acts[c] - key * s)
                        state[n, c] = s
                        sums[c] = s * query if sums[c] is None else sums[c] + s * query
                for c in range(parts):
                    y[c, t, :] = sums[c]
                return carry

            lax.fori_loop(0, STEPS, one, 0)
            rs = at_block(b, size)
            here = pl.ds(pl.multiple_of(b * STEPS, STEPS), STEPS)
            for c in range(parts):
                cols = slice(c * LANES, (c + 1) * LANES)
                gate = entry[parts + c, pl.ds(pl.multiple_of(b * size + halo, TP), size), :]
                skip = r["vec"][CONV + 2 : CONV + 3, cols]
                step[c, rs, :] = (y[c, rs, :] + skip * act[c, rs, :]) * (gate * jax.nn.sigmoid(gate))
                for s in range(TP):
                    r["mixed"][s, here, cols] = step[c, pl.ds(b * size + s, STEPS, stride=TP), :].astype(bf16)
            return carry

        lax.fori_loop(0, blocks, block, 0)
        if not last:
            early.finish()
            moves[0].onward()
        weight = r["wout_all"] if not last else r["wout"]
        scatter = Scatter(r["part"], r["scatter_buf"], r["scatter_sems"])
        down = (lambda: weight[...].reshape(half, width)) if not last else (lambda: weight[...])
        out_partial(scatter, r["part"], r["mixed"], down)
        if last:
            r["result"][...] = scatter.total()
            return
        stream = r["h"][...] + scatter.total()
        r["result"][...] = stream
        r["normed"][...] = (stream * rms(stream) * r["gain"][...]).astype(bf16)
        spread = Gather(r["normed"], r["xg1"], r["gather_sems"])
        spread.start()
        for move in moves[1:]:
            move.onward()
        spread.onward()
        spread.finish()
        for move in moves:
            move.finish()

    return call(body, "layer_forward_last" if last else "layer_forward", 7 if last else 6, ins, outs, scratch)


def out_partial(scatter, part, left, right, turned=False):
    contract = ((1,), (1,)) if turned else ((1,), (0,))
    for i in range(4):
        for core in (1 - scatter.core, scatter.core):
            slot = core * WAYS + scatter.turns[i]
            part[slot] = dot(left[slot], right(), contract).astype(bf16)
        scatter.to_sibling(i)
        if i >= 1:
            scatter.across(i - 1)


class Reduce:
    @staticmethod
    def sems(dma, zh_size):
        far = max(1, zh_size - 1)
        return [dma, dma, dma((far,)), dma((far,))]

    @staticmethod
    def buffers(zh_size, block):
        return [
            pltpu.VMEM((zh_size,) + block, bf16), pltpu.VMEM((zh_size,) + block, bf16),
            pltpu.VMEM((max(1, zh_size - 1),) + block, bf16),
        ]

    def __init__(self, zh_size, src, buffers, sems):
        self.zh_size, self.src = zh_size, src
        self.near, self.mine, self.buf = buffers
        self.x_send, self.x_recv, self.z_send, self.z_recv = sems
        self.x, _, self.zh, _ = place()
        self.side, self.far = dp_peers(zh_size)

    def start(self):
        half = self.src.at[pl.ds((1 - self.x) * self.zh_size, self.zh_size)]
        self.over = remote(half, self.near, self.x_send, self.x_recv, self.side)
        self.over.start()

    def middle(self):
        self.over.wait_recv()
        for k in range(self.zh_size):
            self.mine[k] = (
                self.src[self.x * self.zh_size + k].astype(f32) + self.near[k].astype(f32)
            ).astype(bf16)
        self.along = [
            remote(self.mine.at[to_z], self.buf.at[k], self.z_send.at[k], self.z_recv.at[k], target)
            for k, (target, to_z, _) in enumerate(self.far)
        ]
        for copy in self.along:
            copy.start()

    def total(self):
        value = self.src[self.x * self.zh_size + self.zh].astype(f32) + self.near[self.zh].astype(f32)
        for k in range(self.zh_size - 1):
            self.along[k].wait_recv()
            value = value + self.buf[k].astype(f32)
        self.over.wait_send()
        for copy in self.along:
            copy.wait_send()
        return value


def backward_layer(zh_size, kept, gog, wout, mats, vec, xg, win, gain, h, grad, late=None, onward=True):
    tokens, width = xg.shape[1], xg.shape[2]
    half = win.shape[1] // 2
    parts = half // LANES
    rows = tokens * TP
    size = STEPS * TP
    blocks = rows // size
    halo = (CONV - 1) * TP
    groups = 2 * zh_size
    share = half // groups
    deep = width // (2 * groups)
    far = max(1, zh_size - 1)
    dma = pltpu.SemaphoreType.DMA
    fold = jnp.pad(jnp.repeat(jnp.eye(32, dtype=bf16), LANES, axis=0), ((0, 0), (0, 96)))
    ins = {k: (kept[k], VM) for k in ("entry", "beta", "kq", "proj", "keep")}
    ins.update(
        mats=(mats, VM), wout=(wout, HB), vec=(vec, VM), gain=(gain, VM), h=(h, VM), grad=(grad, VM),
        mixed=(kept["mixed"], HB), e=(spreader(), VM), fold=(fold, VM), gouts=(gog, HB), y=(kept["y"], HB), xg=(xg, HB), win=(win, HB),
    )
    outs = dict(
        prev=(struct(tokens, width), VM), gwin=(struct(2 * groups, deep, 2 * half, dtype=bf16), VM),
        near=(struct(groups, deep, 2 * half, dtype=bf16), HB), gwout=(struct(share, width), VM),
        gmats=(struct(half, 3 * LANES, dtype=bf16), VM), gvec=(struct(8, half), VM),
        ggain=(struct(1, width), VM),
    )
    block_f32 = pltpu.VMEM((parts, rows, LANES), f32)
    scratch = dict(
        a=pltpu.VMEM((TP, tokens, width), bf16), b=pltpu.VMEM(win.shape, bf16),
        gs=block_f32, act=block_f32, gact=block_f32, ggate=block_f32,
        step=pltpu.VMEM((parts, rows + halo, LANES), f32),
        states=pltpu.VMEM((STEPS + 1, STATE, parts, TP, LANES), f32),
        lam=pltpu.VMEM((STATE, parts, TP, LANES), f32), wide=pltpu.VMEM((size, 32 * LANES), f32),
        gstep=pltpu.VMEM((parts, size, LANES), f32),
        gentry=pltpu.VMEM((TP, tokens, 2 * half), bf16),
        payload=pltpu.VMEM((TP, size, 2 * LANES), bf16), parts=pltpu.VMEM((TP - 1, size, 2 * LANES), bf16),
        total=pltpu.VMEM((TP, size, 2 * LANES), bf16), own=pltpu.VMEM((size, 2 * LANES), f32),
        sums=pltpu.VMEM((8, parts, TP, LANES), f32),
        grate=pltpu.VMEM((half, LANES), f32), gselect=pltpu.VMEM((half, 2 * LANES), f32),
        gwo=pltpu.VMEM((groups, share, width), bf16),
        scatter_buf=Scatter.buffers((tokens, width)), reduce_buf=Reduce.buffers(zh_size, (share, width)),
        sum_sems=Sum.sems(dma), scatter_sems=Scatter.sems(dma), reduce_sems=Reduce.sems(dma, zh_size),
        loads=dma((7,)), over=[dma, dma],
    )
    if onward:
        outs["gog"] = (struct(TP, tokens, width, dtype=bf16), HB)
        scratch.update(gout=pltpu.VMEM((tokens, width), bf16), gather_sems=Gather.sems(dma))
    if late is not None:
        ins["late"] = (late, HB)
        outs["late"] = (struct(far, 2, *late.shape[2:], dtype=bf16), HB)
        scratch.update(late_sems=[dma((far,)), dma((far,))])
        ins["late_in"] = ins.pop("late")

    def body(r):
        x, core, zh, q = place()
        side, far_ones = dp_peers(zh_size)
        greet([p[0] for p in tp_peers()] + [side] + [f[0] for f in far_ones])
        entry, act, step, beta, kq = r["entry"], r["act"], r["step"], r["beta"], r["kq"]
        gs, gact, ggate, vec, sums = r["gs"], r["gact"], r["ggate"], r["vec"], r["sums"]
        loads = [
            pltpu.make_async_copy(src, dst, r["loads"].at[i])
            for i, (src, dst) in enumerate(
                (
                    (r["gouts"], r["a"]), (r["mixed"], r["gentry"].at[:, :, :half]),
                    (r["wout"].at[:, : 2 * half], r["b"].at[:half]), (r["wout"].at[:, 2 * half :], r["b"].at[half : 2 * half]),
                    (r["y"], gact), (r["xg"], r["a"]), (r["win"], r["b"]),
                )
            )
        ]
        for copy in loads[:5]:
            copy.start()
        passed = []
        if late is not None:
            for k, (target, to_z, _) in enumerate(far_ones):
                copy = remote(
                    r["late_in"].at[:, to_z], r["late"].at[k], r["late_sems"][0].at[k], r["late_sems"][1].at[k], target
                )
                copy.start()
                passed.append(copy)
        sums[...] = jnp.zeros_like(sums)
        r["grate"][...] = jnp.zeros_like(r["grate"])
        r["gselect"][...] = jnp.zeros_like(r["gselect"])

        def again(b, carry):
            rs = at_block(b, size)
            norm = square_sum(kq[rs, :])
            for c in range(parts):
                conv = conv_of(entry, vec, b * size, size, c)
                act[c, rs, :] = (conv * jax.nn.sigmoid(conv)).astype(bf16).astype(f32)
                rate = beta[c, rs, :]
                step[c, rs, :] = rate / (1.0 + rate * norm)
            return carry

        lax.fori_loop(0, blocks, again, 0)
        loads[0].wait()
        loads[1].wait()

        def outer(c, carry):
            left = r["gentry"][:, :, at_block(c, LANES)].reshape(rows, LANES)
            out = dot(left, r["a"][...].reshape(rows, width), ((0,), (0,))).astype(bf16)
            each = LANES // share
            r["gwo"][pl.ds(c * each, each)] = out.reshape(each, share, width)
            return carry

        lax.fori_loop(0, parts, outer, 0)
        reduce = Reduce(zh_size, r["gwo"], r["reduce_buf"], r["reduce_sems"])
        reduce.start()
        loads[2].wait()
        loads[3].wait()
        for p in range(TP // 2):

            def columns(n, carry, p=p):
                out = 0.0
                for k in range(2):
                    left = r["a"][2 * p : 2 * p + 2, :, 2 * half * k : 2 * half * (k + 1)].reshape(2 * tokens, 2 * half)
                    right = r["b"][pl.ds(pl.multiple_of(half * k + n * 2 * LANES, 2 * LANES), 2 * LANES), :]
                    out = out + dot(left, right, ((1,), (1,)))
                for j in range(2):
                    for c in range(2):
                        gs[2 * n + c, pl.ds(2 * p + j, tokens, stride=TP), :] = out[
                            j * tokens : (j + 1) * tokens, c * LANES : (c + 1) * LANES
                        ]
                return carry

            lax.fori_loop(0, half // (2 * LANES), columns, 0)
        loads[5].start()
        loads[6].start()
        loads[4].wait()

        def gates(b, carry):
            rs = at_block(b, size)
            for c in range(parts):
                cols = slice(c * LANES, (c + 1) * LANES)
                gate = entry[parts + c, pl.ds(pl.multiple_of(b * size + halo, TP), size), :]
                sig = jax.nn.sigmoid(gate)
                g = gs[c, rs, :]
                a = act[c, rs, :]
                down = g * (gate * sig)
                ggate[c, rs, :] = g * (gact[c, rs, :] + vec[CONV + 2 : CONV + 3, cols] * a) * (
                    sig * (1.0 + gate * (1.0 - sig))
                )
                gs[c, rs, :] = down
                sums[CONV + 2, c] += row_sum(down * a)
            return carry

        lax.fori_loop(0, blocks, gates, 0)

        lane = lanes_of((size, LANES))
        states, lam, wide, gstep = r["states"], r["lam"], r["wide"], r["gstep"]
        lam[...] = jnp.zeros_like(lam)
        plus = lambda a, b: b if a is None else a + b
        total = Sum(r["payload"], r["parts"], r["total"], r["sum_sems"])

        def block(bi, carry):
            b = blocks - 1 - bi
            rs = at_block(b, size)
            states[0] = r["keep"][b]
            wide[...] = jnp.dot(spread_keys(kq[rs, :], lane), r["e"][...], preferred_element_type=f32)

            def replay(j, carry):
                t, w = at_block(b * STEPS + j, TP), at_block(j, TP)
                acts = [act[c, t, :] for c in range(parts)]
                steps = [step[c, t, :] for c in range(parts)]
                for n in range(STATE):
                    key = wide[w, n * LANES : (n + 1) * LANES]
                    for c in range(parts):
                        s = states[j, n, c]
                        states[j + 1, n, c] = s + (steps[c] * key) * (acts[c] - key * s)
                return carry

            lax.fori_loop(0, STEPS, replay, 0)

            def back(jj, carry):
                j = STEPS - 1 - jj
                t, w = at_block(b * STEPS + j, TP), at_block(j, TP)
                acts = [act[c, t, :] for c in range(parts)]
                steps = [step[c, t, :] for c in range(parts)]
                gsums = [gs[c, t, :] for c in range(parts)]
                first, second = [None] * parts, [None] * parts
                for n in range(STATE):
                    kcols, qcols = slice(n * LANES, (n + 1) * LANES), slice((STATE + n) * LANES, (STATE + n + 1) * LANES)
                    key, query = wide[w, kcols], wide[w, qcols]
                    key_term, query_term = None, None
                    for c in range(parts):
                        before, after = states[j, n, c], states[j + 1, n, c]
                        grad = lam[n, c] + gsums[c] * query
                        u = key * before
                        d = acts[c] - u
                        gk = grad * key
                        first[c] = plus(first[c], gk * d)
                        second[c] = plus(second[c], gk)
                        key_term = plus(key_term, (steps[c] * grad) * (d - u))
                        query_term = plus(query_term, gsums[c] * after)
                        lam[n, c] = grad - (steps[c] * key) * gk
                    wide[w, kcols] = key_term
                    wide[w, qcols] = query_term
                for c in range(parts):
                    gstep[c, w, :] = first[c]
                    gact[c, t, :] = steps[c] * second[c]
                return carry

            lax.fori_loop(0, STEPS, back, 0)
            terms = wide[...]
            high = terms.astype(bf16)
            low = (terms - high.astype(f32)).astype(bf16)
            gkq = jnp.dot(high, r["fold"][...], preferred_element_type=f32) + jnp.dot(
                low, r["fold"][...], preferred_element_type=f32
            )
            keys = kq[rs, :]
            norm = square_sum(keys)
            gnorm = jnp.zeros((size, 1), f32)
            grates = []
            for c in range(parts):
                cols = slice(c * LANES, (c + 1) * LANES)
                rate = beta[c, rs, :]
                g = gstep[c]
                inverse = 1.0 + rate * norm
                inverse = 1.0 / (inverse * inverse)
                gnorm = gnorm - jnp.sum(g * (rate * rate * inverse), axis=1, keepdims=True)
                grate = g * inverse * rate * (1.0 - rate)
                sums[CONV + 1, c] += row_sum(grate)
                grates.append(grate.astype(bf16))
                gact[c, rs, :] += vec[CONV + 2 : CONV + 3, cols] * gs[c, rs, :]
            grate = jnp.concatenate(grates, axis=1)
            r["grate"][...] += dot(grate, r["proj"][b, :, :RANK], ((0,), (0,)))
            grank = dot(grate, r["mats"][:, :RANK], ((1,), (0,)))
            gkq = gkq + jnp.where(lane < STATE, 2.0 * keys * gnorm, 0.0)
            out = jnp.concatenate([grank, gkq], axis=1)
            r["payload"][b] = encode(out)

            @pl.when(b == total.me)
            def _():
                r["own"][...] = out

            return carry

        lax.fori_loop(0, blocks, block, 0)
        total.start()
        reduce.middle()
        total.middle(r["own"][...])
        total.finish()
        step[:, rows:, :] = jnp.zeros((parts, halo, LANES), f32)
        gconv = step

        def convs(b, carry):
            rs = at_block(b, size)
            gp = r["total"][b]
            gp = jnp.where(lanes_of(gp.shape) < RANK + 2 * STATE, gp.astype(f32), 0.0).astype(bf16)
            r["gselect"][...] += dot(wide_of(act, rs, parts).astype(bf16), gp, ((0,), (0,)))
            more = dot(gp, r["mats"][:, RANK:], ((1,), (1,)))
            for c in range(parts):
                conv = conv_of(entry, vec, b * size, size, c)
                sig = jax.nn.sigmoid(conv)
                g = (gact[c, rs, :] + more[:, c * LANES : (c + 1) * LANES]) * (sig * (1.0 + conv * (1.0 - sig)))
                gconv[c, rs, :] = g
                sums[CONV, c] += row_sum(g)
                for j in range(CONV):
                    inner = entry[c, pl.ds(pl.multiple_of(b * size + TP * j, TP), size), :]
                    sums[j, c] += row_sum(g * inner)
            return carry

        lax.fori_loop(0, blocks, convs, 0)

        def inners(b, carry):
            rs = at_block(b, size)
            here = pl.ds(pl.multiple_of(b * STEPS, STEPS), STEPS)
            for c in range(parts):
                cols = slice(c * LANES, (c + 1) * LANES)
                value = None
                for j in range(CONV):
                    at = pl.ds(pl.multiple_of(b * size + TP * (CONV - 1 - j), TP), size)
                    value = plus(value, vec[j : j + 1, cols] * gconv[c, at, :])
                gs[c, rs, :] = value
                for s in range(TP):
                    at = pl.ds(b * size + s, STEPS, stride=TP)
                    r["gentry"][s, here, cols] = gs[c, at, :].astype(bf16)
                    r["gentry"][s, here, half + c * LANES : half + (c + 1) * LANES] = ggate[c, at, :].astype(bf16)
            return carry

        lax.fori_loop(0, blocks, inners, 0)
        loads[5].wait()
        tile = 2 * LANES

        def outer_in(i, carry):
            left = r["a"][:, :, at_block(i, tile)].reshape(rows, tile)
            out = dot(left, r["gentry"][...].reshape(rows, 2 * half), ((0,), (0,))).astype(bf16)
            each = tile // deep
            r["gwin"][pl.ds(i * each, each)] = out.reshape(each, deep, 2 * half)
            return carry

        lax.fori_loop(0, width // tile, outer_in, 0)
        over = remote(
            r["gwin"].at[pl.ds((1 - x) * groups, groups)], r["near"], r["over"][0], r["over"][1], side
        )
        over.start()
        loads[6].wait()
        scatter = Scatter(r["a"], r["scatter_buf"], r["scatter_sems"])
        out_partial(scatter, r["a"], r["gentry"], lambda: r["b"][...], turned=True)
        r["gmats"][:, :RANK] = r["grate"][...].astype(bf16)
        r["gmats"][:, RANK:] = r["gselect"][...].astype(bf16)
        for j in range(8):
            for c in range(parts):
                r["gvec"][j : j + 1, c * LANES : (c + 1) * LANES] = jnp.sum(sums[j, c], axis=0, keepdims=True)
        r["gwout"][...] = reduce.total()
        gnormed = scatter.total()
        stream = r["h"][...]
        scale = rms(stream)
        r["ggain"][...] = jnp.sum(gnormed * stream * scale, axis=0, keepdims=True)
        scaled = gnormed * r["gain"][...]
        grad = r["grad"][...] + scale * scaled - stream * (scale * scale * scale) * jnp.mean(
            stream * scaled, axis=-1, keepdims=True
        )
        r["prev"][...] = grad
        if onward:
            r["gout"][...] = grad.astype(bf16)
            spread = Gather(r["gout"], r["gog"], r["gather_sems"])
            spread.start()
            spread.onward()
            spread.finish()
        for copy in passed:
            copy.wait()
        over.wait()

    return call(body, "layer_backward", 9 if onward else 8, ins, outs, scratch)


def on_device(
    hidden, cotangent, groups, group_weights, input_weight, select_weight, rate_weight,
    output_weight, norm_gain, conv_taps, conv_shift, rate_shift, skip_gain,
):
    fsdp = lax.axis_size("fsdp")
    zh_size = fsdp // WAYS
    count = 2 * 2 * fsdp
    group_count = 2 * zh_size
    share = conv_shift.shape[1]
    gains = norm_gain.shape[1]
    depth = input_weight.shape[1]
    x, core, zh, q = place()

    labels = jnp.arange(group_weights.shape[0])
    own_weight = jnp.sum(jnp.where(groups[:, None] == labels[None, :], group_weights[None, :], 0.0))

    wins, mats, smalls, misc = [], [], [], []
    for l in range(LAYERS):
        win = input_weight[l].reshape(depth, 2, 2, 2, zh_size, WAYS, share)
        wins.append(win.transpose(3, 5, 0, 1, 2, 4, 6).reshape(TP, depth, 2 * group_count * share))
        both = jnp.concatenate([rate_weight[l].T, select_weight[l]], axis=1)
        mats.append(jnp.pad(both, ((0, 0), (0, 3 * LANES - both.shape[1]))))
        small = jnp.concatenate(
            [conv_taps[l], conv_shift[l][None], rate_shift[l][None], skip_gain[l][None], skip_gain[l][None]]
        ).astype(f32)
        smalls.append(jnp.pad(small, ((0, 0), (0, 128 - share))))
        misc.append(jnp.pad(norm_gain[l].astype(f32)[None], ((0, 0), (0, 128 - gains))))
    misc = jnp.concatenate(misc + [jnp.full((8 - LAYERS, 128), own_weight)])
    win, late, small, misc, mat = gather_weights(
        zh_size, wins[0], wins[1], jnp.concatenate(smalls), misc, mats[0]
    )
    all_weights = misc[:, LAYERS, 0]
    small = small[:, :, :share].transpose(1, 0, 2).reshape(LAYERS, 8, group_count * share)
    gain = [misc[:, l, :gains].reshape(1, count * gains) for l in range(LAYERS)]
    late = late.reshape(2, WAYS * depth, -1)
    width = output_weight.shape[2]
    scales = all_weights / jnp.mean(all_weights)
    table = scales.reshape(2, 2, zh_size, WAYS)
    own_scale = table[x, core, zh, q]
    group_scale = table[x, :, zh, :].reshape(TP)

    group_scale = jnp.broadcast_to(group_scale[:, None], (TP, LANES))

    h0 = hidden[0]
    xg0 = tp_gather((h0 * rms(h0) * gain[0]).astype(bf16))
    grad = cotangent[0] * own_scale
    gog1 = tp_gather(grad.astype(bf16))
    flat = lambda a: a.reshape(group_count * share, -1)
    win0, mat0 = win.reshape(count * depth, -1), flat(mat)
    one = forward_layer(
        zh_size, xg0, win0, mat0, output_weight[0], small[0], group_scale,
        dict(h=h0, gain=gain[1], win=late, mats=mats[1], wout=output_weight[1]),
    )
    win1, mat1 = one["win1_all"].reshape(count * depth, -1), flat(one["mats1_all"])
    wout0, wout1 = flat(one["wout_all"]), flat(one["wout1_all"])
    h1 = one["result"]
    two = forward_layer(zh_size, one["xg1"], win1, mat1, wout1, small[1], group_scale)
    stream = h1 + two["result"]
    sums = [jnp.sum(o["stats"][0]) for o in (one, two)]
    peaks = [jnp.max(o["stats"][1]) for o in (one, two)]
    pad = [jnp.zeros((), f32)] * (4 - LAYERS)
    own_stats = jnp.broadcast_to(jnp.stack(sums + pad + peaks + pad)[:, None], (8, 128))

    down1 = backward_layer(zh_size, two, gog1, wout1, mat1, small[1], one["xg1"], win1, gain[1], h1, grad)
    grid = (2, 2, zh_size, WAYS * depth, -1)
    pick = lambda a, i: lax.dynamic_index_in_dim(a, i, 0, keepdims=False)
    summed = pick(down1["gwin"].reshape(grid), x).astype(f32) + down1["near"].reshape(grid[1:]).astype(f32)
    down0 = backward_layer(
        zh_size, one, down1["gog"], wout0, mat0, small[0], xg0, win0, gain[0], h0, down1["prev"],
        late=summed.astype(bf16), onward=False,
    )
    grad = down0["prev"]
    late = lax.dynamic_index_in_dim(summed, zh, 1, keepdims=False)
    for k in range(zh_size - 1):
        late = late + down0["late"][k].astype(f32)
    late = late.astype(bf16).reshape(TP, depth, -1)
    smalls, gain_sums, mats = [], [], []
    for down in (down0, down1):
        vec = down["gvec"][:7].reshape(7, group_count, share).transpose(1, 0, 2)
        smalls.append(jnp.pad(vec, ((0, 0), (0, 9), (0, 128 - share))))
        part = down["ggain"].reshape(2, 2, zh_size, WAYS, gains).transpose(1, 3, 0, 2, 4)
        gain_sums.append(part.reshape(TP, group_count, gains))
        mats.append(down["gmats"])
    small = jnp.concatenate(smalls, axis=1).reshape(2, zh_size, 16 * LAYERS, 128)
    mats = jnp.concatenate(mats, axis=1).reshape(2, zh_size, share, -1)
    gain = jnp.concatenate(gain_sums, axis=1)
    gain = jnp.pad(gain, ((0, 0), (0, -gain.shape[1] % 8), (0, 128 - gains)))
    first, mats, small, stats, late = scatter_gradients(
        zh_size, down0["gwin"].reshape(grid), down0["near"].reshape(grid[1:]), mats, small, own_stats, gain, late
    )
    outs = [[] for _ in range(9)]
    for l, win in enumerate((first, late)):
        m = mats[:, 3 * LANES * l : 3 * LANES * (l + 1)]
        win = win.reshape(2, WAYS, depth, 2, 2, zh_size, share).transpose(2, 3, 4, 0, 5, 1, 6)
        outs[0].append(win.reshape(depth, -1).astype(f32))
        outs[1].append(m[:, RANK : RANK + select_weight.shape[2]])
        outs[2].append(m[:, :RANK].T)
        outs[3].append((down0, down1)[l]["gwout"])
        vec = small[16 * l : 16 * (l + 1)]
        outs[4].append(vec[8, :gains])
        outs[5].append(vec[:CONV, :share])
        outs[6].append(vec[CONV, :share])
        outs[7].append(vec[CONV + 1, :share])
        outs[8].append(vec[CONV + 2, :share])
    stacked = tuple(jnp.stack(o) for o in outs)
    beta_mean = stats[:LAYERS, 0] / (count * hidden.shape[1] * INNER)
    beta_max = stats[4 : 4 + LAYERS, 0]
    return (stream[None], grad[None]) + stacked + (beta_mean, beta_max)


def solution(mesh):
    both = ("dp", "fsdp")
    placed = (
        P(both, None, None), P(both, None, None), P(both), P(),
        P(None, both, None), P(None, both, None), P(None, None, both), P(None, both, None),
        P(None, both), P(None, None, both), P(None, both), P(None, both), P(None, both),
    )
    return jax.shard_map(
        on_device,
        mesh=mesh,
        in_specs=placed,
        out_specs=(P(both, None, None), P(both, None, None)) + placed[4:] + (P(), P()),
        check_vma=False,
    )
```

```python
import jax
import jax.numpy as jnp
import numpy as np
from jax import lax
from jax.sharding import PartitionSpec as P
import jax.experimental.pallas as pl
import jax.experimental.pallas.tpu as pltpu

INNER = 4096
STATE = 16
RANK = 128
CONV = 4
LAYERS = 2
WAYS = 4
TP = 8
STEPS = 16

eps = 1e-05
MESH = pl.DeviceIdType.MESH
f32 = jnp.float32
bf16 = jnp.bfloat16
VM = pl.BlockSpec(memory_space=pltpu.VMEM)
HB = pl.BlockSpec(memory_space=pl.ANY)


def place():
    dp, fs = lax.axis_index("dp"), lax.axis_index("fsdp")
    return dp // 2, lax.rem(dp, 2), fs // WAYS, lax.rem(fs, WAYS)


def device(x, core, zh, q):
    return (x * 2 + core, zh * WAYS + q)


def remote(src, dst, send, recv, target):
    return pltpu.make_async_remote_copy(
        src_ref=src, dst_ref=dst, send_sem=send, recv_sem=recv, device_id=target, device_id_type=MESH
    )


def greet(targets):
    barrier = pltpu.get_barrier_semaphore()
    for target in targets:
        pl.semaphore_signal(barrier, inc=1, device_id=target, device_id_type=MESH)
    pl.semaphore_wait(barrier, len(targets))


def tp_peers():
    x, core, zh, q = place()
    peers = []
    for dc in (0, 1):
        for dq in (1, 3, 2, 0):
            if dc == 0 and dq == 0:
                continue
            other_core = lax.rem(core + dc, 2)
            to_q, from_q = lax.rem(q + dq, WAYS), lax.rem(q + WAYS - dq, WAYS)
            peers.append(
                (device(x, other_core, zh, to_q), other_core * WAYS + to_q, other_core * WAYS + from_q)
            )
    return peers


def neighbour(q, da, db):
    a, b = lax.rem(q, 2), q // 2
    return (1 - b if db else b) * 2 + (1 - a if da else a)


def total_rank():
    _, core, _, q = place()
    return core * WAYS + q


def dp_peers(zh_size):
    x, core, zh, q = place()
    side = device(1 - x, core, zh, q)
    far = []
    for dz in range(1, zh_size):
        to_z, from_z = lax.rem(zh + dz, zh_size), lax.rem(zh + zh_size - dz, zh_size)
        far.append((device(x, core, to_z, q), to_z, from_z))
    return side, far


def lanes_of(shape):
    return lax.broadcasted_iota(jnp.int32, shape, 1)


def encode(v):
    tail = v[:, RANK:]
    lane = lanes_of(tail.shape)
    high = tail.astype(bf16).astype(f32)
    low = pltpu.roll(tail - high, 32, 1)
    both = jnp.where(lane < 32, high, jnp.where(lane < 64, low, 0.0))
    return jnp.concatenate([v[:, :RANK].astype(bf16), both.astype(bf16)], axis=1)


def decode(v):
    tail = v[:, RANK:].astype(f32)
    lane = lanes_of(tail.shape)
    tail = jnp.where(lane < 32, tail + pltpu.roll(tail, 96, 1), 0.0)
    return jnp.concatenate([v[:, :RANK].astype(f32), tail], axis=1)


def halves(rows):
    return pl.ds(0, rows // 2), pl.ds(rows // 2, rows // 2)


class Gather:
    sems = staticmethod(lambda dma: [dma((6,)), dma((6,)), dma((4,)), dma((4,)), dma])

    def __init__(self, src, out, sems):
        self.src, self.out = src, out
        self.f_send, self.f_recv, self.s_send, self.s_recv, self.own_sem = sems
        x, core, zh, q = place()
        self.core, self.me = core, core * WAYS + q
        self.sibling = device(x, 1 - core, zh, q)
        self.chips = [neighbour(q, 0, 1), neighbour(q, 1, 0), neighbour(q, 1, 1)]
        self.b, self.a = [device(x, core, zh, c) for c in self.chips[:2]]
        self.top, self.low = halves(src.shape[0])

    def send(self, i, src, slot, rows, target):
        copy = remote(src, self.out.at[slot, rows], self.f_send.at[i], self.f_recv.at[i], target)
        copy.start()
        return copy

    def to_sibling(self, i, src, slot):
        copy = remote(src, self.out.at[slot], self.s_send.at[i], self.s_recv.at[i], self.sibling)
        copy.start()
        self.near.append(copy)

    def start(self):
        self.near = []
        self.first = [
            self.send(i, self.src.at[rows], self.me, rows, target)
            for i, (rows, target) in enumerate(
                ((self.top, self.b), (self.low, self.a), (self.low, self.b), (self.top, self.a))
            )
        ]
        self.to_sibling(3, self.src, self.me)
        self.own = pltpu.make_async_copy(self.src, self.out.at[self.me], self.own_sem)
        self.own.start()

    def relay(self):
        for i, rows, target in ((0, self.top, self.a), (1, self.low, self.b)):
            self.first[i].wait_recv()
            slot = self.core * WAYS + self.chips[i]
            self.first.append(self.send(4 + i, self.out.at[slot, rows], slot, rows, target))

    def rest(self):
        for i, ends in enumerate(((2,), (3,), (4, 5))):
            for k in ends:
                self.first[k].wait_recv()
            slot = self.core * WAYS + self.chips[i]
            self.to_sibling(i, self.out.at[slot], slot)

    def finish(self):
        for copy in self.first:
            copy.wait_send()
        for copy in self.near:
            copy.wait()
        self.own.wait()


class Scatter:
    sems = staticmethod(lambda dma: [dma((4,)), dma((4,)), dma((6,)), dma((6,))])

    @staticmethod
    def buffers(block):
        return [pltpu.VMEM((4,) + block, bf16), pltpu.VMEM((3,) + block, bf16), pltpu.VMEM((3,) + block, bf16)]

    def __init__(self, partial, buffers, sems):
        self.partial = partial
        self.near_buf, self.out, self.into = buffers
        self.s_send, self.s_recv, self.f_send, self.f_recv = sems
        x, core, zh, q = place()
        self.core = core
        self.sibling = device(x, 1 - core, zh, q)
        self.turns = [neighbour(q, 1, 1), neighbour(q, 1, 0), neighbour(q, 0, 1), q]
        self.a, self.b = [device(x, core, zh, t) for t in self.turns[1:3]]
        self.top, self.low = halves(partial.shape[1])
        self.near, self.first = [None] * 4, {}

    def to_sibling(self, i):
        slot = (1 - self.core) * WAYS + self.turns[i]
        self.near[i] = remote(
            self.partial.at[slot], self.near_buf.at[i], self.s_send.at[i], self.s_recv.at[i], self.sibling
        )
        self.near[i].start()

    def joined(self, i, rows=slice(None)):
        own = self.partial[self.core * WAYS + self.turns[i], rows]
        return own.astype(f32) + self.near_buf[i, rows].astype(f32)

    def send(self, k, i, rows, target):
        self.first[k] = remote(
            self.out.at[i, rows], self.into.at[i, rows], self.f_send.at[k], self.f_recv.at[k], target
        )
        self.first[k].start()

    def across(self, i):
        self.near[i].wait_recv()
        if i == 0:
            self.out[0] = self.joined(0).astype(bf16)
            self.send(0, 0, self.top, self.a)
            self.send(1, 0, self.low, self.b)
        else:
            rows, target = ((self.top, self.a), (self.low, self.b))[i - 1]
            self.out[i, rows] = self.joined(i, rows).astype(bf16)
            self.send(1 + i, i, rows, target)

    def sums(self):
        for k, i, rows, target in ((1, 1, self.low, self.a), (0, 2, self.top, self.b)):
            self.first[k].wait_recv()
            self.out[i, rows] = (self.joined(i, rows) + self.into[0, rows].astype(f32)).astype(bf16)
            self.send(3 + i, i, rows, target)

    def total(self):
        self.near[3].wait_recv()
        value = self.joined(3)
        for k in (2, 3, 4, 5):
            self.first[k].wait_recv()
        value = value + self.into[1].astype(f32) + self.into[2].astype(f32)
        for copy in self.near + list(self.first.values()):
            copy.wait_send()
        return value


class Spread:
    @staticmethod
    def sems(dma, zh_size):
        far = max(1, zh_size - 1)
        return [dma((far,)), dma((far,)), dma((zh_size,)), dma((zh_size,)), dma]

    def __init__(self, zh_size, src, view, sems, keep=True):
        self.src, self.view, self.keep = src, view, keep
        self.z_send, self.z_recv, self.x_send, self.x_recv, self.own_sem = sems
        self.x, _, self.zh, _ = place()
        self.side, self.far = dp_peers(zh_size)

    def start(self):
        dst = self.view(self.x, self.zh)
        self.along = [
            remote(self.src, dst, self.z_send.at[k], self.z_recv.at[k], target)
            for k, (target, _, _) in enumerate(self.far)
        ]
        self.over = [remote(self.src, dst, self.x_send.at[0], self.x_recv.at[0], self.side)]
        for copy in self.along + self.over:
            copy.start()
        if self.keep:
            self.own = pltpu.make_async_copy(self.src, dst, self.own_sem)
            self.own.start()

    def onward(self):
        for k, (_, _, source) in enumerate(self.far):
            self.along[k].wait_recv()
            slot = self.view(self.x, source)
            copy = remote(slot, slot, self.x_send.at[k + 1], self.x_recv.at[k + 1], self.side)
            copy.start()
            self.over.append(copy)

    def finish(self):
        for copy in self.along:
            copy.wait_send()
        for copy in self.over:
            copy.wait()
        if self.keep:
            self.own.wait()


class Sum:
    sems = staticmethod(lambda dma: [dma((TP - 1,))] * 4)

    def __init__(self, payload, parts, out, sems):
        self.payload, self.parts, self.out = payload, parts, out
        self.a_send, self.a_recv, self.b_send, self.b_recv = sems
        x, core, zh, q = place()
        self.me = core * WAYS + q
        self.peers = tp_peers()

    def start(self):
        self.one = [
            remote(self.payload.at[rank], self.parts.at[i], self.a_send.at[i], self.a_recv.at[i], target)
            for i, (target, rank, _) in enumerate(self.peers)
        ]
        for copy in self.one:
            copy.start()

    def middle(self, own):
        total = own
        for i in range(TP - 1):
            self.one[i].wait_recv()
            total = total + decode(self.parts[i])
        self.out[self.me] = encode(total)
        self.two = [
            remote(self.out.at[self.me], self.out.at[self.me], self.b_send.at[i], self.b_recv.at[i], target)
            for i, (target, _, _) in enumerate(self.peers)
        ]
        for copy in self.two:
            copy.start()

    def finish(self):
        for copy in self.one:
            copy.wait_send()
        for copy in self.two:
            copy.wait()


def call(body, name, collective, ins, outs, scratch, **options):
    names = list(ins) + list(outs) + list(scratch)

    def kernel(*refs):
        named, refs = {}, list(refs)
        flat = []
        for key in names:
            kind = scratch.get(key)
            if isinstance(kind, list):
                named[key] = refs[: len(kind)]
                refs = refs[len(kind) :]
            else:
                named[key] = refs.pop(0)
        body(named)

    flat = []
    for kind in scratch.values():
        flat += kind if isinstance(kind, list) else [kind]
    values = pl.pallas_call(
        kernel,
        out_shape=[shape for shape, _ in outs.values()],
        in_specs=[spec for _, spec in ins.values()],
        out_specs=[spec for _, spec in outs.values()],
        scratch_shapes=flat,
        compiler_params=pltpu.CompilerParams(
            collective_id=collective, has_side_effects=True, vmem_limit_bytes=63 * 2**20
        ),
        name=name,
    )(*[array for array, _ in ins.values()])
    return dict(zip(outs, values))


def spread_keys(kq, lane):
    a = kq.astype(bf16).astype(f32)
    rest = kq - a
    b = rest.astype(bf16).astype(f32)
    c = rest - b
    return jnp.where(lane < 32, a, jnp.where(lane < 64, b, c)).astype(bf16)


def spreader():
    one = np.repeat(np.eye(32, dtype=np.float32), 128, axis=1)
    return jnp.asarray(np.concatenate([one, one, one, np.zeros_like(one)], axis=0), bf16)


def folder():
    return jnp.asarray(np.pad(np.repeat(np.eye(32, dtype=np.float32), 128, axis=0), ((0, 0), (0, 96))), bf16)


def dot(a, b, contract, out=f32):
    return lax.dot_general(a, b, (contract, ((), ())), preferred_element_type=out)


def rms(stream):
    return lax.rsqrt(jnp.mean(jnp.square(stream), axis=-1, keepdims=True) + eps)


LANES = 128


def struct(*shape, dtype=f32):
    return jax.ShapeDtypeStruct(shape, dtype)


def side_by_side(pieces, lanes):
    each = LANES // lanes
    out = []
    for i in range(0, len(pieces), each):
        tile = pieces[i]
        for j in range(1, each):
            tile = tile + pltpu.roll(pieces[i + j], j * lanes, 1)
        out.append(tile)
    return jnp.concatenate(out, axis=1)


def opening(zh_size, gains, share, win, small, misc, mats, h, cot):
    groups = 2 * zh_size
    count = groups * TP
    tokens, width = h.shape
    half = groups * share
    dma = pltpu.SemaphoreType.DMA
    ins = dict(
        win=(win, HB), small=(small, VM), misc=(misc, VM), mats=(mats, HB), h=(h, VM), cot=(cot, VM)
    )
    outs = dict(
        win_all=(struct(count, *win.shape[1:], dtype=bf16), HB),
        mats_all=(struct(groups, *mats.shape, dtype=bf16), HB), vec=(struct(8 * LAYERS, half), VM),
        gains=(struct(8, width), VM), scale=(struct(TP, LANES), VM), grad=(struct(tokens, width), VM),
        gout=(struct(tokens, width, dtype=bf16), VM), xg=(struct(TP, tokens, width, dtype=bf16), HB),
    )
    spread = lambda: Spread.sems(dma, zh_size)
    scratch = dict(
        misc_all=pltpu.VMEM((count,) + misc.shape, f32), small_all=pltpu.VMEM((groups,) + small.shape, f32),
        normed=pltpu.VMEM((tokens, width), bf16), gather_sems=Gather.sems(dma),
        m_sems=[dma((TP - 1,))] * 2, w_sems=[dma((TP - 1,))] * 2,
        s0=spread(), s1=spread(),
    )
    for i in range(TP):
        scratch["sm%d" % i] = spread()
        scratch["sw%d" % i] = spread()

    def body(r):
        x, core, zh, q = place()
        me = core * WAYS + q
        peers = tp_peers()
        side, far = dp_peers(zh_size)
        greet([p[0] for p in peers] + [side] + [f[0] for f in far])

        def row(xx, zz, rank):
            return ((xx * 2 + rank // WAYS) * zh_size + zz) * WAYS + lax.rem(rank, WAYS)

        def views(out, rank):
            return lambda xx, zz: out.at[row(xx, zz, rank)]

        def exchange(src, out, slot, sems):
            copies = []
            for i, (target, rank, _) in enumerate(peers):
                copies.append(remote(src(rank), out.at[slot], sems[0].at[i], sems[1].at[i], target))
                copies[-1].start()
            return copies

        here = row(x, zh, me)
        miscs = exchange(lambda rank: r["misc"], r["misc_all"], here, r["m_sems"])
        misc_moves = [Spread(zh_size, r["misc"], views(r["misc_all"], me), r["sm0"])]
        misc_moves[0].start()
        smalls = Spread(zh_size, r["small"], lambda xx, zz: r["small_all"].at[xx * zh_size + zz], r["s0"])
        smalls.start()
        wins = exchange(lambda rank: r["win"].at[rank], r["win_all"], here, r["w_sems"])
        win_moves = [Spread(zh_size, r["win"].at[me], views(r["win_all"], me), r["sw0"])]
        for i, (_, _, source) in enumerate(peers):
            view = views(r["win_all"], source)
            win_moves.append(Spread(zh_size, view(x, zh), view, r["sw%d" % (i + 1)], keep=False))
        mats_move = Spread(zh_size, r["mats"], lambda xx, zz: r["mats_all"].at[xx * zh_size + zz], r["s1"])

        def step(i):
            if i >= 1:
                wins[i - 1].wait_recv()
            if i >= 2:
                win_moves[i - 2].onward()
            win_moves[i].start()

        step(0)
        for i, (_, _, source) in enumerate(peers):
            miscs[i].wait_recv()
            view = views(r["misc_all"], source)
            misc_moves.append(Spread(zh_size, view(x, zh), view, r["sm%d" % (i + 1)], keep=False))
            misc_moves[-1].start()
        step(1)
        for move in misc_moves:
            move.onward()
        smalls.onward()
        for move in misc_moves:
            move.finish()
        for l in range(LAYERS):
            r["gains"][l : l + 1, :] = side_by_side(
                [r["misc_all"][d, l : l + 1, :] for d in range(count)], gains
            )
        r["gains"][LAYERS:, :] = jnp.zeros((8 - LAYERS, width), f32)
        stream = r["h"][...]
        r["normed"][...] = (stream * rms(stream) * r["gains"][0:1, :]).astype(bf16)
        rows = Gather(r["normed"], r["xg"], r["gather_sems"])
        rows.start()
        step(2)
        mats_move.start()
        total = r["misc_all"][0, LAYERS : LAYERS + 1, :]
        for d in range(1, count):
            total = total + r["misc_all"][d, LAYERS : LAYERS + 1, :]
        inverse = count / total
        for rank in range(TP):
            r["scale"][rank : rank + 1, :] = r["misc_all"][row(x, zh, rank), LAYERS : LAYERS + 1, :] * inverse
        own = (r["misc"][LAYERS : LAYERS + 1, :] * inverse)[:, :1]
        grad = r["cot"][...] * own
        r["grad"][...] = grad
        r["gout"][...] = grad.astype(bf16)
        step(3)
        smalls.finish()
        for l in range(LAYERS):
            r["vec"][8 * l : 8 * (l + 1), :] = side_by_side(
                [r["small_all"][g, 8 * l : 8 * (l + 1), :] for g in range(groups)], share
            )
        step(4)
        mats_move.onward()
        rows.relay()
        step(5)
        step(6)
        rows.rest()
        step(7)
        win_moves[6].onward()
        win_moves[7].onward()
        for copy in miscs + wins:
            copy.wait_send()
        for move in win_moves + [mats_move]:
            move.finish()
        rows.finish()

    return call(body, "opening", 1, ins, outs, scratch)


def at_block(b, size):
    return pl.ds(pl.multiple_of(b * size, size), size)


def conv_of(entry, vec, row, size, c):
    cols = slice(c * LANES, (c + 1) * LANES)
    conv = vec[CONV : CONV + 1, cols]
    for j in range(CONV):
        conv = conv + vec[j : j + 1, cols] * entry[c, pl.ds(pl.multiple_of(row + TP * j, TP), size), :]
    return conv


def wide_of(ref, rows, parts):
    return jnp.concatenate([ref[c, rows, :] for c in range(parts)], axis=1)


def row_sum(value):
    return jnp.sum(value.reshape(-1, TP, value.shape[1]), axis=0)


def square_sum(kq):
    lane = lanes_of(kq.shape)
    return jnp.sum(jnp.where(lane < STATE, kq * kq, 0.0), axis=1, keepdims=True)


def forward_layer(zh_size, layer, xg, win, mats, wout, vec, scale, gout=None, nxt=None):
    tokens, width = xg.shape[1], xg.shape[2]
    half = win.shape[1] // 2
    parts = half // LANES
    rows = tokens * TP
    size = STEPS * TP
    blocks = rows // size
    halo = (CONV - 1) * TP
    dma = pltpu.SemaphoreType.DMA
    last = nxt is None
    groups = 2 * zh_size
    ins = dict(
        xg=(xg, VM), win=(win, VM), mats=(mats, VM), wout=(wout, HB), vec=(vec, VM),
        scale=(scale, VM), e=(spreader(), VM),
    )
    outs = dict(
        entry=(struct(2 * parts, halo + rows, LANES), VM), beta=(struct(parts, rows, LANES), VM),
        kq=(struct(rows, LANES), VM), proj=(struct(TP, size, 2 * LANES, dtype=bf16), VM),
        y=(struct(parts, rows, LANES), VM), keep=(struct(blocks, STATE, parts, TP, LANES), VM),
        mixed=(struct(TP, tokens, half, dtype=bf16), VM), stats=(struct(2, TP, LANES), VM),
    )
    scratch = dict(
        act=pltpu.VMEM((parts, rows, LANES), f32), step=pltpu.VMEM((parts, rows, LANES), f32),
        payload=pltpu.VMEM((TP, size, 2 * LANES), bf16), parts=pltpu.VMEM((TP - 1, size, 2 * LANES), bf16),
        own=pltpu.VMEM((size, 2 * LANES), f32),
        state=pltpu.VMEM((STATE, parts, TP, LANES), f32), wide=pltpu.VMEM((size, 32 * LANES), f32),
        part=pltpu.VMEM((TP, tokens, width), bf16),
        scatter_buf=Scatter.buffers((tokens, width)),
        sum_sems=Sum.sems(dma), scatter_sems=Scatter.sems(dma),
    )
    outs["wout_all"] = (struct(groups, *wout.shape, dtype=bf16), VM)
    scratch["d0"] = Spread.sems(dma, zh_size)
    if last:
        ins["gout"] = (gout, VM)
        outs["gog"] = (struct(TP, tokens, width, dtype=bf16), HB)
        scratch["gather_sems"] = Gather.sems(dma)
        outs["part"] = (struct(TP, tokens, width, dtype=bf16), VM)
        del scratch["part"], scratch["scatter_buf"], scratch["scatter_sems"]
    if not last:
        win1 = nxt["win"]
        ins.update(h=(nxt["h"], VM), gain=(nxt["gain"], VM), win1=(win1, HB), mats1=(nxt["mats"], HB))
        outs.update(
            result=(struct(tokens, width), VM),
            win1_all=(struct(2, 2, zh_size, WAYS, *win1.shape[1:], dtype=bf16), HB),
            mats1_all=(struct(groups, *nxt["mats"].shape, dtype=bf16), HB),
            xg1=(struct(TP, tokens, width, dtype=bf16), HB),
        )
        scratch.update(
            normed=pltpu.VMEM((tokens, width), bf16), gather_sems=Gather.sems(dma),
            turned=pltpu.VMEM(win1.shape, bf16), l_sems=[dma((TP - 1,)), dma((TP - 1,)), dma],
            d1=Spread.sems(dma, zh_size), d2=Spread.sems(dma, zh_size), d3=Spread.sems(dma, zh_size),
        )

    def body(r):
        side, far = dp_peers(zh_size)
        greet([p[0] for p in tp_peers()] + [side] + [f[0] for f in far])
        entry, act, step, beta, kq, y = r["entry"], r["act"], r["step"], r["beta"], r["kq"], r["y"]
        vec = r["vec"].at[8 * layer : 8 * (layer + 1)]
        index = lambda ref: lambda xx, zz: ref.at[xx * zh_size + zz]
        early = Spread(zh_size, r["wout"], index(r["wout_all"]), r["d0"])
        early.start()
        if last:
            gouts = Gather(r["gout"], r["gog"], r["gather_sems"])
        else:
            me = total_rank()
            turned = [pltpu.make_async_copy(r["win1"].at[me], r["turned"].at[me], r["l_sems"][2])]
            for i, (target, rank, _) in enumerate(tp_peers()):
                turned.append(
                    remote(r["win1"].at[rank], r["turned"].at[me], r["l_sems"][0].at[i], r["l_sems"][1].at[i], target)
                )
            for copy in turned:
                copy.start()
            moves = [Spread(zh_size, r["mats1"], index(r["mats1_all"]), r["d3"])]
            for k in range(2):
                view = lambda xx, zz, k=k: r["win1_all"].at[xx, k, zz]
                src = r["turned"].at[k * WAYS : (k + 1) * WAYS]
                moves.append(Spread(zh_size, src, view, r["d1" if k == 0 else "d2"]))

        entry[:, :halo, :] = jnp.zeros((2 * parts, halo, LANES), f32)
        tile = 2 * LANES
        for p in range(TP // 2):

            def columns(n, carry, p=p):
                cols = at_block(n, tile)
                out = jnp.dot(
                    r["xg"][2 * p : 2 * p + 2].reshape(2 * tokens, width), r["win"][:, cols],
                    preferred_element_type=f32,
                )
                for j in range(2):
                    for c in range(2):
                        entry[2 * n + c, pl.ds(halo + 2 * p + j, tokens, stride=TP), :] = out[
                            j * tokens : (j + 1) * tokens, c * LANES : (c + 1) * LANES
                        ]
                return carry

            lax.fori_loop(0, 2 * half // tile, columns, 0)
        if not last:
            for copy in turned:
                copy.wait()

        total = Sum(r["payload"], r["parts"], r["proj"], r["sum_sems"])

        def project(b, carry):
            rs = at_block(b, size)
            for c in range(parts):
                conv = conv_of(entry, vec, b * size, size, c)
                act[c, rs, :] = (conv * jax.nn.sigmoid(conv)).astype(bf16).astype(f32)
            out = jnp.dot(
                wide_of(act, rs, parts).astype(bf16), r["mats"][:, RANK:], preferred_element_type=f32
            )
            r["payload"][b] = encode(out)

            @pl.when(b == total.me)
            def _():
                r["own"][...] = out

            return carry

        lax.fori_loop(0, blocks, project, 0)
        total.start()
        total.middle(r["own"][...])
        total.finish()
        early.onward()
        if last:
            gouts.start()
        else:
            moves[0].start()
            moves[1].start()

        r["stats"][...] = jnp.zeros((2, TP, LANES), f32)

        def rates(b, carry):
            rs = at_block(b, size)
            tail = decode(r["proj"][b])[:, RANK:]
            keys = tail + pltpu.roll(tail, 32, 1) + pltpu.roll(tail, 64, 1)
            kq[rs, :] = keys
            norm = square_sum(keys)
            pre = dot(r["proj"][b, :, :RANK], r["mats"][:, :RANK], ((1,), (1,)))
            for c in range(parts):
                cols = slice(c * LANES, (c + 1) * LANES)
                rate = jax.nn.sigmoid(pre[:, cols] + vec[CONV + 1 : CONV + 2, cols])
                beta[c, rs, :] = rate
                step[c, rs, :] = rate / (1.0 + rate * norm)
                r["stats"][0] += row_sum(rate)
                r["stats"][1] = jnp.maximum(
                    r["stats"][1], jnp.max(rate.reshape(-1, TP, LANES), axis=0)
                )
            return carry

        lax.fori_loop(0, blocks, rates, 0)
        r["stats"][0] = r["stats"][0] * r["scale"][...]
        r["stats"][1] = r["stats"][1] * r["scale"][...]

        lane = lanes_of((size, LANES))
        state, wide = r["state"], r["wide"]
        state[...] = jnp.zeros_like(state)

        def block(b, carry):
            r["keep"][b] = state[...]
            wide[...] = jnp.dot(spread_keys(kq[at_block(b, size), :], lane), r["e"][...], preferred_element_type=f32)

            def one(j, carry):
                t = at_block(b * STEPS + j, TP)
                w = at_block(j, TP)
                acts = [act[c, t, :] for c in range(parts)]
                steps = [step[c, t, :] for c in range(parts)]
                sums = [None] * parts
                for n in range(STATE):
                    key = wide[w, n * LANES : (n + 1) * LANES]
                    query = wide[w, (STATE + n) * LANES : (STATE + n + 1) * LANES]
                    for c in range(parts):
                        s = state[n, c]
                        s = s + (steps[c] * key) * (acts[c] - key * s)
                        state[n, c] = s
                        sums[c] = s * query if sums[c] is None else sums[c] + s * query
                for c in range(parts):
                    y[c, t, :] = sums[c]
                return carry

            lax.fori_loop(0, STEPS, one, 0)
            rs = at_block(b, size)
            here = pl.ds(pl.multiple_of(b * STEPS, STEPS), STEPS)
            for c in range(parts):
                cols = slice(c * LANES, (c + 1) * LANES)
                gate = entry[parts + c, pl.ds(pl.multiple_of(b * size + halo, TP), size), :]
                skip = vec[CONV + 2 : CONV + 3, cols]
                step[c, rs, :] = (y[c, rs, :] + skip * act[c, rs, :]) * (gate * jax.nn.sigmoid(gate))
                for s in range(TP):
                    r["mixed"][s, here, cols] = step[c, pl.ds(b * size + s, STEPS, stride=TP), :].astype(bf16)
            return carry

        if last:
            lax.fori_loop(0, blocks, block, 0)
            gouts.relay()
        else:
            lax.fori_loop(0, blocks // 2, block, 0)
            moves[0].onward()
            moves[2].start()
            lax.fori_loop(blocks // 2, blocks, block, 0)
        early.finish()
        weight = lambda: r["wout_all"][...].reshape(half, width)
        if last:

            def plain(s, carry):
                r["part"][s] = dot(r["mixed"][s], weight(), ((1,), (0,))).astype(bf16)
                return carry

            lax.fori_loop(0, TP // 2, plain, 0)
            gouts.rest()
            lax.fori_loop(TP // 2, TP, plain, 0)
            gouts.finish()
            return
        moves[1].onward()
        scatter = Scatter(r["part"], r["scatter_buf"], r["scatter_sems"])
        out_partial(scatter, r["part"], r["mixed"], weight)
        moves[2].onward()
        stream = r["h"][...] + scatter.total()
        r["result"][...] = stream
        r["normed"][...] = (stream * rms(stream) * r["gain"][layer + 1 : layer + 2, :]).astype(bf16)
        spread = Gather(r["normed"], r["xg1"], r["gather_sems"])
        spread.start()
        spread.relay()
        spread.rest()
        spread.finish()
        for move in moves:
            move.finish()

    return call(body, "layer_forward_last" if last else "layer_forward", 7 if last else 6, ins, outs, scratch)


def out_partial(scatter, part, left, right, turned=False):
    contract = ((1,), (1,)) if turned else ((1,), (0,))
    for i in range(4):
        for core in (1 - scatter.core, scatter.core):
            slot = core * WAYS + scatter.turns[i]
            part[slot] = dot(left[slot], right(), contract).astype(bf16)
        scatter.to_sibling(i)
        if i >= 1:
            scatter.across(i - 1)
    scatter.sums()


class Reduce:
    @staticmethod
    def sems(dma, zh_size):
        far = max(1, zh_size - 1)
        return [dma, dma, dma((far,)), dma((far,))]

    @staticmethod
    def buffers(zh_size, block):
        return [
            pltpu.VMEM((zh_size,) + block, bf16), pltpu.VMEM((zh_size,) + block, bf16),
            pltpu.VMEM((max(1, zh_size - 1),) + block, bf16),
        ]

    def __init__(self, zh_size, src, buffers, sems):
        self.zh_size, self.src = zh_size, src
        self.near, self.mine, self.buf = buffers
        self.x_send, self.x_recv, self.z_send, self.z_recv = sems
        self.x, _, self.zh, _ = place()
        self.side, self.far = dp_peers(zh_size)

    def start(self):
        half = self.src.at[pl.ds((1 - self.x) * self.zh_size, self.zh_size)]
        self.over = remote(half, self.near, self.x_send, self.x_recv, self.side)
        self.over.start()

    def middle(self):
        self.over.wait_recv()
        for k in range(self.zh_size):
            self.mine[k] = (
                self.src[self.x * self.zh_size + k].astype(f32) + self.near[k].astype(f32)
            ).astype(bf16)
        self.along = [
            remote(self.mine.at[to_z], self.buf.at[k], self.z_send.at[k], self.z_recv.at[k], target)
            for k, (target, to_z, _) in enumerate(self.far)
        ]
        for copy in self.along:
            copy.start()

    def total(self):
        value = self.src[self.x * self.zh_size + self.zh].astype(f32) + self.near[self.zh].astype(f32)
        for k in range(self.zh_size - 1):
            self.along[k].wait_recv()
            value = value + self.buf[k].astype(f32)
        self.over.wait_send()
        for copy in self.along:
            copy.wait_send()
        return value


def backward_layer(zh_size, layer, kept, gog, wout, mats, vec, xg, win, gain, h, grad, late=None, part=None):
    tokens, width = xg.shape[1], xg.shape[2]
    half = win.shape[1] // 2
    parts = half // LANES
    rows = tokens * TP
    size = STEPS * TP
    blocks = rows // size
    halo = (CONV - 1) * TP
    groups = 2 * zh_size
    share = half // groups
    deep = width // (2 * groups)
    far = max(1, zh_size - 1)
    dma = pltpu.SemaphoreType.DMA
    onward = part is not None
    ins = {k: (kept[k], VM) for k in ("entry", "beta", "kq", "proj")}
    ins.update(
        mats=(mats, VM), wout=(wout, HB), vec=(vec, VM), gain=(gain, VM), h=(h, VM), grad=(grad, VM),
        mixed=(kept["mixed"], HB), e=(spreader(), VM), fold=(folder(), VM), keep=(kept["keep"], HB), gouts=(gog, HB), y=(kept["y"], HB), xg=(xg, HB), win=(win, HB),
    )
    outs = dict(
        prev=(struct(tokens, width), VM), ginner=(struct(groups, 2, deep, half, dtype=bf16), VM),
        near=(struct(zh_size, 2, deep, half, dtype=bf16), HB), ggate=(struct(2, deep, half, dtype=bf16), VM), gwout=(struct(share, width), VM),
        gmats=(struct(half, 3 * LANES, dtype=bf16), VM), gvec=(struct(8, half), VM),
        ggain=(struct(1, width), VM),
    )
    block_f32 = pltpu.VMEM((parts, rows, LANES), f32)
    scratch = dict(
        a=pltpu.VMEM((TP, tokens, width), bf16), b=pltpu.VMEM(win.shape, bf16),
        gs=block_f32, act=block_f32, gact=block_f32,
        step=pltpu.VMEM((parts, rows + halo, LANES), f32),
        states=pltpu.VMEM((STEPS + 1, STATE, parts, TP, LANES), f32),
        lam=pltpu.VMEM((STATE, parts, TP, LANES), f32), wide=pltpu.VMEM((size, 32 * LANES), f32),
        gstep=pltpu.VMEM((parts, size, LANES), f32),
        gentry=pltpu.VMEM((TP, tokens, 2 * half), bf16),
        payload=pltpu.VMEM((TP, size, 2 * LANES), bf16), parts=pltpu.VMEM((TP - 1, size, 2 * LANES), bf16),
        total=pltpu.VMEM((TP, size, 2 * LANES), bf16), own=pltpu.VMEM((size, 2 * LANES), f32),
        sums=pltpu.VMEM((8, parts, TP, LANES), f32),
        grate=pltpu.VMEM((half, LANES), f32), gselect=pltpu.VMEM((half, 2 * LANES), f32),
        gwo=pltpu.VMEM((groups, share, width), bf16), gwg=pltpu.VMEM((groups, 2, deep, half), bf16),
        gate_buf=Reduce.buffers(zh_size, (2, deep, half)), gate_sems=Reduce.sems(dma, zh_size),
        keeps=pltpu.VMEM((2, STATE, parts, TP, LANES), f32), keep_sems=dma((2,)),
        scatter_buf=Scatter.buffers((tokens, width)), reduce_buf=Reduce.buffers(zh_size, (share, width)),
        sum_sems=Sum.sems(dma), scatter_sems=Scatter.sems(dma), reduce_sems=Reduce.sems(dma, zh_size),
        loads=dma((7,)), over=[dma, dma],
    )
    if onward:
        outs["gog"] = (struct(TP, tokens, width, dtype=bf16), HB)
        ins["part"] = (part, HB)
        outs["parts_all"] = (struct(*part.shape, dtype=bf16), HB)
        scratch.update(part_sems=[dma((TP - 1,)), dma((TP - 1,)), dma])
        scratch.update(gout=pltpu.VMEM((tokens, width), bf16), gather_sems=Gather.sems(dma))
    if late is not None:
        ins["late"] = (late, HB)
        outs["late"] = (struct(far, *late.shape[1:], dtype=bf16), HB)
        scratch.update(late_sems=[dma((far,)), dma((far,))])
        ins["late_in"] = ins.pop("late")

    def body(r):
        x, core, zh, q = place()
        side, far_ones = dp_peers(zh_size)
        greet([p[0] for p in tp_peers()] + [side] + [f[0] for f in far_ones])
        entry, act, step, beta, kq = r["entry"], r["act"], r["step"], r["beta"], r["kq"]
        gs, gact, sums, gstep = r["gs"], r["gact"], r["sums"], r["gstep"]
        vec = r["vec"].at[8 * layer : 8 * (layer + 1)]
        loads = [
            pltpu.make_async_copy(src, dst, r["loads"].at[i])
            for i, (src, dst) in enumerate(
                (
                    (r["gouts"], r["a"]), (r["mixed"], r["gentry"].at[:, :, :half]),
                    (r["wout"].at[:, : 2 * half], r["b"].at[:half]), (r["wout"].at[:, 2 * half :], r["b"].at[half : 2 * half]),
                    (r["y"], gact), (r["xg"], r["a"]), (r["win"], r["b"]),
                )
            )
        ]
        for copy in loads[:5]:
            copy.start()
        passed = []
        if onward:
            me = core * WAYS + q
            for i, (target, rank, _) in enumerate(tp_peers()):
                copy = remote(
                    r["part"].at[rank], r["parts_all"].at[me], r["part_sems"][0].at[i], r["part_sems"][1].at[i], target
                )
                copy.start()
                passed.append(copy)
            passed.append(pltpu.make_async_copy(r["part"].at[me], r["parts_all"].at[me], r["part_sems"][2]))
            passed[-1].start()
        if late is not None:
            for k, (target, to_z, _) in enumerate(far_ones):
                copy = remote(
                    r["late_in"].at[to_z], r["late"].at[k], r["late_sems"][0].at[k], r["late_sems"][1].at[k], target
                )
                copy.start()
                passed.append(copy)
        sums[...] = jnp.zeros_like(sums)
        r["grate"][...] = jnp.zeros_like(r["grate"])
        r["gselect"][...] = jnp.zeros_like(r["gselect"])

        def again(b, carry):
            rs = at_block(b, size)
            norm = square_sum(kq[rs, :])
            for c in range(parts):
                conv = conv_of(entry, vec, b * size, size, c)
                act[c, rs, :] = (conv * jax.nn.sigmoid(conv)).astype(bf16).astype(f32)
                rate = beta[c, rs, :]
                step[c, rs, :] = rate / (1.0 + rate * norm)
            return carry

        lax.fori_loop(0, blocks, again, 0)
        loads[0].wait()
        loads[1].wait()

        def outer(c, carry):
            left = r["gentry"][:, :, at_block(c, LANES)].reshape(rows, LANES)
            out = dot(left, r["a"][...].reshape(rows, width), ((0,), (0,))).astype(bf16)
            each = LANES // share
            r["gwo"][pl.ds(c * each, each)] = out.reshape(each, share, width)
            return carry

        lax.fori_loop(0, parts, outer, 0)
        reduce = Reduce(zh_size, r["gwo"], r["reduce_buf"], r["reduce_sems"])
        reduce.start()
        loads[2].wait()
        loads[3].wait()
        for p in range(TP // 2):

            def columns(n, carry, p=p):
                out = 0.0
                for k in range(2):
                    left = r["a"][2 * p : 2 * p + 2, :, 2 * half * k : 2 * half * (k + 1)].reshape(2 * tokens, 2 * half)
                    right = r["b"][pl.ds(pl.multiple_of(half * k + n * 2 * LANES, 2 * LANES), 2 * LANES), :]
                    out = out + dot(left, right, ((1,), (1,)))
                for j in range(2):
                    for c in range(2):
                        gs[2 * n + c, pl.ds(2 * p + j, tokens, stride=TP), :] = out[
                            j * tokens : (j + 1) * tokens, c * LANES : (c + 1) * LANES
                        ]
                return carry

            lax.fori_loop(0, half // (2 * LANES), columns, 0)
        loads[5].start()
        loads[6].start()
        loads[4].wait()

        def gates(b, carry):
            rs = at_block(b, size)
            here = pl.ds(pl.multiple_of(b * STEPS, STEPS), STEPS)
            for c in range(parts):
                cols = slice(c * LANES, (c + 1) * LANES)
                gate = entry[parts + c, pl.ds(pl.multiple_of(b * size + halo, TP), size), :]
                sig = jax.nn.sigmoid(gate)
                g = gs[c, rs, :]
                a = act[c, rs, :]
                down = g * (gate * sig)
                gstep[c] = g * (gact[c, rs, :] + vec[CONV + 2 : CONV + 3, cols] * a) * (
                    sig * (1.0 + gate * (1.0 - sig))
                )
                gs[c, rs, :] = down
                sums[CONV + 2, c] += row_sum(down * a)
                for s in range(TP):
                    r["gentry"][s, here, half + c * LANES : half + (c + 1) * LANES] = gstep[
                        c, pl.ds(s, STEPS, stride=TP), :
                    ].astype(bf16)
            return carry

        lax.fori_loop(0, blocks, gates, 0)
        loads[5].wait()
        tile = 2 * LANES

        def outer_in(out_ref, first, i, carry):
            left = r["a"][:, :, at_block(i, tile)].reshape(rows, tile)
            out = dot(left, r["gentry"][:, :, first : first + half].reshape(rows, half), ((0,), (0,))).astype(bf16)
            each = tile // deep
            for e in range(each):
                d = i * each + e
                xx, cc, zz = d // (2 * zh_size), lax.rem(d // zh_size, 2), lax.rem(d, zh_size)
                out_ref[xx * zh_size + zz, cc] = out[e * deep : (e + 1) * deep]
            return carry

        lax.fori_loop(0, width // tile, lambda i, k: outer_in(r["gwg"], half, i, k), 0)
        gate_reduce = Reduce(zh_size, r["gwg"], r["gate_buf"], r["gate_sems"])

        lane = lanes_of((size, LANES))
        states, lam, wide = r["states"], r["lam"], r["wide"]
        lam[...] = jnp.zeros_like(lam)
        plus = lambda a, b: b if a is None else a + b
        total = Sum(r["payload"], r["parts"], r["total"], r["sum_sems"])

        def block(bi, carry):
            b = blocks - 1 - bi
            rs = at_block(b, size)
            slot = lax.rem(b, 2)
            pltpu.make_async_copy(r["keep"].at[b], r["keeps"].at[slot], r["keep_sems"].at[slot]).wait()

            @pl.when(b > 0)
            def _():
                ahead = pltpu.make_async_copy(r["keep"].at[b - 1], r["keeps"].at[1 - slot], r["keep_sems"].at[1 - slot])
                ahead.start()

            states[0] = r["keeps"][slot]
            wide[...] = jnp.dot(spread_keys(kq[rs, :], lane), r["e"][...], preferred_element_type=f32)

            def replay(j, carry):
                t, w = at_block(b * STEPS + j, TP), at_block(j, TP)
                acts = [act[c, t, :] for c in range(parts)]
                steps = [step[c, t, :] for c in range(parts)]
                for n in range(STATE):
                    key = wide[w, n * LANES : (n + 1) * LANES]
                    for c in range(parts):
                        s = states[j, n, c]
                        states[j + 1, n, c] = s + (steps[c] * key) * (acts[c] - key * s)
                return carry

            lax.fori_loop(0, STEPS, replay, 0)

            def back(jj, carry):
                j = STEPS - 1 - jj
                t, w = at_block(b * STEPS + j, TP), at_block(j, TP)
                acts = [act[c, t, :] for c in range(parts)]
                steps = [step[c, t, :] for c in range(parts)]
                gsums = [gs[c, t, :] for c in range(parts)]
                first, second = [None] * parts, [None] * parts
                for n in range(STATE):
                    kcols, qcols = slice(n * LANES, (n + 1) * LANES), slice((STATE + n) * LANES, (STATE + n + 1) * LANES)
                    key, query = wide[w, kcols], wide[w, qcols]
                    key_term, query_term = None, None
                    for c in range(parts):
                        before, after = states[j, n, c], states[j + 1, n, c]
                        grad = lam[n, c] + gsums[c] * query
                        u = key * before
                        d = acts[c] - u
                        gk = grad * key
                        first[c] = plus(first[c], gk * d)
                        second[c] = plus(second[c], gk)
                        key_term = plus(key_term, (steps[c] * grad) * (d - u))
                        query_term = plus(query_term, gsums[c] * after)
                        lam[n, c] = grad - (steps[c] * key) * gk
                    wide[w, kcols] = key_term
                    wide[w, qcols] = query_term
                for c in range(parts):
                    gstep[c, w, :] = first[c]
                    gact[c, t, :] = steps[c] * second[c]
                return carry

            lax.fori_loop(0, STEPS, back, 0)
            terms = wide[...]
            high = terms.astype(bf16)
            low = (terms - high.astype(f32)).astype(bf16)
            gkq = jnp.dot(high, r["fold"][...], preferred_element_type=f32) + jnp.dot(
                low, r["fold"][...], preferred_element_type=f32
            )
            keys = kq[rs, :]
            norm = square_sum(keys)
            gnorm = jnp.zeros((size, 1), f32)
            grates = []
            for c in range(parts):
                cols = slice(c * LANES, (c + 1) * LANES)
                rate = beta[c, rs, :]
                g = gstep[c]
                inverse = 1.0 + rate * norm
                inverse = 1.0 / (inverse * inverse)
                gnorm = gnorm - jnp.sum(g * (rate * rate * inverse), axis=1, keepdims=True)
                grate = g * inverse * rate * (1.0 - rate)
                sums[CONV + 1, c] += row_sum(grate)
                grates.append(grate.astype(bf16))
                gact[c, rs, :] += vec[CONV + 2 : CONV + 3, cols] * gs[c, rs, :]
            grate = jnp.concatenate(grates, axis=1)
            r["grate"][...] += dot(grate, r["proj"][b, :, :RANK], ((0,), (0,)))
            grank = dot(grate, r["mats"][:, :RANK], ((1,), (0,)))
            gkq = gkq + jnp.where(lane < STATE, 2.0 * keys * gnorm, 0.0)
            out = jnp.concatenate([grank, gkq], axis=1)
            r["payload"][b] = encode(out)

            @pl.when(b == total.me)
            def _():
                r["own"][...] = out

            return carry

        last = (blocks - 1) % 2
        pltpu.make_async_copy(r["keep"].at[blocks - 1], r["keeps"].at[last], r["keep_sems"].at[last]).start()
        lax.fori_loop(0, blocks // 2, block, 0)
        reduce.middle()
        gate_reduce.start()
        lax.fori_loop(blocks // 2, blocks, block, 0)
        total.start()
        total.middle(r["own"][...])
        total.finish()
        gate_reduce.middle()
        step[:, rows:, :] = jnp.zeros((parts, halo, LANES), f32)
        gconv = step

        def convs(b, carry):
            rs = at_block(b, size)
            gp = r["total"][b]
            gp = jnp.where(lanes_of(gp.shape) < RANK + 2 * STATE, gp.astype(f32), 0.0).astype(bf16)
            r["gselect"][...] += dot(wide_of(act, rs, parts).astype(bf16), gp, ((0,), (0,)))
            more = dot(gp, r["mats"][:, RANK:], ((1,), (1,)))
            for c in range(parts):
                conv = conv_of(entry, vec, b * size, size, c)
                sig = jax.nn.sigmoid(conv)
                g = (gact[c, rs, :] + more[:, c * LANES : (c + 1) * LANES]) * (sig * (1.0 + conv * (1.0 - sig)))
                gconv[c, rs, :] = g
                sums[CONV, c] += row_sum(g)
                for j in range(CONV):
                    inner = entry[c, pl.ds(pl.multiple_of(b * size + TP * j, TP), size), :]
                    sums[j, c] += row_sum(g * inner)
            return carry

        lax.fori_loop(0, blocks, convs, 0)

        def inners(b, carry):
            rs = at_block(b, size)
            here = pl.ds(pl.multiple_of(b * STEPS, STEPS), STEPS)
            for c in range(parts):
                cols = slice(c * LANES, (c + 1) * LANES)
                value = None
                for j in range(CONV):
                    at = pl.ds(pl.multiple_of(b * size + TP * (CONV - 1 - j), TP), size)
                    value = plus(value, vec[j : j + 1, cols] * gconv[c, at, :])
                gs[c, rs, :] = value
                for s in range(TP):
                    at = pl.ds(b * size + s, STEPS, stride=TP)
                    r["gentry"][s, here, cols] = gs[c, at, :].astype(bf16)
            return carry

        lax.fori_loop(0, blocks, inners, 0)
        lax.fori_loop(0, width // tile, lambda i, k: outer_in(r["ginner"], 0, i, k), 0)
        over = remote(
            r["ginner"].at[pl.ds((1 - x) * zh_size, zh_size)], r["near"], r["over"][0], r["over"][1], side
        )
        over.start()
        loads[6].wait()
        scatter = Scatter(r["a"], r["scatter_buf"], r["scatter_sems"])
        out_partial(scatter, r["a"], r["gentry"], lambda: r["b"][...], turned=True)
        r["gmats"][:, :RANK] = r["grate"][...].astype(bf16)
        r["gmats"][:, RANK:] = r["gselect"][...].astype(bf16)
        for j in range(8):
            for c in range(parts):
                r["gvec"][j : j + 1, c * LANES : (c + 1) * LANES] = jnp.sum(sums[j, c], axis=0, keepdims=True)
        r["gwout"][...] = reduce.total()
        r["ggate"][...] = gate_reduce.total().astype(bf16)
        gnormed = scatter.total()
        stream = r["h"][...]
        scale = rms(stream)
        r["ggain"][...] = jnp.sum(gnormed * stream * scale, axis=0, keepdims=True)
        scaled = gnormed * r["gain"][layer : layer + 1, :]
        grad = r["grad"][...] + scale * scaled - stream * (scale * scale * scale) * jnp.mean(
            stream * scaled, axis=-1, keepdims=True
        )
        r["prev"][...] = grad
        if onward:
            r["gout"][...] = grad.astype(bf16)
            spread = Gather(r["gout"], r["gog"], r["gather_sems"])
            spread.start()
            spread.relay()
            spread.rest()
            spread.finish()
        for copy in passed:
            copy.wait()
        over.wait()

    return call(body, "layer_backward", 9 if onward else 8, ins, outs, scratch)


def closing(zh_size, inner, near, mats, small, stats, gain, turns, gwouts, select):
    groups = 2 * zh_size
    count = groups * TP
    far_n = max(1, zh_size - 1)
    dma = pltpu.SemaphoreType.DMA
    depth, half = inner.shape[3] // WAYS, inner.shape[4]
    share, width = gwouts[0].shape
    gains = width // count
    every = (2, zh_size) + stats.shape
    v = pltpu.VMEM
    ins = dict(
        inner=(inner, VM), near=(near, VM), mats=(mats, VM), small=(small, VM), stats=(stats, VM), gain=(gain, VM),
        t0=(turns[0], VM), t1=(turns[1], VM), t2=(turns[2], VM), w0=(gwouts[0], VM), w1=(gwouts[1], VM),
    )
    outs = dict(
        gin=(struct(LAYERS, depth, 2 * count * share), VM), gselect=(struct(LAYERS, share, select), VM),
        grate=(struct(LAYERS, RANK, share), VM), gwout=(struct(LAYERS, share, width), VM),
        ggain=(struct(LAYERS, gains), VM), gtaps=(struct(LAYERS, CONV, share), VM), gshift=(struct(LAYERS, share), VM),
        grate_shift=(struct(LAYERS, share), VM), gskip=(struct(LAYERS, share), VM), stats_all=(struct(*stats.shape), VM),
    )
    chunk = lambda shape, dtype: dict(
        s=v(shape[1:], dtype), z=v((far_n,) + shape[2:], dtype), z_sems=[dma((far_n,)), dma((far_n,))]
    )
    shapes = dict(
        c0=(inner.shape[:2] + inner.shape[3:], bf16), c1=(inner.shape[:2] + inner.shape[3:], bf16),
        mats=(mats.shape, bf16), small=(small.shape, f32), stats=(every, f32),
    )
    scratch = dict(
        vectors=v(small.shape, f32), stats_v=v(every, f32), stats_t=v((TP - 1,) + stats.shape, f32),
        gain_t=v((TP - 1,) + gain.shape[1:], f32), win_t=v((2, WAYS, depth, half), bf16),
        total=v(small.shape[2:], f32),
        g_sems=[dma((TP - 1,))] * 2, s_sems=[dma((TP - 1,))] * 2,
    )
    for i in range(4):
        scratch["b%d" % i] = v((TP, depth, half), bf16)
        scratch["b%d_sems" % i] = [dma((TP - 1,)), dma((TP - 1,))]
    for name, (shape, dtype) in shapes.items():
        for key, value in chunk(shape, dtype).items():
            scratch[name + "_" + key] = value
        if name not in ("c0", "c1"):
            scratch[name + "_near"] = v(shape[1:], dtype)
            scratch[name + "_x"] = [dma, dma]

    def body(r):
        x, core, zh, q = place()
        me = core * WAYS + q
        peers = tp_peers()
        side, far = dp_peers(zh_size)
        greet([p[0] for p in peers] + [side] + [f[0] for f in far])
        sent, full = [], []

        def join(a, b, peaks):
            a, b = a.astype(f32), b.astype(f32)
            if peaks:
                line = lax.broadcasted_iota(jnp.int32, a.shape, len(a.shape) - 2)
                return jnp.where(line < 4, a + b, jnp.maximum(a, b))
            return a + b

        class Chunk:
            def __init__(self, name, src, near=None):
                self.name, self.src, self.near, self.peaks = name, src, near, name == "stats"

            def start(self):
                self.near = r[self.name + "_near"]
                sems = r[self.name + "_x"]
                self.over = remote(self.src.at[1 - x], self.near, sems[0], sems[1], side)
                self.over.start()
                sent.append(self.over)

            def middle(self, arrived=False):
                if not arrived:
                    self.over.wait_recv()
                mine, buf, sems = r[self.name + "_s"], r[self.name + "_z"], r[self.name + "_z_sems"]
                mine[...] = join(self.src[x], self.near[...], self.peaks).astype(mine.dtype)
                self.along = [
                    remote(mine.at[to_z], buf.at[k], sems[0].at[k], sems[1].at[k], target)
                    for k, (target, to_z, _) in enumerate(far)
                ]
                for copy in self.along:
                    copy.start()
                    sent.append(copy)

            def total(self):
                value = join(self.src[x, zh], self.near[zh], self.peaks)
                for k, copy in enumerate(self.along):
                    copy.wait_recv()
                    value = join(value, r[self.name + "_z"][k], self.peaks)
                return value

        def turn(src, i):
            box, sems = r["b%d" % i], r["b%d_sems" % i]
            for k, (target, rank, _) in enumerate(peers):
                copy = remote(src(rank), box.at[me], sems[0].at[k], sems[1].at[k], target)
                copy.start()
                full.append(copy)
            box[me] = src(me)[...]

        cs = [Chunk("c%d" % c, r["inner"].at[:, :, c], r["near"].at[:, c]) for c in range(2)]
        cs[0].middle(arrived=True)
        cs[1].middle(arrived=True)
        gained, shown = [], []
        for i, (target, rank, _) in enumerate(peers):
            for src, buf, sems, copies in (
                (r["gain"].at[rank], r["gain_t"], r["g_sems"], gained),
                (r["stats"], r["stats_t"], r["s_sems"], shown),
            ):
                copy = remote(src, buf.at[i], sems[0].at[i], sems[1].at[i], target)
                copy.start()
                copies.append(copy)
                sent.append(copy)
        mats_c = Chunk("mats", r["mats"])
        mats_c.start()
        for l in range(LAYERS):
            r["gwout"][l] = r["w%d" % l][...]
        for i in range(3):
            turn(lambda rank, i=i: r["t%d" % i].at[rank], i + 1)
        total = r["gain"][me]
        seen = r["stats"][...]
        for i in range(TP - 1):
            gained[i].wait_recv()
            total = total + r["gain_t"][i]
            shown[i].wait_recv()
            seen = join(seen, r["stats_t"][i], True)
        r["vectors"][...] = r["small"][...]
        for l in range(LAYERS):
            for g in range(groups):
                at = l * groups + g
                r["vectors"][g // zh_size, g % zh_size, l * 16 + 8 : l * 16 + 9, :] = total[at : at + 1, :]
        r["stats_v"][...] = jnp.broadcast_to(seen, every)
        rest = [mats_c, Chunk("small", r["vectors"]), Chunk("stats", r["stats_v"])]
        for c in rest[1:]:
            c.start()
        for c in rest:
            c.middle()
        for c in range(2):
            r["win_t"][c] = cs[c].total().astype(bf16).reshape(WAYS, depth, half)
        turn(lambda rank: r["win_t"].at[rank // WAYS, lax.rem(rank, WAYS)], 0)
        m = rest[0].total()
        for l in range(LAYERS):
            base = 3 * LANES * l
            r["grate"][l] = m[:, base : base + RANK].T
            r["gselect"][l] = m[:, base + RANK : base + RANK + select]
        r["total"][...] = rest[1].total()
        for l in range(LAYERS):
            r["gtaps"][l] = r["total"][16 * l : 16 * l + CONV, :share]
            for name, j, size in (
                ("gshift", CONV, share), ("grate_shift", CONV + 1, share), ("gskip", CONV + 2, share), ("ggain", 8, gains)
            ):
                r[name][l : l + 1, :] = r["total"][16 * l + j : 16 * l + j + 1, :size]
        r["stats_all"][...] = rest[2].total()

        def lay(box, l, at):
            for rank in range(TP):
                for g in range(groups):
                    d = ((g // zh_size * 2 + rank // WAYS) * zh_size + g % zh_size) * WAYS + rank % WAYS
                    r["gin"][l, :, at + d * share : at + (d + 1) * share] = box[
                        rank, :, g * share : (g + 1) * share
                    ].astype(f32)

        boxes = {0: (0, 0), 1: (0, count * share), 2: (1, 0), 3: (1, count * share)}
        done = full[: 3 * (TP - 1)]
        for copy in done:
            copy.wait_recv()
        for i in (1, 2, 3):
            lay(r["b%d" % i], *boxes[i])
        late = full[3 * (TP - 1) :]
        for copy in late:
            copy.wait_recv()
        lay(r["b0"], *boxes[0])
        for copy in sent + done + late:
            copy.wait_send()

    return call(body, "closing", 5, ins, outs, scratch)


def on_device(
    hidden, cotangent, groups, group_weights, input_weight, select_weight, rate_weight,
    output_weight, norm_gain, conv_taps, conv_shift, rate_shift, skip_gain,
):
    fsdp = lax.axis_size("fsdp")
    zh_size = fsdp // WAYS
    count = 2 * 2 * fsdp
    group_count = 2 * zh_size
    share = conv_shift.shape[1]
    gains = norm_gain.shape[1]
    depth = input_weight.shape[1]
    half = group_count * share
    x, core, zh, q = place()

    labels = jnp.arange(group_weights.shape[0])
    own_weight = jnp.sum(jnp.where(groups[:, None] == labels[None, :], group_weights[None, :], 0.0))

    wins = input_weight.reshape(LAYERS, depth, 2, 2, 2, zh_size, WAYS, share)
    wins = wins.transpose(0, 4, 6, 1, 2, 3, 5, 7).reshape(LAYERS, TP, depth, 2 * half)
    mats = jnp.concatenate([rate_weight.swapaxes(1, 2), select_weight], axis=2)
    mats = jnp.pad(mats, ((0, 0), (0, 0), (0, 3 * LANES - mats.shape[2])))
    vectors = [conv_taps, conv_shift[:, None], rate_shift[:, None], skip_gain[:, None], skip_gain[:, None]]
    small = jnp.concatenate(vectors, axis=1).astype(f32).reshape(8 * LAYERS, share)
    small = jnp.pad(small, ((0, 0), (0, LANES - share)))
    misc = jnp.pad(norm_gain.astype(f32), ((0, 0), (0, LANES - gains)))
    misc = jnp.concatenate([misc, jnp.full((8 - LAYERS, LANES), own_weight)])

    flat = lambda a: a.reshape(half, -1)
    h0 = hidden[0]
    start = opening(zh_size, gains, share, wins[0], small, misc, mats[0], h0, cotangent[0])
    vec, gain, scale = start["vec"], start["gains"], start["scale"]
    win0, mat0 = start["win_all"].reshape(count * depth, -1), flat(start["mats_all"])
    one = forward_layer(
        zh_size, 0, start["xg"], win0, mat0, output_weight[0], vec, scale,
        nxt=dict(h=h0, gain=gain, win=wins[1], mats=mats[1]),
    )
    win1, mat1 = one["win1_all"].reshape(count * depth, -1), flat(one["mats1_all"])
    h1 = one["result"]
    two = forward_layer(zh_size, 1, one["xg1"], win1, mat1, output_weight[1], vec, scale, gout=start["gout"])

    down1 = backward_layer(
        zh_size, 1, two, two["gog"], flat(two["wout_all"]), mat1, vec, one["xg1"], win1, gain, h1, start["grad"],
        part=two["part"],
    )
    stream = h1 + jnp.sum(down1["parts_all"].astype(f32), axis=0)
    blocks = (2, zh_size) + down1["ginner"].shape[1:]
    pick = lambda a, i: lax.dynamic_index_in_dim(a, i, 0, keepdims=False)
    summed = pick(down1["ginner"].reshape(blocks), x).astype(f32) + down1["near"].astype(f32)
    down0 = backward_layer(
        zh_size, 0, one, down1["gog"], flat(one["wout_all"]), mat0, vec, start["xg"], win0, gain, h0, down1["prev"],
        late=summed.astype(bf16),
    )
    late = pick(summed, zh)
    for k in range(zh_size - 1):
        late = late + down0["late"][k].astype(f32)

    sums = [jnp.sum(o["stats"][0]) for o in (one, two)]
    peaks = [jnp.max(o["stats"][1]) for o in (one, two)]
    pad = [jnp.zeros((), f32)] * (4 - LAYERS)
    own_stats = jnp.broadcast_to(jnp.stack(sums + pad + peaks + pad)[:, None], (8, LANES))
    downs = (down0, down1)
    small = jnp.stack([down["gvec"] for down in downs]).reshape(LAYERS, 8, group_count, share)
    small = jnp.pad(small.transpose(2, 0, 1, 3), ((0, 0), (0, 0), (0, 8), (0, LANES - share)))
    small = small.reshape(2, zh_size, 16 * LAYERS, LANES)
    spread_gain = jnp.stack([down["ggain"][0] for down in downs]).reshape(LAYERS, 2, 2, zh_size, WAYS, gains)
    spread_gain = spread_gain.transpose(2, 4, 0, 1, 3, 5).reshape(TP, LAYERS * group_count, gains)
    spread_gain = jnp.pad(spread_gain, ((0, 0), (0, -LAYERS * group_count % 8), (0, LANES - gains)))
    mats = jnp.concatenate([down["gmats"] for down in downs], axis=1).reshape(2, zh_size, share, -1)
    turns = [down0["ggate"], late.astype(bf16), down1["ggate"]]
    end = closing(
        zh_size, down0["ginner"].reshape(blocks), down0["near"], mats, small, own_stats, spread_gain,
        [t.reshape(TP, depth, half) for t in turns], [down["gwout"] for down in downs], select_weight.shape[2],
    )
    stats = end["stats_all"]
    beta_mean = stats[:LAYERS, 0] / (count * hidden.shape[1] * INNER)
    beta_max = stats[4 : 4 + LAYERS, 0]
    names = ("gin", "gselect", "grate", "gwout", "ggain", "gtaps", "gshift", "grate_shift", "gskip")
    return (stream[None], down0["prev"][None]) + tuple(end[n] for n in names) + (beta_mean, beta_max)


def solution(mesh):
    both = ("dp", "fsdp")
    placed = (
        P(both, None, None), P(both, None, None), P(both), P(),
        P(None, both, None), P(None, both, None), P(None, None, both), P(None, both, None),
        P(None, both), P(None, None, both), P(None, both), P(None, both), P(None, both),
    )
    return jax.shard_map(
        on_device,
        mesh=mesh,
        in_specs=placed,
        out_specs=(P(both, None, None), P(both, None, None)) + placed[4:] + (P(), P()),
        check_vma=False,
    )
```

```python
import types

import jax
import jax.numpy as jnp
import numpy as np
from jax import lax
from jax.sharding import PartitionSpec as P
import jax.experimental.pallas as pl
import jax.experimental.pallas.tpu as pltpu

INNER = 4096
STATE = 16
RANK = 128
CONV = 4
LAYERS = 2
WAYS = 4
TP = 8
STEPS = 16

eps = 1e-05
MESH = pl.DeviceIdType.MESH
f32 = jnp.float32
bf16 = jnp.bfloat16
VM = pl.BlockSpec(memory_space=pltpu.VMEM)
HB = pl.BlockSpec(memory_space=pl.ANY)


def place():
    dp, fs = lax.axis_index("dp"), lax.axis_index("fsdp")
    return dp // 2, lax.rem(dp, 2), fs // WAYS, lax.rem(fs, WAYS)


def device(x, core, zh, q):
    return (x * 2 + core, zh * WAYS + q)


def remote(src, dst, send, recv, target):
    return pltpu.make_async_remote_copy(
        src_ref=src, dst_ref=dst, send_sem=send, recv_sem=recv, device_id=target, device_id_type=MESH
    )


def greet(targets):
    barrier = pltpu.get_barrier_semaphore()
    for target in targets:
        pl.semaphore_signal(barrier, inc=1, device_id=target, device_id_type=MESH)
    pl.semaphore_wait(barrier, len(targets))


def tp_peers():
    x, core, zh, q = place()
    peers = []
    for dc, da, db in ((1, 0, 0), (0, 1, 0), (0, 0, 1), (1, 1, 0), (1, 0, 1), (0, 1, 1), (1, 1, 1)):
        other_core, other_q = lax.rem(core + dc, 2), neighbour(q, da, db)
        rank = other_core * WAYS + other_q
        peers.append((device(x, other_core, zh, other_q), rank, rank))
    return peers


def neighbour(q, da, db):
    a, b = lax.rem(q, 2), q // 2
    return (1 - b if db else b) * 2 + (1 - a if da else a)


def total_rank():
    _, core, _, q = place()
    return core * WAYS + q


def dp_peers(zh_size):
    x, core, zh, q = place()
    side = device(1 - x, core, zh, q)
    far = []
    for dz in range(1, zh_size):
        to_z, from_z = lax.rem(zh + dz, zh_size), lax.rem(zh + zh_size - dz, zh_size)
        far.append((device(x, core, to_z, q), to_z, from_z))
    return side, far


def lanes_of(shape):
    return lax.broadcasted_iota(jnp.int32, shape, 1)


def encode(v):
    tail = v[:, RANK:]
    lane = lanes_of(tail.shape)
    high = tail.astype(bf16).astype(f32)
    low = pltpu.roll(tail - high, 32, 1)
    both = jnp.where(lane < 32, high, jnp.where(lane < 64, low, 0.0))
    return jnp.concatenate([v[:, :RANK].astype(bf16), both.astype(bf16)], axis=1)


def decode(v):
    tail = v[:, RANK:].astype(f32)
    lane = lanes_of(tail.shape)
    tail = jnp.where(lane < 32, tail + pltpu.roll(tail, 96, 1), 0.0)
    return jnp.concatenate([v[:, :RANK].astype(f32), tail], axis=1)


def halves(rows):
    return pl.ds(0, rows // 2), pl.ds(rows // 2, rows // 2)


class Gather:
    sems = staticmethod(lambda dma: [dma((6,)), dma((6,)), dma((4,)), dma((4,)), dma])

    def __init__(self, src, out, sems):
        self.src, self.out = src, out
        self.f_send, self.f_recv, self.s_send, self.s_recv, self.own_sem = sems
        x, core, zh, q = place()
        self.core, self.me = core, core * WAYS + q
        self.sibling = device(x, 1 - core, zh, q)
        self.chips = [neighbour(q, 0, 1), neighbour(q, 1, 0), neighbour(q, 1, 1)]
        self.b, self.a = [device(x, core, zh, c) for c in self.chips[:2]]
        self.top, self.low = halves(src.shape[0])

    def send(self, i, src, slot, rows, target):
        copy = remote(src, self.out.at[slot, rows], self.f_send.at[i], self.f_recv.at[i], target)
        copy.start()
        return copy

    def to_sibling(self, i, src, slot):
        copy = remote(src, self.out.at[slot], self.s_send.at[i], self.s_recv.at[i], self.sibling)
        copy.start()
        self.near.append(copy)

    def start(self):
        self.near = []
        self.first = [
            self.send(i, self.src.at[rows], self.me, rows, target)
            for i, (rows, target) in enumerate(
                ((self.top, self.b), (self.low, self.a), (self.low, self.b), (self.top, self.a))
            )
        ]
        self.to_sibling(3, self.src, self.me)
        self.own = pltpu.make_async_copy(self.src, self.out.at[self.me], self.own_sem)
        self.own.start()

    def relay(self):
        for i, rows, target in ((0, self.top, self.a), (1, self.low, self.b)):
            self.first[i].wait_recv()
            slot = self.core * WAYS + self.chips[i]
            self.first.append(self.send(4 + i, self.out.at[slot, rows], slot, rows, target))

    def rest(self):
        for i, ends in enumerate(((2,), (3,), (4, 5))):
            for k in ends:
                self.first[k].wait_recv()
            slot = self.core * WAYS + self.chips[i]
            self.to_sibling(i, self.out.at[slot], slot)

    def finish(self):
        for copy in self.first:
            copy.wait_send()
        for copy in self.near:
            copy.wait()
        self.own.wait()


class Scatter:
    sems = staticmethod(lambda dma: [dma((4,)), dma((4,)), dma((6,)), dma((6,))])

    @staticmethod
    def buffers(block):
        return [pltpu.VMEM((4,) + block, bf16), pltpu.VMEM((3,) + block, bf16), pltpu.VMEM((3,) + block, bf16)]

    def __init__(self, partial, buffers, sems):
        self.partial = partial
        self.near_buf, self.out, self.into = buffers
        self.s_send, self.s_recv, self.f_send, self.f_recv = sems
        x, core, zh, q = place()
        self.core = core
        self.sibling = device(x, 1 - core, zh, q)
        self.turns = [neighbour(q, 1, 1), neighbour(q, 1, 0), neighbour(q, 0, 1), q]
        self.a, self.b = [device(x, core, zh, t) for t in self.turns[1:3]]
        self.top, self.low = halves(partial.shape[1])
        self.near, self.first = [None] * 4, {}

    def to_sibling(self, i):
        slot = (1 - self.core) * WAYS + self.turns[i]
        self.near[i] = remote(
            self.partial.at[slot], self.near_buf.at[i], self.s_send.at[i], self.s_recv.at[i], self.sibling
        )
        self.near[i].start()

    def joined(self, i, rows=slice(None)):
        own = self.partial[self.core * WAYS + self.turns[i], rows]
        return own.astype(f32) + self.near_buf[i, rows].astype(f32)

    def send(self, k, i, rows, target):
        self.first[k] = remote(
            self.out.at[i, rows], self.into.at[i, rows], self.f_send.at[k], self.f_recv.at[k], target
        )
        self.first[k].start()

    def across(self, i):
        self.near[i].wait_recv()
        if i == 0:
            self.out[0] = self.joined(0).astype(bf16)
            self.send(0, 0, self.top, self.a)
            self.send(1, 0, self.low, self.b)
        else:
            rows, target = ((self.top, self.a), (self.low, self.b))[i - 1]
            self.out[i, rows] = self.joined(i, rows).astype(bf16)
            self.send(1 + i, i, rows, target)

    def sums(self):
        for k, i, rows, target in ((1, 1, self.low, self.a), (0, 2, self.top, self.b)):
            self.first[k].wait_recv()
            self.out[i, rows] = (self.joined(i, rows) + self.into[0, rows].astype(f32)).astype(bf16)
            self.send(3 + i, i, rows, target)

    def total(self):
        self.near[3].wait_recv()
        value = self.joined(3)
        for k in (2, 3, 4, 5):
            self.first[k].wait_recv()
        value = value + self.into[1].astype(f32) + self.into[2].astype(f32)
        for copy in self.near + list(self.first.values()):
            copy.wait_send()
        return value


class Spread:
    @staticmethod
    def sems(dma, zh_size):
        far = max(1, zh_size - 1)
        return [dma((far,)), dma((far,)), dma((zh_size,)), dma((zh_size,)), dma]

    def __init__(self, zh_size, src, view, sems, keep=True):
        self.src, self.view, self.keep = src, view, keep
        self.z_send, self.z_recv, self.x_send, self.x_recv, self.own_sem = sems
        self.x, _, self.zh, _ = place()
        self.side, self.far = dp_peers(zh_size)

    def start(self):
        dst = self.view(self.x, self.zh)
        self.along = [
            remote(self.src, dst, self.z_send.at[k], self.z_recv.at[k], target)
            for k, (target, _, _) in enumerate(self.far)
        ]
        self.over = [remote(self.src, dst, self.x_send.at[0], self.x_recv.at[0], self.side)]
        for copy in self.along + self.over:
            copy.start()
        if self.keep:
            self.own = pltpu.make_async_copy(self.src, dst, self.own_sem)
            self.own.start()

    def onward(self):
        for k, (_, _, source) in enumerate(self.far):
            self.along[k].wait_recv()
            slot = self.view(self.x, source)
            copy = remote(slot, slot, self.x_send.at[k + 1], self.x_recv.at[k + 1], self.side)
            copy.start()
            self.over.append(copy)

    def finish(self):
        for copy in self.along:
            copy.wait_send()
        for copy in self.over:
            copy.wait()
        if self.keep:
            self.own.wait()


class Sum:
    sems = staticmethod(lambda dma: [dma((TP - 1,))] * 4)

    def __init__(self, payload, parts, out, sems):
        self.payload, self.parts, self.out = payload, parts, out
        self.a_send, self.a_recv, self.b_send, self.b_recv = sems
        x, core, zh, q = place()
        self.me = core * WAYS + q
        self.peers = tp_peers()

    def start(self):
        self.one = [
            remote(self.payload.at[rank], self.parts.at[i], self.a_send.at[i], self.a_recv.at[i], target)
            for i, (target, rank, _) in enumerate(self.peers)
        ]
        for copy in self.one:
            copy.start()

    def middle(self, own):
        total = own
        for i in range(TP - 1):
            self.one[i].wait_recv()
            total = total + decode(self.parts[i])
        self.out[self.me] = encode(total)
        self.two = [
            remote(self.out.at[self.me], self.out.at[self.me], self.b_send.at[i], self.b_recv.at[i], target)
            for i, (target, _, _) in enumerate(self.peers)
        ]
        for copy in self.two:
            copy.start()

    def finish(self):
        for copy in self.one:
            copy.wait_send()
        for copy in self.two:
            copy.wait()


def call(body, collective, ins, outs, scratch):
    def flatten(kind):
        return [leaf for each in kind for leaf in flatten(each)] if isinstance(kind, list) else [kind]

    def rebuild(kind, refs):
        return [rebuild(each, refs) for each in kind] if isinstance(kind, list) else refs.pop(0)

    def kernel(*refs):
        refs = list(refs)
        named = {key: refs.pop(0) for key in list(ins) + list(outs)}
        named.update({key: rebuild(kind, refs) for key, kind in scratch.items()})
        body(types.SimpleNamespace(**named))

    values = pl.pallas_call(
        kernel,
        out_shape=[shape for shape, _ in outs.values()],
        in_specs=[spec for _, spec in ins.values()],
        out_specs=[spec for _, spec in outs.values()],
        scratch_shapes=flatten(list(scratch.values())),
        compiler_params=pltpu.CompilerParams(
            collective_id=collective, has_side_effects=True, vmem_limit_bytes=63 * 2**20
        ),
    )(*[array for array, _ in ins.values()])
    return types.SimpleNamespace(**dict(zip(outs, values)))


def spread_keys(kq, lane):
    a = kq.astype(bf16).astype(f32)
    rest = kq - a
    b = rest.astype(bf16).astype(f32)
    c = rest - b
    return jnp.where(lane < 32, a, jnp.where(lane < 64, b, c)).astype(bf16)


def spreader():
    one = np.repeat(np.eye(32, dtype=np.float32), 128, axis=1)
    return jnp.asarray(np.concatenate([one, one, one, np.zeros_like(one)], axis=0), bf16)


def folder():
    return jnp.asarray(np.pad(np.repeat(np.eye(32, dtype=np.float32), 128, axis=0), ((0, 0), (0, 96))), bf16)


def dot(a, b, contract, out=f32):
    return lax.dot_general(a, b, (contract, ((), ())), preferred_element_type=out)


def rms(stream):
    return lax.rsqrt(jnp.mean(jnp.square(stream), axis=-1, keepdims=True) + eps)


LANES = 128


def struct(*shape, dtype=f32):
    return jax.ShapeDtypeStruct(shape, dtype)


def side_by_side(pieces, lanes):
    each = LANES // lanes
    out = []
    for i in range(0, len(pieces), each):
        tile = pieces[i]
        for j in range(1, each):
            tile = tile + pltpu.roll(pieces[i + j], j * lanes, 1)
        out.append(tile)
    return jnp.concatenate(out, axis=1)


def turn_pieces(zh_size, win, layer, out, rank):
    if len(win.shape) == 4:
        return [(win.at[layer, rank], out)]
    groups = 2 * zh_size
    share = win.shape[2] // (2 * groups * TP)
    pieces = []
    for part in range(2):
        for g in range(groups):
            d = ((g // zh_size * 2 + rank // WAYS) * zh_size + g % zh_size) * WAYS + lax.rem(rank, WAYS)
            first = pl.multiple_of((part * groups * TP + d) * share, share)
            pieces.append(
                (win.at[layer, :, pl.ds(first, share)], out.at[:, pl.ds((part * groups + g) * share, share)])
            )
    return pieces


class Turn:
    def __init__(self, zh_size, win, layer, out, slot, sems):
        self.out, self.slot, self.sems = out, slot, sems
        self.me = total_rank()
        self.peers = tp_peers()
        self.pieces = lambda rank: turn_pieces(zh_size, win, layer, out.at[slot(self.me)], rank)

    def start(self):
        for i, (target, rank, _) in enumerate(self.peers):
            for src, dst in self.pieces(rank):
                remote(src, dst, self.sems[0].at[i], self.sems[1].at[i], target).start()

    def whole(self, i, rank):
        block = self.out.at[self.slot(rank)]
        return remote(block, block, self.sems[0].at[i], self.sems[1].at[i], self.peers[i][0])

    def arrived(self, i):
        self.whole(i, self.peers[i][2]).wait_recv()

    def sent(self):
        for i in range(TP - 1):
            self.whole(i, self.me).wait_send()


def opening(zh_size, gains, share, win, small, misc, mats, h, cot):
    groups = 2 * zh_size
    count = groups * TP
    tokens, width = h.shape
    half = groups * share
    depth = win.shape[-2]
    dma = pltpu.SemaphoreType.DMA
    ins = dict(
        win=(win, HB), small=(small, VM), misc=(misc, VM), mats=(mats, HB), h=(h, VM), cot=(cot, VM)
    )
    outs = dict(
        win_all=(struct(count, depth, 2 * half, dtype=bf16), HB),
        mats_all=(struct(groups, *mats.shape[1:], dtype=bf16), HB), vec=(struct(8 * LAYERS, half), VM),
        gains=(struct(8, width), VM), scale=(struct(TP, LANES), VM), grad=(struct(tokens, width), VM),
        gout=(struct(tokens, width, dtype=bf16), VM), xg=(struct(TP, tokens, width, dtype=bf16), HB),
    )
    spread = lambda: Spread.sems(dma, zh_size)
    scratch = dict(
        misc_all=pltpu.VMEM((count,) + misc.shape, f32), small_all=pltpu.VMEM((groups,) + small.shape, f32),
        normed=pltpu.VMEM((tokens, width), bf16), gather_sems=Gather.sems(dma),
        m_sems=[dma((TP - 1,))] * 2, w_sems=[dma((TP - 1,))] * 2, own_sem=dma,
        own=pltpu.VMEM((depth, 2 * half), bf16), s0=spread(), s1=spread(),
        sm=[spread() for _ in range(TP)], sw=[spread() for _ in range(TP)],
    )

    def body(r):
        x, core, zh, q = place()
        me = core * WAYS + q
        peers = tp_peers()
        side, far = dp_peers(zh_size)
        greet([p[0] for p in peers] + [side] + [f[0] for f in far])

        def row(xx, zz, rank):
            return ((xx * 2 + rank // WAYS) * zh_size + zz) * WAYS + lax.rem(rank, WAYS)

        def views(out, rank):
            return lambda xx, zz: out.at[row(xx, zz, rank)]

        here = row(x, zh, me)
        miscs = []
        for i, (target, rank, _) in enumerate(peers):
            miscs.append(remote(r.misc, r.misc_all.at[here], r.m_sems[0].at[i], r.m_sems[1].at[i], target))
            miscs[-1].start()
        misc_moves = [Spread(zh_size, r.misc, views(r.misc_all, me), r.sm[0])]
        misc_moves[0].start()
        smalls = Spread(zh_size, r.small, lambda xx, zz: r.small_all.at[xx * zh_size + zz], r.s0)
        smalls.start()
        wins = Turn(zh_size, r.win, 0, r.win_all, lambda rank: row(x, zh, rank), r.w_sems)
        wins.start()
        own_pieces = [
            pltpu.make_async_copy(src, dst, r.own_sem)
            for src, dst in turn_pieces(zh_size, r.win, 0, r.own, me)
        ]
        for copy in own_pieces:
            copy.start()
        pltpu.make_async_copy(r.own, r.own, r.own_sem).wait()
        win_moves = [Spread(zh_size, r.own, views(r.win_all, me), r.sw[0])]
        for i, (_, _, source) in enumerate(peers):
            view = views(r.win_all, source)
            win_moves.append(Spread(zh_size, view(x, zh), view, r.sw[i + 1], keep=False))
        mats_move = Spread(zh_size, r.mats.at[0], lambda xx, zz: r.mats_all.at[xx * zh_size + zz], r.s1)

        def step(i):
            if i >= 1:
                wins.arrived(i - 1)
            if i >= 2:
                win_moves[i - 2].onward()
            win_moves[i].start()

        step(0)
        for i, (_, _, source) in enumerate(peers):
            miscs[i].wait_recv()
            view = views(r.misc_all, source)
            misc_moves.append(Spread(zh_size, view(x, zh), view, r.sm[i + 1], keep=False))
            misc_moves[-1].start()
        step(1)
        for move in misc_moves:
            move.onward()
        smalls.onward()
        for move in misc_moves:
            move.finish()
        for l in range(LAYERS):
            r.gains[l : l + 1, :] = side_by_side(
                [r.misc_all[d, l : l + 1, :] for d in range(count)], gains
            )
        r.gains[LAYERS:, :] = jnp.zeros((8 - LAYERS, width), f32)
        stream = r.h[...]
        r.normed[...] = (stream * rms(stream) * r.gains[0:1, :]).astype(bf16)
        rows = Gather(r.normed, r.xg, r.gather_sems)
        rows.start()
        step(2)
        mats_move.start()
        total = r.misc_all[0, LAYERS : LAYERS + 1, :]
        for d in range(1, count):
            total = total + r.misc_all[d, LAYERS : LAYERS + 1, :]
        inverse = count / total
        for rank in range(TP):
            r.scale[rank : rank + 1, :] = r.misc_all[row(x, zh, rank), LAYERS : LAYERS + 1, :] * inverse
        own = (r.misc[LAYERS : LAYERS + 1, :] * inverse)[:, :1]
        grad = r.cot[...] * own
        r.grad[...] = grad
        r.gout[...] = grad.astype(bf16)
        step(3)
        smalls.finish()
        for l in range(LAYERS):
            r.vec[8 * l : 8 * (l + 1), :] = side_by_side(
                [r.small_all[g, 8 * l : 8 * (l + 1), :] for g in range(groups)], share
            )
        step(4)
        mats_move.onward()
        rows.relay()
        step(5)
        step(6)
        rows.rest()
        step(7)
        win_moves[6].onward()
        win_moves[7].onward()
        wins.sent()
        for copy in miscs:
            copy.wait_send()
        for move in win_moves + [mats_move]:
            move.finish()
        rows.finish()

    return call(body, 1, ins, outs, scratch)


def at_block(b, size):
    return pl.ds(pl.multiple_of(b * size, size), size)


def conv_of(entry, vec, row, size, c):
    cols = slice(c * LANES, (c + 1) * LANES)
    conv = vec[CONV : CONV + 1, cols]
    for j in range(CONV):
        conv = conv + vec[j : j + 1, cols] * entry[c, pl.ds(pl.multiple_of(row + TP * j, TP), size), :]
    return conv


def wide_of(ref, rows, parts):
    return jnp.concatenate([ref[c, rows, :] for c in range(parts)], axis=1)


def row_sum(value):
    return jnp.sum(value.reshape(-1, TP, value.shape[1]), axis=0)


def square_sum(kq):
    lane = lanes_of(kq.shape)
    return jnp.sum(jnp.where(lane < STATE, kq * kq, 0.0), axis=1, keepdims=True)


def forward_layer(zh_size, layer, xg, win, mats, wout, vec, scale, gout=None, nxt=None):
    tokens, width = xg.shape[1], xg.shape[2]
    half = win.shape[1] // 2
    parts = half // LANES
    rows = tokens * TP
    size = STEPS * TP
    blocks = rows // size
    halo = (CONV - 1) * TP
    dma = pltpu.SemaphoreType.DMA
    last = nxt is None
    groups = 2 * zh_size
    ins = dict(
        xg=(xg, VM), win=(win, VM), mats=(mats, VM), wout=(wout, HB), vec=(vec, VM),
        scale=(scale, VM), e=(spreader(), VM),
    )
    outs = dict(
        entry=(struct(2 * parts, halo + rows, LANES), VM), beta=(struct(parts, rows, LANES), VM),
        kq=(struct(rows, LANES), VM), proj=(struct(TP, size, 2 * LANES, dtype=bf16), VM),
        y=(struct(parts, rows, LANES), VM), keep=(struct(blocks, STATE, parts, TP, LANES), VM),
        mixed=(struct(TP, tokens, half, dtype=bf16), VM), stats=(struct(2, TP, LANES), VM),
    )
    scratch = dict(
        act=pltpu.VMEM((parts, rows, LANES), f32), step=pltpu.VMEM((parts, rows, LANES), f32),
        payload=pltpu.VMEM((TP, size, 2 * LANES), bf16), parts=pltpu.VMEM((TP - 1, size, 2 * LANES), bf16),
        own=pltpu.VMEM((size, 2 * LANES), f32),
        state=pltpu.VMEM((STATE, parts, TP, LANES), f32), wide=pltpu.VMEM((size, 32 * LANES), f32),
        sum_sems=Sum.sems(dma),
    )
    outs.update(wout_all=(struct(groups, *wout.shape[1:], dtype=bf16), VM))
    scratch.update(d0=Spread.sems(dma, zh_size))
    if last:
        ins.update(gout=(gout, VM))
        outs.update(
            gog=(struct(TP, tokens, width, dtype=bf16), HB), part=(struct(TP, tokens, width, dtype=bf16), VM)
        )
        scratch.update(gather_sems=Gather.sems(dma))
    if not last:
        win1 = nxt.win
        depth = win1.shape[-2]
        ins.update(h=(nxt.h, VM), gain=(nxt.gain, VM), win1=(win1, HB), mats1=(nxt.mats, HB))
        outs.update(
            result=(struct(tokens, width), VM),
            win1_all=(struct(2, 2, zh_size, WAYS, depth, 2 * half, dtype=bf16), HB),
            mats1_all=(struct(groups, *nxt.mats.shape[1:], dtype=bf16), HB),
            xg1=(struct(TP, tokens, width, dtype=bf16), HB),
        )
        scratch.update(
            normed=pltpu.VMEM((tokens, width), bf16), gather_sems=Gather.sems(dma),
            part=pltpu.VMEM((TP, tokens, width), bf16), scatter_buf=Scatter.buffers((tokens, width)),
            scatter_sems=Scatter.sems(dma),
            turned=pltpu.VMEM((TP, depth, 2 * half), bf16), l_sems=[dma((TP - 1,)), dma((TP - 1,))], l_own=dma,
            d1=Spread.sems(dma, zh_size), d2=Spread.sems(dma, zh_size), d3=Spread.sems(dma, zh_size),
        )

    def body(r):
        side, far = dp_peers(zh_size)
        greet([p[0] for p in tp_peers()] + [side] + [f[0] for f in far])
        entry, act, step, beta, kq, y = r.entry, r.act, r.step, r.beta, r.kq, r.y
        vec = r.vec.at[8 * layer : 8 * (layer + 1)]
        index = lambda ref: lambda xx, zz: ref.at[xx * zh_size + zz]
        early = Spread(zh_size, r.wout.at[layer], index(r.wout_all), r.d0)
        early.start()
        if last:
            gouts = Gather(r.gout, r.gog, r.gather_sems)
        else:
            turned = Turn(zh_size, r.win1, layer + 1, r.turned, lambda rank: rank, r.l_sems)
            turned.start()
            for src, dst in turned.pieces(turned.me):
                pltpu.make_async_copy(src, dst, r.l_own).start()
            moves = [Spread(zh_size, r.mats1.at[layer + 1], index(r.mats1_all), r.d3)]
            for k in range(2):
                view = lambda xx, zz, k=k: r.win1_all.at[xx, k, zz]
                src = r.turned.at[k * WAYS : (k + 1) * WAYS]
                moves.append(Spread(zh_size, src, view, (r.d1 if k == 0 else r.d2)))

        entry[:, :halo, :] = jnp.zeros((2 * parts, halo, LANES), f32)
        tile = 2 * LANES
        for p in range(TP // 2):

            def columns(n, carry, p=p):
                cols = at_block(n, tile)
                out = jnp.dot(
                    r.xg[2 * p : 2 * p + 2].reshape(2 * tokens, width), r.win[:, cols],
                    preferred_element_type=f32,
                )
                for j in range(2):
                    for c in range(2):
                        entry[2 * n + c, pl.ds(halo + 2 * p + j, tokens, stride=TP), :] = out[
                            j * tokens : (j + 1) * tokens, c * LANES : (c + 1) * LANES
                        ]
                return carry

            lax.fori_loop(0, 2 * half // tile, columns, 0)
        total = Sum(r.payload, r.parts, r.proj, r.sum_sems)

        def project(b, carry):
            rs = at_block(b, size)
            for c in range(parts):
                conv = conv_of(entry, vec, b * size, size, c)
                act[c, rs, :] = (conv * jax.nn.sigmoid(conv)).astype(bf16).astype(f32)
            out = jnp.dot(
                wide_of(act, rs, parts).astype(bf16), r.mats[:, RANK:], preferred_element_type=f32
            )
            r.payload[b] = encode(out)

            @pl.when(b == total.me)
            def _():
                r.own[...] = out

            return carry

        lax.fori_loop(0, blocks, project, 0)
        total.start()
        if not last:
            for i in range(TP - 1):
                turned.arrived(i)
            mine = r.turned.at[turned.me]
            pltpu.make_async_copy(mine, mine, r.l_own).wait()
            moves[0].start()
            moves[1].start()
        total.middle(r.own[...])
        total.finish()
        if last:
            gouts.start()
        else:
            turned.sent()
            moves[2].start()

        r.stats[...] = jnp.zeros((2, TP, LANES), f32)

        def rates(b, carry):
            rs = at_block(b, size)
            tail = decode(r.proj[b])[:, RANK:]
            keys = tail + pltpu.roll(tail, 32, 1) + pltpu.roll(tail, 64, 1)
            kq[rs, :] = keys
            norm = square_sum(keys)
            pre = dot(r.proj[b, :, :RANK], r.mats[:, :RANK], ((1,), (1,)))
            for c in range(parts):
                cols = slice(c * LANES, (c + 1) * LANES)
                rate = jax.nn.sigmoid(pre[:, cols] + vec[CONV + 1 : CONV + 2, cols])
                beta[c, rs, :] = rate
                step[c, rs, :] = rate / (1.0 + rate * norm)
                r.stats[0] += row_sum(rate)
                r.stats[1] = jnp.maximum(
                    r.stats[1], jnp.max(rate.reshape(-1, TP, LANES), axis=0)
                )
            return carry

        lax.fori_loop(0, blocks, rates, 0)
        r.stats[0] = r.stats[0] * r.scale[...]
        r.stats[1] = r.stats[1] * r.scale[...]

        lane = lanes_of((size, LANES))
        state, wide = r.state, r.wide
        state[...] = jnp.zeros_like(state)

        def block(b, carry):
            r.keep[b] = state[...]
            wide[...] = jnp.dot(spread_keys(kq[at_block(b, size), :], lane), r.e[...], preferred_element_type=f32)

            def one(j, carry):
                t = at_block(b * STEPS + j, TP)
                w = at_block(j, TP)
                acts = [act[c, t, :] for c in range(parts)]
                steps = [step[c, t, :] for c in range(parts)]
                sums = [None] * parts
                for n in range(STATE):
                    key = wide[w, n * LANES : (n + 1) * LANES]
                    query = wide[w, (STATE + n) * LANES : (STATE + n + 1) * LANES]
                    for c in range(parts):
                        s = state[n, c]
                        s = s + (steps[c] * key) * (acts[c] - key * s)
                        state[n, c] = s
                        sums[c] = s * query if sums[c] is None else sums[c] + s * query
                for c in range(parts):
                    y[c, t, :] = sums[c]
                return carry

            lax.fori_loop(0, STEPS, one, 0)
            rs = at_block(b, size)
            here = pl.ds(pl.multiple_of(b * STEPS, STEPS), STEPS)
            for c in range(parts):
                cols = slice(c * LANES, (c + 1) * LANES)
                gate = entry[parts + c, pl.ds(pl.multiple_of(b * size + halo, TP), size), :]
                skip = vec[CONV + 2 : CONV + 3, cols]
                step[c, rs, :] = (y[c, rs, :] + skip * act[c, rs, :]) * (gate * jax.nn.sigmoid(gate))
                for s in range(TP):
                    r.mixed[s, here, cols] = step[c, pl.ds(b * size + s, STEPS, stride=TP), :].astype(bf16)
            return carry

        early.onward()
        lax.fori_loop(0, blocks // 2, block, 0)
        if last:
            gouts.relay()
        else:
            moves[0].onward()
        lax.fori_loop(blocks // 2, blocks, block, 0)
        early.finish()
        weight = lambda: r.wout_all[...].reshape(half, width)
        if last:

            def plain(s, carry):
                two = r.mixed[pl.ds(2 * s, 2)].reshape(2 * tokens, half)
                out = dot(two, weight(), ((1,), (0,))).astype(bf16)
                r.part[pl.ds(2 * s, 2)] = out.reshape(2, tokens, width)
                return carry

            lax.fori_loop(0, TP // 4, plain, 0)
            gouts.rest()
            lax.fori_loop(TP // 4, TP // 2, plain, 0)
            gouts.finish()
            return
        scatter = Scatter(r.part, r.scatter_buf, r.scatter_sems)
        out_partial(scatter, r.part, r.mixed, weight)
        moves[1].onward()
        stream = r.h[...] + scatter.total()
        r.result[...] = stream
        r.normed[...] = (stream * rms(stream) * r.gain[layer + 1 : layer + 2, :]).astype(bf16)
        spread = Gather(r.normed, r.xg1, r.gather_sems)
        spread.start()
        spread.relay()
        moves[2].onward()
        spread.rest()
        spread.finish()
        for move in moves:
            move.finish()

    return call(body, 7 if last else 6, ins, outs, scratch)


def out_partial(scatter, part, left, right, turned=False):
    contract = ((1,), (1,)) if turned else ((1,), (0,))
    for i in range(4):
        slots = [core * WAYS + scatter.turns[i] for core in (1 - scatter.core, scatter.core)]
        rows = left.shape[1]
        both = dot(jnp.concatenate([left[slot] for slot in slots], axis=0), right(), contract).astype(bf16)
        part[slots[0]] = both[:rows]
        part[slots[1]] = both[rows:]
        scatter.to_sibling(i)
        if i >= 1:
            scatter.across(i - 1)
    scatter.sums()


class Reduce:
    @staticmethod
    def sems(dma, zh_size):
        far = max(1, zh_size - 1)
        return [dma, dma, dma((far,)), dma((far,))]

    @staticmethod
    def buffers(zh_size, block):
        return [
            pltpu.VMEM((zh_size,) + block, bf16), pltpu.VMEM((zh_size,) + block, bf16),
            pltpu.VMEM((max(1, zh_size - 1),) + block, bf16),
        ]

    def __init__(self, zh_size, src, buffers, sems):
        self.zh_size, self.src = zh_size, src
        self.near, self.mine, self.buf = buffers
        self.x_send, self.x_recv, self.z_send, self.z_recv = sems
        self.x, _, self.zh, _ = place()
        self.side, self.far = dp_peers(zh_size)

    def start(self):
        half = self.src.at[pl.ds((1 - self.x) * self.zh_size, self.zh_size)]
        self.over = remote(half, self.near, self.x_send, self.x_recv, self.side)
        self.over.start()

    def middle(self):
        self.over.wait_recv()
        for k in range(self.zh_size):
            self.mine[k] = (
                self.src[self.x * self.zh_size + k].astype(f32) + self.near[k].astype(f32)
            ).astype(bf16)
        self.along = [
            remote(self.mine.at[to_z], self.buf.at[k], self.z_send.at[k], self.z_recv.at[k], target)
            for k, (target, to_z, _) in enumerate(self.far)
        ]
        for copy in self.along:
            copy.start()

    def total(self):
        value = self.src[self.x * self.zh_size + self.zh].astype(f32) + self.near[self.zh].astype(f32)
        for k in range(self.zh_size - 1):
            self.along[k].wait_recv()
            value = value + self.buf[k].astype(f32)
        self.over.wait_send()
        for copy in self.along:
            copy.wait_send()
        return value


def backward_layer(zh_size, layer, kept, gog, wout, mats, vec, xg, win, gain, h, grad, late=None, part=None):
    tokens, width = xg.shape[1], xg.shape[2]
    half = win.shape[1] // 2
    parts = half // LANES
    rows = tokens * TP
    size = STEPS * TP
    blocks = rows // size
    halo = (CONV - 1) * TP
    groups = 2 * zh_size
    share = half // groups
    deep = width // (2 * groups)
    far = max(1, zh_size - 1)
    dma = pltpu.SemaphoreType.DMA
    onward = part is not None
    ins = dict(entry=(kept.entry, VM), beta=(kept.beta, VM), kq=(kept.kq, VM), proj=(kept.proj, VM))
    ins.update(
        mats=(mats, VM), wout=(wout, HB), vec=(vec, VM), gain=(gain, VM), h=(h, VM), grad=(grad, VM),
        mixed=(kept.mixed, HB), e=(spreader(), VM), fold=(folder(), VM), keep=(kept.keep, HB), gouts=(gog, HB), y=(kept.y, HB), xg=(xg, HB), win=(win, HB),
    )
    outs = dict(
        prev=(struct(tokens, width), VM), ginner=(struct(groups, 2, deep, half, dtype=bf16), VM),
        near=(struct(zh_size, 2, deep, half, dtype=bf16), HB), ggate=(struct(2, deep, half, dtype=bf16), VM), gwout=(struct(share, width), VM),
        gmats=(struct(half, 3 * LANES, dtype=bf16), VM), gvec=(struct(8, half), VM),
        ggain=(struct(1, width), VM),
    )
    block_f32 = pltpu.VMEM((parts, rows, LANES), f32)
    scratch = dict(
        a=pltpu.VMEM((TP, tokens, width), bf16), b=pltpu.VMEM(win.shape, bf16),
        gs=block_f32, act=block_f32, gact=block_f32,
        step=pltpu.VMEM((parts, rows + halo, LANES), f32),
        states=pltpu.VMEM((STEPS + 1, STATE, parts, TP, LANES), f32),
        lam=pltpu.VMEM((STATE, parts, TP, LANES), f32), wide=pltpu.VMEM((size, 32 * LANES), f32),
        gstep=pltpu.VMEM((parts, size, LANES), f32),
        gentry=pltpu.VMEM((TP, tokens, 2 * half), bf16),
        payload=pltpu.VMEM((TP, size, 2 * LANES), bf16), parts=pltpu.VMEM((TP - 1, size, 2 * LANES), bf16),
        total=pltpu.VMEM((TP, size, 2 * LANES), bf16), own=pltpu.VMEM((size, 2 * LANES), f32),
        sums=pltpu.VMEM((8, parts, TP, LANES), f32),
        grate=pltpu.VMEM((half, LANES), f32), gselect=pltpu.VMEM((half, 2 * LANES), f32),
        gwo=pltpu.VMEM((groups, share, width), bf16), gwg=pltpu.VMEM((groups, 2, deep, half), bf16),
        gate_buf=Reduce.buffers(zh_size, (2, deep, half)), gate_sems=Reduce.sems(dma, zh_size),
        keeps=pltpu.VMEM((2, STATE, parts, TP, LANES), f32), keep_sems=dma((2,)),
        scatter_buf=Scatter.buffers((tokens, width)), reduce_buf=Reduce.buffers(zh_size, (share, width)),
        sum_sems=Sum.sems(dma), scatter_sems=Scatter.sems(dma), reduce_sems=Reduce.sems(dma, zh_size),
        loads=dma((7,)), over=[dma, dma],
    )
    if onward:
        outs.update(gog=(struct(TP, tokens, width, dtype=bf16), HB))
        ins.update(part=(part, HB))
        outs.update(parts_all=(struct(*part.shape, dtype=bf16), HB))
        scratch.update(part_sems=[dma((TP - 1,)), dma((TP - 1,)), dma])
        scratch.update(gout=pltpu.VMEM((tokens, width), bf16), gather_sems=Gather.sems(dma))
    if late is not None:
        ins.update(late_in=(late, HB))
        outs.update(late=(struct(far, *late.shape[1:], dtype=bf16), HB))
        scratch.update(late_sems=[dma((far,)), dma((far,))])

    def body(r):
        x, core, zh, q = place()
        side, far_ones = dp_peers(zh_size)
        greet([p[0] for p in tp_peers()] + [side] + [f[0] for f in far_ones])
        entry, act, step, beta, kq = r.entry, r.act, r.step, r.beta, r.kq
        gs, gact, sums, gstep = r.gs, r.gact, r.sums, r.gstep
        vec = r.vec.at[8 * layer : 8 * (layer + 1)]
        loads = [
            pltpu.make_async_copy(src, dst, r.loads.at[i])
            for i, (src, dst) in enumerate(
                (
                    (r.gouts, r.a), (r.mixed, r.gentry.at[:, :, :half]),
                    (r.wout.at[:, : 2 * half], r.b.at[:half]), (r.wout.at[:, 2 * half :], r.b.at[half : 2 * half]),
                    (r.y, gact), (r.xg, r.a), (r.win, r.b),
                )
            )
        ]
        for copy in loads[:5]:
            copy.start()
        passed = []
        if onward:
            me = core * WAYS + q
            for i, (target, rank, _) in enumerate(tp_peers()):
                copy = remote(
                    r.part.at[rank], r.parts_all.at[me], r.part_sems[0].at[i], r.part_sems[1].at[i], target
                )
                copy.start()
                passed.append(copy)
            passed.append(pltpu.make_async_copy(r.part.at[me], r.parts_all.at[me], r.part_sems[2]))
            passed[-1].start()
        if late is not None:
            for k, (target, to_z, _) in enumerate(far_ones):
                copy = remote(
                    r.late_in.at[to_z], r.late.at[k], r.late_sems[0].at[k], r.late_sems[1].at[k], target
                )
                copy.start()
                passed.append(copy)
        sums[...] = jnp.zeros_like(sums)
        r.grate[...] = jnp.zeros_like(r.grate)
        r.gselect[...] = jnp.zeros_like(r.gselect)

        def again(b, carry):
            rs = at_block(b, size)
            norm = square_sum(kq[rs, :])
            for c in range(parts):
                conv = conv_of(entry, vec, b * size, size, c)
                act[c, rs, :] = (conv * jax.nn.sigmoid(conv)).astype(bf16).astype(f32)
                rate = beta[c, rs, :]
                step[c, rs, :] = rate / (1.0 + rate * norm)
            return carry

        lax.fori_loop(0, blocks, again, 0)
        loads[0].wait()
        loads[1].wait()

        def outer(c, carry):
            left = r.gentry[:, :, at_block(c, LANES)].reshape(rows, LANES)
            out = dot(left, r.a[...].reshape(rows, width), ((0,), (0,))).astype(bf16)
            each = LANES // share
            r.gwo[pl.ds(c * each, each)] = out.reshape(each, share, width)
            return carry

        lax.fori_loop(0, parts, outer, 0)
        reduce = Reduce(zh_size, r.gwo, r.reduce_buf, r.reduce_sems)
        reduce.start()
        loads[2].wait()
        loads[3].wait()
        for p in range(TP // 2):

            def columns(n, carry, p=p):
                out = 0.0
                for k in range(2):
                    left = r.a[2 * p : 2 * p + 2, :, 2 * half * k : 2 * half * (k + 1)].reshape(2 * tokens, 2 * half)
                    right = r.b[pl.ds(pl.multiple_of(half * k + n * 2 * LANES, 2 * LANES), 2 * LANES), :]
                    out = out + dot(left, right, ((1,), (1,)))
                for j in range(2):
                    for c in range(2):
                        gs[2 * n + c, pl.ds(2 * p + j, tokens, stride=TP), :] = out[
                            j * tokens : (j + 1) * tokens, c * LANES : (c + 1) * LANES
                        ]
                return carry

            lax.fori_loop(0, half // (2 * LANES), columns, 0)
        loads[5].start()
        loads[6].start()
        loads[4].wait()

        def gates(b, carry):
            rs = at_block(b, size)
            here = pl.ds(pl.multiple_of(b * STEPS, STEPS), STEPS)
            for c in range(parts):
                cols = slice(c * LANES, (c + 1) * LANES)
                gate = entry[parts + c, pl.ds(pl.multiple_of(b * size + halo, TP), size), :]
                sig = jax.nn.sigmoid(gate)
                g = gs[c, rs, :]
                a = act[c, rs, :]
                down = g * (gate * sig)
                gstep[c] = g * (gact[c, rs, :] + vec[CONV + 2 : CONV + 3, cols] * a) * (
                    sig * (1.0 + gate * (1.0 - sig))
                )
                gs[c, rs, :] = down
                sums[CONV + 2, c] += row_sum(down * a)
                for s in range(TP):
                    r.gentry[s, here, half + c * LANES : half + (c + 1) * LANES] = gstep[
                        c, pl.ds(s, STEPS, stride=TP), :
                    ].astype(bf16)
            return carry

        lax.fori_loop(0, blocks, gates, 0)
        loads[5].wait()
        tile = 2 * LANES

        def outer_in(out_ref, first, i, carry):
            left = r.a[:, :, at_block(i, tile)].reshape(rows, tile)
            out = dot(left, r.gentry[:, :, first : first + half].reshape(rows, half), ((0,), (0,))).astype(bf16)
            each = tile // deep
            for e in range(each):
                d = i * each + e
                xx, cc, zz = d // (2 * zh_size), lax.rem(d // zh_size, 2), lax.rem(d, zh_size)
                out_ref[xx * zh_size + zz, cc] = out[e * deep : (e + 1) * deep]
            return carry

        lax.fori_loop(0, width // tile, lambda i, k: outer_in(r.gwg, half, i, k), 0)
        gate_reduce = Reduce(zh_size, r.gwg, r.gate_buf, r.gate_sems)

        lane = lanes_of((size, LANES))
        states, lam, wide = r.states, r.lam, r.wide
        lam[...] = jnp.zeros_like(lam)
        plus = lambda a, b: b if a is None else a + b
        total = Sum(r.payload, r.parts, r.total, r.sum_sems)

        def block(bi, carry):
            b = blocks - 1 - bi
            rs = at_block(b, size)
            slot = lax.rem(b, 2)
            pltpu.make_async_copy(r.keep.at[b], r.keeps.at[slot], r.keep_sems.at[slot]).wait()

            @pl.when(b > 0)
            def _():
                ahead = pltpu.make_async_copy(r.keep.at[b - 1], r.keeps.at[1 - slot], r.keep_sems.at[1 - slot])
                ahead.start()

            states[0] = r.keeps[slot]
            wide[...] = jnp.dot(spread_keys(kq[rs, :], lane), r.e[...], preferred_element_type=f32)

            def replay(j, carry):
                t, w = at_block(b * STEPS + j, TP), at_block(j, TP)
                acts = [act[c, t, :] for c in range(parts)]
                steps = [step[c, t, :] for c in range(parts)]
                for n in range(STATE):
                    key = wide[w, n * LANES : (n + 1) * LANES]
                    for c in range(parts):
                        s = states[j, n, c]
                        states[j + 1, n, c] = s + (steps[c] * key) * (acts[c] - key * s)
                return carry

            lax.fori_loop(0, STEPS, replay, 0)

            def back(jj, carry):
                j = STEPS - 1 - jj
                t, w = at_block(b * STEPS + j, TP), at_block(j, TP)
                acts = [act[c, t, :] for c in range(parts)]
                steps = [step[c, t, :] for c in range(parts)]
                gsums = [gs[c, t, :] for c in range(parts)]
                first, second = [None] * parts, [None] * parts
                for n in range(STATE):
                    kcols, qcols = slice(n * LANES, (n + 1) * LANES), slice((STATE + n) * LANES, (STATE + n + 1) * LANES)
                    key, query = wide[w, kcols], wide[w, qcols]
                    square = key * key
                    key_term, query_term = None, None
                    for c in range(parts):
                        before, after = states[j, n, c], states[j + 1, n, c]
                        grad = lam[n, c] + gsums[c] * query
                        u = key * before
                        d = acts[c] - u
                        gk = grad * key
                        sg = steps[c] * grad
                        first[c] = plus(first[c], gk * d)
                        second[c] = plus(second[c], gk)
                        key_term = plus(key_term, sg * (d - u))
                        query_term = plus(query_term, gsums[c] * after)
                        lam[n, c] = grad - sg * square
                    wide[w, kcols] = key_term
                    wide[w, qcols] = query_term
                for c in range(parts):
                    gstep[c, w, :] = first[c]
                    gact[c, t, :] = steps[c] * second[c]
                return carry

            lax.fori_loop(0, STEPS, back, 0)
            terms = wide[...]
            high = terms.astype(bf16)
            low = (terms - high.astype(f32)).astype(bf16)
            gkq = jnp.dot(high, r.fold[...], preferred_element_type=f32) + jnp.dot(
                low, r.fold[...], preferred_element_type=f32
            )
            keys = kq[rs, :]
            norm = square_sum(keys)
            gnorm = jnp.zeros((size, 1), f32)
            grates = []
            for c in range(parts):
                cols = slice(c * LANES, (c + 1) * LANES)
                rate = beta[c, rs, :]
                g = gstep[c]
                inverse = 1.0 + rate * norm
                inverse = 1.0 / (inverse * inverse)
                gnorm = gnorm - jnp.sum(g * (rate * rate * inverse), axis=1, keepdims=True)
                grate = g * inverse * rate * (1.0 - rate)
                sums[CONV + 1, c] += row_sum(grate)
                grates.append(grate.astype(bf16))
                gact[c, rs, :] += vec[CONV + 2 : CONV + 3, cols] * gs[c, rs, :]
            grate = jnp.concatenate(grates, axis=1)
            r.grate[...] += dot(grate, r.proj[b, :, :RANK], ((0,), (0,)))
            grank = dot(grate, r.mats[:, :RANK], ((1,), (0,)))
            gkq = gkq + jnp.where(lane < STATE, 2.0 * keys * gnorm, 0.0)
            out = jnp.concatenate([grank, gkq], axis=1)
            r.payload[b] = encode(out)

            @pl.when(b == total.me)
            def _():
                r.own[...] = out

            return carry

        last = (blocks - 1) % 2
        pltpu.make_async_copy(r.keep.at[blocks - 1], r.keeps.at[last], r.keep_sems.at[last]).start()
        lax.fori_loop(0, blocks // 2, block, 0)
        reduce.middle()
        gate_reduce.start()
        lax.fori_loop(blocks // 2, blocks, block, 0)
        total.start()
        total.middle(r.own[...])
        total.finish()
        gate_reduce.middle()
        step[:, rows:, :] = jnp.zeros((parts, halo, LANES), f32)
        gconv = step

        def convs(b, carry):
            rs = at_block(b, size)
            gp = r.total[b]
            gp = jnp.where(lanes_of(gp.shape) < RANK + 2 * STATE, gp.astype(f32), 0.0).astype(bf16)
            r.gselect[...] += dot(wide_of(act, rs, parts).astype(bf16), gp, ((0,), (0,)))
            more = dot(gp, r.mats[:, RANK:], ((1,), (1,)))
            for c in range(parts):
                conv = conv_of(entry, vec, b * size, size, c)
                sig = jax.nn.sigmoid(conv)
                g = (gact[c, rs, :] + more[:, c * LANES : (c + 1) * LANES]) * (sig * (1.0 + conv * (1.0 - sig)))
                gconv[c, rs, :] = g
                sums[CONV, c] += row_sum(g)
                for j in range(CONV):
                    inner = entry[c, pl.ds(pl.multiple_of(b * size + TP * j, TP), size), :]
                    sums[j, c] += row_sum(g * inner)
            return carry

        lax.fori_loop(0, blocks, convs, 0)

        def inners(b, carry):
            rs = at_block(b, size)
            here = pl.ds(pl.multiple_of(b * STEPS, STEPS), STEPS)
            for c in range(parts):
                cols = slice(c * LANES, (c + 1) * LANES)
                value = None
                for j in range(CONV):
                    at = pl.ds(pl.multiple_of(b * size + TP * (CONV - 1 - j), TP), size)
                    value = plus(value, vec[j : j + 1, cols] * gconv[c, at, :])
                gs[c, rs, :] = value
                for s in range(TP):
                    at = pl.ds(b * size + s, STEPS, stride=TP)
                    r.gentry[s, here, cols] = gs[c, at, :].astype(bf16)
            return carry

        lax.fori_loop(0, blocks, inners, 0)
        lax.fori_loop(0, width // tile, lambda i, k: outer_in(r.ginner, 0, i, k), 0)
        over = remote(
            r.ginner.at[pl.ds((1 - x) * zh_size, zh_size)], r.near, r.over[0], r.over[1], side
        )
        over.start()
        loads[6].wait()
        scatter = Scatter(r.a, r.scatter_buf, r.scatter_sems)
        out_partial(scatter, r.a, r.gentry, lambda: r.b[...], turned=True)
        r.gmats[:, :RANK] = r.grate[...].astype(bf16)
        r.gmats[:, RANK:] = r.gselect[...].astype(bf16)
        for j in range(8):
            for c in range(parts):
                r.gvec[j : j + 1, c * LANES : (c + 1) * LANES] = jnp.sum(sums[j, c], axis=0, keepdims=True)
        r.gwout[...] = reduce.total()
        r.ggate[...] = gate_reduce.total().astype(bf16)
        gnormed = scatter.total()
        stream = r.h[...]
        scale = rms(stream)
        r.ggain[...] = jnp.sum(gnormed * stream * scale, axis=0, keepdims=True)
        scaled = gnormed * r.gain[layer : layer + 1, :]
        grad = r.grad[...] + scale * scaled - stream * (scale * scale * scale) * jnp.mean(
            stream * scaled, axis=-1, keepdims=True
        )
        r.prev[...] = grad
        if onward:
            r.gout[...] = grad.astype(bf16)
            spread = Gather(r.gout, r.gog, r.gather_sems)
            spread.start()
            spread.relay()
            spread.rest()
            spread.finish()
        for copy in passed:
            copy.wait()
        over.wait()

    return call(body, 9 if onward else 8, ins, outs, scratch)


def closing(zh_size, inner, near, mats, small, stats, gain, turns, share, width, select):
    groups = 2 * zh_size
    count = groups * TP
    far_n = max(1, zh_size - 1)
    dma = pltpu.SemaphoreType.DMA
    depth, half = inner.shape[3] // WAYS, inner.shape[4]
    gains = width // count
    every = (2, zh_size) + stats.shape
    v = pltpu.VMEM
    ins = dict(
        inner=(inner, VM), near=(near, VM), mats=(mats, VM), small=(small, VM), stats=(stats, VM), gain=(gain, VM),
        t0=(turns[0], VM), t1=(turns[1], VM), t2=(turns[2], VM),
    )
    outs = dict(
        gin=(struct(LAYERS, depth, 2 * count * share), VM), gselect=(struct(LAYERS, share, select), VM),
        grate=(struct(LAYERS, RANK, share), VM),
        ggain=(struct(LAYERS, gains), VM), gtaps=(struct(LAYERS, CONV, share), VM), gshift=(struct(LAYERS, share), VM),
        grate_shift=(struct(LAYERS, share), VM), gskip=(struct(LAYERS, share), VM), stats_all=(struct(*stats.shape), VM),
    )

    def chunk(shape, dtype):
        return [
            v(shape[1:], dtype), v((far_n,) + shape[2:], dtype), dma((far_n,)), dma((far_n,)), v(shape[1:], dtype), dma, dma
        ]

    piece = inner.shape[:2] + inner.shape[3:]
    scratch = dict(
        vectors=v(small.shape, f32), stats_v=v(every, f32), stats_t=v((TP - 1,) + stats.shape, f32),
        gain_t=v((TP - 1,) + gain.shape[1:], f32), win_t=v((2, WAYS, depth, half), bf16),
        total=v(small.shape[2:], f32),
        g_sems=[dma((TP - 1,))] * 2, s_sems=[dma((TP - 1,))] * 2,
    )
    scratch.update(
        boxes=v((4, TP, depth, half), bf16), turn_sems=[[dma((TP - 1,)), dma((TP - 1,))] for _ in range(4)],
        chunks=[chunk(piece, bf16), chunk(piece, bf16), chunk(mats.shape, bf16), chunk(small.shape, f32), chunk(every, f32)],
    )

    def body(r):
        x, core, zh, q = place()
        me = core * WAYS + q
        peers = tp_peers()
        side, far = dp_peers(zh_size)
        greet([p[0] for p in peers] + [side] + [f[0] for f in far])
        sent, full = [], []

        def join(a, b, peaks):
            a, b = a.astype(f32), b.astype(f32)
            if peaks:
                line = lax.broadcasted_iota(jnp.int32, a.shape, len(a.shape) - 2)
                return jnp.where(line < 4, a + b, jnp.maximum(a, b))
            return a + b

        class Chunk:
            def __init__(self, number, src, near=None):
                self.src, self.peaks = src, number == 4
                self.mine, self.buf, self.z_send, self.z_recv, spare, self.x_send, self.x_recv = r.chunks[number]
                self.near = spare if near is None else near

            def start(self):
                self.over = remote(self.src.at[1 - x], self.near, self.x_send, self.x_recv, side)
                self.over.start()
                sent.append(self.over)

            def middle(self, arrived=False):
                if not arrived:
                    self.over.wait_recv()
                mine, buf = self.mine, self.buf
                mine[...] = join(self.src[x], self.near[...], self.peaks).astype(mine.dtype)
                self.along = [
                    remote(mine.at[to_z], buf.at[k], self.z_send.at[k], self.z_recv.at[k], target)
                    for k, (target, to_z, _) in enumerate(far)
                ]
                for copy in self.along:
                    copy.start()
                    sent.append(copy)

            def total(self):
                value = join(self.src[x, zh], self.near[zh], self.peaks)
                for k, copy in enumerate(self.along):
                    copy.wait_recv()
                    value = join(value, self.buf[k], self.peaks)
                return value

        def turn(src, i):
            box, sems = r.boxes.at[i], r.turn_sems[i]
            for k, (target, rank, _) in enumerate(peers):
                copy = remote(src(rank), box.at[me], sems[0].at[k], sems[1].at[k], target)
                copy.start()
                full.append(copy)
            box[me] = src(me)[...]

        cs = [Chunk(c, r.inner.at[:, :, c], r.near.at[:, c]) for c in range(2)]
        cs[0].middle(arrived=True)
        cs[1].middle(arrived=True)
        gained, shown = [], []
        for i, (target, rank, _) in enumerate(peers):
            for src, buf, sems, copies in (
                (r.gain.at[rank], r.gain_t, r.g_sems, gained),
                (r.stats, r.stats_t, r.s_sems, shown),
            ):
                copy = remote(src, buf.at[i], sems[0].at[i], sems[1].at[i], target)
                copy.start()
                copies.append(copy)
                sent.append(copy)
        mats_c = Chunk(2, r.mats)
        mats_c.start()
        sources = (r.t0, r.t1, r.t2)
        for i in range(3):
            turn(lambda rank, i=i: sources[i].at[rank], i + 1)
        total = r.gain[me]
        seen = r.stats[...]
        for i in range(TP - 1):
            gained[i].wait_recv()
            total = total + r.gain_t[i]
            shown[i].wait_recv()
            seen = join(seen, r.stats_t[i], True)
        r.vectors[...] = r.small[...]
        for l in range(LAYERS):
            for g in range(groups):
                at = l * groups + g
                r.vectors[g // zh_size, g % zh_size, l * 16 + 8 : l * 16 + 9, :] = total[at : at + 1, :]
        r.stats_v[...] = jnp.broadcast_to(seen, every)
        rest = [mats_c, Chunk(3, r.vectors), Chunk(4, r.stats_v)]
        for c in rest[1:]:
            c.start()
        for c in rest:
            c.middle()
        for c in range(2):
            r.win_t[c] = cs[c].total().astype(bf16).reshape(WAYS, depth, half)
        turn(lambda rank: r.win_t.at[rank // WAYS, lax.rem(rank, WAYS)], 0)
        m = rest[0].total()
        for l in range(LAYERS):
            base = 3 * LANES * l
            r.grate[l] = m[:, base : base + RANK].T
            r.gselect[l] = m[:, base + RANK : base + RANK + select]
        r.total[...] = rest[1].total()
        for l in range(LAYERS):
            r.gtaps[l] = r.total[16 * l : 16 * l + CONV, :share]
            for out, j, size in (
                (r.gshift, CONV, share), (r.grate_shift, CONV + 1, share), (r.gskip, CONV + 2, share), (r.ggain, 8, gains)
            ):
                out[l : l + 1, :] = r.total[16 * l + j : 16 * l + j + 1, :size]
        r.stats_all[...] = rest[2].total()

        def lay(i):
            for rank in range(TP):
                for g in range(groups):
                    d = ((g // zh_size * 2 + rank // WAYS) * zh_size + g % zh_size) * WAYS + rank % WAYS
                    first = i % 2 * count * share + d * share
                    r.gin[i // 2, :, first : first + share] = r.boxes[i, rank, :, g * share : (g + 1) * share].astype(f32)

        early, late = full[: 3 * (TP - 1)], full[3 * (TP - 1) :]
        for copy in early:
            copy.wait_recv()
        for i in (1, 2, 3):
            lay(i)
        for copy in late:
            copy.wait_recv()
        lay(0)
        for copy in sent + full:
            copy.wait_send()

    return call(body, 5, ins, outs, scratch)


def on_device(
    hidden, cotangent, groups, group_weights, input_weight, select_weight, rate_weight,
    output_weight, norm_gain, conv_taps, conv_shift, rate_shift, skip_gain,
):
    fsdp = lax.axis_size("fsdp")
    zh_size = fsdp // WAYS
    count = 2 * 2 * fsdp
    group_count = 2 * zh_size
    share = conv_shift.shape[1]
    gains = norm_gain.shape[1]
    depth = input_weight.shape[1]
    half = group_count * share
    x, core, zh, q = place()

    labels = jnp.arange(group_weights.shape[0])
    own_weight = jnp.sum(jnp.where(groups[:, None] == labels[None, :], group_weights[None, :], 0.0))

    wins = input_weight
    if share % LANES:
        wins = wins.reshape(LAYERS, depth, 2, 2, 2, zh_size, WAYS, share)
        wins = wins.transpose(0, 4, 6, 1, 2, 3, 5, 7).reshape(LAYERS, TP, depth, 2 * half)
    mats = jnp.concatenate([rate_weight.swapaxes(1, 2), select_weight], axis=2)
    mats = jnp.pad(mats, ((0, 0), (0, 0), (0, 3 * LANES - mats.shape[2])))
    vectors = [conv_taps, conv_shift[:, None], rate_shift[:, None], skip_gain[:, None], skip_gain[:, None]]
    small = jnp.concatenate(vectors, axis=1).astype(f32).reshape(8 * LAYERS, share)
    small = jnp.pad(small, ((0, 0), (0, LANES - share)))
    misc = jnp.pad(norm_gain.astype(f32), ((0, 0), (0, LANES - gains)))
    misc = jnp.concatenate([misc, jnp.full((8 - LAYERS, LANES), own_weight)])

    flat = lambda a: a.reshape(half, -1)
    h0 = hidden[0]
    start = opening(zh_size, gains, share, wins, small, misc, mats, h0, cotangent[0])
    vec, gain, scale = start.vec, start.gains, start.scale
    win0, mat0 = start.win_all.reshape(count * depth, -1), flat(start.mats_all)
    one = forward_layer(
        zh_size, 0, start.xg, win0, mat0, output_weight, vec, scale,
        nxt=types.SimpleNamespace(h=h0, gain=gain, win=wins, mats=mats),
    )
    win1, mat1 = one.win1_all.reshape(count * depth, -1), flat(one.mats1_all)
    h1 = one.result
    two = forward_layer(zh_size, 1, one.xg1, win1, mat1, output_weight, vec, scale, gout=start.gout)

    down1 = backward_layer(
        zh_size, 1, two, two.gog, flat(two.wout_all), mat1, vec, one.xg1, win1, gain, h1, start.grad,
        part=two.part,
    )
    stream = h1 + jnp.sum(down1.parts_all.astype(f32), axis=0)
    blocks = (2, zh_size) + down1.ginner.shape[1:]
    pick = lambda a, i: lax.dynamic_index_in_dim(a, i, 0, keepdims=False)
    summed = pick(down1.ginner.reshape(blocks), x).astype(f32) + down1.near.astype(f32)
    down0 = backward_layer(
        zh_size, 0, one, down1.gog, flat(one.wout_all), mat0, vec, start.xg, win0, gain, h0, down1.prev,
        late=summed.astype(bf16),
    )
    late = pick(summed, zh)
    for k in range(zh_size - 1):
        late = late + down0.late[k].astype(f32)

    sums = [jnp.sum(o.stats[0]) for o in (one, two)]
    peaks = [jnp.max(o.stats[1]) for o in (one, two)]
    pad = [jnp.zeros((), f32)] * (4 - LAYERS)
    own_stats = jnp.broadcast_to(jnp.stack(sums + pad + peaks + pad)[:, None], (8, LANES))
    downs = (down0, down1)
    small = jnp.stack([down.gvec for down in downs]).reshape(LAYERS, 8, group_count, share)
    small = jnp.pad(small.transpose(2, 0, 1, 3), ((0, 0), (0, 0), (0, 8), (0, LANES - share)))
    small = small.reshape(2, zh_size, 16 * LAYERS, LANES)
    spread_gain = jnp.stack([down.ggain[0] for down in downs]).reshape(LAYERS, 2, 2, zh_size, WAYS, gains)
    spread_gain = spread_gain.transpose(2, 4, 0, 1, 3, 5).reshape(TP, LAYERS * group_count, gains)
    spread_gain = jnp.pad(spread_gain, ((0, 0), (0, -LAYERS * group_count % 8), (0, LANES - gains)))
    mats = jnp.concatenate([down.gmats for down in downs], axis=1).reshape(2, zh_size, share, -1)
    turns = [down0.ggate, late.astype(bf16), down1.ggate]
    end = closing(
        zh_size, down0.ginner.reshape(blocks), down0.near, mats, small, own_stats, spread_gain,
        [t.reshape(TP, depth, half) for t in turns], share, output_weight.shape[2], select_weight.shape[2],
    )
    stats = end.stats_all
    beta_mean = stats[:LAYERS, 0] / (count * hidden.shape[1] * INNER)
    beta_max = stats[4 : 4 + LAYERS, 0]
    gwout = jnp.stack([down.gwout for down in downs])
    return (
        stream[None], down0.prev[None], end.gin, end.gselect, end.grate, gwout, end.ggain, end.gtaps, end.gshift,
        end.grate_shift, end.gskip, beta_mean, beta_max,
    )


def solution(mesh):
    both = ("dp", "fsdp")
    placed = (
        P(both, None, None), P(both, None, None), P(both), P(),
        P(None, both, None), P(None, both, None), P(None, None, both), P(None, both, None),
        P(None, both), P(None, None, both), P(None, both), P(None, both), P(None, both),
    )
    return jax.shard_map(
        on_device,
        mesh=mesh,
        in_specs=placed,
        out_specs=(P(both, None, None), P(both, None, None)) + placed[4:] + (P(), P()),
        check_vma=False,
    )
```

```python
import types

import jax
import jax.numpy as jnp
import numpy as np
from jax import lax
from jax.sharding import PartitionSpec as P
import jax.experimental.pallas as pl
import jax.experimental.pallas.tpu as pltpu

INNER = 4096
STATE = 16
RANK = 128
CONV = 4
LAYERS = 2
WAYS = 4
TP = 8
STEPS = 16

eps = 1e-05
MESH = pl.DeviceIdType.MESH
f32 = jnp.float32
bf16 = jnp.bfloat16
VM = pl.BlockSpec(memory_space=pltpu.VMEM)
HB = pl.BlockSpec(memory_space=pl.ANY)
EARLY, LATE = object(), object()


def place():
    dp, fs = lax.axis_index("dp"), lax.axis_index("fsdp")
    return dp // 2, lax.rem(dp, 2), fs // WAYS, lax.rem(fs, WAYS)


def device(x, core, zh, q):
    return (x * 2 + core, zh * WAYS + q)


def remote(src, dst, send, recv, target):
    return pltpu.make_async_remote_copy(
        src_ref=src, dst_ref=dst, send_sem=send, recv_sem=recv, device_id=target, device_id_type=MESH
    )


def greet(targets):
    barrier = pltpu.get_barrier_semaphore()
    for target in targets:
        pl.semaphore_signal(barrier, inc=1, device_id=target, device_id_type=MESH)
    pl.semaphore_wait(barrier, len(targets))


def tp_peers():
    x, core, zh, q = place()
    peers = []
    for dc, da, db in ((1, 0, 0), (0, 1, 0), (0, 0, 1), (1, 1, 0), (1, 0, 1), (0, 1, 1), (1, 1, 1)):
        other_core, other_q = lax.rem(core + dc, 2), neighbour(q, da, db)
        rank = other_core * WAYS + other_q
        peers.append((device(x, other_core, zh, other_q), rank, rank))
    return peers


def neighbour(q, da, db):
    a, b = lax.rem(q, 2), q // 2
    return (1 - b if db else b) * 2 + (1 - a if da else a)


def total_rank():
    _, core, _, q = place()
    return core * WAYS + q


def dp_peers(zh_size):
    x, core, zh, q = place()
    side = device(1 - x, core, zh, q)
    far = []
    for dz in range(1, zh_size):
        to_z, from_z = lax.rem(zh + dz, zh_size), lax.rem(zh + zh_size - dz, zh_size)
        far.append((device(x, core, to_z, q), to_z, from_z))
    return side, far


def lanes_of(shape):
    return lax.broadcasted_iota(jnp.int32, shape, 1)


def encode(v):
    tail = v[:, RANK:]
    lane = lanes_of(tail.shape)
    high = tail.astype(bf16).astype(f32)
    low = pltpu.roll(tail - high, 32, 1)
    both = jnp.where(lane < 32, high, jnp.where(lane < 64, low, 0.0))
    return jnp.concatenate([v[:, :RANK].astype(bf16), both.astype(bf16)], axis=1)


def decode(v):
    tail = v[:, RANK:].astype(f32)
    lane = lanes_of(tail.shape)
    tail = jnp.where(lane < 32, tail + pltpu.roll(tail, 96, 1), 0.0)
    return jnp.concatenate([v[:, :RANK].astype(f32), tail], axis=1)


def halves(rows):
    return pl.ds(0, rows // 2), pl.ds(rows // 2, rows // 2)


class Gather:
    sems = staticmethod(lambda dma: [dma((6,)), dma((6,)), dma((4,)), dma((4,)), dma])

    def __init__(self, src, out, sems):
        self.src, self.out = src, out
        self.f_send, self.f_recv, self.s_send, self.s_recv, self.own_sem = sems
        x, core, zh, q = place()
        self.core, self.me = core, core * WAYS + q
        self.sibling = device(x, 1 - core, zh, q)
        self.chips = [neighbour(q, 0, 1), neighbour(q, 1, 0), neighbour(q, 1, 1)]
        self.b, self.a = [device(x, core, zh, c) for c in self.chips[:2]]
        self.top, self.low = halves(src.shape[0])

    def send(self, i, src, slot, rows, target):
        copy = remote(src, self.out.at[slot, rows], self.f_send.at[i], self.f_recv.at[i], target)
        copy.start()
        return copy

    def to_sibling(self, i, src, slot):
        copy = remote(src, self.out.at[slot], self.s_send.at[i], self.s_recv.at[i], self.sibling)
        copy.start()
        self.near.append(copy)

    def start(self):
        self.near = []
        self.first = [
            self.send(i, self.src.at[rows], self.me, rows, target)
            for i, (rows, target) in enumerate(
                ((self.top, self.b), (self.low, self.a), (self.low, self.b), (self.top, self.a))
            )
        ]
        self.to_sibling(3, self.src, self.me)
        self.own = pltpu.make_async_copy(self.src, self.out.at[self.me], self.own_sem)
        self.own.start()

    def relay(self):
        for i, rows, target in ((0, self.top, self.a), (1, self.low, self.b)):
            self.first[i].wait_recv()
            slot = self.core * WAYS + self.chips[i]
            self.first.append(self.send(4 + i, self.out.at[slot, rows], slot, rows, target))

    def rest(self):
        for i, ends in enumerate(((2,), (3,), (4, 5))):
            for k in ends:
                self.first[k].wait_recv()
            slot = self.core * WAYS + self.chips[i]
            self.to_sibling(i, self.out.at[slot], slot)

    def finish(self):
        for copy in self.first:
            copy.wait_send()
        for copy in self.near:
            copy.wait()
        self.own.wait()


class Scatter:
    sems = staticmethod(lambda dma: [dma((4,)), dma((4,)), dma((6,)), dma((6,))])

    @staticmethod
    def buffers(block):
        return [pltpu.VMEM((4,) + block, bf16), pltpu.VMEM((3,) + block, bf16), pltpu.VMEM((3,) + block, bf16)]

    def __init__(self, partial, buffers, sems):
        self.partial = partial
        self.near_buf, self.out, self.into = buffers
        self.s_send, self.s_recv, self.f_send, self.f_recv = sems
        x, core, zh, q = place()
        self.core = core
        self.sibling = device(x, 1 - core, zh, q)
        self.turns = [neighbour(q, 1, 1), neighbour(q, 1, 0), neighbour(q, 0, 1), q]
        self.a, self.b = [device(x, core, zh, t) for t in self.turns[1:3]]
        self.top, self.low = halves(partial.shape[1])
        self.near, self.first = [None] * 4, {}

    def to_sibling(self, i):
        slot = (1 - self.core) * WAYS + self.turns[i]
        self.near[i] = remote(
            self.partial.at[slot], self.near_buf.at[i], self.s_send.at[i], self.s_recv.at[i], self.sibling
        )
        self.near[i].start()

    def joined(self, i, rows=slice(None)):
        own = self.partial[self.core * WAYS + self.turns[i], rows]
        return own.astype(f32) + self.near_buf[i, rows].astype(f32)

    def send(self, k, i, rows, target):
        self.first[k] = remote(
            self.out.at[i, rows], self.into.at[i, rows], self.f_send.at[k], self.f_recv.at[k], target
        )
        self.first[k].start()

    def across(self, i):
        self.near[i].wait_recv()
        if i == 0:
            self.out[0] = self.joined(0).astype(bf16)
            self.send(0, 0, self.top, self.a)
            self.send(1, 0, self.low, self.b)
        else:
            rows, target = ((self.top, self.a), (self.low, self.b))[i - 1]
            self.out[i, rows] = self.joined(i, rows).astype(bf16)
            self.send(1 + i, i, rows, target)

    def sums(self):
        for k, i, rows, target in ((1, 1, self.low, self.a), (0, 2, self.top, self.b)):
            self.first[k].wait_recv()
            self.out[i, rows] = (self.joined(i, rows) + self.into[0, rows].astype(f32)).astype(bf16)
            self.send(3 + i, i, rows, target)

    def total(self):
        self.near[3].wait_recv()
        value = self.joined(3)
        for k in (2, 3, 4, 5):
            self.first[k].wait_recv()
        value = value + self.into[1].astype(f32) + self.into[2].astype(f32)
        for copy in self.near + list(self.first.values()):
            copy.wait_send()
        return value


class Spread:
    @staticmethod
    def sems(dma, zh_size):
        far = max(1, zh_size - 1)
        return [dma((far,)), dma((far,)), dma((zh_size,)), dma((zh_size,)), dma]

    def __init__(self, zh_size, src, view, sems, keep=True):
        self.src, self.view, self.keep = src, view, keep
        self.z_send, self.z_recv, self.x_send, self.x_recv, self.own_sem = sems
        self.x, _, self.zh, _ = place()
        self.side, self.far = dp_peers(zh_size)

    def start(self):
        dst = self.view(self.x, self.zh)
        self.along = [
            remote(self.src, dst, self.z_send.at[k], self.z_recv.at[k], target)
            for k, (target, _, _) in enumerate(self.far)
        ]
        self.over = [remote(self.src, dst, self.x_send.at[0], self.x_recv.at[0], self.side)]
        for copy in self.along + self.over:
            copy.start()
        if self.keep:
            self.own = pltpu.make_async_copy(self.src, dst, self.own_sem)
            self.own.start()

    def onward(self):
        for k, (_, _, source) in enumerate(self.far):
            self.along[k].wait_recv()
            slot = self.view(self.x, source)
            copy = remote(slot, slot, self.x_send.at[k + 1], self.x_recv.at[k + 1], self.side)
            copy.start()
            self.over.append(copy)

    def finish(self):
        for copy in self.along:
            copy.wait_send()
        for copy in self.over:
            copy.wait()
        if self.keep:
            self.own.wait()


class Sum:
    sems = staticmethod(lambda dma: [dma((TP - 1,))] * 4)

    def __init__(self, payload, parts, out, sems):
        self.payload, self.parts, self.out = payload, parts, out
        self.a_send, self.a_recv, self.b_send, self.b_recv = sems
        x, core, zh, q = place()
        self.me = core * WAYS + q
        self.peers = tp_peers()

    def start(self):
        self.one = [
            remote(self.payload.at[rank], self.parts.at[i], self.a_send.at[i], self.a_recv.at[i], target)
            for i, (target, rank, _) in enumerate(self.peers)
        ]
        for copy in self.one:
            copy.start()

    def middle(self, own):
        total = own
        for i in range(TP - 1):
            self.one[i].wait_recv()
            total = total + decode(self.parts[i])
        self.out[self.me] = encode(total)
        self.two = [
            remote(self.out.at[self.me], self.out.at[self.me], self.b_send.at[i], self.b_recv.at[i], target)
            for i, (target, _, _) in enumerate(self.peers)
        ]
        for copy in self.two:
            copy.start()

    def finish(self):
        for copy in self.one:
            copy.wait_send()
        for copy in self.two:
            copy.wait()


def call(body, collective, ins, outs, scratch):
    def flatten(kind):
        return [leaf for each in kind for leaf in flatten(each)] if isinstance(kind, list) else [kind]

    def rebuild(kind, refs):
        return [rebuild(each, refs) for each in kind] if isinstance(kind, list) else refs.pop(0)

    early = [key for key, (_, spec) in ins.items() if spec is EARLY]
    late = [key for key, (_, spec) in outs.items() if spec is LATE]
    space = lambda spec: HB if spec is EARLY or spec is LATE else spec
    held = [pltpu.VMEM(ins[key][0].shape, ins[key][0].dtype) for key in early]
    held += [pltpu.VMEM(outs[key][0].shape, outs[key][0].dtype) for key in late]
    extra = [held, [pltpu.SemaphoreType.DMA] * len(held)]

    def kernel(*refs):
        refs = list(refs)
        named = {key: refs.pop(0) for key in list(ins) + list(outs)}
        named.update({key: rebuild(kind, refs) for key, kind in scratch.items()})
        buffers, sems = rebuild(extra, refs)
        loads, stores = {}, {}
        for key, buffer, sem in zip(early + late, buffers, sems):
            if key in early:
                loads[key] = pltpu.make_async_copy(named[key], buffer, sem)
            else:
                stores[key] = pltpu.make_async_copy(buffer, named[key], sem)
            named[key] = buffer
        r = types.SimpleNamespace(**named)
        r.load = lambda: [copy.start() for copy in loads.values()]
        r.need = types.SimpleNamespace(**{key: copy.wait for key, copy in loads.items()})
        r.put = types.SimpleNamespace(**{key: copy.start for key, copy in stores.items()})
        r.done = lambda: [copy.wait() for copy in stores.values()]
        body(r)

    values = pl.pallas_call(
        kernel,
        out_shape=[shape for shape, _ in outs.values()],
        in_specs=[space(spec) for _, spec in ins.values()],
        out_specs=[space(spec) for _, spec in outs.values()],
        scratch_shapes=flatten(list(scratch.values()) + extra),
        compiler_params=pltpu.CompilerParams(
            collective_id=collective, has_side_effects=True, vmem_limit_bytes=63 * 2**20
        ),
    )(*[array for array, _ in ins.values()])
    return types.SimpleNamespace(**dict(zip(outs, values)))


def spread_keys(kq, lane):
    a = kq.astype(bf16).astype(f32)
    rest = kq - a
    b = rest.astype(bf16).astype(f32)
    c = rest - b
    return jnp.where(lane < 32, a, jnp.where(lane < 64, b, c)).astype(bf16)


def spreader():
    one = np.repeat(np.eye(32, dtype=np.float32), 128, axis=1)
    return jnp.asarray(np.concatenate([one, one, one, np.zeros_like(one)], axis=0), bf16)


def folder():
    return jnp.asarray(np.pad(np.repeat(np.eye(32, dtype=np.float32), 128, axis=0), ((0, 0), (0, 96))), bf16)


def dot(a, b, contract, out=f32):
    return lax.dot_general(a, b, (contract, ((), ())), preferred_element_type=out)


def rms(stream):
    return lax.rsqrt(jnp.mean(jnp.square(stream), axis=-1, keepdims=True) + eps)


LANES = 128


def struct(*shape, dtype=f32):
    return jax.ShapeDtypeStruct(shape, dtype)


def side_by_side(pieces, lanes):
    each = LANES // lanes
    out = []
    for i in range(0, len(pieces), each):
        tile = pieces[i]
        for j in range(1, each):
            tile = tile + pltpu.roll(pieces[i + j], j * lanes, 1)
        out.append(tile)
    return jnp.concatenate(out, axis=1)


def turn_pieces(zh_size, win, layer, out, rank):
    if len(win.shape) == 4:
        return [(win.at[layer, rank], out)]
    groups = 2 * zh_size
    share = win.shape[2] // (2 * groups * TP)
    pieces = []
    for part in range(2):
        for g in range(groups):
            d = ((g // zh_size * 2 + rank // WAYS) * zh_size + g % zh_size) * WAYS + lax.rem(rank, WAYS)
            first = pl.multiple_of((part * groups * TP + d) * share, share)
            pieces.append(
                (win.at[layer, :, pl.ds(first, share)], out.at[:, pl.ds((part * groups + g) * share, share)])
            )
    return pieces


class Turn:
    def __init__(self, zh_size, win, layer, out, slot, sems):
        self.out, self.slot, self.sems = out, slot, sems
        self.me = total_rank()
        self.peers = tp_peers()
        self.pieces = lambda rank: turn_pieces(zh_size, win, layer, out.at[slot(self.me)], rank)

    def start(self):
        for i, (target, rank, _) in enumerate(self.peers):
            for src, dst in self.pieces(rank):
                remote(src, dst, self.sems[0].at[i], self.sems[1].at[i], target).start()

    def whole(self, i, rank):
        block = self.out.at[self.slot(rank)]
        return remote(block, block, self.sems[0].at[i], self.sems[1].at[i], self.peers[i][0])

    def arrived(self, i):
        self.whole(i, self.peers[i][2]).wait_recv()

    def sent(self):
        for i in range(TP - 1):
            self.whole(i, self.me).wait_send()


def opening(zh_size, gains, share, win, small, misc, mats, h, cot):
    groups = 2 * zh_size
    count = groups * TP
    tokens, width = h.shape
    half = groups * share
    depth = win.shape[-2]
    dma = pltpu.SemaphoreType.DMA
    ins = dict(
        win=(win, HB), small=(small, VM), misc=(misc, VM), mats=(mats, HB), h=(h, VM), cot=(cot, VM)
    )
    outs = dict(
        win_all=(struct(count, depth, 2 * half, dtype=bf16), HB),
        mats_all=(struct(groups, *mats.shape[1:], dtype=bf16), HB), vec=(struct(8 * LAYERS, half), VM),
        gains=(struct(8, width), VM), scale=(struct(TP, LANES), VM), grad=(struct(tokens, width), VM),
        gout=(struct(tokens, width, dtype=bf16), VM), xg=(struct(TP, tokens, width, dtype=bf16), HB),
    )
    spread = lambda: Spread.sems(dma, zh_size)
    scratch = dict(
        misc_all=pltpu.VMEM((count,) + misc.shape, f32), small_all=pltpu.VMEM((groups,) + small.shape, f32),
        normed=pltpu.VMEM((tokens, width), bf16), gather_sems=Gather.sems(dma),
        m_sems=[dma((TP - 1,))] * 2, w_sems=[dma((TP - 1,))] * 2, own_sem=dma,
        own=pltpu.VMEM((depth, 2 * half), bf16), s0=spread(), s1=spread(),
        sm=[spread() for _ in range(TP)], sw=[spread() for _ in range(TP)],
    )

    def body(r):
        x, core, zh, q = place()
        me = core * WAYS + q
        peers = tp_peers()
        side, far = dp_peers(zh_size)
        greet([p[0] for p in peers] + [side] + [f[0] for f in far])

        def row(xx, zz, rank):
            return ((xx * 2 + rank // WAYS) * zh_size + zz) * WAYS + lax.rem(rank, WAYS)

        def views(out, rank):
            return lambda xx, zz: out.at[row(xx, zz, rank)]

        here = row(x, zh, me)
        miscs = []
        for i, (target, rank, _) in enumerate(peers):
            miscs.append(remote(r.misc, r.misc_all.at[here], r.m_sems[0].at[i], r.m_sems[1].at[i], target))
            miscs[-1].start()
        misc_moves = [Spread(zh_size, r.misc, views(r.misc_all, me), r.sm[0])]
        misc_moves[0].start()
        smalls = Spread(zh_size, r.small, lambda xx, zz: r.small_all.at[xx * zh_size + zz], r.s0)
        smalls.start()
        wins = Turn(zh_size, r.win, 0, r.win_all, lambda rank: row(x, zh, rank), r.w_sems)
        wins.start()
        own_pieces = [
            pltpu.make_async_copy(src, dst, r.own_sem)
            for src, dst in turn_pieces(zh_size, r.win, 0, r.own, me)
        ]
        for copy in own_pieces:
            copy.start()
        pltpu.make_async_copy(r.own, r.own, r.own_sem).wait()
        win_moves = [Spread(zh_size, r.own, views(r.win_all, me), r.sw[0])]
        for i, (_, _, source) in enumerate(peers):
            view = views(r.win_all, source)
            win_moves.append(Spread(zh_size, view(x, zh), view, r.sw[i + 1], keep=False))
        mats_move = Spread(zh_size, r.mats.at[0], lambda xx, zz: r.mats_all.at[xx * zh_size + zz], r.s1)

        def step(i):
            if i >= 1:
                wins.arrived(i - 1)
            if i >= 2:
                win_moves[i - 2].onward()
            win_moves[i].start()

        step(0)
        for i, (_, _, source) in enumerate(peers):
            miscs[i].wait_recv()
            view = views(r.misc_all, source)
            misc_moves.append(Spread(zh_size, view(x, zh), view, r.sm[i + 1], keep=False))
            misc_moves[-1].start()
        step(1)
        for move in misc_moves:
            move.onward()
        smalls.onward()
        for move in misc_moves:
            move.finish()
        for l in range(LAYERS):
            r.gains[l : l + 1, :] = side_by_side(
                [r.misc_all[d, l : l + 1, :] for d in range(count)], gains
            )
        r.gains[LAYERS:, :] = jnp.zeros((8 - LAYERS, width), f32)
        stream = r.h[...]
        r.normed[...] = (stream * rms(stream) * r.gains[0:1, :]).astype(bf16)
        rows = Gather(r.normed, r.xg, r.gather_sems)
        rows.start()
        step(2)
        mats_move.start()
        total = r.misc_all[0, LAYERS : LAYERS + 1, :]
        for d in range(1, count):
            total = total + r.misc_all[d, LAYERS : LAYERS + 1, :]
        inverse = count / total
        for rank in range(TP):
            r.scale[rank : rank + 1, :] = r.misc_all[row(x, zh, rank), LAYERS : LAYERS + 1, :] * inverse
        own = (r.misc[LAYERS : LAYERS + 1, :] * inverse)[:, :1]
        grad = r.cot[...] * own
        r.grad[...] = grad
        r.gout[...] = grad.astype(bf16)
        step(3)
        smalls.finish()
        for l in range(LAYERS):
            r.vec[8 * l : 8 * (l + 1), :] = side_by_side(
                [r.small_all[g, 8 * l : 8 * (l + 1), :] for g in range(groups)], share
            )
        step(4)
        mats_move.onward()
        rows.relay()
        step(5)
        step(6)
        rows.rest()
        step(7)
        win_moves[6].onward()
        win_moves[7].onward()
        wins.sent()
        for copy in miscs:
            copy.wait_send()
        for move in win_moves + [mats_move]:
            move.finish()
        rows.finish()

    return call(body, 1, ins, outs, scratch)


def at_block(b, size):
    return pl.ds(pl.multiple_of(b * size, size), size)


def conv_of(entry, vec, row, size, c):
    cols = slice(c * LANES, (c + 1) * LANES)
    conv = vec[CONV : CONV + 1, cols]
    for j in range(CONV):
        conv = conv + vec[j : j + 1, cols] * entry[c, pl.ds(pl.multiple_of(row + TP * j, TP), size), :]
    return conv


def wide_of(ref, rows, parts):
    return jnp.concatenate([ref[c, rows, :] for c in range(parts)], axis=1)


def row_sum(value):
    return jnp.sum(value.reshape(-1, TP, value.shape[1]), axis=0)


def square_sum(kq):
    lane = lanes_of(kq.shape)
    return jnp.sum(jnp.where(lane < STATE, kq * kq, 0.0), axis=1, keepdims=True)


def forward_layer(zh_size, layer, xg, win, mats, wout, vec, scale, gout=None, nxt=None):
    tokens, width = xg.shape[1], xg.shape[2]
    half = win.shape[1] // 2
    parts = half // LANES
    rows = tokens * TP
    size = STEPS * TP
    blocks = rows // size
    halo = (CONV - 1) * TP
    dma = pltpu.SemaphoreType.DMA
    last = nxt is None
    groups = 2 * zh_size
    ins = dict(
        xg=(xg, EARLY), win=(win, EARLY), mats=(mats, EARLY), wout=(wout, HB), vec=(vec, VM),
        scale=(scale, VM), e=(spreader(), EARLY),
    )
    outs = dict(
        entry=(struct(2 * parts, halo + rows, LANES), LATE), beta=(struct(parts, rows, LANES), LATE),
        kq=(struct(rows, LANES), LATE), proj=(struct(TP, size, 2 * LANES, dtype=bf16), LATE),
        y=(struct(parts, rows, LANES), LATE), keep=(struct(blocks, STATE, parts, TP, LANES), LATE),
        mixed=(struct(TP, tokens, half, dtype=bf16), LATE), stats=(struct(2, TP, LANES), VM),
    )
    scratch = dict(
        act=pltpu.VMEM((parts, rows, LANES), f32), step=pltpu.VMEM((parts, rows, LANES), f32),
        payload=pltpu.VMEM((TP, size, 2 * LANES), bf16), parts=pltpu.VMEM((TP - 1, size, 2 * LANES), bf16),
        own=pltpu.VMEM((size, 2 * LANES), f32),
        state=pltpu.VMEM((STATE, parts, TP, LANES), f32), wide=pltpu.VMEM((size, 32 * LANES), f32),
        sum_sems=Sum.sems(dma),
    )
    outs.update(wout_all=(struct(groups, *wout.shape[1:], dtype=bf16), LATE))
    scratch.update(d0=Spread.sems(dma, zh_size))
    if last:
        ins.update(gout=(gout, VM))
        outs.update(
            gog=(struct(TP, tokens, width, dtype=bf16), HB), part=(struct(TP, tokens, width, dtype=bf16), LATE)
        )
        scratch.update(gather_sems=Gather.sems(dma))
    if not last:
        win1 = nxt.win
        depth = win1.shape[-2]
        ins.update(h=(nxt.h, EARLY), gain=(nxt.gain, VM), win1=(win1, HB), mats1=(nxt.mats, HB))
        outs.update(
            result=(struct(tokens, width), VM),
            win1_all=(struct(2, 2, zh_size, WAYS, depth, 2 * half, dtype=bf16), HB),
            mats1_all=(struct(groups, *nxt.mats.shape[1:], dtype=bf16), HB),
            xg1=(struct(TP, tokens, width, dtype=bf16), HB),
        )
        scratch.update(
            normed=pltpu.VMEM((tokens, width), bf16), gather_sems=Gather.sems(dma),
            part=pltpu.VMEM((TP, tokens, width), bf16), scatter_buf=Scatter.buffers((tokens, width)),
            scatter_sems=Scatter.sems(dma),
            turned=pltpu.VMEM((TP, depth, 2 * half), bf16), l_sems=[dma((TP - 1,)), dma((TP - 1,))], l_own=dma,
            d1=Spread.sems(dma, zh_size), d2=Spread.sems(dma, zh_size), d3=Spread.sems(dma, zh_size),
        )

    def body(r):
        r.load()
        side, far = dp_peers(zh_size)
        greet([p[0] for p in tp_peers()] + [side] + [f[0] for f in far])
        entry, act, step, beta, kq, y = r.entry, r.act, r.step, r.beta, r.kq, r.y
        vec = r.vec.at[8 * layer : 8 * (layer + 1)]
        index = lambda ref: lambda xx, zz: ref.at[xx * zh_size + zz]
        early = Spread(zh_size, r.wout.at[layer], index(r.wout_all), r.d0)
        early.start()
        if last:
            gouts = Gather(r.gout, r.gog, r.gather_sems)
        else:
            turned = Turn(zh_size, r.win1, layer + 1, r.turned, lambda rank: rank, r.l_sems)
            turned.start()
            for src, dst in turned.pieces(turned.me):
                pltpu.make_async_copy(src, dst, r.l_own).start()
            moves = [Spread(zh_size, r.mats1.at[layer + 1], index(r.mats1_all), r.d3)]
            for k in range(2):
                view = lambda xx, zz, k=k: r.win1_all.at[xx, k, zz]
                src = r.turned.at[k * WAYS : (k + 1) * WAYS]
                moves.append(Spread(zh_size, src, view, (r.d1 if k == 0 else r.d2)))

        r.need.xg()
        r.need.win()
        entry[:, :halo, :] = jnp.zeros((2 * parts, halo, LANES), f32)
        tile = 2 * LANES
        for p in range(TP // 2):

            def columns(n, carry, p=p):
                cols = at_block(n, tile)
                out = jnp.dot(
                    r.xg[2 * p : 2 * p + 2].reshape(2 * tokens, width), r.win[:, cols],
                    preferred_element_type=f32,
                )
                for j in range(2):
                    for c in range(2):
                        entry[2 * n + c, pl.ds(halo + 2 * p + j, tokens, stride=TP), :] = out[
                            j * tokens : (j + 1) * tokens, c * LANES : (c + 1) * LANES
                        ]
                return carry

            lax.fori_loop(0, 2 * half // tile, columns, 0)
        r.put.entry()
        r.need.mats()
        total = Sum(r.payload, r.parts, r.proj, r.sum_sems)

        def project(b, carry):
            rs = at_block(b, size)
            for c in range(parts):
                conv = conv_of(entry, vec, b * size, size, c)
                act[c, rs, :] = (conv * jax.nn.sigmoid(conv)).astype(bf16).astype(f32)
            out = jnp.dot(
                wide_of(act, rs, parts).astype(bf16), r.mats[:, RANK:], preferred_element_type=f32
            )
            r.payload[b] = encode(out)

            @pl.when(b == total.me)
            def _():
                r.own[...] = out

            return carry

        lax.fori_loop(0, blocks, project, 0)
        total.start()
        if not last:
            for i in range(TP - 1):
                turned.arrived(i)
            mine = r.turned.at[turned.me]
            pltpu.make_async_copy(mine, mine, r.l_own).wait()
            moves[0].start()
            moves[1].start()
        total.middle(r.own[...])
        total.finish()
        r.put.proj()
        if last:
            gouts.start()
        else:
            turned.sent()
            moves[2].start()

        r.stats[...] = jnp.zeros((2, TP, LANES), f32)

        def rates(b, carry):
            rs = at_block(b, size)
            tail = decode(r.proj[b])[:, RANK:]
            keys = tail + pltpu.roll(tail, 32, 1) + pltpu.roll(tail, 64, 1)
            kq[rs, :] = keys
            norm = square_sum(keys)
            pre = dot(r.proj[b, :, :RANK], r.mats[:, :RANK], ((1,), (1,)))
            for c in range(parts):
                cols = slice(c * LANES, (c + 1) * LANES)
                rate = jax.nn.sigmoid(pre[:, cols] + vec[CONV + 1 : CONV + 2, cols])
                beta[c, rs, :] = rate
                step[c, rs, :] = rate / (1.0 + rate * norm)
                r.stats[0] += row_sum(rate)
                r.stats[1] = jnp.maximum(
                    r.stats[1], jnp.max(rate.reshape(-1, TP, LANES), axis=0)
                )
            return carry

        lax.fori_loop(0, blocks, rates, 0)
        r.put.beta()
        r.put.kq()
        r.need.e()
        r.stats[0] = r.stats[0] * r.scale[...]
        r.stats[1] = r.stats[1] * r.scale[...]

        lane = lanes_of((size, LANES))
        state, wide = r.state, r.wide
        state[...] = jnp.zeros_like(state)

        def block(b, carry):
            r.keep[b] = state[...]
            wide[...] = jnp.dot(spread_keys(kq[at_block(b, size), :], lane), r.e[...], preferred_element_type=f32)

            def one(j, carry):
                t = at_block(b * STEPS + j, TP)
                w = at_block(j, TP)
                acts = [act[c, t, :] for c in range(parts)]
                steps = [step[c, t, :] for c in range(parts)]
                sums = [None] * parts
                for n in range(STATE):
                    key = wide[w, n * LANES : (n + 1) * LANES]
                    query = wide[w, (STATE + n) * LANES : (STATE + n + 1) * LANES]
                    for c in range(parts):
                        s = state[n, c]
                        s = s + (steps[c] * key) * (acts[c] - key * s)
                        state[n, c] = s
                        sums[c] = s * query if sums[c] is None else sums[c] + s * query
                for c in range(parts):
                    y[c, t, :] = sums[c]
                return carry

            lax.fori_loop(0, STEPS, one, 0)
            rs = at_block(b, size)
            here = pl.ds(pl.multiple_of(b * STEPS, STEPS), STEPS)
            for c in range(parts):
                cols = slice(c * LANES, (c + 1) * LANES)
                gate = entry[parts + c, pl.ds(pl.multiple_of(b * size + halo, TP), size), :]
                skip = vec[CONV + 2 : CONV + 3, cols]
                step[c, rs, :] = (y[c, rs, :] + skip * act[c, rs, :]) * (gate * jax.nn.sigmoid(gate))
                for s in range(TP):
                    r.mixed[s, here, cols] = step[c, pl.ds(b * size + s, STEPS, stride=TP), :].astype(bf16)
            return carry

        early.onward()
        lax.fori_loop(0, blocks // 2, block, 0)
        if last:
            gouts.relay()
        else:
            moves[0].onward()
        lax.fori_loop(blocks // 2, blocks, block, 0)
        early.finish()
        for start in (r.put.y, r.put.keep, r.put.mixed, r.put.wout_all):
            start()
        weight = lambda: r.wout_all[...].reshape(half, width)
        if last:

            def plain(s, carry):
                two = r.mixed[pl.ds(2 * s, 2)].reshape(2 * tokens, half)
                out = dot(two, weight(), ((1,), (0,))).astype(bf16)
                r.part[pl.ds(2 * s, 2)] = out.reshape(2, tokens, width)
                return carry

            lax.fori_loop(0, TP // 4, plain, 0)
            gouts.rest()
            lax.fori_loop(TP // 4, TP // 2, plain, 0)
            r.put.part()
            gouts.finish()
            r.done()
            return
        scatter = Scatter(r.part, r.scatter_buf, r.scatter_sems)
        out_partial(scatter, r.part, r.mixed, weight)
        moves[1].onward()
        r.need.h()
        stream = r.h[...] + scatter.total()
        r.result[...] = stream
        r.normed[...] = (stream * rms(stream) * r.gain[layer + 1 : layer + 2, :]).astype(bf16)
        spread = Gather(r.normed, r.xg1, r.gather_sems)
        spread.start()
        spread.relay()
        moves[2].onward()
        spread.rest()
        spread.finish()
        for move in moves:
            move.finish()
        r.done()

    return call(body, 7 if last else 6, ins, outs, scratch)


def out_partial(scatter, part, left, right, turned=False):
    contract = ((1,), (1,)) if turned else ((1,), (0,))
    for i in range(4):
        slots = [core * WAYS + scatter.turns[i] for core in (1 - scatter.core, scatter.core)]
        rows = left.shape[1]
        both = dot(jnp.concatenate([left[slot] for slot in slots], axis=0), right(), contract).astype(bf16)
        part[slots[0]] = both[:rows]
        part[slots[1]] = both[rows:]
        scatter.to_sibling(i)
        if i >= 1:
            scatter.across(i - 1)
    scatter.sums()


class Reduce:
    @staticmethod
    def sems(dma, zh_size):
        far = max(1, zh_size - 1)
        return [dma, dma, dma((far,)), dma((far,))]

    @staticmethod
    def buffers(zh_size, block):
        return [
            pltpu.VMEM((zh_size,) + block, bf16), pltpu.VMEM((zh_size,) + block, bf16),
            pltpu.VMEM((max(1, zh_size - 1),) + block, bf16),
        ]

    def __init__(self, zh_size, src, buffers, sems):
        self.zh_size, self.src = zh_size, src
        self.near, self.mine, self.buf = buffers
        self.x_send, self.x_recv, self.z_send, self.z_recv = sems
        self.x, _, self.zh, _ = place()
        self.side, self.far = dp_peers(zh_size)

    def start(self):
        half = self.src.at[pl.ds((1 - self.x) * self.zh_size, self.zh_size)]
        self.over = remote(half, self.near, self.x_send, self.x_recv, self.side)
        self.over.start()

    def middle(self):
        self.over.wait_recv()
        for k in range(self.zh_size):
            self.mine[k] = (
                self.src[self.x * self.zh_size + k].astype(f32) + self.near[k].astype(f32)
            ).astype(bf16)
        self.along = [
            remote(self.mine.at[to_z], self.buf.at[k], self.z_send.at[k], self.z_recv.at[k], target)
            for k, (target, to_z, _) in enumerate(self.far)
        ]
        for copy in self.along:
            copy.start()

    def total(self):
        value = self.src[self.x * self.zh_size + self.zh].astype(f32) + self.near[self.zh].astype(f32)
        for k in range(self.zh_size - 1):
            self.along[k].wait_recv()
            value = value + self.buf[k].astype(f32)
        self.over.wait_send()
        for copy in self.along:
            copy.wait_send()
        return value


def backward_layer(zh_size, layer, kept, gog, wout, mats, vec, xg, win, gain, h, grad, late=None, part=None):
    tokens, width = xg.shape[1], xg.shape[2]
    half = win.shape[1] // 2
    parts = half // LANES
    rows = tokens * TP
    size = STEPS * TP
    blocks = rows // size
    halo = (CONV - 1) * TP
    groups = 2 * zh_size
    share = half // groups
    deep = width // (2 * groups)
    far = max(1, zh_size - 1)
    dma = pltpu.SemaphoreType.DMA
    onward = part is not None
    ins = dict(entry=(kept.entry, EARLY), kq=(kept.kq, EARLY), beta=(kept.beta, EARLY), proj=(kept.proj, EARLY))
    ins.update(
        mats=(mats, EARLY), wout=(wout, HB), vec=(vec, VM), gain=(gain, VM), h=(h, EARLY), grad=(grad, EARLY),
        mixed=(kept.mixed, HB), e=(spreader(), EARLY), fold=(folder(), EARLY), keep=(kept.keep, HB), gouts=(gog, HB), y=(kept.y, HB), xg=(xg, HB), win=(win, HB),
    )
    outs = dict(
        prev=(struct(tokens, width), VM), ginner=(struct(groups, 2, deep, half, dtype=bf16), LATE),
        near=(struct(zh_size, 2, deep, half, dtype=bf16), HB), ggate=(struct(2, deep, half, dtype=bf16), VM), gwout=(struct(share, width), VM),
        gmats=(struct(half, 3 * LANES, dtype=bf16), VM), gvec=(struct(8, half), VM),
        ggain=(struct(1, width), VM),
    )
    block_f32 = pltpu.VMEM((parts, rows, LANES), f32)
    scratch = dict(
        a=pltpu.VMEM((TP, tokens, width), bf16), b=pltpu.VMEM(win.shape, bf16),
        gs=block_f32, act=block_f32, gact=block_f32,
        step=pltpu.VMEM((parts, rows + halo, LANES), f32),
        states=pltpu.VMEM((STEPS + 1, STATE, parts, TP, LANES), f32),
        lam=pltpu.VMEM((STATE, parts, TP, LANES), f32), wide=pltpu.VMEM((size, 32 * LANES), f32),
        gstep=pltpu.VMEM((parts, size, LANES), f32),
        gentry=pltpu.VMEM((TP, tokens, 2 * half), bf16),
        payload=pltpu.VMEM((TP, size, 2 * LANES), bf16), parts=pltpu.VMEM((TP - 1, size, 2 * LANES), bf16),
        total=pltpu.VMEM((TP, size, 2 * LANES), bf16), own=pltpu.VMEM((size, 2 * LANES), f32),
        sums=pltpu.VMEM((8, parts, TP, LANES), f32),
        grate=pltpu.VMEM((half, LANES), f32), gselect=pltpu.VMEM((half, 2 * LANES), f32),
        gwo=pltpu.VMEM((groups, share, width), bf16), gwg=pltpu.VMEM((groups, 2, deep, half), bf16),
        gate_buf=Reduce.buffers(zh_size, (2, deep, half)), gate_sems=Reduce.sems(dma, zh_size),
        keeps=pltpu.VMEM((2, STATE, parts, TP, LANES), f32), keep_sems=dma((2,)),
        scatter_buf=Scatter.buffers((tokens, width)), reduce_buf=Reduce.buffers(zh_size, (share, width)),
        sum_sems=Sum.sems(dma), scatter_sems=Scatter.sems(dma), reduce_sems=Reduce.sems(dma, zh_size),
        loads=dma((7,)), over=[dma, dma],
    )
    if onward:
        outs.update(gog=(struct(TP, tokens, width, dtype=bf16), HB))
        ins.update(part=(part, HB))
        outs.update(parts_all=(struct(*part.shape, dtype=bf16), HB))
        scratch.update(part_sems=[dma((TP - 1,)), dma((TP - 1,)), dma])
        scratch.update(gout=pltpu.VMEM((tokens, width), bf16), gather_sems=Gather.sems(dma))
    if late is not None:
        ins.update(late_in=(late, HB))
        outs.update(late=(struct(far, *late.shape[1:], dtype=bf16), HB))
        scratch.update(late_sems=[dma((far,)), dma((far,))])

    def body(r):
        x, core, zh, q = place()
        side, far_ones = dp_peers(zh_size)
        greet([p[0] for p in tp_peers()] + [side] + [f[0] for f in far_ones])
        entry, act, step, beta, kq = r.entry, r.act, r.step, r.beta, r.kq
        gs, gact, sums, gstep = r.gs, r.gact, r.sums, r.gstep
        vec = r.vec.at[8 * layer : 8 * (layer + 1)]
        loads = [
            pltpu.make_async_copy(src, dst, r.loads.at[i])
            for i, (src, dst) in enumerate(
                (
                    (r.gouts, r.a), (r.mixed, r.gentry.at[:, :, :half]),
                    (r.wout.at[:, : 2 * half], r.b.at[:half]), (r.wout.at[:, 2 * half :], r.b.at[half : 2 * half]),
                    (r.y, gact), (r.xg, r.a), (r.win, r.b),
                )
            )
        ]
        for copy in loads[:4]:
            copy.start()
        r.load()
        loads[4].start()
        passed = []
        if onward:
            me = core * WAYS + q
            for i, (target, rank, _) in enumerate(tp_peers()):
                copy = remote(
                    r.part.at[rank], r.parts_all.at[me], r.part_sems[0].at[i], r.part_sems[1].at[i], target
                )
                copy.start()
                passed.append(copy)
            passed.append(pltpu.make_async_copy(r.part.at[me], r.parts_all.at[me], r.part_sems[2]))
            passed[-1].start()
        if late is not None:
            for k, (target, to_z, _) in enumerate(far_ones):
                copy = remote(
                    r.late_in.at[to_z], r.late.at[k], r.late_sems[0].at[k], r.late_sems[1].at[k], target
                )
                copy.start()
                passed.append(copy)
        sums[...] = jnp.zeros_like(sums)
        r.grate[...] = jnp.zeros_like(r.grate)
        r.gselect[...] = jnp.zeros_like(r.gselect)

        loads[0].wait()
        loads[1].wait()

        def outer(c, carry):
            left = r.gentry[:, :, at_block(c, LANES)].reshape(rows, LANES)
            out = dot(left, r.a[...].reshape(rows, width), ((0,), (0,))).astype(bf16)
            each = LANES // share
            r.gwo[pl.ds(c * each, each)] = out.reshape(each, share, width)
            return carry

        lax.fori_loop(0, parts, outer, 0)
        reduce = Reduce(zh_size, r.gwo, r.reduce_buf, r.reduce_sems)
        reduce.start()
        loads[2].wait()
        loads[3].wait()
        for p in range(TP // 2):

            def columns(n, carry, p=p):
                out = 0.0
                for k in range(2):
                    left = r.a[2 * p : 2 * p + 2, :, 2 * half * k : 2 * half * (k + 1)].reshape(2 * tokens, 2 * half)
                    right = r.b[pl.ds(pl.multiple_of(half * k + n * 2 * LANES, 2 * LANES), 2 * LANES), :]
                    out = out + dot(left, right, ((1,), (1,)))
                for j in range(2):
                    for c in range(2):
                        gs[2 * n + c, pl.ds(2 * p + j, tokens, stride=TP), :] = out[
                            j * tokens : (j + 1) * tokens, c * LANES : (c + 1) * LANES
                        ]
                return carry

            lax.fori_loop(0, half // (2 * LANES), columns, 0)
        loads[5].start()
        loads[6].start()
        r.need.entry()
        r.need.kq()
        r.need.beta()

        def again(b, carry):
            rs = at_block(b, size)
            norm = square_sum(kq[rs, :])
            for c in range(parts):
                conv = conv_of(entry, vec, b * size, size, c)
                act[c, rs, :] = (conv * jax.nn.sigmoid(conv)).astype(bf16).astype(f32)
                rate = beta[c, rs, :]
                step[c, rs, :] = rate / (1.0 + rate * norm)
            return carry

        lax.fori_loop(0, blocks, again, 0)
        loads[4].wait()

        def gates(b, carry):
            rs = at_block(b, size)
            here = pl.ds(pl.multiple_of(b * STEPS, STEPS), STEPS)
            for c in range(parts):
                cols = slice(c * LANES, (c + 1) * LANES)
                gate = entry[parts + c, pl.ds(pl.multiple_of(b * size + halo, TP), size), :]
                sig = jax.nn.sigmoid(gate)
                g = gs[c, rs, :]
                a = act[c, rs, :]
                down = g * (gate * sig)
                gstep[c] = g * (gact[c, rs, :] + vec[CONV + 2 : CONV + 3, cols] * a) * (
                    sig * (1.0 + gate * (1.0 - sig))
                )
                gs[c, rs, :] = down
                sums[CONV + 2, c] += row_sum(down * a)
                for s in range(TP):
                    r.gentry[s, here, half + c * LANES : half + (c + 1) * LANES] = gstep[
                        c, pl.ds(s, STEPS, stride=TP), :
                    ].astype(bf16)
            return carry

        lax.fori_loop(0, blocks, gates, 0)
        loads[5].wait()
        tile = 2 * LANES

        def outer_in(out_ref, first, i, carry):
            left = r.a[:, :, at_block(i, tile)].reshape(rows, tile)
            out = dot(left, r.gentry[:, :, first : first + half].reshape(rows, half), ((0,), (0,))).astype(bf16)
            each = tile // deep
            for e in range(each):
                d = i * each + e
                xx, cc, zz = d // (2 * zh_size), lax.rem(d // zh_size, 2), lax.rem(d, zh_size)
                out_ref[xx * zh_size + zz, cc] = out[e * deep : (e + 1) * deep]
            return carry

        lax.fori_loop(0, width // tile, lambda i, k: outer_in(r.gwg, half, i, k), 0)
        gate_reduce = Reduce(zh_size, r.gwg, r.gate_buf, r.gate_sems)

        lane = lanes_of((size, LANES))
        states, lam, wide = r.states, r.lam, r.wide
        lam[...] = jnp.zeros_like(lam)
        plus = lambda a, b: b if a is None else a + b
        total = Sum(r.payload, r.parts, r.total, r.sum_sems)

        def block(bi, carry):
            b = blocks - 1 - bi
            rs = at_block(b, size)
            slot = lax.rem(b, 2)
            pltpu.make_async_copy(r.keep.at[b], r.keeps.at[slot], r.keep_sems.at[slot]).wait()

            @pl.when(b > 0)
            def _():
                ahead = pltpu.make_async_copy(r.keep.at[b - 1], r.keeps.at[1 - slot], r.keep_sems.at[1 - slot])
                ahead.start()

            states[0] = r.keeps[slot]
            wide[...] = jnp.dot(spread_keys(kq[rs, :], lane), r.e[...], preferred_element_type=f32)

            def replay(j, carry):
                t, w = at_block(b * STEPS + j, TP), at_block(j, TP)
                acts = [act[c, t, :] for c in range(parts)]
                steps = [step[c, t, :] for c in range(parts)]
                for n in range(STATE):
                    key = wide[w, n * LANES : (n + 1) * LANES]
                    for c in range(parts):
                        s = states[j, n, c]
                        states[j + 1, n, c] = s + (steps[c] * key) * (acts[c] - key * s)
                return carry

            lax.fori_loop(0, STEPS, replay, 0)

            def back(jj, carry):
                j = STEPS - 1 - jj
                t, w = at_block(b * STEPS + j, TP), at_block(j, TP)
                acts = [act[c, t, :] for c in range(parts)]
                steps = [step[c, t, :] for c in range(parts)]
                gsums = [gs[c, t, :] for c in range(parts)]
                first, second = [None] * parts, [None] * parts
                for n in range(STATE):
                    kcols, qcols = slice(n * LANES, (n + 1) * LANES), slice((STATE + n) * LANES, (STATE + n + 1) * LANES)
                    key, query = wide[w, kcols], wide[w, qcols]
                    square = key * key
                    key_term, query_term = None, None
                    for c in range(parts):
                        before, after = states[j, n, c], states[j + 1, n, c]
                        grad = lam[n, c] + gsums[c] * query
                        u = key * before
                        d = acts[c] - u
                        gk = grad * key
                        sg = steps[c] * grad
                        first[c] = plus(first[c], gk * d)
                        second[c] = plus(second[c], gk)
                        key_term = plus(key_term, sg * (d - u))
                        query_term = plus(query_term, gsums[c] * after)
                        lam[n, c] = grad - sg * square
                    wide[w, kcols] = key_term
                    wide[w, qcols] = query_term
                for c in range(parts):
                    gstep[c, w, :] = first[c]
                    gact[c, t, :] = steps[c] * second[c]
                return carry

            lax.fori_loop(0, STEPS, back, 0)
            terms = wide[...]
            high = terms.astype(bf16)
            low = (terms - high.astype(f32)).astype(bf16)
            gkq = jnp.dot(high, r.fold[...], preferred_element_type=f32) + jnp.dot(
                low, r.fold[...], preferred_element_type=f32
            )
            keys = kq[rs, :]
            norm = square_sum(keys)
            gnorm = jnp.zeros((size, 1), f32)
            grates = []
            for c in range(parts):
                cols = slice(c * LANES, (c + 1) * LANES)
                rate = beta[c, rs, :]
                g = gstep[c]
                inverse = 1.0 + rate * norm
                inverse = 1.0 / (inverse * inverse)
                gnorm = gnorm - jnp.sum(g * (rate * rate * inverse), axis=1, keepdims=True)
                grate = g * inverse * rate * (1.0 - rate)
                sums[CONV + 1, c] += row_sum(grate)
                grates.append(grate.astype(bf16))
                gact[c, rs, :] += vec[CONV + 2 : CONV + 3, cols] * gs[c, rs, :]
            grate = jnp.concatenate(grates, axis=1)
            r.grate[...] += dot(grate, r.proj[b, :, :RANK], ((0,), (0,)))
            grank = dot(grate, r.mats[:, :RANK], ((1,), (0,)))
            gkq = gkq + jnp.where(lane < STATE, 2.0 * keys * gnorm, 0.0)
            out = jnp.concatenate([grank, gkq], axis=1)
            r.payload[b] = encode(out)

            @pl.when(b == total.me)
            def _():
                r.own[...] = out

            return carry

        for wait in (r.need.proj, r.need.mats, r.need.e, r.need.fold):
            wait()
        last = (blocks - 1) % 2
        pltpu.make_async_copy(r.keep.at[blocks - 1], r.keeps.at[last], r.keep_sems.at[last]).start()
        lax.fori_loop(0, blocks // 2, block, 0)
        reduce.middle()
        gate_reduce.start()
        lax.fori_loop(blocks // 2, blocks, block, 0)
        total.start()
        total.middle(r.own[...])
        total.finish()
        gate_reduce.middle()
        step[:, rows:, :] = jnp.zeros((parts, halo, LANES), f32)
        gconv = step

        def convs(b, carry):
            rs = at_block(b, size)
            gp = r.total[b]
            gp = jnp.where(lanes_of(gp.shape) < RANK + 2 * STATE, gp.astype(f32), 0.0).astype(bf16)
            r.gselect[...] += dot(wide_of(act, rs, parts).astype(bf16), gp, ((0,), (0,)))
            more = dot(gp, r.mats[:, RANK:], ((1,), (1,)))
            for c in range(parts):
                conv = conv_of(entry, vec, b * size, size, c)
                sig = jax.nn.sigmoid(conv)
                g = (gact[c, rs, :] + more[:, c * LANES : (c + 1) * LANES]) * (sig * (1.0 + conv * (1.0 - sig)))
                gconv[c, rs, :] = g
                sums[CONV, c] += row_sum(g)
                for j in range(CONV):
                    inner = entry[c, pl.ds(pl.multiple_of(b * size + TP * j, TP), size), :]
                    sums[j, c] += row_sum(g * inner)
            return carry

        lax.fori_loop(0, blocks, convs, 0)

        def inners(b, carry):
            rs = at_block(b, size)
            here = pl.ds(pl.multiple_of(b * STEPS, STEPS), STEPS)
            for c in range(parts):
                cols = slice(c * LANES, (c + 1) * LANES)
                value = None
                for j in range(CONV):
                    at = pl.ds(pl.multiple_of(b * size + TP * (CONV - 1 - j), TP), size)
                    value = plus(value, vec[j : j + 1, cols] * gconv[c, at, :])
                gs[c, rs, :] = value
                for s in range(TP):
                    at = pl.ds(b * size + s, STEPS, stride=TP)
                    r.gentry[s, here, cols] = gs[c, at, :].astype(bf16)
            return carry

        lax.fori_loop(0, blocks, inners, 0)
        lax.fori_loop(0, width // tile, lambda i, k: outer_in(r.ginner, 0, i, k), 0)
        over = remote(
            r.ginner.at[pl.ds((1 - x) * zh_size, zh_size)], r.near, r.over[0], r.over[1], side
        )
        over.start()
        r.put.ginner()
        loads[6].wait()
        scatter = Scatter(r.a, r.scatter_buf, r.scatter_sems)
        out_partial(scatter, r.a, r.gentry, lambda: r.b[...], turned=True)
        r.gmats[:, :RANK] = r.grate[...].astype(bf16)
        r.gmats[:, RANK:] = r.gselect[...].astype(bf16)
        for j in range(8):
            for c in range(parts):
                r.gvec[j : j + 1, c * LANES : (c + 1) * LANES] = jnp.sum(sums[j, c], axis=0, keepdims=True)
        r.gwout[...] = reduce.total()
        r.ggate[...] = gate_reduce.total().astype(bf16)
        gnormed = scatter.total()
        r.need.h()
        r.need.grad()
        stream = r.h[...]
        scale = rms(stream)
        r.ggain[...] = jnp.sum(gnormed * stream * scale, axis=0, keepdims=True)
        scaled = gnormed * r.gain[layer : layer + 1, :]
        grad = r.grad[...] + scale * scaled - stream * (scale * scale * scale) * jnp.mean(
            stream * scaled, axis=-1, keepdims=True
        )
        r.prev[...] = grad
        if onward:
            r.gout[...] = grad.astype(bf16)
            spread = Gather(r.gout, r.gog, r.gather_sems)
            spread.start()
            spread.relay()
            spread.rest()
            spread.finish()
        for copy in passed:
            copy.wait()
        over.wait()
        r.done()

    return call(body, 9 if onward else 8, ins, outs, scratch)


def closing(zh_size, inner, near, mats, small, stats, gain, turns, share, width, select):
    groups = 2 * zh_size
    count = groups * TP
    far_n = max(1, zh_size - 1)
    dma = pltpu.SemaphoreType.DMA
    depth, half = inner.shape[3] // WAYS, inner.shape[4]
    gains = width // count
    every = (2, zh_size) + stats.shape
    v = pltpu.VMEM
    ins = dict(
        inner=(inner, VM), near=(near, VM), mats=(mats, VM), small=(small, VM), stats=(stats, VM), gain=(gain, VM),
        t0=(turns[0], VM), t1=(turns[1], VM), t2=(turns[2], VM),
    )
    outs = dict(
        gin=(struct(LAYERS, depth, 2 * count * share), VM), gselect=(struct(LAYERS, share, select), VM),
        grate=(struct(LAYERS, RANK, share), VM),
        ggain=(struct(LAYERS, gains), VM), gtaps=(struct(LAYERS, CONV, share), VM), gshift=(struct(LAYERS, share), VM),
        grate_shift=(struct(LAYERS, share), VM), gskip=(struct(LAYERS, share), VM), stats_all=(struct(*stats.shape), VM),
    )

    def chunk(shape, dtype):
        return [
            v(shape[1:], dtype), v((far_n,) + shape[2:], dtype), dma((far_n,)), dma((far_n,)), v(shape[1:], dtype), dma, dma
        ]

    piece = inner.shape[:2] + inner.shape[3:]
    scratch = dict(
        vectors=v(small.shape, f32), stats_v=v(every, f32), stats_t=v((TP - 1,) + stats.shape, f32),
        gain_t=v((TP - 1,) + gain.shape[1:], f32), win_t=v((2, WAYS, depth, half), bf16),
        total=v(small.shape[2:], f32),
        g_sems=[dma((TP - 1,))] * 2, s_sems=[dma((TP - 1,))] * 2,
    )
    scratch.update(
        boxes=v((4, TP, depth, half), bf16), turn_sems=[[dma((TP - 1,)), dma((TP - 1,))] for _ in range(4)],
        chunks=[chunk(piece, bf16), chunk(piece, bf16), chunk(mats.shape, bf16), chunk(small.shape, f32), chunk(every, f32)],
    )

    def body(r):
        x, core, zh, q = place()
        me = core * WAYS + q
        peers = tp_peers()
        side, far = dp_peers(zh_size)
        greet([p[0] for p in peers] + [side] + [f[0] for f in far])
        sent, full = [], []

        def join(a, b, peaks):
            a, b = a.astype(f32), b.astype(f32)
            if peaks:
                line = lax.broadcasted_iota(jnp.int32, a.shape, len(a.shape) - 2)
                return jnp.where(line < 4, a + b, jnp.maximum(a, b))
            return a + b

        class Chunk:
            def __init__(self, number, src, near=None):
                self.src, self.peaks = src, number == 4
                self.mine, self.buf, self.z_send, self.z_recv, spare, self.x_send, self.x_recv = r.chunks[number]
                self.near = spare if near is None else near

            def start(self):
                self.over = remote(self.src.at[1 - x], self.near, self.x_send, self.x_recv, side)
                self.over.start()
                sent.append(self.over)

            def middle(self, arrived=False):
                if not arrived:
                    self.over.wait_recv()
                mine, buf = self.mine, self.buf
                mine[...] = join(self.src[x], self.near[...], self.peaks).astype(mine.dtype)
                self.along = [
                    remote(mine.at[to_z], buf.at[k], self.z_send.at[k], self.z_recv.at[k], target)
                    for k, (target, to_z, _) in enumerate(far)
                ]
                for copy in self.along:
                    copy.start()
                    sent.append(copy)

            def total(self):
                value = join(self.src[x, zh], self.near[zh], self.peaks)
                for k, copy in enumerate(self.along):
                    copy.wait_recv()
                    value = join(value, self.buf[k], self.peaks)
                return value

        def turn(src, i):
            box, sems = r.boxes.at[i], r.turn_sems[i]
            for k, (target, rank, _) in enumerate(peers):
                copy = remote(src(rank), box.at[me], sems[0].at[k], sems[1].at[k], target)
                copy.start()
                full.append(copy)
            box[me] = src(me)[...]

        cs = [Chunk(c, r.inner.at[:, :, c], r.near.at[:, c]) for c in range(2)]
        cs[0].middle(arrived=True)
        cs[1].middle(arrived=True)
        gained, shown = [], []
        for i, (target, rank, _) in enumerate(peers):
            for src, buf, sems, copies in (
                (r.gain.at[rank], r.gain_t, r.g_sems, gained),
                (r.stats, r.stats_t, r.s_sems, shown),
            ):
                copy = remote(src, buf.at[i], sems[0].at[i], sems[1].at[i], target)
                copy.start()
                copies.append(copy)
                sent.append(copy)
        mats_c = Chunk(2, r.mats)
        mats_c.start()
        sources = (r.t0, r.t1, r.t2)
        for i in range(3):
            turn(lambda rank, i=i: sources[i].at[rank], i + 1)
        total = r.gain[me]
        seen = r.stats[...]
        for i in range(TP - 1):
            gained[i].wait_recv()
            total = total + r.gain_t[i]
            shown[i].wait_recv()
            seen = join(seen, r.stats_t[i], True)
        r.vectors[...] = r.small[...]
        for l in range(LAYERS):
            for g in range(groups):
                at = l * groups + g
                r.vectors[g // zh_size, g % zh_size, l * 16 + 8 : l * 16 + 9, :] = total[at : at + 1, :]
        r.stats_v[...] = jnp.broadcast_to(seen, every)
        rest = [mats_c, Chunk(3, r.vectors), Chunk(4, r.stats_v)]
        for c in rest[1:]:
            c.start()
        for c in rest:
            c.middle()
        for c in range(2):
            r.win_t[c] = cs[c].total().astype(bf16).reshape(WAYS, depth, half)
        turn(lambda rank: r.win_t.at[rank // WAYS, lax.rem(rank, WAYS)], 0)
        m = rest[0].total()
        for l in range(LAYERS):
            base = 3 * LANES * l
            r.grate[l] = m[:, base : base + RANK].T
            r.gselect[l] = m[:, base + RANK : base + RANK + select]
        r.total[...] = rest[1].total()
        for l in range(LAYERS):
            r.gtaps[l] = r.total[16 * l : 16 * l + CONV, :share]
            for out, j, size in (
                (r.gshift, CONV, share), (r.grate_shift, CONV + 1, share), (r.gskip, CONV + 2, share), (r.ggain, 8, gains)
            ):
                out[l : l + 1, :] = r.total[16 * l + j : 16 * l + j + 1, :size]
        r.stats_all[...] = rest[2].total()

        def lay(i):
            for rank in range(TP):
                for g in range(groups):
                    d = ((g // zh_size * 2 + rank // WAYS) * zh_size + g % zh_size) * WAYS + rank % WAYS
                    first = i % 2 * count * share + d * share
                    r.gin[i // 2, :, first : first + share] = r.boxes[i, rank, :, g * share : (g + 1) * share].astype(f32)

        early, late = full[: 3 * (TP - 1)], full[3 * (TP - 1) :]
        for copy in early:
            copy.wait_recv()
        for i in (1, 2, 3):
            lay(i)
        for copy in late:
            copy.wait_recv()
        lay(0)
        for copy in sent + full:
            copy.wait_send()

    return call(body, 5, ins, outs, scratch)


def on_device(
    hidden, cotangent, groups, group_weights, input_weight, select_weight, rate_weight,
    output_weight, norm_gain, conv_taps, conv_shift, rate_shift, skip_gain,
):
    fsdp = lax.axis_size("fsdp")
    zh_size = fsdp // WAYS
    count = 2 * 2 * fsdp
    group_count = 2 * zh_size
    share = conv_shift.shape[1]
    gains = norm_gain.shape[1]
    depth = input_weight.shape[1]
    half = group_count * share
    x, core, zh, q = place()

    labels = jnp.arange(group_weights.shape[0])
    own_weight = jnp.sum(jnp.where(groups[:, None] == labels[None, :], group_weights[None, :], 0.0))

    wins = input_weight
    if share % LANES:
        wins = wins.reshape(LAYERS, depth, 2, 2, 2, zh_size, WAYS, share)
        wins = wins.transpose(0, 4, 6, 1, 2, 3, 5, 7).reshape(LAYERS, TP, depth, 2 * half)
    mats = jnp.concatenate([rate_weight.swapaxes(1, 2), select_weight], axis=2)
    mats = jnp.pad(mats, ((0, 0), (0, 0), (0, 3 * LANES - mats.shape[2])))
    vectors = [conv_taps, conv_shift[:, None], rate_shift[:, None], skip_gain[:, None], skip_gain[:, None]]
    small = jnp.concatenate(vectors, axis=1).astype(f32).reshape(8 * LAYERS, share)
    small = jnp.pad(small, ((0, 0), (0, LANES - share)))
    misc = jnp.pad(norm_gain.astype(f32), ((0, 0), (0, LANES - gains)))
    misc = jnp.concatenate([misc, jnp.full((8 - LAYERS, LANES), own_weight)])

    flat = lambda a: a.reshape(half, -1)
    h0 = hidden[0]
    start = opening(zh_size, gains, share, wins, small, misc, mats, h0, cotangent[0])
    vec, gain, scale = start.vec, start.gains, start.scale
    win0, mat0 = start.win_all.reshape(count * depth, -1), flat(start.mats_all)
    one = forward_layer(
        zh_size, 0, start.xg, win0, mat0, output_weight, vec, scale,
        nxt=types.SimpleNamespace(h=h0, gain=gain, win=wins, mats=mats),
    )
    win1, mat1 = one.win1_all.reshape(count * depth, -1), flat(one.mats1_all)
    h1 = one.result
    two = forward_layer(zh_size, 1, one.xg1, win1, mat1, output_weight, vec, scale, gout=start.gout)

    down1 = backward_layer(
        zh_size, 1, two, two.gog, flat(two.wout_all), mat1, vec, one.xg1, win1, gain, h1, start.grad,
        part=two.part,
    )
    stream = h1 + jnp.sum(down1.parts_all.astype(f32), axis=0)
    blocks = (2, zh_size) + down1.ginner.shape[1:]
    pick = lambda a, i: lax.dynamic_index_in_dim(a, i, 0, keepdims=False)
    summed = pick(down1.ginner.reshape(blocks), x).astype(f32) + down1.near.astype(f32)
    down0 = backward_layer(
        zh_size, 0, one, down1.gog, flat(one.wout_all), mat0, vec, start.xg, win0, gain, h0, down1.prev,
        late=summed.astype(bf16),
    )
    late = pick(summed, zh)
    for k in range(zh_size - 1):
        late = late + down0.late[k].astype(f32)

    sums = [jnp.sum(o.stats[0]) for o in (one, two)]
    peaks = [jnp.max(o.stats[1]) for o in (one, two)]
    pad = [jnp.zeros((), f32)] * (4 - LAYERS)
    own_stats = jnp.broadcast_to(jnp.stack(sums + pad + peaks + pad)[:, None], (8, LANES))
    downs = (down0, down1)
    small = jnp.stack([down.gvec for down in downs]).reshape(LAYERS, 8, group_count, share)
    small = jnp.pad(small.transpose(2, 0, 1, 3), ((0, 0), (0, 0), (0, 8), (0, LANES - share)))
    small = small.reshape(2, zh_size, 16 * LAYERS, LANES)
    spread_gain = jnp.stack([down.ggain[0] for down in downs]).reshape(LAYERS, 2, 2, zh_size, WAYS, gains)
    spread_gain = spread_gain.transpose(2, 4, 0, 1, 3, 5).reshape(TP, LAYERS * group_count, gains)
    spread_gain = jnp.pad(spread_gain, ((0, 0), (0, -LAYERS * group_count % 8), (0, LANES - gains)))
    mats = jnp.concatenate([down.gmats for down in downs], axis=1).reshape(2, zh_size, share, -1)
    turns = [down0.ggate, late.astype(bf16), down1.ggate]
    end = closing(
        zh_size, down0.ginner.reshape(blocks), down0.near, mats, small, own_stats, spread_gain,
        [t.reshape(TP, depth, half) for t in turns], share, output_weight.shape[2], select_weight.shape[2],
    )
    stats = end.stats_all
    beta_mean = stats[:LAYERS, 0] / (count * hidden.shape[1] * INNER)
    beta_max = stats[4 : 4 + LAYERS, 0]
    gwout = jnp.stack([down.gwout for down in downs])
    return (
        stream[None], down0.prev[None], end.gin, end.gselect, end.grate, gwout, end.ggain, end.gtaps, end.gshift,
        end.grate_shift, end.gskip, beta_mean, beta_max,
    )


def solution(mesh):
    both = ("dp", "fsdp")
    placed = (
        P(both, None, None), P(both, None, None), P(both), P(),
        P(None, both, None), P(None, both, None), P(None, None, both), P(None, both, None),
        P(None, both), P(None, None, both), P(None, both), P(None, both), P(None, both),
    )
    return jax.shard_map(
        on_device,
        mesh=mesh,
        in_specs=placed,
        out_specs=(P(both, None, None), P(both, None, None)) + placed[4:] + (P(), P()),
        check_vma=False,
    )
```

```python
import types

import jax
import jax.numpy as jnp
import numpy as np
from jax import lax
from jax.sharding import PartitionSpec as P
import jax.experimental.pallas as pl
import jax.experimental.pallas.tpu as pltpu

INNER = 4096
STATE = 16
RANK = 128
CONV = 4
LAYERS = 2
WAYS = 4
TP = 8
STEPS = 16

eps = 1e-05
MESH = pl.DeviceIdType.MESH
f32 = jnp.float32
bf16 = jnp.bfloat16
VM = pl.BlockSpec(memory_space=pltpu.VMEM)
HB = pl.BlockSpec(memory_space=pl.ANY)
EARLY, LATE = object(), object()


def place():
    dp, fs = lax.axis_index("dp"), lax.axis_index("fsdp")
    return dp // 2, lax.rem(dp, 2), fs // WAYS, lax.rem(fs, WAYS)


def device(x, core, zh, q):
    return (x * 2 + core, zh * WAYS + q)


def remote(src, dst, send, recv, target):
    return pltpu.make_async_remote_copy(
        src_ref=src, dst_ref=dst, send_sem=send, recv_sem=recv, device_id=target, device_id_type=MESH
    )


def greet(targets):
    barrier = pltpu.get_barrier_semaphore()
    for target in targets:
        pl.semaphore_signal(barrier, inc=1, device_id=target, device_id_type=MESH)
    pl.semaphore_wait(barrier, len(targets))


def tp_peers():
    x, core, zh, q = place()
    peers = []
    for dc, da, db in ((1, 0, 0), (0, 1, 0), (0, 0, 1), (1, 1, 0), (1, 0, 1), (0, 1, 1), (1, 1, 1)):
        other_core, other_q = lax.rem(core + dc, 2), neighbour(q, da, db)
        rank = other_core * WAYS + other_q
        peers.append((device(x, other_core, zh, other_q), rank, rank))
    return peers


def neighbour(q, da, db):
    a, b = lax.rem(q, 2), q // 2
    return (1 - b if db else b) * 2 + (1 - a if da else a)


def total_rank():
    _, core, _, q = place()
    return core * WAYS + q


def dp_peers(zh_size):
    x, core, zh, q = place()
    side = device(1 - x, core, zh, q)
    far = []
    for dz in range(1, zh_size):
        to_z, from_z = lax.rem(zh + dz, zh_size), lax.rem(zh + zh_size - dz, zh_size)
        far.append((device(x, core, to_z, q), to_z, from_z))
    return side, far


def lanes_of(shape):
    return lax.broadcasted_iota(jnp.int32, shape, 1)


def encode(v):
    tail = v[:, RANK:]
    lane = lanes_of(tail.shape)
    high = tail.astype(bf16).astype(f32)
    low = pltpu.roll(tail - high, 32, 1)
    both = jnp.where(lane < 32, high, jnp.where(lane < 64, low, 0.0))
    return jnp.concatenate([v[:, :RANK].astype(bf16), both.astype(bf16)], axis=1)


def decode(v):
    tail = v[:, RANK:].astype(f32)
    lane = lanes_of(tail.shape)
    tail = jnp.where(lane < 32, tail + pltpu.roll(tail, 96, 1), 0.0)
    return jnp.concatenate([v[:, :RANK].astype(f32), tail], axis=1)


def halves(rows):
    return pl.ds(0, rows // 2), pl.ds(rows // 2, rows // 2)


class Gather:
    sems = staticmethod(lambda dma: [dma((6,)), dma((6,)), dma((4,)), dma((4,)), dma])

    def __init__(self, src, out, sems):
        self.src, self.out = src, out
        self.f_send, self.f_recv, self.s_send, self.s_recv, self.own_sem = sems
        x, core, zh, q = place()
        self.core, self.me = core, core * WAYS + q
        self.sibling = device(x, 1 - core, zh, q)
        self.chips = [neighbour(q, 0, 1), neighbour(q, 1, 0), neighbour(q, 1, 1)]
        self.b, self.a = [device(x, core, zh, c) for c in self.chips[:2]]
        self.top, self.low = halves(src.shape[0])

    def send(self, i, src, slot, rows, target):
        copy = remote(src, self.out.at[slot, rows], self.f_send.at[i], self.f_recv.at[i], target)
        copy.start()
        return copy

    def to_sibling(self, i, src, slot):
        copy = remote(src, self.out.at[slot], self.s_send.at[i], self.s_recv.at[i], self.sibling)
        copy.start()
        self.near.append(copy)

    def start(self):
        self.near = []
        self.first = [
            self.send(i, self.src.at[rows], self.me, rows, target)
            for i, (rows, target) in enumerate(
                ((self.top, self.b), (self.low, self.a), (self.low, self.b), (self.top, self.a))
            )
        ]
        self.to_sibling(3, self.src, self.me)
        self.own = pltpu.make_async_copy(self.src, self.out.at[self.me], self.own_sem)
        self.own.start()

    def relay(self):
        for i, rows, target in ((0, self.top, self.a), (1, self.low, self.b)):
            self.first[i].wait_recv()
            slot = self.core * WAYS + self.chips[i]
            self.first.append(self.send(4 + i, self.out.at[slot, rows], slot, rows, target))

    def rest(self):
        for i, ends in enumerate(((2,), (3,), (4, 5))):
            for k in ends:
                self.first[k].wait_recv()
            slot = self.core * WAYS + self.chips[i]
            self.to_sibling(i, self.out.at[slot], slot)

    def finish(self):
        for copy in self.first:
            copy.wait_send()
        for copy in self.near:
            copy.wait()
        self.own.wait()


class Scatter:
    sems = staticmethod(lambda dma: [dma((4,)), dma((4,)), dma((6,)), dma((6,))])

    @staticmethod
    def buffers(block):
        return [pltpu.VMEM((4,) + block, bf16), pltpu.VMEM((3,) + block, bf16), pltpu.VMEM((3,) + block, bf16)]

    def __init__(self, partial, buffers, sems):
        self.partial = partial
        self.near_buf, self.out, self.into = buffers
        self.s_send, self.s_recv, self.f_send, self.f_recv = sems
        x, core, zh, q = place()
        self.core = core
        self.sibling = device(x, 1 - core, zh, q)
        self.turns = [neighbour(q, 1, 1), neighbour(q, 1, 0), neighbour(q, 0, 1), q]
        self.a, self.b = [device(x, core, zh, t) for t in self.turns[1:3]]
        self.top, self.low = halves(partial.shape[1])
        self.near, self.first = [None] * 4, {}

    def to_sibling(self, i):
        slot = (1 - self.core) * WAYS + self.turns[i]
        self.near[i] = remote(
            self.partial.at[slot], self.near_buf.at[i], self.s_send.at[i], self.s_recv.at[i], self.sibling
        )
        self.near[i].start()

    def joined(self, i, rows=slice(None)):
        own = self.partial[self.core * WAYS + self.turns[i], rows]
        return own.astype(f32) + self.near_buf[i, rows].astype(f32)

    def send(self, k, i, rows, target):
        self.first[k] = remote(
            self.out.at[i, rows], self.into.at[i, rows], self.f_send.at[k], self.f_recv.at[k], target
        )
        self.first[k].start()

    def across(self, i):
        self.near[i].wait_recv()
        if i == 0:
            self.out[0] = self.joined(0).astype(bf16)
            self.send(0, 0, self.top, self.a)
            self.send(1, 0, self.low, self.b)
        else:
            rows, target = ((self.top, self.a), (self.low, self.b))[i - 1]
            self.out[i, rows] = self.joined(i, rows).astype(bf16)
            self.send(1 + i, i, rows, target)

    def sums(self):
        for k, i, rows, target in ((1, 1, self.low, self.a), (0, 2, self.top, self.b)):
            self.first[k].wait_recv()
            self.out[i, rows] = (self.joined(i, rows) + self.into[0, rows].astype(f32)).astype(bf16)
            self.send(3 + i, i, rows, target)

    def total(self):
        self.near[3].wait_recv()
        value = self.joined(3)
        for k in (2, 3, 4, 5):
            self.first[k].wait_recv()
        value = value + self.into[1].astype(f32) + self.into[2].astype(f32)
        for copy in self.near + list(self.first.values()):
            copy.wait_send()
        return value


class Spread:
    @staticmethod
    def sems(dma, zh_size):
        far = max(1, zh_size - 1)
        return [dma((far,)), dma((far,)), dma((zh_size,)), dma((zh_size,)), dma]

    def __init__(self, zh_size, src, view, sems, keep=True):
        self.src, self.view, self.keep = src, view, keep
        self.z_send, self.z_recv, self.x_send, self.x_recv, self.own_sem = sems
        self.x, _, self.zh, _ = place()
        self.side, self.far = dp_peers(zh_size)

    def start(self):
        dst = self.view(self.x, self.zh)
        self.along = [
            remote(self.src, dst, self.z_send.at[k], self.z_recv.at[k], target)
            for k, (target, _, _) in enumerate(self.far)
        ]
        self.over = [remote(self.src, dst, self.x_send.at[0], self.x_recv.at[0], self.side)]
        for copy in self.along + self.over:
            copy.start()
        if self.keep:
            self.own = pltpu.make_async_copy(self.src, dst, self.own_sem)
            self.own.start()

    def onward(self):
        for k, (_, _, source) in enumerate(self.far):
            self.along[k].wait_recv()
            slot = self.view(self.x, source)
            copy = remote(slot, slot, self.x_send.at[k + 1], self.x_recv.at[k + 1], self.side)
            copy.start()
            self.over.append(copy)

    def finish(self):
        for copy in self.along:
            copy.wait_send()
        for copy in self.over:
            copy.wait()
        if self.keep:
            self.own.wait()


class Sum:
    sems = staticmethod(
        lambda dma: [dma, dma, dma((3,)), dma((3,)), dma((4,)), dma((4,)), dma((3,)), dma((3,))]
    )

    def __init__(self, payload, parts, out, sems):
        self.payload, self.out = payload, out
        self.near, self.into = parts.at[:WAYS], parts.at[WAYS:]
        self.a_send, self.a_recv, self.b_send, self.b_recv, self.c_send, self.c_recv, self.d_send, self.d_recv = sems
        x, core, zh, q = place()
        self.q, self.base, self.me = q, core * WAYS, core * WAYS + q
        self.other = (1 - core) * WAYS
        self.sibling = device(x, 1 - core, zh, q)
        self.chips = [neighbour(q, 1, 1), neighbour(q, 1, 0), neighbour(q, 0, 1)]
        self.far = [device(x, core, zh, t) for t in self.chips]

    def start(self):
        swap = remote(
            self.payload.at[pl.ds(self.other, WAYS)], self.near, self.a_send, self.a_recv, self.sibling
        )
        swap.start()
        swap.wait_recv()
        self.one = [swap]
        for i, t in enumerate(self.chips):
            slot = self.base + t
            self.payload[slot] = encode(decode(self.payload[slot]) + decode(self.near[t]))
            copy = remote(self.payload.at[slot], self.into.at[i], self.b_send.at[i], self.b_recv.at[i], self.far[i])
            copy.start()
            self.one.append(copy)

    def middle(self, own):
        total = own + decode(self.near[self.q])
        for i in range(3):
            self.one[1 + i].wait_recv()
            total = total + decode(self.into[i])
        self.out[self.me] = encode(total)
        mine = self.out.at[self.me]
        self.two = [
            remote(mine, mine, self.c_send.at[i], self.c_recv.at[i], target)
            for i, target in enumerate(self.far + [self.sibling])
        ]
        for copy in self.two:
            copy.start()

    def finish(self):
        last = []
        for i in (1, 2, 0):
            self.two[i].wait_recv()
            slot = self.out.at[self.base + self.chips[i]]
            copy = remote(slot, slot, self.d_send.at[i], self.d_recv.at[i], self.sibling)
            copy.start()
            last.append(copy)
        self.two[3].wait_recv()
        for copy in self.one + self.two:
            copy.wait_send()
        for copy in last:
            copy.wait()


def call(body, collective, ins, outs, scratch):
    def flatten(kind):
        return [leaf for each in kind for leaf in flatten(each)] if isinstance(kind, list) else [kind]

    def rebuild(kind, refs):
        return [rebuild(each, refs) for each in kind] if isinstance(kind, list) else refs.pop(0)

    early = [key for key, (_, spec) in ins.items() if spec is EARLY]
    late = [key for key, (_, spec) in outs.items() if spec is LATE]
    space = lambda spec: HB if spec is EARLY or spec is LATE else spec
    held = [pltpu.VMEM(ins[key][0].shape, ins[key][0].dtype) for key in early]
    held += [pltpu.VMEM(outs[key][0].shape, outs[key][0].dtype) for key in late]
    extra = [held, [pltpu.SemaphoreType.DMA] * len(held)]

    def kernel(*refs):
        refs = list(refs)
        named = {key: refs.pop(0) for key in list(ins) + list(outs)}
        named.update({key: rebuild(kind, refs) for key, kind in scratch.items()})
        buffers, sems = rebuild(extra, refs)
        loads, stores = {}, {}
        for key, buffer, sem in zip(early + late, buffers, sems):
            if key in early:
                loads[key] = pltpu.make_async_copy(named[key], buffer, sem)
            else:
                stores[key] = pltpu.make_async_copy(buffer, named[key], sem)
            named[key] = buffer
        r = types.SimpleNamespace(**named)
        r.load = lambda: [copy.start() for copy in loads.values()]
        r.need = types.SimpleNamespace(**{key: copy.wait for key, copy in loads.items()})
        r.put = types.SimpleNamespace(**{key: copy.start for key, copy in stores.items()})
        r.done = lambda: [copy.wait() for copy in stores.values()]
        body(r)

    values = pl.pallas_call(
        kernel,
        out_shape=[shape for shape, _ in outs.values()],
        in_specs=[space(spec) for _, spec in ins.values()],
        out_specs=[space(spec) for _, spec in outs.values()],
        scratch_shapes=flatten(list(scratch.values()) + extra),
        compiler_params=pltpu.CompilerParams(
            collective_id=collective, has_side_effects=True, vmem_limit_bytes=63 * 2**20
        ),
    )(*[array for array, _ in ins.values()])
    return types.SimpleNamespace(**dict(zip(outs, values)))


def spread_keys(kq, lane):
    a = kq.astype(bf16).astype(f32)
    rest = kq - a
    b = rest.astype(bf16).astype(f32)
    c = rest - b
    return jnp.where(lane < 32, a, jnp.where(lane < 64, b, c)).astype(bf16)


def spreader():
    one = np.repeat(np.eye(32, dtype=np.float32), 128, axis=1)
    return jnp.asarray(np.concatenate([one, one, one, np.zeros_like(one)], axis=0), bf16)


def folder():
    return jnp.asarray(np.pad(np.repeat(np.eye(32, dtype=np.float32), 128, axis=0), ((0, 0), (0, 96))), bf16)


def dot(a, b, contract, out=f32):
    return lax.dot_general(a, b, (contract, ((), ())), preferred_element_type=out)


def rms(stream):
    return lax.rsqrt(jnp.mean(jnp.square(stream), axis=-1, keepdims=True) + eps)


LANES = 128


def struct(*shape, dtype=f32):
    return jax.ShapeDtypeStruct(shape, dtype)


def side_by_side(pieces, lanes):
    each = LANES // lanes
    out = []
    for i in range(0, len(pieces), each):
        tile = pieces[i]
        for j in range(1, each):
            tile = tile + pltpu.roll(pieces[i + j], j * lanes, 1)
        out.append(tile)
    return jnp.concatenate(out, axis=1)


def turn_pieces(zh_size, win, layer, out, rank):
    if len(win.shape) == 4:
        return [(win.at[layer, rank], out)]
    groups = 2 * zh_size
    share = win.shape[2] // (2 * groups * TP)
    pieces = []
    for part in range(2):
        for g in range(groups):
            d = ((g // zh_size * 2 + rank // WAYS) * zh_size + g % zh_size) * WAYS + lax.rem(rank, WAYS)
            first = pl.multiple_of((part * groups * TP + d) * share, share)
            pieces.append(
                (win.at[layer, :, pl.ds(first, share)], out.at[:, pl.ds((part * groups + g) * share, share)])
            )
    return pieces


class Turn:
    def __init__(self, zh_size, win, layer, out, slot, sems):
        self.out, self.slot, self.sems = out, slot, sems
        self.me = total_rank()
        self.peers = tp_peers()
        self.pieces = lambda rank: turn_pieces(zh_size, win, layer, out.at[slot(self.me)], rank)

    def start(self):
        for i, (target, rank, _) in enumerate(self.peers):
            for src, dst in self.pieces(rank):
                remote(src, dst, self.sems[0].at[i], self.sems[1].at[i], target).start()

    def whole(self, i, rank):
        block = self.out.at[self.slot(rank)]
        return remote(block, block, self.sems[0].at[i], self.sems[1].at[i], self.peers[i][0])

    def arrived(self, i):
        self.whole(i, self.peers[i][2]).wait_recv()

    def sent(self):
        for i in range(TP - 1):
            self.whole(i, self.me).wait_send()


def opening(zh_size, gains, share, win, small, misc, mats, h, cot):
    groups = 2 * zh_size
    count = groups * TP
    tokens, width = h.shape
    half = groups * share
    depth = win.shape[-2]
    dma = pltpu.SemaphoreType.DMA
    ins = dict(
        win=(win, HB), small=(small, VM), misc=(misc, VM), mats=(mats, HB), h=(h, VM), cot=(cot, VM)
    )
    outs = dict(
        win_all=(struct(count, depth, 2 * half, dtype=bf16), HB),
        mats_all=(struct(groups, *mats.shape[1:], dtype=bf16), HB), vec=(struct(8 * LAYERS, half), VM),
        gains=(struct(8, width), VM), scale=(struct(TP, LANES), VM), grad=(struct(tokens, width), VM),
        gout=(struct(tokens, width, dtype=bf16), VM), xg=(struct(TP, tokens, width, dtype=bf16), HB),
    )
    spread = lambda: Spread.sems(dma, zh_size)
    scratch = dict(
        misc_all=pltpu.VMEM((count,) + misc.shape, f32), small_all=pltpu.VMEM((groups,) + small.shape, f32),
        normed=pltpu.VMEM((tokens, width), bf16), gather_sems=Gather.sems(dma),
        m_sems=[dma((TP - 1,))] * 2, w_sems=[dma((TP - 1,))] * 2, own_sem=dma,
        own=pltpu.VMEM((depth, 2 * half), bf16), s0=spread(), s1=spread(),
        sm=[spread() for _ in range(TP)], sw=[spread() for _ in range(TP)],
    )

    def body(r):
        x, core, zh, q = place()
        me = core * WAYS + q
        peers = tp_peers()
        side, far = dp_peers(zh_size)
        greet([p[0] for p in peers] + [side] + [f[0] for f in far])

        def row(xx, zz, rank):
            return ((xx * 2 + rank // WAYS) * zh_size + zz) * WAYS + lax.rem(rank, WAYS)

        def views(out, rank):
            return lambda xx, zz: out.at[row(xx, zz, rank)]

        here = row(x, zh, me)
        miscs = []
        for i, (target, rank, _) in enumerate(peers):
            miscs.append(remote(r.misc, r.misc_all.at[here], r.m_sems[0].at[i], r.m_sems[1].at[i], target))
            miscs[-1].start()
        misc_moves = [Spread(zh_size, r.misc, views(r.misc_all, me), r.sm[0])]
        misc_moves[0].start()
        smalls = Spread(zh_size, r.small, lambda xx, zz: r.small_all.at[xx * zh_size + zz], r.s0)
        smalls.start()
        wins = Turn(zh_size, r.win, 0, r.win_all, lambda rank: row(x, zh, rank), r.w_sems)
        wins.start()
        own_pieces = [
            pltpu.make_async_copy(src, dst, r.own_sem)
            for src, dst in turn_pieces(zh_size, r.win, 0, r.own, me)
        ]
        for copy in own_pieces:
            copy.start()
        pltpu.make_async_copy(r.own, r.own, r.own_sem).wait()
        win_moves = [Spread(zh_size, r.own, views(r.win_all, me), r.sw[0])]
        for i, (_, _, source) in enumerate(peers):
            view = views(r.win_all, source)
            win_moves.append(Spread(zh_size, view(x, zh), view, r.sw[i + 1], keep=False))
        mats_move = Spread(zh_size, r.mats.at[0], lambda xx, zz: r.mats_all.at[xx * zh_size + zz], r.s1)

        def step(i):
            if i >= 1:
                wins.arrived(i - 1)
            if i >= 2:
                win_moves[i - 2].onward()
            win_moves[i].start()

        step(0)
        for i, (_, _, source) in enumerate(peers):
            miscs[i].wait_recv()
            view = views(r.misc_all, source)
            misc_moves.append(Spread(zh_size, view(x, zh), view, r.sm[i + 1], keep=False))
            misc_moves[-1].start()
        step(1)
        for move in misc_moves:
            move.onward()
        smalls.onward()
        for move in misc_moves:
            move.finish()
        for l in range(LAYERS):
            r.gains[l : l + 1, :] = side_by_side(
                [r.misc_all[d, l : l + 1, :] for d in range(count)], gains
            )
        r.gains[LAYERS:, :] = jnp.zeros((8 - LAYERS, width), f32)
        stream = r.h[...]
        r.normed[...] = (stream * rms(stream) * r.gains[0:1, :]).astype(bf16)
        rows = Gather(r.normed, r.xg, r.gather_sems)
        rows.start()
        step(2)
        mats_move.start()
        total = r.misc_all[0, LAYERS : LAYERS + 1, :]
        for d in range(1, count):
            total = total + r.misc_all[d, LAYERS : LAYERS + 1, :]
        inverse = count / total
        for rank in range(TP):
            r.scale[rank : rank + 1, :] = r.misc_all[row(x, zh, rank), LAYERS : LAYERS + 1, :] * inverse
        own = (r.misc[LAYERS : LAYERS + 1, :] * inverse)[:, :1]
        grad = r.cot[...] * own
        r.grad[...] = grad
        r.gout[...] = grad.astype(bf16)
        step(3)
        smalls.finish()
        for l in range(LAYERS):
            r.vec[8 * l : 8 * (l + 1), :] = side_by_side(
                [r.small_all[g, 8 * l : 8 * (l + 1), :] for g in range(groups)], share
            )
        step(4)
        mats_move.onward()
        rows.relay()
        step(5)
        step(6)
        rows.rest()
        step(7)
        win_moves[6].onward()
        win_moves[7].onward()
        wins.sent()
        for copy in miscs:
            copy.wait_send()
        for move in win_moves + [mats_move]:
            move.finish()
        rows.finish()

    return call(body, 1, ins, outs, scratch)


def at_block(b, size):
    return pl.ds(pl.multiple_of(b * size, size), size)


def conv_of(entry, vec, row, size, c):
    cols = slice(c * LANES, (c + 1) * LANES)
    conv = vec[CONV : CONV + 1, cols]
    for j in range(CONV):
        conv = conv + vec[j : j + 1, cols] * entry[c, pl.ds(pl.multiple_of(row + TP * j, TP), size), :]
    return conv


def wide_of(ref, rows, parts):
    return jnp.concatenate([ref[c, rows, :] for c in range(parts)], axis=1)


def row_sum(value):
    return jnp.sum(value.reshape(-1, TP, value.shape[1]), axis=0)


def square_sum(kq):
    lane = lanes_of(kq.shape)
    return jnp.sum(jnp.where(lane < STATE, kq * kq, 0.0), axis=1, keepdims=True)


def forward_layer(zh_size, layer, xg, win, mats, wout, vec, scale, gout=None, nxt=None):
    tokens, width = xg.shape[1], xg.shape[2]
    half = win.shape[1] // 2
    parts = half // LANES
    rows = tokens * TP
    size = STEPS * TP
    blocks = rows // size
    halo = (CONV - 1) * TP
    dma = pltpu.SemaphoreType.DMA
    last = nxt is None
    groups = 2 * zh_size
    ins = dict(
        xg=(xg, EARLY), win=(win, EARLY), mats=(mats, EARLY), wout=(wout, HB), vec=(vec, VM),
        scale=(scale, VM), e=(spreader(), EARLY),
    )
    outs = dict(
        entry=(struct(2 * parts, halo + rows, LANES), LATE), beta=(struct(parts, rows, LANES), LATE),
        kq=(struct(rows, LANES), LATE), proj=(struct(TP, size, 2 * LANES, dtype=bf16), LATE),
        y=(struct(parts, rows, LANES), LATE), keep=(struct(blocks, STATE, parts, TP, LANES), LATE),
        mixed=(struct(TP, tokens, half, dtype=bf16), LATE), stats=(struct(2, TP, LANES), VM),
    )
    scratch = dict(
        act=pltpu.VMEM((parts, rows, LANES), f32), step=pltpu.VMEM((parts, rows, LANES), f32),
        payload=pltpu.VMEM((TP, size, 2 * LANES), bf16), parts=pltpu.VMEM((TP - 1, size, 2 * LANES), bf16),
        own=pltpu.VMEM((size, 2 * LANES), f32),
        state=pltpu.VMEM((STATE, parts, TP, LANES), f32), wide=pltpu.VMEM((size, 32 * LANES), f32),
        sum_sems=Sum.sems(dma),
    )
    outs.update(wout_all=(struct(groups, *wout.shape[1:], dtype=bf16), LATE))
    scratch.update(d0=Spread.sems(dma, zh_size))
    if last:
        ins.update(gout=(gout, VM))
        outs.update(
            gog=(struct(TP, tokens, width, dtype=bf16), HB), part=(struct(TP, tokens, width, dtype=bf16), LATE)
        )
        scratch.update(gather_sems=Gather.sems(dma))
    if not last:
        win1 = nxt.win
        depth = win1.shape[-2]
        ins.update(h=(nxt.h, EARLY), gain=(nxt.gain, VM), win1=(win1, HB), mats1=(nxt.mats, HB))
        outs.update(
            result=(struct(tokens, width), VM),
            win1_all=(struct(2, 2, zh_size, WAYS, depth, 2 * half, dtype=bf16), HB),
            mats1_all=(struct(groups, *nxt.mats.shape[1:], dtype=bf16), HB),
            xg1=(struct(TP, tokens, width, dtype=bf16), HB),
        )
        scratch.update(
            normed=pltpu.VMEM((tokens, width), bf16), gather_sems=Gather.sems(dma),
            part=pltpu.VMEM((TP, tokens, width), bf16), scatter_buf=Scatter.buffers((tokens, width)),
            scatter_sems=Scatter.sems(dma),
            turned=pltpu.VMEM((TP, depth, 2 * half), bf16), l_sems=[dma((TP - 1,)), dma((TP - 1,))], l_own=dma,
            d1=Spread.sems(dma, zh_size), d2=Spread.sems(dma, zh_size), d3=Spread.sems(dma, zh_size),
        )

    def body(r):
        r.load()
        side, far = dp_peers(zh_size)
        greet([p[0] for p in tp_peers()] + [side] + [f[0] for f in far])
        entry, act, step, beta, kq, y = r.entry, r.act, r.step, r.beta, r.kq, r.y
        vec = r.vec.at[8 * layer : 8 * (layer + 1)]
        index = lambda ref: lambda xx, zz: ref.at[xx * zh_size + zz]
        early = Spread(zh_size, r.wout.at[layer], index(r.wout_all), r.d0)
        early.start()
        if last:
            gouts = Gather(r.gout, r.gog, r.gather_sems)
        else:
            turned = Turn(zh_size, r.win1, layer + 1, r.turned, lambda rank: rank, r.l_sems)
            turned.start()
            for src, dst in turned.pieces(turned.me):
                pltpu.make_async_copy(src, dst, r.l_own).start()
            moves = [Spread(zh_size, r.mats1.at[layer + 1], index(r.mats1_all), r.d3)]
            for k in range(2):
                view = lambda xx, zz, k=k: r.win1_all.at[xx, k, zz]
                src = r.turned.at[k * WAYS : (k + 1) * WAYS]
                moves.append(Spread(zh_size, src, view, (r.d1 if k == 0 else r.d2)))

        r.need.xg()
        r.need.win()
        entry[:, :halo, :] = jnp.zeros((2 * parts, halo, LANES), f32)
        tile = 2 * LANES
        for p in range(TP // 2):

            def columns(n, carry, p=p):
                cols = at_block(n, tile)
                out = jnp.dot(
                    r.xg[2 * p : 2 * p + 2].reshape(2 * tokens, width), r.win[:, cols],
                    preferred_element_type=f32,
                )
                for j in range(2):
                    for c in range(2):
                        entry[2 * n + c, pl.ds(halo + 2 * p + j, tokens, stride=TP), :] = out[
                            j * tokens : (j + 1) * tokens, c * LANES : (c + 1) * LANES
                        ]
                return carry

            lax.fori_loop(0, 2 * half // tile, columns, 0)
        r.put.entry()
        r.need.mats()
        total = Sum(r.payload, r.parts, r.proj, r.sum_sems)

        def project(b, carry):
            rs = at_block(b, size)
            for c in range(parts):
                conv = conv_of(entry, vec, b * size, size, c)
                act[c, rs, :] = (conv * jax.nn.sigmoid(conv)).astype(bf16).astype(f32)
            out = jnp.dot(
                wide_of(act, rs, parts).astype(bf16), r.mats[:, RANK:], preferred_element_type=f32
            )
            r.payload[b] = encode(out)

            @pl.when(b == total.me)
            def _():
                r.own[...] = out

            return carry

        lax.fori_loop(0, blocks, project, 0)
        total.start()
        if not last:
            for i in range(TP - 1):
                turned.arrived(i)
            mine = r.turned.at[turned.me]
            pltpu.make_async_copy(mine, mine, r.l_own).wait()
            moves[0].start()
            moves[1].start()
        total.middle(r.own[...])
        total.finish()
        r.put.proj()
        if last:
            gouts.start()
        else:
            turned.sent()
            moves[2].start()

        r.stats[...] = jnp.zeros((2, TP, LANES), f32)

        def rates(b, carry):
            rs = at_block(b, size)
            tail = decode(r.proj[b])[:, RANK:]
            keys = tail + pltpu.roll(tail, 32, 1) + pltpu.roll(tail, 64, 1)
            kq[rs, :] = keys
            norm = square_sum(keys)
            pre = dot(r.proj[b, :, :RANK], r.mats[:, :RANK], ((1,), (1,)))
            for c in range(parts):
                cols = slice(c * LANES, (c + 1) * LANES)
                rate = jax.nn.sigmoid(pre[:, cols] + vec[CONV + 1 : CONV + 2, cols])
                beta[c, rs, :] = rate
                step[c, rs, :] = rate / (1.0 + rate * norm)
                r.stats[0] += row_sum(rate)
                r.stats[1] = jnp.maximum(
                    r.stats[1], jnp.max(rate.reshape(-1, TP, LANES), axis=0)
                )
            return carry

        lax.fori_loop(0, blocks, rates, 0)
        r.put.beta()
        r.put.kq()
        r.need.e()
        r.stats[0] = r.stats[0] * r.scale[...]
        r.stats[1] = r.stats[1] * r.scale[...]

        lane = lanes_of((size, LANES))
        state, wide = r.state, r.wide
        state[...] = jnp.zeros_like(state)

        def block(b, carry):
            r.keep[b] = state[...]
            wide[...] = jnp.dot(spread_keys(kq[at_block(b, size), :], lane), r.e[...], preferred_element_type=f32)

            def one(j, carry):
                t = at_block(b * STEPS + j, TP)
                w = at_block(j, TP)
                acts = [act[c, t, :] for c in range(parts)]
                steps = [step[c, t, :] for c in range(parts)]
                sums = [None] * parts
                for n in range(STATE):
                    key = wide[w, n * LANES : (n + 1) * LANES]
                    query = wide[w, (STATE + n) * LANES : (STATE + n + 1) * LANES]
                    for c in range(parts):
                        s = state[n, c]
                        s = s + (steps[c] * key) * (acts[c] - key * s)
                        state[n, c] = s
                        sums[c] = s * query if sums[c] is None else sums[c] + s * query
                for c in range(parts):
                    y[c, t, :] = sums[c]
                return carry

            lax.fori_loop(0, STEPS, one, 0)
            rs = at_block(b, size)
            here = pl.ds(pl.multiple_of(b * STEPS, STEPS), STEPS)
            for c in range(parts):
                cols = slice(c * LANES, (c + 1) * LANES)
                gate = entry[parts + c, pl.ds(pl.multiple_of(b * size + halo, TP), size), :]
                skip = vec[CONV + 2 : CONV + 3, cols]
                step[c, rs, :] = (y[c, rs, :] + skip * act[c, rs, :]) * (gate * jax.nn.sigmoid(gate))
                for s in range(TP):
                    r.mixed[s, here, cols] = step[c, pl.ds(b * size + s, STEPS, stride=TP), :].astype(bf16)
            return carry

        early.onward()
        lax.fori_loop(0, blocks // 2, block, 0)
        if last:
            gouts.relay()
        else:
            moves[0].onward()
        lax.fori_loop(blocks // 2, blocks, block, 0)
        early.finish()
        for start in (r.put.y, r.put.keep, r.put.mixed, r.put.wout_all):
            start()
        weight = lambda: r.wout_all[...].reshape(half, width)
        if last:

            def plain(s, carry):
                two = r.mixed[pl.ds(2 * s, 2)].reshape(2 * tokens, half)
                out = dot(two, weight(), ((1,), (0,))).astype(bf16)
                r.part[pl.ds(2 * s, 2)] = out.reshape(2, tokens, width)
                return carry

            lax.fori_loop(0, TP // 4, plain, 0)
            gouts.rest()
            lax.fori_loop(TP // 4, TP // 2, plain, 0)
            r.put.part()
            gouts.finish()
            r.done()
            return
        scatter = Scatter(r.part, r.scatter_buf, r.scatter_sems)
        out_partial(scatter, r.part, r.mixed, weight)
        moves[1].onward()
        r.need.h()
        stream = r.h[...] + scatter.total()
        r.result[...] = stream
        r.normed[...] = (stream * rms(stream) * r.gain[layer + 1 : layer + 2, :]).astype(bf16)
        spread = Gather(r.normed, r.xg1, r.gather_sems)
        spread.start()
        spread.relay()
        moves[2].onward()
        spread.rest()
        spread.finish()
        for move in moves:
            move.finish()
        r.done()

    return call(body, 7 if last else 6, ins, outs, scratch)


def out_partial(scatter, part, left, right, turned=False):
    contract = ((1,), (1,)) if turned else ((1,), (0,))
    for i in range(4):
        slots = [core * WAYS + scatter.turns[i] for core in (1 - scatter.core, scatter.core)]
        rows = left.shape[1]
        both = dot(jnp.concatenate([left[slot] for slot in slots], axis=0), right(), contract).astype(bf16)
        part[slots[0]] = both[:rows]
        part[slots[1]] = both[rows:]
        scatter.to_sibling(i)
        if i >= 1:
            scatter.across(i - 1)
    scatter.sums()


class Reduce:
    @staticmethod
    def sems(dma, zh_size):
        far = max(1, zh_size - 1)
        return [dma, dma, dma((far,)), dma((far,))]

    @staticmethod
    def buffers(zh_size, block):
        return [
            pltpu.VMEM((zh_size,) + block, bf16), pltpu.VMEM((zh_size,) + block, bf16),
            pltpu.VMEM((max(1, zh_size - 1),) + block, bf16),
        ]

    def __init__(self, zh_size, src, buffers, sems):
        self.zh_size, self.src = zh_size, src
        self.near, self.mine, self.buf = buffers
        self.x_send, self.x_recv, self.z_send, self.z_recv = sems
        self.x, _, self.zh, _ = place()
        self.side, self.far = dp_peers(zh_size)

    def start(self):
        half = self.src.at[pl.ds((1 - self.x) * self.zh_size, self.zh_size)]
        self.over = remote(half, self.near, self.x_send, self.x_recv, self.side)
        self.over.start()

    def middle(self):
        self.over.wait_recv()
        for k in range(self.zh_size):
            self.mine[k] = (
                self.src[self.x * self.zh_size + k].astype(f32) + self.near[k].astype(f32)
            ).astype(bf16)
        self.along = [
            remote(self.mine.at[to_z], self.buf.at[k], self.z_send.at[k], self.z_recv.at[k], target)
            for k, (target, to_z, _) in enumerate(self.far)
        ]
        for copy in self.along:
            copy.start()

    def total(self):
        value = self.src[self.x * self.zh_size + self.zh].astype(f32) + self.near[self.zh].astype(f32)
        for k in range(self.zh_size - 1):
            self.along[k].wait_recv()
            value = value + self.buf[k].astype(f32)
        self.over.wait_send()
        for copy in self.along:
            copy.wait_send()
        return value


def backward_layer(zh_size, layer, kept, gog, wout, mats, vec, xg, win, gain, h, grad, late=None, part=None):
    tokens, width = xg.shape[1], xg.shape[2]
    half = win.shape[1] // 2
    parts = half // LANES
    rows = tokens * TP
    size = STEPS * TP
    blocks = rows // size
    halo = (CONV - 1) * TP
    groups = 2 * zh_size
    share = half // groups
    deep = width // (2 * groups)
    far = max(1, zh_size - 1)
    dma = pltpu.SemaphoreType.DMA
    onward = part is not None
    ins = dict(entry=(kept.entry, EARLY), kq=(kept.kq, EARLY), beta=(kept.beta, EARLY), proj=(kept.proj, EARLY))
    ins.update(
        mats=(mats, EARLY), wout=(wout, HB), vec=(vec, VM), gain=(gain, VM), h=(h, EARLY), grad=(grad, EARLY),
        mixed=(kept.mixed, HB), e=(spreader(), EARLY), fold=(folder(), EARLY), keep=(kept.keep, HB), gouts=(gog, HB), y=(kept.y, HB), xg=(xg, HB), win=(win, HB),
    )
    outs = dict(
        prev=(struct(tokens, width), VM), ginner=(struct(groups, 2, deep, half, dtype=bf16), LATE),
        near=(struct(zh_size, 2, deep, half, dtype=bf16), HB), ggate=(struct(2, deep, half, dtype=bf16), VM), gwout=(struct(share, width), VM),
        gmats=(struct(half, 3 * LANES, dtype=bf16), VM), gvec=(struct(8, half), VM),
        ggain=(struct(1, width), VM),
    )
    block_f32 = pltpu.VMEM((parts, rows, LANES), f32)
    scratch = dict(
        a=pltpu.VMEM((TP, tokens, width), bf16), b=pltpu.VMEM(win.shape, bf16),
        gs=block_f32, act=block_f32, gact=block_f32,
        step=pltpu.VMEM((parts, rows + halo, LANES), f32),
        states=pltpu.VMEM((STEPS + 1, STATE, parts, TP, LANES), f32),
        lam=pltpu.VMEM((STATE, parts, TP, LANES), f32), wide=pltpu.VMEM((size, 32 * LANES), f32),
        gstep=pltpu.VMEM((parts, size, LANES), f32),
        gentry=pltpu.VMEM((TP, tokens, 2 * half), bf16),
        payload=pltpu.VMEM((TP, size, 2 * LANES), bf16), parts=pltpu.VMEM((TP - 1, size, 2 * LANES), bf16),
        total=pltpu.VMEM((TP, size, 2 * LANES), bf16), own=pltpu.VMEM((size, 2 * LANES), f32),
        sums=pltpu.VMEM((8, parts, TP, LANES), f32),
        grate=pltpu.VMEM((half, LANES), f32), gselect=pltpu.VMEM((half, 2 * LANES), f32),
        gwo=pltpu.VMEM((groups, share, width), bf16), gwg=pltpu.VMEM((groups, 2, deep, half), bf16),
        gate_buf=Reduce.buffers(zh_size, (2, deep, half)), gate_sems=Reduce.sems(dma, zh_size),
        keeps=pltpu.VMEM((2, STATE, parts, TP, LANES), f32), keep_sems=dma((2,)),
        scatter_buf=Scatter.buffers((tokens, width)), reduce_buf=Reduce.buffers(zh_size, (share, width)),
        sum_sems=Sum.sems(dma), scatter_sems=Scatter.sems(dma), reduce_sems=Reduce.sems(dma, zh_size),
        loads=dma((7,)), over=[dma, dma],
    )
    if onward:
        outs.update(gog=(struct(TP, tokens, width, dtype=bf16), HB))
        ins.update(part=(part, HB))
        outs.update(parts_all=(struct(*part.shape, dtype=bf16), HB))
        scratch.update(part_sems=[dma((TP - 1,)), dma((TP - 1,)), dma])
        scratch.update(gout=pltpu.VMEM((tokens, width), bf16), gather_sems=Gather.sems(dma))
    if late is not None:
        ins.update(late_in=(late, HB))
        outs.update(late=(struct(far, *late.shape[1:], dtype=bf16), HB))
        scratch.update(late_sems=[dma((far,)), dma((far,))])

    def body(r):
        x, core, zh, q = place()
        side, far_ones = dp_peers(zh_size)
        greet([p[0] for p in tp_peers()] + [side] + [f[0] for f in far_ones])
        entry, act, step, beta, kq = r.entry, r.act, r.step, r.beta, r.kq
        gs, gact, sums, gstep = r.gs, r.gact, r.sums, r.gstep
        vec = r.vec.at[8 * layer : 8 * (layer + 1)]
        loads = [
            pltpu.make_async_copy(src, dst, r.loads.at[i])
            for i, (src, dst) in enumerate(
                (
                    (r.gouts, r.a), (r.mixed, r.gentry.at[:, :, :half]),
                    (r.wout.at[:, : 2 * half], r.b.at[:half]), (r.wout.at[:, 2 * half :], r.b.at[half : 2 * half]),
                    (r.y, gact), (r.xg, r.a), (r.win, r.b),
                )
            )
        ]
        for copy in loads[:4]:
            copy.start()
        r.load()
        loads[4].start()
        passed = []
        if onward:
            me = core * WAYS + q
            for i, (target, rank, _) in enumerate(tp_peers()):
                copy = remote(
                    r.part.at[rank], r.parts_all.at[me], r.part_sems[0].at[i], r.part_sems[1].at[i], target
                )
                copy.start()
                passed.append(copy)
            passed.append(pltpu.make_async_copy(r.part.at[me], r.parts_all.at[me], r.part_sems[2]))
            passed[-1].start()
        if late is not None:
            for k, (target, to_z, _) in enumerate(far_ones):
                copy = remote(
                    r.late_in.at[to_z], r.late.at[k], r.late_sems[0].at[k], r.late_sems[1].at[k], target
                )
                copy.start()
                passed.append(copy)
        sums[...] = jnp.zeros_like(sums)
        r.grate[...] = jnp.zeros_like(r.grate)
        r.gselect[...] = jnp.zeros_like(r.gselect)

        loads[0].wait()
        loads[1].wait()

        def outer(c, carry):
            left = r.gentry[:, :, at_block(c, LANES)].reshape(rows, LANES)
            out = dot(left, r.a[...].reshape(rows, width), ((0,), (0,))).astype(bf16)
            each = LANES // share
            r.gwo[pl.ds(c * each, each)] = out.reshape(each, share, width)
            return carry

        lax.fori_loop(0, parts, outer, 0)
        reduce = Reduce(zh_size, r.gwo, r.reduce_buf, r.reduce_sems)
        reduce.start()
        loads[2].wait()
        loads[3].wait()
        for p in range(TP // 2):

            def columns(n, carry, p=p):
                out = 0.0
                for k in range(2):
                    left = r.a[2 * p : 2 * p + 2, :, 2 * half * k : 2 * half * (k + 1)].reshape(2 * tokens, 2 * half)
                    right = r.b[pl.ds(pl.multiple_of(half * k + n * 2 * LANES, 2 * LANES), 2 * LANES), :]
                    out = out + dot(left, right, ((1,), (1,)))
                for j in range(2):
                    for c in range(2):
                        gs[2 * n + c, pl.ds(2 * p + j, tokens, stride=TP), :] = out[
                            j * tokens : (j + 1) * tokens, c * LANES : (c + 1) * LANES
                        ]
                return carry

            lax.fori_loop(0, half // (2 * LANES), columns, 0)
        loads[5].start()
        loads[6].start()
        r.need.entry()
        r.need.kq()
        r.need.beta()

        def again(b, carry):
            rs = at_block(b, size)
            norm = square_sum(kq[rs, :])
            for c in range(parts):
                conv = conv_of(entry, vec, b * size, size, c)
                act[c, rs, :] = (conv * jax.nn.sigmoid(conv)).astype(bf16).astype(f32)
                rate = beta[c, rs, :]
                step[c, rs, :] = rate / (1.0 + rate * norm)
            return carry

        lax.fori_loop(0, blocks, again, 0)
        loads[4].wait()

        def gates(b, carry):
            rs = at_block(b, size)
            here = pl.ds(pl.multiple_of(b * STEPS, STEPS), STEPS)
            for c in range(parts):
                cols = slice(c * LANES, (c + 1) * LANES)
                gate = entry[parts + c, pl.ds(pl.multiple_of(b * size + halo, TP), size), :]
                sig = jax.nn.sigmoid(gate)
                g = gs[c, rs, :]
                a = act[c, rs, :]
                down = g * (gate * sig)
                gstep[c] = g * (gact[c, rs, :] + vec[CONV + 2 : CONV + 3, cols] * a) * (
                    sig * (1.0 + gate * (1.0 - sig))
                )
                gs[c, rs, :] = down
                sums[CONV + 2, c] += row_sum(down * a)
                for s in range(TP):
                    r.gentry[s, here, half + c * LANES : half + (c + 1) * LANES] = gstep[
                        c, pl.ds(s, STEPS, stride=TP), :
                    ].astype(bf16)
            return carry

        lax.fori_loop(0, blocks, gates, 0)
        loads[5].wait()
        tile = 2 * LANES

        def outer_in(out_ref, first, i, carry):
            left = r.a[:, :, at_block(i, tile)].reshape(rows, tile)
            out = dot(left, r.gentry[:, :, first : first + half].reshape(rows, half), ((0,), (0,))).astype(bf16)
            each = tile // deep
            for e in range(each):
                d = i * each + e
                xx, cc, zz = d // (2 * zh_size), lax.rem(d // zh_size, 2), lax.rem(d, zh_size)
                out_ref[xx * zh_size + zz, cc] = out[e * deep : (e + 1) * deep]
            return carry

        lax.fori_loop(0, width // tile, lambda i, k: outer_in(r.gwg, half, i, k), 0)
        gate_reduce = Reduce(zh_size, r.gwg, r.gate_buf, r.gate_sems)

        lane = lanes_of((size, LANES))
        states, lam, wide = r.states, r.lam, r.wide
        lam[...] = jnp.zeros_like(lam)
        plus = lambda a, b: b if a is None else a + b
        total = Sum(r.payload, r.parts, r.total, r.sum_sems)

        def block(bi, carry):
            b = blocks - 1 - bi
            rs = at_block(b, size)
            slot = lax.rem(b, 2)
            pltpu.make_async_copy(r.keep.at[b], r.keeps.at[slot], r.keep_sems.at[slot]).wait()

            @pl.when(b > 0)
            def _():
                ahead = pltpu.make_async_copy(r.keep.at[b - 1], r.keeps.at[1 - slot], r.keep_sems.at[1 - slot])
                ahead.start()

            states[0] = r.keeps[slot]
            wide[...] = jnp.dot(spread_keys(kq[rs, :], lane), r.e[...], preferred_element_type=f32)

            def replay(j, carry):
                t, w = at_block(b * STEPS + j, TP), at_block(j, TP)
                acts = [act[c, t, :] for c in range(parts)]
                steps = [step[c, t, :] for c in range(parts)]
                for n in range(STATE):
                    key = wide[w, n * LANES : (n + 1) * LANES]
                    for c in range(parts):
                        s = states[j, n, c]
                        states[j + 1, n, c] = s + (steps[c] * key) * (acts[c] - key * s)
                return carry

            lax.fori_loop(0, STEPS, replay, 0)

            def back(jj, carry):
                j = STEPS - 1 - jj
                t, w = at_block(b * STEPS + j, TP), at_block(j, TP)
                acts = [act[c, t, :] for c in range(parts)]
                steps = [step[c, t, :] for c in range(parts)]
                gsums = [gs[c, t, :] for c in range(parts)]
                first, second = [None] * parts, [None] * parts
                for n in range(STATE):
                    kcols, qcols = slice(n * LANES, (n + 1) * LANES), slice((STATE + n) * LANES, (STATE + n + 1) * LANES)
                    key, query = wide[w, kcols], wide[w, qcols]
                    square = key * key
                    key_term, query_term = None, None
                    for c in range(parts):
                        before, after = states[j, n, c], states[j + 1, n, c]
                        grad = lam[n, c] + gsums[c] * query
                        u = key * before
                        d = acts[c] - u
                        gk = grad * key
                        sg = steps[c] * grad
                        first[c] = plus(first[c], gk * d)
                        second[c] = plus(second[c], gk)
                        key_term = plus(key_term, sg * (d - u))
                        query_term = plus(query_term, gsums[c] * after)
                        lam[n, c] = grad - sg * square
                    wide[w, kcols] = key_term
                    wide[w, qcols] = query_term
                for c in range(parts):
                    gstep[c, w, :] = first[c]
                    gact[c, t, :] = steps[c] * second[c]
                return carry

            lax.fori_loop(0, STEPS, back, 0)
            terms = wide[...]
            high = terms.astype(bf16)
            low = (terms - high.astype(f32)).astype(bf16)
            gkq = jnp.dot(high, r.fold[...], preferred_element_type=f32) + jnp.dot(
                low, r.fold[...], preferred_element_type=f32
            )
            keys = kq[rs, :]
            norm = square_sum(keys)
            gnorm = jnp.zeros((size, 1), f32)
            grates = []
            for c in range(parts):
                cols = slice(c * LANES, (c + 1) * LANES)
                rate = beta[c, rs, :]
                g = gstep[c]
                inverse = 1.0 + rate * norm
                inverse = 1.0 / (inverse * inverse)
                gnorm = gnorm - jnp.sum(g * (rate * rate * inverse), axis=1, keepdims=True)
                grate = g * inverse * rate * (1.0 - rate)
                sums[CONV + 1, c] += row_sum(grate)
                grates.append(grate.astype(bf16))
                gact[c, rs, :] += vec[CONV + 2 : CONV + 3, cols] * gs[c, rs, :]
            grate = jnp.concatenate(grates, axis=1)
            r.grate[...] += dot(grate, r.proj[b, :, :RANK], ((0,), (0,)))
            grank = dot(grate, r.mats[:, :RANK], ((1,), (0,)))
            gkq = gkq + jnp.where(lane < STATE, 2.0 * keys * gnorm, 0.0)
            out = jnp.concatenate([grank, gkq], axis=1)
            r.payload[b] = encode(out)

            @pl.when(b == total.me)
            def _():
                r.own[...] = out

            return carry

        for wait in (r.need.proj, r.need.mats, r.need.e, r.need.fold):
            wait()
        last = (blocks - 1) % 2
        pltpu.make_async_copy(r.keep.at[blocks - 1], r.keeps.at[last], r.keep_sems.at[last]).start()
        lax.fori_loop(0, blocks // 2, block, 0)
        reduce.middle()
        gate_reduce.start()
        lax.fori_loop(blocks // 2, blocks, block, 0)
        total.start()
        total.middle(r.own[...])
        total.finish()
        gate_reduce.middle()
        step[:, rows:, :] = jnp.zeros((parts, halo, LANES), f32)
        gconv = step

        def convs(b, carry):
            rs = at_block(b, size)
            gp = r.total[b]
            gp = jnp.where(lanes_of(gp.shape) < RANK + 2 * STATE, gp.astype(f32), 0.0).astype(bf16)
            r.gselect[...] += dot(wide_of(act, rs, parts).astype(bf16), gp, ((0,), (0,)))
            more = dot(gp, r.mats[:, RANK:], ((1,), (1,)))
            for c in range(parts):
                conv = conv_of(entry, vec, b * size, size, c)
                sig = jax.nn.sigmoid(conv)
                g = (gact[c, rs, :] + more[:, c * LANES : (c + 1) * LANES]) * (sig * (1.0 + conv * (1.0 - sig)))
                gconv[c, rs, :] = g
                sums[CONV, c] += row_sum(g)
                for j in range(CONV):
                    inner = entry[c, pl.ds(pl.multiple_of(b * size + TP * j, TP), size), :]
                    sums[j, c] += row_sum(g * inner)
            return carry

        lax.fori_loop(0, blocks, convs, 0)

        def inners(b, carry):
            rs = at_block(b, size)
            here = pl.ds(pl.multiple_of(b * STEPS, STEPS), STEPS)
            for c in range(parts):
                cols = slice(c * LANES, (c + 1) * LANES)
                value = None
                for j in range(CONV):
                    at = pl.ds(pl.multiple_of(b * size + TP * (CONV - 1 - j), TP), size)
                    value = plus(value, vec[j : j + 1, cols] * gconv[c, at, :])
                gs[c, rs, :] = value
                for s in range(TP):
                    at = pl.ds(b * size + s, STEPS, stride=TP)
                    r.gentry[s, here, cols] = gs[c, at, :].astype(bf16)
            return carry

        lax.fori_loop(0, blocks, inners, 0)
        lax.fori_loop(0, width // tile, lambda i, k: outer_in(r.ginner, 0, i, k), 0)
        over = remote(
            r.ginner.at[pl.ds((1 - x) * zh_size, zh_size)], r.near, r.over[0], r.over[1], side
        )
        over.start()
        r.put.ginner()
        loads[6].wait()
        scatter = Scatter(r.a, r.scatter_buf, r.scatter_sems)
        out_partial(scatter, r.a, r.gentry, lambda: r.b[...], turned=True)
        r.gmats[:, :RANK] = r.grate[...].astype(bf16)
        r.gmats[:, RANK:] = r.gselect[...].astype(bf16)
        for j in range(8):
            for c in range(parts):
                r.gvec[j : j + 1, c * LANES : (c + 1) * LANES] = jnp.sum(sums[j, c], axis=0, keepdims=True)
        r.gwout[...] = reduce.total()
        r.ggate[...] = gate_reduce.total().astype(bf16)
        gnormed = scatter.total()
        r.need.h()
        r.need.grad()
        stream = r.h[...]
        scale = rms(stream)
        r.ggain[...] = jnp.sum(gnormed * stream * scale, axis=0, keepdims=True)
        scaled = gnormed * r.gain[layer : layer + 1, :]
        grad = r.grad[...] + scale * scaled - stream * (scale * scale * scale) * jnp.mean(
            stream * scaled, axis=-1, keepdims=True
        )
        r.prev[...] = grad
        if onward:
            r.gout[...] = grad.astype(bf16)
            spread = Gather(r.gout, r.gog, r.gather_sems)
            spread.start()
            spread.relay()
            spread.rest()
            spread.finish()
        for copy in passed:
            copy.wait()
        over.wait()
        r.done()

    return call(body, 9 if onward else 8, ins, outs, scratch)


def closing(zh_size, inner, near, mats, small, stats, gain, turns, share, width, select):
    groups = 2 * zh_size
    count = groups * TP
    far_n = max(1, zh_size - 1)
    dma = pltpu.SemaphoreType.DMA
    depth, half = inner.shape[3] // WAYS, inner.shape[4]
    gains = width // count
    every = (2, zh_size) + stats.shape
    v = pltpu.VMEM
    ins = dict(
        inner=(inner, VM), near=(near, VM), mats=(mats, VM), small=(small, VM), stats=(stats, VM), gain=(gain, VM),
        t0=(turns[0], VM), t1=(turns[1], VM), t2=(turns[2], VM),
    )
    outs = dict(
        gin=(struct(LAYERS, depth, 2 * count * share), VM), gselect=(struct(LAYERS, share, select), VM),
        grate=(struct(LAYERS, RANK, share), VM),
        ggain=(struct(LAYERS, gains), VM), gtaps=(struct(LAYERS, CONV, share), VM), gshift=(struct(LAYERS, share), VM),
        grate_shift=(struct(LAYERS, share), VM), gskip=(struct(LAYERS, share), VM), stats_all=(struct(*stats.shape), VM),
    )

    def chunk(shape, dtype):
        return [
            v(shape[1:], dtype), v((far_n,) + shape[2:], dtype), dma((far_n,)), dma((far_n,)), v(shape[1:], dtype), dma, dma
        ]

    piece = inner.shape[:2] + inner.shape[3:]
    scratch = dict(
        vectors=v(small.shape, f32), stats_v=v(every, f32), stats_t=v((TP - 1,) + stats.shape, f32),
        gain_t=v((TP - 1,) + gain.shape[1:], f32), win_t=v((2, WAYS, depth, half), bf16),
        total=v(small.shape[2:], f32),
        g_sems=[dma((TP - 1,))] * 2, s_sems=[dma((TP - 1,))] * 2,
    )
    scratch.update(
        boxes=v((4, TP, depth, half), bf16), turn_sems=[[dma((TP - 1,)), dma((TP - 1,))] for _ in range(4)],
        chunks=[chunk(piece, bf16), chunk(piece, bf16), chunk(mats.shape, bf16), chunk(small.shape, f32), chunk(every, f32)],
    )

    def body(r):
        x, core, zh, q = place()
        me = core * WAYS + q
        peers = tp_peers()
        side, far = dp_peers(zh_size)
        greet([p[0] for p in peers] + [side] + [f[0] for f in far])
        sent, full = [], []

        def join(a, b, peaks):
            a, b = a.astype(f32), b.astype(f32)
            if peaks:
                line = lax.broadcasted_iota(jnp.int32, a.shape, len(a.shape) - 2)
                return jnp.where(line < 4, a + b, jnp.maximum(a, b))
            return a + b

        class Chunk:
            def __init__(self, number, src, near=None):
                self.src, self.peaks = src, number == 4
                self.mine, self.buf, self.z_send, self.z_recv, spare, self.x_send, self.x_recv = r.chunks[number]
                self.near = spare if near is None else near

            def start(self):
                self.over = remote(self.src.at[1 - x], self.near, self.x_send, self.x_recv, side)
                self.over.start()
                sent.append(self.over)

            def middle(self, arrived=False):
                if not arrived:
                    self.over.wait_recv()
                mine, buf = self.mine, self.buf
                mine[...] = join(self.src[x], self.near[...], self.peaks).astype(mine.dtype)
                self.along = [
                    remote(mine.at[to_z], buf.at[k], self.z_send.at[k], self.z_recv.at[k], target)
                    for k, (target, to_z, _) in enumerate(far)
                ]
                for copy in self.along:
                    copy.start()
                    sent.append(copy)

            def total(self):
                value = join(self.src[x, zh], self.near[zh], self.peaks)
                for k, copy in enumerate(self.along):
                    copy.wait_recv()
                    value = join(value, self.buf[k], self.peaks)
                return value

        def turn(src, i):
            box, sems = r.boxes.at[i], r.turn_sems[i]
            for k, (target, rank, _) in enumerate(peers):
                copy = remote(src(rank), box.at[me], sems[0].at[k], sems[1].at[k], target)
                copy.start()
                full.append(copy)
            box[me] = src(me)[...]

        cs = [Chunk(c, r.inner.at[:, :, c], r.near.at[:, c]) for c in range(2)]
        cs[0].middle(arrived=True)
        cs[1].middle(arrived=True)
        gained, shown = [], []
        for i, (target, rank, _) in enumerate(peers):
            for src, buf, sems, copies in (
                (r.gain.at[rank], r.gain_t, r.g_sems, gained),
                (r.stats, r.stats_t, r.s_sems, shown),
            ):
                copy = remote(src, buf.at[i], sems[0].at[i], sems[1].at[i], target)
                copy.start()
                copies.append(copy)
                sent.append(copy)
        mats_c = Chunk(2, r.mats)
        mats_c.start()
        sources = (r.t0, r.t1, r.t2)
        for i in range(3):
            turn(lambda rank, i=i: sources[i].at[rank], i + 1)
        total = r.gain[me]
        seen = r.stats[...]
        for i in range(TP - 1):
            gained[i].wait_recv()
            total = total + r.gain_t[i]
            shown[i].wait_recv()
            seen = join(seen, r.stats_t[i], True)
        r.vectors[...] = r.small[...]
        for l in range(LAYERS):
            for g in range(groups):
                at = l * groups + g
                r.vectors[g // zh_size, g % zh_size, l * 16 + 8 : l * 16 + 9, :] = total[at : at + 1, :]
        r.stats_v[...] = jnp.broadcast_to(seen, every)
        rest = [mats_c, Chunk(3, r.vectors), Chunk(4, r.stats_v)]
        for c in rest[1:]:
            c.start()
        for c in rest:
            c.middle()
        for c in range(2):
            r.win_t[c] = cs[c].total().astype(bf16).reshape(WAYS, depth, half)
        turn(lambda rank: r.win_t.at[rank // WAYS, lax.rem(rank, WAYS)], 0)
        m = rest[0].total()
        for l in range(LAYERS):
            base = 3 * LANES * l
            r.grate[l] = m[:, base : base + RANK].T
            r.gselect[l] = m[:, base + RANK : base + RANK + select]
        r.total[...] = rest[1].total()
        for l in range(LAYERS):
            r.gtaps[l] = r.total[16 * l : 16 * l + CONV, :share]
            for out, j, size in (
                (r.gshift, CONV, share), (r.grate_shift, CONV + 1, share), (r.gskip, CONV + 2, share), (r.ggain, 8, gains)
            ):
                out[l : l + 1, :] = r.total[16 * l + j : 16 * l + j + 1, :size]
        r.stats_all[...] = rest[2].total()

        def lay(i):
            for rank in range(TP):
                for g in range(groups):
                    d = ((g // zh_size * 2 + rank // WAYS) * zh_size + g % zh_size) * WAYS + rank % WAYS
                    first = i % 2 * count * share + d * share
                    r.gin[i // 2, :, first : first + share] = r.boxes[i, rank, :, g * share : (g + 1) * share].astype(f32)

        early, late = full[: 3 * (TP - 1)], full[3 * (TP - 1) :]
        for copy in early:
            copy.wait_recv()
        for i in (1, 2, 3):
            lay(i)
        for copy in late:
            copy.wait_recv()
        lay(0)
        for copy in sent + full:
            copy.wait_send()

    return call(body, 5, ins, outs, scratch)


def on_device(
    hidden, cotangent, groups, group_weights, input_weight, select_weight, rate_weight,
    output_weight, norm_gain, conv_taps, conv_shift, rate_shift, skip_gain,
):
    fsdp = lax.axis_size("fsdp")
    zh_size = fsdp // WAYS
    count = 2 * 2 * fsdp
    group_count = 2 * zh_size
    share = conv_shift.shape[1]
    gains = norm_gain.shape[1]
    depth = input_weight.shape[1]
    half = group_count * share
    x, core, zh, q = place()

    labels = jnp.arange(group_weights.shape[0])
    own_weight = jnp.sum(jnp.where(groups[:, None] == labels[None, :], group_weights[None, :], 0.0))

    wins = input_weight
    if share % LANES:
        wins = wins.reshape(LAYERS, depth, 2, 2, 2, zh_size, WAYS, share)
        wins = wins.transpose(0, 4, 6, 1, 2, 3, 5, 7).reshape(LAYERS, TP, depth, 2 * half)
    mats = jnp.concatenate([rate_weight.swapaxes(1, 2), select_weight], axis=2)
    mats = jnp.pad(mats, ((0, 0), (0, 0), (0, 3 * LANES - mats.shape[2])))
    vectors = [conv_taps, conv_shift[:, None], rate_shift[:, None], skip_gain[:, None], skip_gain[:, None]]
    small = jnp.concatenate(vectors, axis=1).astype(f32).reshape(8 * LAYERS, share)
    small = jnp.pad(small, ((0, 0), (0, LANES - share)))
    misc = jnp.pad(norm_gain.astype(f32), ((0, 0), (0, LANES - gains)))
    misc = jnp.concatenate([misc, jnp.full((8 - LAYERS, LANES), own_weight)])

    flat = lambda a: a.reshape(half, -1)
    h0 = hidden[0]
    start = opening(zh_size, gains, share, wins, small, misc, mats, h0, cotangent[0])
    vec, gain, scale = start.vec, start.gains, start.scale
    win0, mat0 = start.win_all.reshape(count * depth, -1), flat(start.mats_all)
    one = forward_layer(
        zh_size, 0, start.xg, win0, mat0, output_weight, vec, scale,
        nxt=types.SimpleNamespace(h=h0, gain=gain, win=wins, mats=mats),
    )
    win1, mat1 = one.win1_all.reshape(count * depth, -1), flat(one.mats1_all)
    h1 = one.result
    two = forward_layer(zh_size, 1, one.xg1, win1, mat1, output_weight, vec, scale, gout=start.gout)

    down1 = backward_layer(
        zh_size, 1, two, two.gog, flat(two.wout_all), mat1, vec, one.xg1, win1, gain, h1, start.grad,
        part=two.part,
    )
    stream = h1 + jnp.sum(down1.parts_all.astype(f32), axis=0)
    blocks = (2, zh_size) + down1.ginner.shape[1:]
    pick = lambda a, i: lax.dynamic_index_in_dim(a, i, 0, keepdims=False)
    summed = pick(down1.ginner.reshape(blocks), x).astype(f32) + down1.near.astype(f32)
    down0 = backward_layer(
        zh_size, 0, one, down1.gog, flat(one.wout_all), mat0, vec, start.xg, win0, gain, h0, down1.prev,
        late=summed.astype(bf16),
    )
    late = pick(summed, zh)
    for k in range(zh_size - 1):
        late = late + down0.late[k].astype(f32)

    sums = [jnp.sum(o.stats[0]) for o in (one, two)]
    peaks = [jnp.max(o.stats[1]) for o in (one, two)]
    pad = [jnp.zeros((), f32)] * (4 - LAYERS)
    own_stats = jnp.broadcast_to(jnp.stack(sums + pad + peaks + pad)[:, None], (8, LANES))
    downs = (down0, down1)
    small = jnp.stack([down.gvec for down in downs]).reshape(LAYERS, 8, group_count, share)
    small = jnp.pad(small.transpose(2, 0, 1, 3), ((0, 0), (0, 0), (0, 8), (0, LANES - share)))
    small = small.reshape(2, zh_size, 16 * LAYERS, LANES)
    spread_gain = jnp.stack([down.ggain[0] for down in downs]).reshape(LAYERS, 2, 2, zh_size, WAYS, gains)
    spread_gain = spread_gain.transpose(2, 4, 0, 1, 3, 5).reshape(TP, LAYERS * group_count, gains)
    spread_gain = jnp.pad(spread_gain, ((0, 0), (0, -LAYERS * group_count % 8), (0, LANES - gains)))
    mats = jnp.concatenate([down.gmats for down in downs], axis=1).reshape(2, zh_size, share, -1)
    turns = [down0.ggate, late.astype(bf16), down1.ggate]
    end = closing(
        zh_size, down0.ginner.reshape(blocks), down0.near, mats, small, own_stats, spread_gain,
        [t.reshape(TP, depth, half) for t in turns], share, output_weight.shape[2], select_weight.shape[2],
    )
    stats = end.stats_all
    beta_mean = stats[:LAYERS, 0] / (count * hidden.shape[1] * INNER)
    beta_max = stats[4 : 4 + LAYERS, 0]
    gwout = jnp.stack([down.gwout for down in downs])
    return (
        stream[None], down0.prev[None], end.gin, end.gselect, end.grate, gwout, end.ggain, end.gtaps, end.gshift,
        end.grate_shift, end.gskip, beta_mean, beta_max,
    )


def solution(mesh):
    both = ("dp", "fsdp")
    placed = (
        P(both, None, None), P(both, None, None), P(both), P(),
        P(None, both, None), P(None, both, None), P(None, None, both), P(None, both, None),
        P(None, both), P(None, None, both), P(None, both), P(None, both), P(None, both),
    )
    return jax.shard_map(
        on_device,
        mesh=mesh,
        in_specs=placed,
        out_specs=(P(both, None, None), P(both, None, None)) + placed[4:] + (P(), P()),
        check_vma=False,
    )
```

```python
import types

import jax
import jax.numpy as jnp
import numpy as np
from jax import lax
from jax.sharding import PartitionSpec as P
import jax.experimental.pallas as pl
import jax.experimental.pallas.tpu as pltpu

INNER = 4096
STATE = 16
RANK = 128
CONV = 4
LAYERS = 2
WAYS = 4
TP = 8
STEPS = 16

eps = 1e-05
MESH = pl.DeviceIdType.MESH
f32 = jnp.float32
bf16 = jnp.bfloat16
VM = pl.BlockSpec(memory_space=pltpu.VMEM)
HB = pl.BlockSpec(memory_space=pl.ANY)
EARLY, LATE = object(), object()


def place():
    dp, fs = lax.axis_index("dp"), lax.axis_index("fsdp")
    return dp // 2, lax.rem(dp, 2), fs // WAYS, lax.rem(fs, WAYS)


def device(x, core, zh, q):
    return (x * 2 + core, zh * WAYS + q)


def remote(src, dst, send, recv, target):
    return pltpu.make_async_remote_copy(
        src_ref=src, dst_ref=dst, send_sem=send, recv_sem=recv, device_id=target, device_id_type=MESH
    )


def greet(targets):
    barrier = pltpu.get_barrier_semaphore()
    for target in targets:
        pl.semaphore_signal(barrier, inc=1, device_id=target, device_id_type=MESH)
    pl.semaphore_wait(barrier, len(targets))


def tp_peers():
    x, core, zh, q = place()
    peers = []
    for dc, da, db in ((1, 0, 0), (0, 1, 0), (0, 0, 1), (1, 1, 0), (1, 0, 1), (0, 1, 1), (1, 1, 1)):
        other_core, other_q = lax.rem(core + dc, 2), neighbour(q, da, db)
        rank = other_core * WAYS + other_q
        peers.append((device(x, other_core, zh, other_q), rank, rank))
    return peers


def neighbour(q, da, db):
    a, b = lax.rem(q, 2), q // 2
    return (1 - b if db else b) * 2 + (1 - a if da else a)


def total_rank():
    _, core, _, q = place()
    return core * WAYS + q


def dp_peers(zh_size):
    x, core, zh, q = place()
    side = device(1 - x, core, zh, q)
    far = []
    for dz in range(1, zh_size):
        to_z, from_z = lax.rem(zh + dz, zh_size), lax.rem(zh + zh_size - dz, zh_size)
        far.append((device(x, core, to_z, q), to_z, from_z))
    return side, far


def lanes_of(shape):
    return lax.broadcasted_iota(jnp.int32, shape, 1)


def encode(v):
    tail = v[:, RANK:]
    lane = lanes_of(tail.shape)
    high = tail.astype(bf16).astype(f32)
    low = pltpu.roll(tail - high, 32, 1)
    both = jnp.where(lane < 32, high, jnp.where(lane < 64, low, 0.0))
    return jnp.concatenate([v[:, :RANK].astype(bf16), both.astype(bf16)], axis=1)


def decode(v):
    tail = v[:, RANK:].astype(f32)
    lane = lanes_of(tail.shape)
    tail = jnp.where(lane < 32, tail + pltpu.roll(tail, 96, 1), 0.0)
    return jnp.concatenate([v[:, :RANK].astype(f32), tail], axis=1)


def halves(rows):
    return pl.ds(0, rows // 2), pl.ds(rows // 2, rows // 2)


class Gather:
    sems = staticmethod(lambda dma: [dma((6,)), dma((6,)), dma((4,)), dma((4,)), dma])

    def __init__(self, src, out, sems):
        self.src, self.out = src, out
        self.f_send, self.f_recv, self.s_send, self.s_recv, self.own_sem = sems
        x, core, zh, q = place()
        self.core, self.me = core, core * WAYS + q
        self.sibling = device(x, 1 - core, zh, q)
        self.chips = [neighbour(q, 0, 1), neighbour(q, 1, 0), neighbour(q, 1, 1)]
        self.b, self.a = [device(x, core, zh, c) for c in self.chips[:2]]
        self.top, self.low = halves(src.shape[0])

    def send(self, i, src, slot, rows, target):
        copy = remote(src, self.out.at[slot, rows], self.f_send.at[i], self.f_recv.at[i], target)
        copy.start()
        return copy

    def to_sibling(self, i, src, slot):
        copy = remote(src, self.out.at[slot], self.s_send.at[i], self.s_recv.at[i], self.sibling)
        copy.start()
        self.near.append(copy)

    def start(self):
        self.near = []
        self.first = [
            self.send(i, self.src.at[rows], self.me, rows, target)
            for i, (rows, target) in enumerate(
                ((self.top, self.b), (self.low, self.a), (self.low, self.b), (self.top, self.a))
            )
        ]
        self.to_sibling(3, self.src, self.me)
        self.own = pltpu.make_async_copy(self.src, self.out.at[self.me], self.own_sem)
        self.own.start()

    def relay(self):
        for i, rows, target in ((0, self.top, self.a), (1, self.low, self.b)):
            self.first[i].wait_recv()
            slot = self.core * WAYS + self.chips[i]
            self.first.append(self.send(4 + i, self.out.at[slot, rows], slot, rows, target))

    def rest(self):
        for i, ends in enumerate(((2,), (3,), (4, 5))):
            for k in ends:
                self.first[k].wait_recv()
            slot = self.core * WAYS + self.chips[i]
            self.to_sibling(i, self.out.at[slot], slot)

    def finish(self):
        for copy in self.first:
            copy.wait_send()
        for copy in self.near:
            copy.wait()
        self.own.wait()


class Scatter:
    sems = staticmethod(lambda dma: [dma((4,)), dma((4,)), dma((6,)), dma((6,))])

    @staticmethod
    def buffers(block):
        return [pltpu.VMEM((4,) + block, bf16), pltpu.VMEM((3,) + block, bf16), pltpu.VMEM((3,) + block, bf16)]

    def __init__(self, partial, buffers, sems):
        self.partial = partial
        self.near_buf, self.out, self.into = buffers
        self.s_send, self.s_recv, self.f_send, self.f_recv = sems
        x, core, zh, q = place()
        self.core = core
        self.sibling = device(x, 1 - core, zh, q)
        self.turns = [neighbour(q, 1, 1), neighbour(q, 1, 0), neighbour(q, 0, 1), q]
        self.a, self.b = [device(x, core, zh, t) for t in self.turns[1:3]]
        self.top, self.low = halves(partial.shape[1])
        self.near, self.first = [None] * 4, {}

    def to_sibling(self, i):
        slot = (1 - self.core) * WAYS + self.turns[i]
        self.near[i] = remote(
            self.partial.at[slot], self.near_buf.at[i], self.s_send.at[i], self.s_recv.at[i], self.sibling
        )
        self.near[i].start()

    def joined(self, i, rows=slice(None)):
        own = self.partial[self.core * WAYS + self.turns[i], rows]
        return own.astype(f32) + self.near_buf[i, rows].astype(f32)

    def send(self, k, i, rows, target):
        self.first[k] = remote(
            self.out.at[i, rows], self.into.at[i, rows], self.f_send.at[k], self.f_recv.at[k], target
        )
        self.first[k].start()

    def across(self, i):
        self.near[i].wait_recv()
        if i == 0:
            self.out[0] = self.joined(0).astype(bf16)
            self.send(0, 0, self.top, self.a)
            self.send(1, 0, self.low, self.b)
        else:
            rows, target = ((self.top, self.a), (self.low, self.b))[i - 1]
            self.out[i, rows] = self.joined(i, rows).astype(bf16)
            self.send(1 + i, i, rows, target)

    def sums(self):
        for k, i, rows, target in ((1, 1, self.low, self.a), (0, 2, self.top, self.b)):
            self.first[k].wait_recv()
            self.out[i, rows] = (self.joined(i, rows) + self.into[0, rows].astype(f32)).astype(bf16)
            self.send(3 + i, i, rows, target)

    def total(self):
        self.near[3].wait_recv()
        value = self.joined(3)
        for k in (2, 3, 4, 5):
            self.first[k].wait_recv()
        value = value + self.into[1].astype(f32) + self.into[2].astype(f32)
        for copy in self.near + list(self.first.values()):
            copy.wait_send()
        return value


class Spread:
    @staticmethod
    def sems(dma, zh_size):
        far = max(1, zh_size - 1)
        return [dma((far,)), dma((far,)), dma((zh_size,)), dma((zh_size,)), dma]

    def __init__(self, zh_size, src, view, sems, keep=True):
        self.src, self.view, self.keep = src, view, keep
        self.z_send, self.z_recv, self.x_send, self.x_recv, self.own_sem = sems
        self.x, _, self.zh, _ = place()
        self.side, self.far = dp_peers(zh_size)

    def start(self):
        dst = self.view(self.x, self.zh)
        self.along = [
            remote(self.src, dst, self.z_send.at[k], self.z_recv.at[k], target)
            for k, (target, _, _) in enumerate(self.far)
        ]
        self.over = [remote(self.src, dst, self.x_send.at[0], self.x_recv.at[0], self.side)]
        for copy in self.along + self.over:
            copy.start()
        if self.keep:
            self.own = pltpu.make_async_copy(self.src, dst, self.own_sem)
            self.own.start()

    def onward(self):
        for k, (_, _, source) in enumerate(self.far):
            self.along[k].wait_recv()
            slot = self.view(self.x, source)
            copy = remote(slot, slot, self.x_send.at[k + 1], self.x_recv.at[k + 1], self.side)
            copy.start()
            self.over.append(copy)

    def finish(self):
        for copy in self.along:
            copy.wait_send()
        for copy in self.over:
            copy.wait()
        if self.keep:
            self.own.wait()


class Sum:
    sems = staticmethod(
        lambda dma: [dma, dma, dma((3,)), dma((3,)), dma((4,)), dma((4,)), dma((3,)), dma((3,))]
    )

    def __init__(self, payload, parts, out, sems):
        self.payload, self.out = payload, out
        self.near, self.into = parts.at[:WAYS], parts.at[WAYS:]
        self.a_send, self.a_recv, self.b_send, self.b_recv, self.c_send, self.c_recv, self.d_send, self.d_recv = sems
        x, core, zh, q = place()
        self.q, self.base, self.me = q, core * WAYS, core * WAYS + q
        self.other = (1 - core) * WAYS
        self.sibling = device(x, 1 - core, zh, q)
        self.chips = [neighbour(q, 1, 1), neighbour(q, 1, 0), neighbour(q, 0, 1)]
        self.far = [device(x, core, zh, t) for t in self.chips]

    def start(self):
        swap = remote(
            self.payload.at[pl.ds(self.other, WAYS)], self.near, self.a_send, self.a_recv, self.sibling
        )
        swap.start()
        swap.wait_recv()
        self.one = [swap]
        for i, t in enumerate(self.chips):
            slot = self.base + t
            self.payload[slot] = encode(decode(self.payload[slot]) + decode(self.near[t]))
            copy = remote(self.payload.at[slot], self.into.at[i], self.b_send.at[i], self.b_recv.at[i], self.far[i])
            copy.start()
            self.one.append(copy)

    def middle(self, own):
        total = own + decode(self.near[self.q])
        for i in range(3):
            self.one[1 + i].wait_recv()
            total = total + decode(self.into[i])
        self.out[self.me] = encode(total)
        mine = self.out.at[self.me]
        self.two = [
            remote(mine, mine, self.c_send.at[i], self.c_recv.at[i], target)
            for i, target in enumerate(self.far + [self.sibling])
        ]
        for copy in self.two:
            copy.start()

    def finish(self):
        last = []
        for i in (1, 2, 0):
            self.two[i].wait_recv()
            slot = self.out.at[self.base + self.chips[i]]
            copy = remote(slot, slot, self.d_send.at[i], self.d_recv.at[i], self.sibling)
            copy.start()
            last.append(copy)
        self.two[3].wait_recv()
        for copy in self.one + self.two:
            copy.wait_send()
        for copy in last:
            copy.wait()


def call(body, collective, ins, outs, scratch):
    def flatten(kind):
        return [leaf for each in kind for leaf in flatten(each)] if isinstance(kind, list) else [kind]

    def rebuild(kind, refs):
        return [rebuild(each, refs) for each in kind] if isinstance(kind, list) else refs.pop(0)

    early = [key for key, (_, spec) in ins.items() if spec is EARLY]
    late = [key for key, (_, spec) in outs.items() if spec is LATE]
    space = lambda spec: HB if spec is EARLY or spec is LATE else spec
    held = [pltpu.VMEM(ins[key][0].shape, ins[key][0].dtype) for key in early]
    held += [pltpu.VMEM(outs[key][0].shape, outs[key][0].dtype) for key in late]
    extra = [held, [pltpu.SemaphoreType.DMA] * len(held)]

    def kernel(*refs):
        refs = list(refs)
        named = {key: refs.pop(0) for key in list(ins) + list(outs)}
        named.update({key: rebuild(kind, refs) for key, kind in scratch.items()})
        buffers, sems = rebuild(extra, refs)
        loads, stores = {}, {}
        for key, buffer, sem in zip(early + late, buffers, sems):
            if key in early:
                loads[key] = pltpu.make_async_copy(named[key], buffer, sem)
            else:
                stores[key] = pltpu.make_async_copy(buffer, named[key], sem)
            named[key] = buffer
        r = types.SimpleNamespace(**named)
        r.load = lambda: [copy.start() for copy in loads.values()]
        r.need = types.SimpleNamespace(**{key: copy.wait for key, copy in loads.items()})
        r.put = types.SimpleNamespace(**{key: copy.start for key, copy in stores.items()})
        r.done = lambda: [copy.wait() for copy in stores.values()]
        body(r)

    values = pl.pallas_call(
        kernel,
        out_shape=[shape for shape, _ in outs.values()],
        in_specs=[space(spec) for _, spec in ins.values()],
        out_specs=[space(spec) for _, spec in outs.values()],
        scratch_shapes=flatten(list(scratch.values()) + extra),
        compiler_params=pltpu.CompilerParams(
            collective_id=collective, has_side_effects=True, vmem_limit_bytes=63 * 2**20
        ),
    )(*[array for array, _ in ins.values()])
    return types.SimpleNamespace(**dict(zip(outs, values)))


def spread_keys(kq, lane):
    a = kq.astype(bf16).astype(f32)
    rest = kq - a
    b = rest.astype(bf16).astype(f32)
    c = rest - b
    return jnp.where(lane < 32, a, jnp.where(lane < 64, b, c)).astype(bf16)


def spreader():
    one = np.repeat(np.eye(32, dtype=np.float32), 128, axis=1)
    return jnp.asarray(np.concatenate([one, one, one, np.zeros_like(one)], axis=0), bf16)


def folder():
    return jnp.asarray(np.pad(np.repeat(np.eye(32, dtype=np.float32), 128, axis=0), ((0, 0), (0, 96))), bf16)


def dot(a, b, contract, out=f32):
    return lax.dot_general(a, b, (contract, ((), ())), preferred_element_type=out)


def rms(stream):
    return lax.rsqrt(jnp.mean(jnp.square(stream), axis=-1, keepdims=True) + eps)


LANES = 128


def struct(*shape, dtype=f32):
    return jax.ShapeDtypeStruct(shape, dtype)


def side_by_side(pieces, lanes):
    each = LANES // lanes
    out = []
    for i in range(0, len(pieces), each):
        tile = pieces[i]
        for j in range(1, each):
            tile = tile + pltpu.roll(pieces[i + j], j * lanes, 1)
        out.append(tile)
    return jnp.concatenate(out, axis=1)


def turn_pieces(zh_size, win, layer, out, rank):
    if len(win.shape) == 4:
        return [(win.at[layer, rank], out)]
    groups = 2 * zh_size
    share = win.shape[2] // (2 * groups * TP)
    pieces = []
    for part in range(2):
        for g in range(groups):
            d = ((g // zh_size * 2 + rank // WAYS) * zh_size + g % zh_size) * WAYS + lax.rem(rank, WAYS)
            first = pl.multiple_of((part * groups * TP + d) * share, share)
            pieces.append(
                (win.at[layer, :, pl.ds(first, share)], out.at[:, pl.ds((part * groups + g) * share, share)])
            )
    return pieces


class Turn:
    def __init__(self, zh_size, win, layer, out, slot, sems):
        self.out, self.slot, self.sems = out, slot, sems
        self.me = total_rank()
        self.peers = tp_peers()
        self.pieces = lambda rank: turn_pieces(zh_size, win, layer, out.at[slot(self.me)], rank)

    def start(self):
        for i, (target, rank, _) in enumerate(self.peers):
            for src, dst in self.pieces(rank):
                remote(src, dst, self.sems[0].at[i], self.sems[1].at[i], target).start()

    def whole(self, i, rank):
        block = self.out.at[self.slot(rank)]
        return remote(block, block, self.sems[0].at[i], self.sems[1].at[i], self.peers[i][0])

    def arrived(self, i):
        self.whole(i, self.peers[i][2]).wait_recv()

    def sent(self):
        for i in range(TP - 1):
            self.whole(i, self.me).wait_send()


def opening(zh_size, gains, share, win, small, misc, mats, h, cot):
    groups = 2 * zh_size
    count = groups * TP
    tokens, width = h.shape
    half = groups * share
    depth = win.shape[-2]
    dma = pltpu.SemaphoreType.DMA
    ins = dict(
        win=(win, HB), small=(small, VM), misc=(misc, VM), mats=(mats, HB), h=(h, VM), cot=(cot, VM)
    )
    outs = dict(
        win_all=(struct(count, depth, 2 * half, dtype=bf16), HB),
        mats_all=(struct(groups, *mats.shape[1:], dtype=bf16), HB), vec=(struct(8 * LAYERS, half), VM),
        gains=(struct(8, width), VM), scale=(struct(TP, LANES), VM), grad=(struct(tokens, width), VM),
        gout=(struct(tokens, width, dtype=bf16), VM), xg=(struct(TP, tokens, width, dtype=bf16), HB),
    )
    spread = lambda: Spread.sems(dma, zh_size)
    scratch = dict(
        misc_all=pltpu.VMEM((count,) + misc.shape, f32), small_all=pltpu.VMEM((groups,) + small.shape, f32),
        normed=pltpu.VMEM((tokens, width), bf16), gather_sems=Gather.sems(dma),
        m_sems=[dma((TP - 1,))] * 2, w_sems=[dma((TP - 1,))] * 2, own_sem=dma,
        own=pltpu.VMEM((depth, 2 * half), bf16), s0=spread(), s1=spread(),
        sm=[spread() for _ in range(TP)], sw=[spread() for _ in range(TP)],
    )

    def body(r):
        x, core, zh, q = place()
        me = core * WAYS + q
        peers = tp_peers()
        side, far = dp_peers(zh_size)
        greet([p[0] for p in peers] + [side] + [f[0] for f in far])

        def row(xx, zz, rank):
            return ((xx * 2 + rank // WAYS) * zh_size + zz) * WAYS + lax.rem(rank, WAYS)

        def views(out, rank):
            return lambda xx, zz: out.at[row(xx, zz, rank)]

        here = row(x, zh, me)
        miscs = []
        for i, (target, rank, _) in enumerate(peers):
            miscs.append(remote(r.misc, r.misc_all.at[here], r.m_sems[0].at[i], r.m_sems[1].at[i], target))
            miscs[-1].start()
        misc_moves = [Spread(zh_size, r.misc, views(r.misc_all, me), r.sm[0])]
        misc_moves[0].start()
        smalls = Spread(zh_size, r.small, lambda xx, zz: r.small_all.at[xx * zh_size + zz], r.s0)
        smalls.start()
        wins = Turn(zh_size, r.win, 0, r.win_all, lambda rank: row(x, zh, rank), r.w_sems)
        wins.start()
        own_pieces = [
            pltpu.make_async_copy(src, dst, r.own_sem)
            for src, dst in turn_pieces(zh_size, r.win, 0, r.own, me)
        ]
        for copy in own_pieces:
            copy.start()
        pltpu.make_async_copy(r.own, r.own, r.own_sem).wait()
        win_moves = [Spread(zh_size, r.own, views(r.win_all, me), r.sw[0])]
        for i, (_, _, source) in enumerate(peers):
            view = views(r.win_all, source)
            win_moves.append(Spread(zh_size, view(x, zh), view, r.sw[i + 1], keep=False))
        mats_move = Spread(zh_size, r.mats.at[0], lambda xx, zz: r.mats_all.at[xx * zh_size + zz], r.s1)

        def step(i):
            if i >= 1:
                wins.arrived(i - 1)
            if i >= 2:
                win_moves[i - 2].onward()
            win_moves[i].start()

        step(0)
        for i, (_, _, source) in enumerate(peers):
            miscs[i].wait_recv()
            view = views(r.misc_all, source)
            misc_moves.append(Spread(zh_size, view(x, zh), view, r.sm[i + 1], keep=False))
            misc_moves[-1].start()
        step(1)
        for move in misc_moves:
            move.onward()
        smalls.onward()
        for move in misc_moves:
            move.finish()
        for l in range(LAYERS):
            r.gains[l : l + 1, :] = side_by_side(
                [r.misc_all[d, l : l + 1, :] for d in range(count)], gains
            )
        r.gains[LAYERS:, :] = jnp.zeros((8 - LAYERS, width), f32)
        stream = r.h[...]
        r.normed[...] = (stream * rms(stream) * r.gains[0:1, :]).astype(bf16)
        rows = Gather(r.normed, r.xg, r.gather_sems)
        rows.start()
        step(2)
        mats_move.start()
        total = r.misc_all[0, LAYERS : LAYERS + 1, :]
        for d in range(1, count):
            total = total + r.misc_all[d, LAYERS : LAYERS + 1, :]
        inverse = count / total
        for rank in range(TP):
            r.scale[rank : rank + 1, :] = r.misc_all[row(x, zh, rank), LAYERS : LAYERS + 1, :] * inverse
        own = (r.misc[LAYERS : LAYERS + 1, :] * inverse)[:, :1]
        grad = r.cot[...] * own
        r.grad[...] = grad
        r.gout[...] = grad.astype(bf16)
        step(3)
        smalls.finish()
        for l in range(LAYERS):
            r.vec[8 * l : 8 * (l + 1), :] = side_by_side(
                [r.small_all[g, 8 * l : 8 * (l + 1), :] for g in range(groups)], share
            )
        step(4)
        mats_move.onward()
        rows.relay()
        step(5)
        step(6)
        rows.rest()
        step(7)
        win_moves[6].onward()
        win_moves[7].onward()
        wins.sent()
        for copy in miscs:
            copy.wait_send()
        for move in win_moves + [mats_move]:
            move.finish()
        rows.finish()

    return call(body, 1, ins, outs, scratch)


def at_block(b, size):
    return pl.ds(pl.multiple_of(b * size, size), size)


def conv_of(entry, vec, row, size, c):
    cols = slice(c * LANES, (c + 1) * LANES)
    conv = vec[CONV : CONV + 1, cols]
    for j in range(CONV):
        conv = conv + vec[j : j + 1, cols] * entry[c, pl.ds(pl.multiple_of(row + TP * j, TP), size), :]
    return conv


def wide_of(ref, rows, parts):
    return jnp.concatenate([ref[c, rows, :] for c in range(parts)], axis=1)


def row_sum(value):
    return jnp.sum(value.reshape(-1, TP, value.shape[1]), axis=0)


def square_sum(kq):
    lane = lanes_of(kq.shape)
    return jnp.sum(jnp.where(lane < STATE, kq * kq, 0.0), axis=1, keepdims=True)


def forward_layer(zh_size, layer, xg, win, mats, wout, vec, scale, gout=None, nxt=None):
    tokens, width = xg.shape[1], xg.shape[2]
    half = win.shape[1] // 2
    parts = half // LANES
    rows = tokens * TP
    size = STEPS * TP
    blocks = rows // size
    halo = (CONV - 1) * TP
    dma = pltpu.SemaphoreType.DMA
    last = nxt is None
    groups = 2 * zh_size
    ins = dict(
        xg=(xg, EARLY), win=(win, EARLY), mats=(mats, EARLY), wout=(wout, HB), vec=(vec, VM),
        scale=(scale, VM), e=(spreader(), EARLY),
    )
    outs = dict(
        entry=(struct(2 * parts, halo + rows, LANES), LATE), beta=(struct(parts, rows, LANES), LATE),
        kq=(struct(rows, LANES), LATE), proj=(struct(TP, size, 2 * LANES, dtype=bf16), LATE),
        y=(struct(parts, rows, LANES), LATE), keep=(struct(blocks, STATE, parts, TP, LANES), LATE),
        mixed=(struct(TP, tokens, half, dtype=bf16), LATE), stats=(struct(2, TP, LANES), VM),
    )
    scratch = dict(
        act=pltpu.VMEM((parts, rows, LANES), f32), step=pltpu.VMEM((parts, rows, LANES), f32),
        payload=pltpu.VMEM((TP, size, 2 * LANES), bf16), parts=pltpu.VMEM((TP - 1, size, 2 * LANES), bf16),
        own=pltpu.VMEM((size, 2 * LANES), f32),
        state=pltpu.VMEM((STATE, parts, TP, LANES), f32), wide=pltpu.VMEM((size, 32 * LANES), f32),
        sum_sems=Sum.sems(dma),
    )
    outs.update(wout_all=(struct(groups, *wout.shape[1:], dtype=bf16), LATE))
    scratch.update(d0=Spread.sems(dma, zh_size))
    if last:
        ins.update(gout=(gout, VM))
        outs.update(
            gog=(struct(TP, tokens, width, dtype=bf16), HB), part=(struct(TP, tokens, width, dtype=bf16), LATE)
        )
        scratch.update(gather_sems=Gather.sems(dma))
    if not last:
        win1 = nxt.win
        depth = win1.shape[-2]
        ins.update(h=(nxt.h, EARLY), gain=(nxt.gain, VM), win1=(win1, HB), mats1=(nxt.mats, HB))
        outs.update(
            result=(struct(tokens, width), VM),
            win1_all=(struct(2, 2, zh_size, WAYS, depth, 2 * half, dtype=bf16), HB),
            mats1_all=(struct(groups, *nxt.mats.shape[1:], dtype=bf16), HB),
            xg1=(struct(TP, tokens, width, dtype=bf16), HB),
        )
        scratch.update(
            normed=pltpu.VMEM((tokens, width), bf16), gather_sems=Gather.sems(dma),
            part=pltpu.VMEM((TP, tokens, width), bf16), scatter_buf=Scatter.buffers((tokens, width)),
            scatter_sems=Scatter.sems(dma),
            turned=pltpu.VMEM((TP, depth, 2 * half), bf16), l_sems=[dma((TP - 1,)), dma((TP - 1,))], l_own=dma,
            d1=Spread.sems(dma, zh_size), d2=Spread.sems(dma, zh_size), d3=Spread.sems(dma, zh_size),
        )

    def body(r):
        r.load()
        side, far = dp_peers(zh_size)
        greet([p[0] for p in tp_peers()] + [side] + [f[0] for f in far])
        entry, act, step, beta, kq, y = r.entry, r.act, r.step, r.beta, r.kq, r.y
        vec = r.vec.at[8 * layer : 8 * (layer + 1)]
        index = lambda ref: lambda xx, zz: ref.at[xx * zh_size + zz]
        early = Spread(zh_size, r.wout.at[layer], index(r.wout_all), r.d0)
        early.start()
        if last:
            gouts = Gather(r.gout, r.gog, r.gather_sems)
        else:
            turned = Turn(zh_size, r.win1, layer + 1, r.turned, lambda rank: rank, r.l_sems)
            turned.start()
            for src, dst in turned.pieces(turned.me):
                pltpu.make_async_copy(src, dst, r.l_own).start()
            moves = [Spread(zh_size, r.mats1.at[layer + 1], index(r.mats1_all), r.d3)]
            for k in range(2):
                view = lambda xx, zz, k=k: r.win1_all.at[xx, k, zz]
                src = r.turned.at[k * WAYS : (k + 1) * WAYS]
                moves.append(Spread(zh_size, src, view, (r.d1 if k == 0 else r.d2)))

        r.need.xg()
        r.need.win()
        entry[:, :halo, :] = jnp.zeros((2 * parts, halo, LANES), f32)
        tile = 2 * LANES
        for p in range(TP // 2):

            def columns(n, carry, p=p):
                cols = at_block(n, tile)
                out = jnp.dot(
                    r.xg[2 * p : 2 * p + 2].reshape(2 * tokens, width), r.win[:, cols],
                    preferred_element_type=f32,
                )
                for j in range(2):
                    for c in range(2):
                        entry[2 * n + c, pl.ds(halo + 2 * p + j, tokens, stride=TP), :] = out[
                            j * tokens : (j + 1) * tokens, c * LANES : (c + 1) * LANES
                        ]
                return carry

            lax.fori_loop(0, 2 * half // tile, columns, 0)
        r.put.entry()
        r.need.mats()
        total = Sum(r.payload, r.parts, r.proj, r.sum_sems)

        def project(b, carry):
            rs = at_block(b, size)
            for c in range(parts):
                conv = conv_of(entry, vec, b * size, size, c)
                act[c, rs, :] = (conv * jax.nn.sigmoid(conv)).astype(bf16).astype(f32)
            out = jnp.dot(
                wide_of(act, rs, parts).astype(bf16), r.mats[:, RANK:], preferred_element_type=f32
            )
            r.payload[b] = encode(out)

            @pl.when(b == total.me)
            def _():
                r.own[...] = out

            return carry

        lax.fori_loop(0, blocks, project, 0)
        total.start()
        if not last:
            for i in range(TP - 1):
                turned.arrived(i)
            mine = r.turned.at[turned.me]
            pltpu.make_async_copy(mine, mine, r.l_own).wait()
            moves[0].start()
            moves[1].start()
        total.middle(r.own[...])
        total.finish()
        r.put.proj()
        if last:
            gouts.start()
        else:
            turned.sent()
            moves[2].start()

        r.stats[...] = jnp.zeros((2, TP, LANES), f32)

        def rates(b, carry):
            rs = at_block(b, size)
            tail = decode(r.proj[b])[:, RANK:]
            keys = tail + pltpu.roll(tail, 32, 1) + pltpu.roll(tail, 64, 1)
            kq[rs, :] = keys
            norm = square_sum(keys)
            pre = dot(r.proj[b, :, :RANK], r.mats[:, :RANK], ((1,), (1,)))
            for c in range(parts):
                cols = slice(c * LANES, (c + 1) * LANES)
                rate = jax.nn.sigmoid(pre[:, cols] + vec[CONV + 1 : CONV + 2, cols])
                beta[c, rs, :] = rate
                step[c, rs, :] = rate / (1.0 + rate * norm)
                r.stats[0] += row_sum(rate)
                r.stats[1] = jnp.maximum(
                    r.stats[1], jnp.max(rate.reshape(-1, TP, LANES), axis=0)
                )
            return carry

        lax.fori_loop(0, blocks, rates, 0)
        r.put.beta()
        r.put.kq()
        r.need.e()
        r.stats[0] = r.stats[0] * r.scale[...]
        r.stats[1] = r.stats[1] * r.scale[...]

        lane = lanes_of((size, LANES))
        state, wide = r.state, r.wide
        state[...] = jnp.zeros_like(state)

        def block(b, carry):
            r.keep[b] = state[...]
            wide[...] = jnp.dot(spread_keys(kq[at_block(b, size), :], lane), r.e[...], preferred_element_type=f32)

            def one(j, carry):
                t = at_block(b * STEPS + j, TP)
                w = at_block(j, TP)
                acts = [act[c, t, :] for c in range(parts)]
                steps = [step[c, t, :] for c in range(parts)]
                sums = [None] * parts
                for n in range(STATE):
                    key = wide[w, n * LANES : (n + 1) * LANES]
                    query = wide[w, (STATE + n) * LANES : (STATE + n + 1) * LANES]
                    for c in range(parts):
                        s = state[n, c]
                        s = s + (steps[c] * key) * (acts[c] - key * s)
                        state[n, c] = s
                        sums[c] = s * query if sums[c] is None else sums[c] + s * query
                for c in range(parts):
                    y[c, t, :] = sums[c]
                return carry

            lax.fori_loop(0, STEPS, one, 0)
            rs = at_block(b, size)
            here = pl.ds(pl.multiple_of(b * STEPS, STEPS), STEPS)
            for c in range(parts):
                cols = slice(c * LANES, (c + 1) * LANES)
                gate = entry[parts + c, pl.ds(pl.multiple_of(b * size + halo, TP), size), :]
                skip = vec[CONV + 2 : CONV + 3, cols]
                step[c, rs, :] = (y[c, rs, :] + skip * act[c, rs, :]) * (gate * jax.nn.sigmoid(gate))
                for s in range(TP):
                    r.mixed[s, here, cols] = step[c, pl.ds(b * size + s, STEPS, stride=TP), :].astype(bf16)
            return carry

        early.onward()
        lax.fori_loop(0, blocks // 2, block, 0)
        if last:
            gouts.relay()
        else:
            moves[0].onward()
        lax.fori_loop(blocks // 2, blocks, block, 0)
        early.finish()
        for start in (r.put.y, r.put.keep, r.put.mixed, r.put.wout_all):
            start()
        weight = lambda: r.wout_all[...].reshape(half, width)
        if last:

            def plain(s, carry):
                two = r.mixed[pl.ds(2 * s, 2)].reshape(2 * tokens, half)
                out = dot(two, weight(), ((1,), (0,))).astype(bf16)
                r.part[pl.ds(2 * s, 2)] = out.reshape(2, tokens, width)
                return carry

            lax.fori_loop(0, TP // 4, plain, 0)
            gouts.rest()
            lax.fori_loop(TP // 4, TP // 2, plain, 0)
            r.put.part()
            gouts.finish()
            r.done()
            return
        scatter = Scatter(r.part, r.scatter_buf, r.scatter_sems)
        out_partial(scatter, r.part, r.mixed, weight)
        moves[1].onward()
        r.need.h()
        stream = r.h[...] + scatter.total()
        r.result[...] = stream
        r.normed[...] = (stream * rms(stream) * r.gain[layer + 1 : layer + 2, :]).astype(bf16)
        spread = Gather(r.normed, r.xg1, r.gather_sems)
        spread.start()
        spread.relay()
        moves[2].onward()
        spread.rest()
        spread.finish()
        for move in moves:
            move.finish()
        r.done()

    return call(body, 7 if last else 6, ins, outs, scratch)


def out_partial(scatter, part, left, right, turned=False):
    contract = ((1,), (1,)) if turned else ((1,), (0,))
    for i in range(4):
        slots = [core * WAYS + scatter.turns[i] for core in (1 - scatter.core, scatter.core)]
        rows = left.shape[1]
        both = dot(jnp.concatenate([left[slot] for slot in slots], axis=0), right(), contract).astype(bf16)
        part[slots[0]] = both[:rows]
        part[slots[1]] = both[rows:]
        scatter.to_sibling(i)
        if i >= 1:
            scatter.across(i - 1)
    scatter.sums()


class Reduce:
    @staticmethod
    def sems(dma, zh_size):
        far = max(1, zh_size - 1)
        return [dma, dma, dma((far,)), dma((far,))]

    @staticmethod
    def buffers(zh_size, block):
        return [
            pltpu.VMEM((zh_size,) + block, bf16), pltpu.VMEM((zh_size,) + block, bf16),
            pltpu.VMEM((max(1, zh_size - 1),) + block, bf16),
        ]

    def __init__(self, zh_size, src, buffers, sems):
        self.zh_size, self.src = zh_size, src
        self.near, self.mine, self.buf = buffers
        self.x_send, self.x_recv, self.z_send, self.z_recv = sems
        self.x, _, self.zh, _ = place()
        self.side, self.far = dp_peers(zh_size)

    def start(self):
        half = self.src.at[pl.ds((1 - self.x) * self.zh_size, self.zh_size)]
        self.over = remote(half, self.near, self.x_send, self.x_recv, self.side)
        self.over.start()

    def middle(self):
        self.over.wait_recv()
        for k in range(self.zh_size):
            self.mine[k] = (
                self.src[self.x * self.zh_size + k].astype(f32) + self.near[k].astype(f32)
            ).astype(bf16)
        self.along = [
            remote(self.mine.at[to_z], self.buf.at[k], self.z_send.at[k], self.z_recv.at[k], target)
            for k, (target, to_z, _) in enumerate(self.far)
        ]
        for copy in self.along:
            copy.start()

    def total(self):
        value = self.src[self.x * self.zh_size + self.zh].astype(f32) + self.near[self.zh].astype(f32)
        for k in range(self.zh_size - 1):
            self.along[k].wait_recv()
            value = value + self.buf[k].astype(f32)
        self.over.wait_send()
        for copy in self.along:
            copy.wait_send()
        return value


def backward_layer(zh_size, layer, kept, gog, wout, mats, vec, xg, win, gain, h, grad, late=None, part=None):
    tokens, width = xg.shape[1], xg.shape[2]
    half = win.shape[1] // 2
    parts = half // LANES
    rows = tokens * TP
    size = STEPS * TP
    blocks = rows // size
    halo = (CONV - 1) * TP
    groups = 2 * zh_size
    share = half // groups
    deep = width // (2 * groups)
    far = max(1, zh_size - 1)
    dma = pltpu.SemaphoreType.DMA
    onward = part is not None
    ins = dict(entry=(kept.entry, EARLY), kq=(kept.kq, EARLY), beta=(kept.beta, EARLY), proj=(kept.proj, EARLY))
    ins.update(
        mats=(mats, EARLY), wout=(wout, HB), vec=(vec, VM), gain=(gain, VM), h=(h, EARLY), grad=(grad, EARLY),
        mixed=(kept.mixed, HB), e=(spreader(), EARLY), fold=(folder(), EARLY), keep=(kept.keep, HB), gouts=(gog, HB), y=(kept.y, HB), xg=(xg, HB), win=(win, HB),
    )
    outs = dict(
        prev=(struct(tokens, width), VM), ginner=(struct(groups, 2, deep, half, dtype=bf16), LATE),
        near=(struct(zh_size, 2, deep, half, dtype=bf16), HB), ggate=(struct(2, deep, half, dtype=bf16), VM), gwout=(struct(share, width), VM),
        gmats=(struct(half, 3 * LANES, dtype=bf16), VM), gvec=(struct(8, half), VM),
        ggain=(struct(1, width), VM),
    )
    block_f32 = pltpu.VMEM((parts, rows, LANES), f32)
    scratch = dict(
        a=pltpu.VMEM((TP, tokens, width), bf16), b=pltpu.VMEM(win.shape, bf16),
        gs=block_f32, act=block_f32, gact=block_f32,
        step=pltpu.VMEM((parts, rows + halo, LANES), f32),
        states=pltpu.VMEM((STEPS + 1, STATE, parts, TP, LANES), f32),
        lam=pltpu.VMEM((STATE, parts, TP, LANES), f32), wide=pltpu.VMEM((size, 32 * LANES), f32),
        gstep=pltpu.VMEM((parts, size, LANES), f32),
        gentry=pltpu.VMEM((TP, tokens, 2 * half), bf16),
        payload=pltpu.VMEM((TP, size, 2 * LANES), bf16), parts=pltpu.VMEM((TP - 1, size, 2 * LANES), bf16),
        total=pltpu.VMEM((TP, size, 2 * LANES), bf16), own=pltpu.VMEM((size, 2 * LANES), f32),
        sums=pltpu.VMEM((8, parts, TP, LANES), f32),
        grate=pltpu.VMEM((half, LANES), f32), gselect=pltpu.VMEM((half, 2 * LANES), f32),
        gwo=pltpu.VMEM((groups, share, width), bf16), gwg=pltpu.VMEM((groups, 2, deep, half), bf16),
        gate_buf=Reduce.buffers(zh_size, (2, deep, half)), gate_sems=Reduce.sems(dma, zh_size),
        keeps=pltpu.VMEM((2, STATE, parts, TP, LANES), f32), keep_sems=dma((2,)),
        scatter_buf=Scatter.buffers((tokens, width)), reduce_buf=Reduce.buffers(zh_size, (share, width)),
        sum_sems=Sum.sems(dma), scatter_sems=Scatter.sems(dma), reduce_sems=Reduce.sems(dma, zh_size),
        loads=dma((7,)), over=[dma, dma],
    )
    if onward:
        outs.update(gog=(struct(TP, tokens, width, dtype=bf16), HB))
        ins.update(part=(part, HB))
        outs.update(parts_all=(struct(*part.shape, dtype=bf16), HB))
        scratch.update(part_sems=[dma((TP - 1,)), dma((TP - 1,)), dma])
        scratch.update(gout=pltpu.VMEM((tokens, width), bf16), gather_sems=Gather.sems(dma))
    if late is not None:
        ins.update(late_in=(late, HB))
        outs.update(late=(struct(far, *late.shape[1:], dtype=bf16), HB))
        scratch.update(late_sems=[dma((far,)), dma((far,))])

    def body(r):
        x, core, zh, q = place()
        side, far_ones = dp_peers(zh_size)
        greet([p[0] for p in tp_peers()] + [side] + [f[0] for f in far_ones])
        entry, act, step, beta, kq = r.entry, r.act, r.step, r.beta, r.kq
        gs, gact, sums, gstep = r.gs, r.gact, r.sums, r.gstep
        vec = r.vec.at[8 * layer : 8 * (layer + 1)]
        loads = [
            pltpu.make_async_copy(src, dst, r.loads.at[i])
            for i, (src, dst) in enumerate(
                (
                    (r.gouts, r.a), (r.mixed, r.gentry.at[:, :, :half]),
                    (r.wout.at[:, : 2 * half], r.b.at[:half]), (r.wout.at[:, 2 * half :], r.b.at[half : 2 * half]),
                    (r.y, gact), (r.xg, r.a), (r.win, r.b),
                )
            )
        ]
        for copy in loads[:4]:
            copy.start()
        r.load()
        loads[4].start()
        passed = []
        if onward:
            me = core * WAYS + q
            for i, (target, rank, _) in enumerate(tp_peers()):
                copy = remote(
                    r.part.at[rank], r.parts_all.at[me], r.part_sems[0].at[i], r.part_sems[1].at[i], target
                )
                copy.start()
                passed.append(copy)
            passed.append(pltpu.make_async_copy(r.part.at[me], r.parts_all.at[me], r.part_sems[2]))
            passed[-1].start()
        if late is not None:
            for k, (target, to_z, _) in enumerate(far_ones):
                copy = remote(
                    r.late_in.at[to_z], r.late.at[k], r.late_sems[0].at[k], r.late_sems[1].at[k], target
                )
                copy.start()
                passed.append(copy)
        sums[...] = jnp.zeros_like(sums)
        r.grate[...] = jnp.zeros_like(r.grate)
        r.gselect[...] = jnp.zeros_like(r.gselect)

        loads[0].wait()
        loads[1].wait()

        def outer(c, carry):
            left = r.gentry[:, :, at_block(c, LANES)].reshape(rows, LANES)
            out = dot(left, r.a[...].reshape(rows, width), ((0,), (0,))).astype(bf16)
            each = LANES // share
            r.gwo[pl.ds(c * each, each)] = out.reshape(each, share, width)
            return carry

        lax.fori_loop(0, parts, outer, 0)
        reduce = Reduce(zh_size, r.gwo, r.reduce_buf, r.reduce_sems)
        reduce.start()
        loads[2].wait()
        loads[3].wait()
        for p in range(TP // 2):

            def columns(n, carry, p=p):
                out = 0.0
                for k in range(2):
                    left = r.a[2 * p : 2 * p + 2, :, 2 * half * k : 2 * half * (k + 1)].reshape(2 * tokens, 2 * half)
                    right = r.b[pl.ds(pl.multiple_of(half * k + n * 2 * LANES, 2 * LANES), 2 * LANES), :]
                    out = out + dot(left, right, ((1,), (1,)))
                for j in range(2):
                    for c in range(2):
                        gs[2 * n + c, pl.ds(2 * p + j, tokens, stride=TP), :] = out[
                            j * tokens : (j + 1) * tokens, c * LANES : (c + 1) * LANES
                        ]
                return carry

            lax.fori_loop(0, half // (2 * LANES), columns, 0)
        loads[5].start()
        loads[6].start()
        r.need.entry()
        r.need.kq()
        r.need.beta()

        def again(b, carry):
            rs = at_block(b, size)
            norm = square_sum(kq[rs, :])
            for c in range(parts):
                conv = conv_of(entry, vec, b * size, size, c)
                act[c, rs, :] = (conv * jax.nn.sigmoid(conv)).astype(bf16).astype(f32)
                rate = beta[c, rs, :]
                step[c, rs, :] = rate / (1.0 + rate * norm)
            return carry

        lax.fori_loop(0, blocks, again, 0)
        loads[4].wait()

        def gates(b, carry):
            rs = at_block(b, size)
            here = pl.ds(pl.multiple_of(b * STEPS, STEPS), STEPS)
            for c in range(parts):
                cols = slice(c * LANES, (c + 1) * LANES)
                gate = entry[parts + c, pl.ds(pl.multiple_of(b * size + halo, TP), size), :]
                sig = jax.nn.sigmoid(gate)
                g = gs[c, rs, :]
                a = act[c, rs, :]
                down = g * (gate * sig)
                gstep[c] = g * (gact[c, rs, :] + vec[CONV + 2 : CONV + 3, cols] * a) * (
                    sig * (1.0 + gate * (1.0 - sig))
                )
                gs[c, rs, :] = down
                sums[CONV + 2, c] += row_sum(down * a)
                for s in range(TP):
                    r.gentry[s, here, half + c * LANES : half + (c + 1) * LANES] = gstep[
                        c, pl.ds(s, STEPS, stride=TP), :
                    ].astype(bf16)
            return carry

        lax.fori_loop(0, blocks, gates, 0)
        loads[5].wait()
        tile = 2 * LANES

        def outer_in(out_ref, first, i, carry):
            left = r.a[:, :, at_block(i, tile)].reshape(rows, tile)
            out = dot(left, r.gentry[:, :, first : first + half].reshape(rows, half), ((0,), (0,))).astype(bf16)
            each = tile // deep
            for e in range(each):
                d = i * each + e
                xx, cc, zz = d // (2 * zh_size), lax.rem(d // zh_size, 2), lax.rem(d, zh_size)
                out_ref[xx * zh_size + zz, cc] = out[e * deep : (e + 1) * deep]
            return carry

        lax.fori_loop(0, width // tile, lambda i, k: outer_in(r.gwg, half, i, k), 0)
        gate_reduce = Reduce(zh_size, r.gwg, r.gate_buf, r.gate_sems)

        lane = lanes_of((size, LANES))
        states, lam, wide = r.states, r.lam, r.wide
        lam[...] = jnp.zeros_like(lam)
        plus = lambda a, b: b if a is None else a + b
        total = Sum(r.payload, r.parts, r.total, r.sum_sems)

        def block(bi, carry):
            b = blocks - 1 - bi
            rs = at_block(b, size)
            slot = lax.rem(b, 2)
            pltpu.make_async_copy(r.keep.at[b], r.keeps.at[slot], r.keep_sems.at[slot]).wait()

            @pl.when(b > 0)
            def _():
                ahead = pltpu.make_async_copy(r.keep.at[b - 1], r.keeps.at[1 - slot], r.keep_sems.at[1 - slot])
                ahead.start()

            states[0] = r.keeps[slot]
            wide[...] = jnp.dot(spread_keys(kq[rs, :], lane), r.e[...], preferred_element_type=f32)

            def replay(j, carry):
                t, w = at_block(b * STEPS + j, TP), at_block(j, TP)
                acts = [act[c, t, :] for c in range(parts)]
                steps = [step[c, t, :] for c in range(parts)]
                for n in range(STATE):
                    key = wide[w, n * LANES : (n + 1) * LANES]
                    for c in range(parts):
                        s = states[j, n, c]
                        states[j + 1, n, c] = s + (steps[c] * key) * (acts[c] - key * s)
                return carry

            lax.fori_loop(0, STEPS, replay, 0)

            def back(jj, carry):
                j = STEPS - 1 - jj
                t, w = at_block(b * STEPS + j, TP), at_block(j, TP)
                acts = [act[c, t, :] for c in range(parts)]
                steps = [step[c, t, :] for c in range(parts)]
                gsums = [gs[c, t, :] for c in range(parts)]
                first, second = [None] * parts, [None] * parts
                for n in range(STATE):
                    kcols, qcols = slice(n * LANES, (n + 1) * LANES), slice((STATE + n) * LANES, (STATE + n + 1) * LANES)
                    key, query = wide[w, kcols], wide[w, qcols]
                    square = key * key
                    key_term, query_term = None, None
                    for c in range(parts):
                        before, after = states[j, n, c], states[j + 1, n, c]
                        grad = lam[n, c] + gsums[c] * query
                        u = key * before
                        d = acts[c] - u
                        gk = grad * key
                        sg = steps[c] * grad
                        first[c] = plus(first[c], gk * d)
                        second[c] = plus(second[c], gk)
                        key_term = plus(key_term, sg * (d - u))
                        query_term = plus(query_term, gsums[c] * after)
                        lam[n, c] = grad - sg * square
                    wide[w, kcols] = key_term
                    wide[w, qcols] = query_term
                for c in range(parts):
                    gstep[c, w, :] = first[c]
                    gact[c, t, :] = steps[c] * second[c]
                return carry

            lax.fori_loop(0, STEPS, back, 0)
            terms = wide[...]
            high = terms.astype(bf16)
            low = (terms - high.astype(f32)).astype(bf16)
            gkq = jnp.dot(high, r.fold[...], preferred_element_type=f32) + jnp.dot(
                low, r.fold[...], preferred_element_type=f32
            )
            keys = kq[rs, :]
            norm = square_sum(keys)
            gnorm = jnp.zeros((size, 1), f32)
            grates = []
            for c in range(parts):
                cols = slice(c * LANES, (c + 1) * LANES)
                rate = beta[c, rs, :]
                g = gstep[c]
                inverse = 1.0 + rate * norm
                inverse = 1.0 / (inverse * inverse)
                gnorm = gnorm - jnp.sum(g * (rate * rate * inverse), axis=1, keepdims=True)
                grate = g * inverse * rate * (1.0 - rate)
                sums[CONV + 1, c] += row_sum(grate)
                grates.append(grate.astype(bf16))
                gact[c, rs, :] += vec[CONV + 2 : CONV + 3, cols] * gs[c, rs, :]
            grate = jnp.concatenate(grates, axis=1)
            r.grate[...] += dot(grate, r.proj[b, :, :RANK], ((0,), (0,)))
            grank = dot(grate, r.mats[:, :RANK], ((1,), (0,)))
            gkq = gkq + jnp.where(lane < STATE, 2.0 * keys * gnorm, 0.0)
            out = jnp.concatenate([grank, gkq], axis=1)
            r.payload[b] = encode(out)

            @pl.when(b == total.me)
            def _():
                r.own[...] = out

            return carry

        for wait in (r.need.proj, r.need.mats, r.need.e, r.need.fold):
            wait()
        last = (blocks - 1) % 2
        pltpu.make_async_copy(r.keep.at[blocks - 1], r.keeps.at[last], r.keep_sems.at[last]).start()
        lax.fori_loop(0, blocks // 2, block, 0)
        reduce.middle()
        gate_reduce.start()
        lax.fori_loop(blocks // 2, blocks, block, 0)
        total.start()
        total.middle(r.own[...])
        if onward:
            gate_reduce.middle()
        total.finish()
        if not onward:
            gate_reduce.middle()
        step[:, rows:, :] = jnp.zeros((parts, halo, LANES), f32)
        gconv = step

        def convs(b, carry):
            rs = at_block(b, size)
            gp = r.total[b]
            gp = jnp.where(lanes_of(gp.shape) < RANK + 2 * STATE, gp.astype(f32), 0.0).astype(bf16)
            r.gselect[...] += dot(wide_of(act, rs, parts).astype(bf16), gp, ((0,), (0,)))
            more = dot(gp, r.mats[:, RANK:], ((1,), (1,)))
            for c in range(parts):
                conv = conv_of(entry, vec, b * size, size, c)
                sig = jax.nn.sigmoid(conv)
                g = (gact[c, rs, :] + more[:, c * LANES : (c + 1) * LANES]) * (sig * (1.0 + conv * (1.0 - sig)))
                gconv[c, rs, :] = g
                sums[CONV, c] += row_sum(g)
                for j in range(CONV):
                    inner = entry[c, pl.ds(pl.multiple_of(b * size + TP * j, TP), size), :]
                    sums[j, c] += row_sum(g * inner)
            return carry

        lax.fori_loop(0, blocks, convs, 0)

        def inners(b, carry):
            rs = at_block(b, size)
            here = pl.ds(pl.multiple_of(b * STEPS, STEPS), STEPS)
            for c in range(parts):
                cols = slice(c * LANES, (c + 1) * LANES)
                value = None
                for j in range(CONV):
                    at = pl.ds(pl.multiple_of(b * size + TP * (CONV - 1 - j), TP), size)
                    value = plus(value, vec[j : j + 1, cols] * gconv[c, at, :])
                gs[c, rs, :] = value
                for s in range(TP):
                    at = pl.ds(b * size + s, STEPS, stride=TP)
                    r.gentry[s, here, cols] = gs[c, at, :].astype(bf16)
            return carry

        lax.fori_loop(0, blocks, inners, 0)
        lax.fori_loop(0, width // tile, lambda i, k: outer_in(r.ginner, 0, i, k), 0)
        over = remote(
            r.ginner.at[pl.ds((1 - x) * zh_size, zh_size)], r.near, r.over[0], r.over[1], side
        )
        over.start()
        r.put.ginner()
        loads[6].wait()
        scatter = Scatter(r.a, r.scatter_buf, r.scatter_sems)
        out_partial(scatter, r.a, r.gentry, lambda: r.b[...], turned=True)
        r.gmats[:, :RANK] = r.grate[...].astype(bf16)
        r.gmats[:, RANK:] = r.gselect[...].astype(bf16)
        for j in range(8):
            for c in range(parts):
                r.gvec[j : j + 1, c * LANES : (c + 1) * LANES] = jnp.sum(sums[j, c], axis=0, keepdims=True)
        r.gwout[...] = reduce.total()
        r.ggate[...] = gate_reduce.total().astype(bf16)
        gnormed = scatter.total()
        r.need.h()
        r.need.grad()
        stream = r.h[...]
        scale = rms(stream)
        r.ggain[...] = jnp.sum(gnormed * stream * scale, axis=0, keepdims=True)
        scaled = gnormed * r.gain[layer : layer + 1, :]
        grad = r.grad[...] + scale * scaled - stream * (scale * scale * scale) * jnp.mean(
            stream * scaled, axis=-1, keepdims=True
        )
        r.prev[...] = grad
        if onward:
            r.gout[...] = grad.astype(bf16)
            spread = Gather(r.gout, r.gog, r.gather_sems)
            spread.start()
            spread.relay()
            spread.rest()
            spread.finish()
        for copy in passed:
            copy.wait()
        over.wait()
        r.done()

    return call(body, 9 if onward else 8, ins, outs, scratch)


def closing(zh_size, inner, near, mats, small, stats, gain, turns, share, width, select):
    groups = 2 * zh_size
    count = groups * TP
    far_n = max(1, zh_size - 1)
    dma = pltpu.SemaphoreType.DMA
    depth, half = inner.shape[3] // WAYS, inner.shape[4]
    gains = width // count
    every = (2, zh_size) + stats.shape
    v = pltpu.VMEM
    ins = dict(
        inner=(inner, VM), near=(near, VM), mats=(mats, VM), small=(small, VM), stats=(stats, VM), gain=(gain, VM),
        t0=(turns[0], VM), t1=(turns[1], VM), t2=(turns[2], VM),
    )
    outs = dict(
        gin=(struct(LAYERS, depth, 2 * count * share), VM), gselect=(struct(LAYERS, share, select), VM),
        grate=(struct(LAYERS, RANK, share), VM),
        ggain=(struct(LAYERS, gains), VM), gtaps=(struct(LAYERS, CONV, share), VM), gshift=(struct(LAYERS, share), VM),
        grate_shift=(struct(LAYERS, share), VM), gskip=(struct(LAYERS, share), VM), stats_all=(struct(*stats.shape), VM),
    )

    def chunk(shape, dtype):
        return [
            v(shape[1:], dtype), v((far_n,) + shape[2:], dtype), dma((far_n,)), dma((far_n,)), v(shape[1:], dtype), dma, dma
        ]

    piece = inner.shape[:2] + inner.shape[3:]
    scratch = dict(
        vectors=v(small.shape, f32), stats_v=v(every, f32), stats_t=v((TP - 1,) + stats.shape, f32),
        gain_t=v((TP - 1,) + gain.shape[1:], f32), win_t=v((2, WAYS, depth, half), bf16),
        total=v(small.shape[2:], f32),
        g_sems=[dma((TP - 1,))] * 2, s_sems=[dma((TP - 1,))] * 2,
    )
    scratch.update(
        boxes=v((4, TP, depth, half), bf16), turn_sems=[[dma((TP - 1,)), dma((TP - 1,))] for _ in range(4)],
        chunks=[chunk(piece, bf16), chunk(piece, bf16), chunk(mats.shape, bf16), chunk(small.shape, f32), chunk(every, f32)],
    )

    def body(r):
        x, core, zh, q = place()
        me = core * WAYS + q
        peers = tp_peers()
        side, far = dp_peers(zh_size)
        greet([p[0] for p in peers] + [side] + [f[0] for f in far])
        sent, full = [], []

        def join(a, b, peaks):
            a, b = a.astype(f32), b.astype(f32)
            if peaks:
                line = lax.broadcasted_iota(jnp.int32, a.shape, len(a.shape) - 2)
                return jnp.where(line < 4, a + b, jnp.maximum(a, b))
            return a + b

        class Chunk:
            def __init__(self, number, src, near=None):
                self.src, self.peaks = src, number == 4
                self.mine, self.buf, self.z_send, self.z_recv, spare, self.x_send, self.x_recv = r.chunks[number]
                self.near = spare if near is None else near

            def start(self):
                self.over = remote(self.src.at[1 - x], self.near, self.x_send, self.x_recv, side)
                self.over.start()
                sent.append(self.over)

            def middle(self, arrived=False):
                if not arrived:
                    self.over.wait_recv()
                mine, buf = self.mine, self.buf
                mine[...] = join(self.src[x], self.near[...], self.peaks).astype(mine.dtype)
                self.along = [
                    remote(mine.at[to_z], buf.at[k], self.z_send.at[k], self.z_recv.at[k], target)
                    for k, (target, to_z, _) in enumerate(far)
                ]
                for copy in self.along:
                    copy.start()
                    sent.append(copy)

            def total(self):
                value = join(self.src[x, zh], self.near[zh], self.peaks)
                for k, copy in enumerate(self.along):
                    copy.wait_recv()
                    value = join(value, self.buf[k], self.peaks)
                return value

        def turn(src, i):
            box, sems = r.boxes.at[i], r.turn_sems[i]
            for k, (target, rank, _) in enumerate(peers):
                copy = remote(src(rank), box.at[me], sems[0].at[k], sems[1].at[k], target)
                copy.start()
                full.append(copy)
            box[me] = src(me)[...]

        cs = [Chunk(c, r.inner.at[:, :, c], r.near.at[:, c]) for c in range(2)]
        cs[0].middle(arrived=True)
        cs[1].middle(arrived=True)
        gained, shown = [], []
        for i, (target, rank, _) in enumerate(peers):
            for src, buf, sems, copies in (
                (r.gain.at[rank], r.gain_t, r.g_sems, gained),
                (r.stats, r.stats_t, r.s_sems, shown),
            ):
                copy = remote(src, buf.at[i], sems[0].at[i], sems[1].at[i], target)
                copy.start()
                copies.append(copy)
                sent.append(copy)
        mats_c = Chunk(2, r.mats)
        mats_c.start()
        sources = (r.t0, r.t1, r.t2)
        for i in range(3):
            turn(lambda rank, i=i: sources[i].at[rank], i + 1)
        total = r.gain[me]
        seen = r.stats[...]
        for i in range(TP - 1):
            gained[i].wait_recv()
            total = total + r.gain_t[i]
            shown[i].wait_recv()
            seen = join(seen, r.stats_t[i], True)
        r.vectors[...] = r.small[...]
        for l in range(LAYERS):
            for g in range(groups):
                at = l * groups + g
                r.vectors[g // zh_size, g % zh_size, l * 16 + 8 : l * 16 + 9, :] = total[at : at + 1, :]
        r.stats_v[...] = jnp.broadcast_to(seen, every)
        rest = [mats_c, Chunk(3, r.vectors), Chunk(4, r.stats_v)]
        for c in rest[1:]:
            c.start()
        for c in rest:
            c.middle()
        for c in range(2):
            r.win_t[c] = cs[c].total().astype(bf16).reshape(WAYS, depth, half)
        turn(lambda rank: r.win_t.at[rank // WAYS, lax.rem(rank, WAYS)], 0)
        m = rest[0].total()
        for l in range(LAYERS):
            base = 3 * LANES * l
            r.grate[l] = m[:, base : base + RANK].T
            r.gselect[l] = m[:, base + RANK : base + RANK + select]
        r.total[...] = rest[1].total()
        for l in range(LAYERS):
            r.gtaps[l] = r.total[16 * l : 16 * l + CONV, :share]
            for out, j, size in (
                (r.gshift, CONV, share), (r.grate_shift, CONV + 1, share), (r.gskip, CONV + 2, share), (r.ggain, 8, gains)
            ):
                out[l : l + 1, :] = r.total[16 * l + j : 16 * l + j + 1, :size]
        r.stats_all[...] = rest[2].total()

        def lay(i):
            for rank in range(TP):
                for g in range(groups):
                    d = ((g // zh_size * 2 + rank // WAYS) * zh_size + g % zh_size) * WAYS + rank % WAYS
                    first = i % 2 * count * share + d * share
                    r.gin[i // 2, :, first : first + share] = r.boxes[i, rank, :, g * share : (g + 1) * share].astype(f32)

        early, late = full[: 3 * (TP - 1)], full[3 * (TP - 1) :]
        for copy in early:
            copy.wait_recv()
        for i in (1, 2, 3):
            lay(i)
        for copy in late:
            copy.wait_recv()
        lay(0)
        for copy in sent + full:
            copy.wait_send()

    return call(body, 5, ins, outs, scratch)


def on_device(
    hidden, cotangent, groups, group_weights, input_weight, select_weight, rate_weight,
    output_weight, norm_gain, conv_taps, conv_shift, rate_shift, skip_gain,
):
    fsdp = lax.axis_size("fsdp")
    zh_size = fsdp // WAYS
    count = 2 * 2 * fsdp
    group_count = 2 * zh_size
    share = conv_shift.shape[1]
    gains = norm_gain.shape[1]
    depth = input_weight.shape[1]
    half = group_count * share
    x, core, zh, q = place()

    labels = jnp.arange(group_weights.shape[0])
    own_weight = jnp.sum(jnp.where(groups[:, None] == labels[None, :], group_weights[None, :], 0.0))

    wins = input_weight
    if share % LANES:
        wins = wins.reshape(LAYERS, depth, 2, 2, 2, zh_size, WAYS, share)
        wins = wins.transpose(0, 4, 6, 1, 2, 3, 5, 7).reshape(LAYERS, TP, depth, 2 * half)
    mats = jnp.concatenate([rate_weight.swapaxes(1, 2), select_weight], axis=2)
    mats = jnp.pad(mats, ((0, 0), (0, 0), (0, 3 * LANES - mats.shape[2])))
    vectors = [conv_taps, conv_shift[:, None], rate_shift[:, None], skip_gain[:, None], skip_gain[:, None]]
    small = jnp.concatenate(vectors, axis=1).astype(f32).reshape(8 * LAYERS, share)
    small = jnp.pad(small, ((0, 0), (0, LANES - share)))
    misc = jnp.pad(norm_gain.astype(f32), ((0, 0), (0, LANES - gains)))
    misc = jnp.concatenate([misc, jnp.full((8 - LAYERS, LANES), own_weight)])

    flat = lambda a: a.reshape(half, -1)
    h0 = hidden[0]
    start = opening(zh_size, gains, share, wins, small, misc, mats, h0, cotangent[0])
    vec, gain, scale = start.vec, start.gains, start.scale
    win0, mat0 = start.win_all.reshape(count * depth, -1), flat(start.mats_all)
    one = forward_layer(
        zh_size, 0, start.xg, win0, mat0, output_weight, vec, scale,
        nxt=types.SimpleNamespace(h=h0, gain=gain, win=wins, mats=mats),
    )
    win1, mat1 = one.win1_all.reshape(count * depth, -1), flat(one.mats1_all)
    h1 = one.result
    two = forward_layer(zh_size, 1, one.xg1, win1, mat1, output_weight, vec, scale, gout=start.gout)

    down1 = backward_layer(
        zh_size, 1, two, two.gog, flat(two.wout_all), mat1, vec, one.xg1, win1, gain, h1, start.grad,
        part=two.part,
    )
    stream = h1 + jnp.sum(down1.parts_all.astype(f32), axis=0)
    blocks = (2, zh_size) + down1.ginner.shape[1:]
    pick = lambda a, i: lax.dynamic_index_in_dim(a, i, 0, keepdims=False)
    summed = pick(down1.ginner.reshape(blocks), x).astype(f32) + down1.near.astype(f32)
    down0 = backward_layer(
        zh_size, 0, one, down1.gog, flat(one.wout_all), mat0, vec, start.xg, win0, gain, h0, down1.prev,
        late=summed.astype(bf16),
    )
    late = pick(summed, zh)
    for k in range(zh_size - 1):
        late = late + down0.late[k].astype(f32)

    sums = [jnp.sum(o.stats[0]) for o in (one, two)]
    peaks = [jnp.max(o.stats[1]) for o in (one, two)]
    pad = [jnp.zeros((), f32)] * (4 - LAYERS)
    own_stats = jnp.broadcast_to(jnp.stack(sums + pad + peaks + pad)[:, None], (8, LANES))
    downs = (down0, down1)
    small = jnp.stack([down.gvec for down in downs]).reshape(LAYERS, 8, group_count, share)
    small = jnp.pad(small.transpose(2, 0, 1, 3), ((0, 0), (0, 0), (0, 8), (0, LANES - share)))
    small = small.reshape(2, zh_size, 16 * LAYERS, LANES)
    spread_gain = jnp.stack([down.ggain[0] for down in downs]).reshape(LAYERS, 2, 2, zh_size, WAYS, gains)
    spread_gain = spread_gain.transpose(2, 4, 0, 1, 3, 5).reshape(TP, LAYERS * group_count, gains)
    spread_gain = jnp.pad(spread_gain, ((0, 0), (0, -LAYERS * group_count % 8), (0, LANES - gains)))
    mats = jnp.concatenate([down.gmats for down in downs], axis=1).reshape(2, zh_size, share, -1)
    turns = [down0.ggate, late.astype(bf16), down1.ggate]
    end = closing(
        zh_size, down0.ginner.reshape(blocks), down0.near, mats, small, own_stats, spread_gain,
        [t.reshape(TP, depth, half) for t in turns], share, output_weight.shape[2], select_weight.shape[2],
    )
    stats = end.stats_all
    beta_mean = stats[:LAYERS, 0] / (count * hidden.shape[1] * INNER)
    beta_max = stats[4 : 4 + LAYERS, 0]
    gwout = jnp.stack([down.gwout for down in downs])
    return (
        stream[None], down0.prev[None], end.gin, end.gselect, end.grate, gwout, end.ggain, end.gtaps, end.gshift,
        end.grate_shift, end.gskip, beta_mean, beta_max,
    )


def solution(mesh):
    both = ("dp", "fsdp")
    placed = (
        P(both, None, None), P(both, None, None), P(both), P(),
        P(None, both, None), P(None, both, None), P(None, None, both), P(None, both, None),
        P(None, both), P(None, None, both), P(None, both), P(None, both), P(None, both),
    )
    return jax.shard_map(
        on_device,
        mesh=mesh,
        in_specs=placed,
        out_specs=(P(both, None, None), P(both, None, None)) + placed[4:] + (P(), P()),
        check_vma=False,
    )
```
